32 devices in a mesh: seq: 16 (over z, y, x), head: 2 (over core).
Axes of the slice: x: 2, y: 2, z: 4, core: 2. Of those that a mesh axis runs over, the one named last changes fastest.
Arguments:
- tokens: bfloat16 [4, 4096, 2048], P(None, 'seq'), may hold values from -6 to 6
- norm_gain: float32 [2048], replicated, may hold values from 0.1 to 1.9
- in_weight: bfloat16 [2048, 2, 4096], P(None, None, 'head'), may hold values from -0.125 to 0.125
- bc_weight: bfloat16 [2048, 256], replicated, may hold values from -0.125 to 0.125
- dt_weight: bfloat16 [2048, 64], P(None, 'head'), may hold values from -0.125 to 0.125
- dt_bias: float32 [64], P('head'), may hold values from -1 to 0.5
- a_log: float32 [64], P('head'), may hold values from -14 to -2
- conv_weight: float32 [4, 4096], P(None, 'head'), may hold values from -3 to 3
- conv_bias: float32 [4096], P('head'), may hold values from -0.5 to 0.5
- bc_conv_weight: float32 [4, 256], replicated, may hold values from -3 to 3
- bc_conv_bias: float32 [256], replicated, may hold values from -0.5 to 0.5
- d_skip: float32 [64], P('head'), may hold values from 0.5 to 1.5
- gate_gain: float32 [4096], P('head'), may hold values from 0.1 to 1.9
- out_weight: bfloat16 [2048, 4096], P(None, 'head'), may hold values from -0.09375 to 0.09375
- cotangent: bfloat16 [4, 4096, 2048], P(None, 'seq'), may hold values from -6 to 6
- seq_lengths: int32 [2, 3], replicated, may hold values from 1 to 2048, 4096 in all within a row
Outputs:
- block_out: bfloat16 [4, 4096, 2048], P(None, 'seq', 'head')
- grad_tokens: float32 [4, 4096, 2048], P(None, 'seq')
- grad_norm_gain: float32 [2048], replicated
- grad_in_weight: float32 [2048, 2, 4096], P('seq', None, 'head')
- grad_bc_weight: float32 [2048, 256], replicated
- grad_dt_weight: float32 [2048, 64], P(None, 'head')
- grad_dt_bias: float32 [64], P('head')
- grad_a_log: float32 [64], P('head')
- grad_d_skip: float32 [64], P('head')
- grad_conv_weight: float32 [4, 4096], P(None, 'head')
- grad_conv_bias: float32 [4096], P('head')
- grad_bc_conv_weight: float32 [4, 256], replicated
- grad_bc_conv_bias: float32 [256], replicated
- grad_gate_gain: float32 [4096], P('head')
- grad_out_weight: float32 [2048, 4096], P('seq', 'head')
The draws below stay inside these ranges and needn't reach their ends.
Inputs may be any that keep to these rules, and one draw needn't show every extreme that they name: `seq_lengths`: row m lists, in order, the lengths of the sequences packed into micro-batch m; each row sums to 4096 and its largest entry is 2048.
All inputs are finite; a program needn't handle non-finite values.
Results may differ from the reference program's by a relative error of at most 0.006.
The reference program's roundings to bfloat16 on the way count: a program that leaves them out, or rounds other values in their place, can miss the bound.
Values sent between devices are 32-bit elements; how exact they have to be, the bound alone decides.
A program may use at most 384 MiB of HBM per device.

```python
import math
import jax
import jax.numpy as jnp
import numpy as np
from jax import lax

D = 2048
NHEADS = 64
HEADDIM = 64
NSTATE = 128
DINNER = 4096
CONV = 4
BLOCK = 256
MICRO = 4
TOK_MB = 4096
SHORT_LEN = 2048
SHORT_SEQS = 3


def draw_a_log(key, part):
    key = jax.random.fold_in(key, 11)
    pick_key, slow_key, fast_key = jax.random.split(key, 3)
    share = 0.5
    slow = jax.random.uniform(slow_key, (NHEADS,), jnp.float32, math.log(0.05 / TOK_MB), math.log(0.4 / TOK_MB))
    fast = jax.random.uniform(fast_key, (NHEADS,), jnp.float32, math.log(0.04), math.log(0.12))
    chosen = jax.random.uniform(pick_key, (NHEADS,), jnp.float32) < share
    return jnp.where(chosen, slow, fast).astype(jnp.float32)


def levels(key, shape, shards, low, top_value):
    def one(dim, blocks):
        heights = jax.random.uniform(jax.random.fold_in(jax.random.fold_in(key, 6), dim), (blocks,), jnp.float32, low / len(shards), top_value / len(shards))
        return jnp.repeat(jnp.exp(heights), shape[dim] // blocks).reshape((-1,) + (1,) * (len(shape) - dim - 1))

    factor_of = one(*shards[0])
    for cut in shards[1:]:
        factor_of = factor_of * one(*cut)
    return factor_of


def length_profile(amount, total, bound, lean):
    portions = [(1 << 20) // math.isqrt(rank ** lean) + 1 for rank in range(2, amount + 1)]
    surplus, counts = total - bound - (amount - 1), [1] * (amount - 1)
    while surplus > 0:
        free = [i for i in range(amount - 1) if counts[i] < bound]
        pool, left = sum([portions[i] for i in free]), surplus
        for i in free:
            more = min(bound - counts[i], max(1, left * portions[i] // pool), surplus)
            counts[i] = counts[i] + more
            surplus = surplus - more
    return np.array([bound] + counts)


def uneven_parts(own_key, count, total, bound, skew):
    if count == 2:
        one = jax.random.randint(own_key, (), max(1, total - bound), min(bound, total - 1) + 1)
        return jnp.stack([one, total - one])
    sizes = jnp.asarray(length_profile(count, total, bound, skew), jnp.int32)
    twos = (count - 1) // 2
    giver, receiver = sizes[1:1 + 2 * twos:2], sizes[2:2 + 2 * twos:2]
    room = jnp.minimum(giver - 1, bound - receiver)
    shifted = jax.random.randint(jax.random.fold_in(own_key, 1), (twos,), 0, 1 << 20) % (room + 1)
    sizes = sizes.at[1:1 + 2 * twos:2].set(giver - shifted).at[2:2 + 2 * twos:2].set(receiver + shifted)
    return sizes[jax.random.permutation(jax.random.fold_in(own_key, 2), count)]


def centred(own_key, dims, scale, bound, shards=(), kind=jnp.bfloat16):
    factor_of = levels(own_key, dims, shards, -0.22, 0.18) if shards else 1.0
    drawn = jax.random.normal(own_key, dims, jnp.float32) * scale * factor_of
    return jnp.minimum(jnp.maximum(drawn, -bound), bound).astype(kind)


def setup_inputs(seed: int = 0) -> dict:
    splits = jax.random.split(jax.random.key(seed), 17)
    tokens = centred(splits[0], (MICRO, TOK_MB, D), 1.0, 6.0, ((1, 16),))
    norm_gain = jnp.clip(1.0 + 0.18 * jax.random.normal(splits[1], (D,), jnp.float32), 0.1, 1.9)
    in_weight = centred(splits[2], (D, 2, DINNER), D ** -0.5, 0.125, ((2, 2),))
    bc_weight = centred(splits[3], (D, 2 * NSTATE), D ** -0.5, 0.125)
    dt_weight = centred(splits[4], (D, NHEADS), D ** -0.5, 0.125, ((1, 2),))
    dt_bias = jnp.clip(-1.0 + 1.5 * jax.random.uniform(splits[5], (NHEADS,), jnp.float32) ** levels(splits[5], (NHEADS,), ((0, 2),), -0.2, 0.2), -1.0, 0.5)
    a_log = draw_a_log(jax.random.fold_in(splits[16], 71), 0)
    conv_weight = centred(splits[7], (CONV, DINNER), CONV ** -0.5, 3.0, ((1, 2),), jnp.float32)
    conv_bias = jnp.clip(jax.random.uniform(splits[8], (DINNER,), jnp.float32, -0.5, 0.5) * levels(splits[8], (DINNER,), ((0, 2),), -0.4, 0.0), -0.5, 0.5)
    bc_conv_weight = centred(splits[9], (CONV, 2 * NSTATE), CONV ** -0.5, 3.0, (), jnp.float32)
    bc_conv_bias = jnp.clip(jax.random.uniform(splits[10], (2 * NSTATE,), jnp.float32, -0.5, 0.5), -0.5, 0.5)
    d_skip = jnp.clip(0.5 + 1.0 * jax.random.uniform(splits[11], (NHEADS,), jnp.float32) ** levels(splits[11], (NHEADS,), ((0, 2),), -0.2, 0.2), 0.5, 1.5)
    gate_gain = jnp.clip(1.0 + 0.18 * jax.random.normal(splits[12], (DINNER,), jnp.float32), 0.1, 1.9)
    out_weight = centred(splits[13], (D, DINNER), DINNER ** -0.5, 0.09375, ((1, 2),))
    cotangent = centred(splits[14], (MICRO, TOK_MB, D), 1.0, 6.0, ((1, 16),))
    seq_lengths = jax.vmap(lambda own: uneven_parts(own, SHORT_SEQS, TOK_MB, SHORT_LEN, 1))(jax.random.split(splits[15], (MICRO // 2))).reshape((MICRO // 2, SHORT_SEQS)).astype(jnp.int32)
    return {"tokens": tokens, "norm_gain": norm_gain, "in_weight": in_weight, "bc_weight": bc_weight, "dt_weight": dt_weight, "dt_bias": dt_bias, "a_log": a_log, "conv_weight": conv_weight, "conv_bias": conv_bias, "bc_conv_weight": bc_conv_weight, "bc_conv_bias": bc_conv_bias, "d_skip": d_skip, "gate_gain": gate_gain, "out_weight": out_weight, "cotangent": cotangent, "seq_lengths": seq_lengths}


EPSILON = 1e-05
HIGHEST = lax.Precision.HIGHEST

@jax.custom_vjp
def low(v):
    return lax.optimization_barrier(v.astype(jnp.bfloat16)).astype(jnp.float32)

@jax.custom_vjp
def low_back(v):
    return v

def low_keep(v):
    return (low(v), None)

def low_pass(kept, grad):
    return (grad,)

def back_keep(v):
    return (v, None)

def back_low(kept, grad):
    return (low(grad),)
low.defvjp(low_keep, low_pass)
low_back.defvjp(back_keep, back_low)

def segment_ids(seq_lengths, first, count, micro):
    places = first + jnp.arange(count, dtype=jnp.int32)
    starts = jnp.cumsum(seq_lengths, axis=-1).astype(jnp.int32) - seq_lengths
    short_ids = lax.optimization_barrier(jnp.sum((starts[:, None, :] <= places[None, :, None]).astype(jnp.int32), axis=-1)) - 1
    long_ids = jnp.zeros((micro - seq_lengths.shape[0], count), jnp.int32)
    labels = jnp.concatenate([short_ids, long_ids], axis=0)
    return jnp.where(places[None, :] >= 0, labels, -1)

def rms_scale(values, gain):
    return values * lax.rsqrt(lax.optimization_barrier(jnp.mean(values * values, axis=-1, keepdims=True)) + EPSILON) * gain

def conv_silu(values, weight, bias, labels):
    total = bias + weight[0] * values
    for shift in range(1, CONV):
        moved = jnp.concatenate([jnp.zeros((shift, values.shape[1]), values.dtype), values[:-shift]], axis=0)
        moved_labels = jnp.concatenate([jnp.full((shift,), -1, jnp.int32), labels[:-shift]])
        total = total + weight[shift] * moved * (moved_labels == labels).astype(values.dtype)[:, None]
    return jax.nn.silu(total)

def decay_tables(decays, own_labels, label_before):
    running = jnp.cumsum(decays, axis=0)
    order = jnp.arange(decays.shape[0])
    causal = (own_labels[:, None] == own_labels[None, :]) & (order[:, None] >= order[None, :])
    spread = running[:, None, :] - running[None, :, :]
    inside = jnp.where(causal[:, :, None], jnp.exp(jnp.where(causal[:, :, None], spread, 0.0)), 0.0)
    living = (own_labels == label_before).astype(decays.dtype)
    carried = jnp.exp(running) * living[:, None]
    return (running, inside, carried)

def block_output(values, b_rows, c_rows, steps, decays, skip, carry_in, own_labels, label_before):
    running, inside, carried = decay_tables(decays, own_labels, label_before)
    scores = jnp.dot(c_rows, b_rows.T, precision=HIGHEST)
    weights = inside * scores[:, :, None] * steps[None, :, :]
    result = jnp.einsum('ijh,jhp->ihp', weights, values, precision=HIGHEST)
    result = result + carried[:, :, None] * jnp.einsum('hpn,in->ihp', carry_in, c_rows, precision=HIGHEST)
    return result + skip[None, :, None] * values

def block_state(values, b_rows, steps, decays, carry_in, own_labels, label_before):
    running = jnp.cumsum(decays, axis=0)
    living = (own_labels[-1] == label_before).astype(decays.dtype)
    tail = (own_labels == own_labels[-1]).astype(decays.dtype)
    weights = jnp.exp(running[-1][None, :] - running) * tail[:, None] * steps
    kept = (jnp.exp(running[-1]) * living)[:, None, None] * carry_in
    return kept + jnp.einsum('jh,jhp,jn->hpn', weights, values, b_rows, precision=HIGHEST)

def mixer(values, b_rows, c_rows, steps, decays, skip, labels):
    length = values.shape[0]
    count = length // BLOCK
    before = jnp.concatenate([jnp.full((1,), -1, jnp.int32), labels[:-1]])
    blocks = (values.reshape(count, BLOCK, NHEADS, HEADDIM), b_rows.reshape(count, BLOCK, NSTATE), c_rows.reshape(count, BLOCK, NSTATE), steps.reshape(count, BLOCK, NHEADS), decays.reshape(count, BLOCK, NHEADS), labels.reshape(count, BLOCK), before.reshape(count, BLOCK)[:, 0])

    def advance(carry, parts):
        block_values, block_b, block_c, block_steps, block_decays, block_labels, block_before = parts
        result = block_output(block_values, block_b, block_c, block_steps, block_decays, skip, carry, block_labels, block_before)
        following = block_state(block_values, block_b, block_steps, block_decays, carry, block_labels, block_before)
        return (following, result)
    start = jnp.zeros((NHEADS, HEADDIM, NSTATE), values.dtype)
    _, results = lax.scan(jax.checkpoint(advance), start, blocks)
    return results.reshape(length, NHEADS * HEADDIM)

def layer(params, inputs, labels):
    norm_gain, in_weight, bc_weight, dt_weight, dt_bias, a_log, conv_weight, conv_bias, bc_conv_weight, bc_conv_bias, d_skip, gate_gain, out_weight = params
    length = inputs.shape[0]
    normed = low(rms_scale(inputs, norm_gain))
    gate_x = low_back(jnp.einsum('td,dkc->tkc', normed, in_weight, precision=HIGHEST))
    bc_pre = jnp.dot(normed, bc_weight, precision=HIGHEST)
    delta_pre = jnp.dot(normed, dt_weight, precision=HIGHEST)
    x_act = low(conv_silu(gate_x[:, 1], conv_weight, conv_bias, labels))
    bc_act = low(conv_silu(bc_pre, bc_conv_weight, bc_conv_bias, labels))
    delta = jax.nn.softplus(delta_pre + dt_bias)
    decay = -jnp.exp(a_log) * delta
    mixed = low_back(mixer(x_act.reshape(length, NHEADS, HEADDIM), bc_act[:, :NSTATE], bc_act[:, NSTATE:], delta, decay, d_skip, labels))
    gated = mixed * jax.nn.silu(gate_x[:, 0])
    scale = lax.rsqrt(lax.optimization_barrier(jnp.mean(gated * gated, axis=-1, keepdims=True)) + EPSILON)
    normed_gate = low(gated * scale * gate_gain)
    return inputs + jnp.dot(normed_gate, out_weight.T, precision=HIGHEST)

def reference(tokens, norm_gain, in_weight, bc_weight, dt_weight, dt_bias, a_log, conv_weight, conv_bias, bc_conv_weight, bc_conv_bias, d_skip, gate_gain, out_weight, cotangent, seq_lengths):
    labels = segment_ids(seq_lengths, 0, TOK_MB, MICRO)
    params = [item.astype(jnp.float32) for item in (norm_gain, in_weight, bc_weight, dt_weight, dt_bias, a_log, conv_weight, conv_bias, bc_conv_weight, bc_conv_bias, d_skip, gate_gain, out_weight)]
    inputs = tokens.astype(jnp.float32)

    def forward(weights, values):

        def single(pair):
            return layer(weights, pair[0], pair[1])
        return lax.map(jax.checkpoint(single), (values, labels))
    outputs, pullback = jax.vjp(forward, params, inputs)
    grads, grad_tokens = pullback(cotangent.astype(jnp.float32))
    return (outputs.astype(jnp.bfloat16), grad_tokens, grads[0], grads[1], grads[2], grads[3], grads[4], grads[5], grads[10], grads[6], grads[7], grads[8], grads[9], grads[11], grads[12])
```

```python
import functools

import jax
import jax.numpy as jnp
from jax import lax
from jax.experimental import pallas as pl
from jax.experimental.pallas import tpu as pltpu
from jax.sharding import PartitionSpec as P

BLOCK = 256


EPSILON = 1e-05
HIGHEST = lax.Precision.HIGHEST


def shifted(shard, axis, by):
    length = lax.axis_size(axis)
    pairs = [(i, i + by) for i in range(length) if 0 <= i + by < length]
    return lax.ppermute(shard, axis, pairs)


def segment_ids(seq_lengths, first, count, micro):
    places = first + jnp.arange(count, dtype=jnp.int32)
    starts = jnp.cumsum(seq_lengths, axis=-1) - seq_lengths
    short_ids = (
        jnp.sum((starts[:, None, :] <= places[None, :, None]).astype(jnp.int32), axis=-1) - 1
    )
    long_ids = jnp.zeros((micro - seq_lengths.shape[0], count), jnp.int32)
    labels = jnp.concatenate([short_ids, long_ids], axis=0)
    return jnp.where(places[None, :] >= 0, labels, -1)


def rms_scale(values, gain):
    return values * lax.rsqrt(jnp.mean(values * values, axis=-1, keepdims=True) + EPSILON) * gain


def conv_silu(extended, weight, bias, labels):
    taps = weight.shape[0]
    count = extended.shape[0] - taps + 1
    own = labels[taps - 1 :]
    total = bias + weight[0] * extended[taps - 1 :]
    for shift in range(1, taps):
        first = taps - 1 - shift
        mask = (labels[first : first + count] == own).astype(extended.dtype)
        total = total + weight[shift] * extended[first : first + count] * mask[:, None]
    return jax.nn.silu(total)


def step_sizes(delta_pre, dt_bias, a_log):
    delta = jax.nn.softplus(delta_pre + dt_bias)
    return (delta, -jnp.exp(a_log) * delta)


def decay_tables(decays, own_labels, label_before):
    running = jnp.cumsum(decays, axis=0)
    by_head = running.T
    order = jnp.arange(decays.shape[0])
    causal = ((own_labels[:, None] == own_labels[None, :]) & (order[:, None] >= order[None, :]))[
        None
    ]
    spread = by_head[:, :, None] - by_head[:, None, :]
    inside = jnp.where(causal, jnp.exp(jnp.where(causal, spread, 0.0)), 0.0)
    living = (own_labels == label_before).astype(decays.dtype)
    carried = jnp.exp(running) * living[:, None]
    return (running, inside, carried)


def block_output(values, c_rows, steps, decays, skip, carry_in, scores, own_labels, label_before):
    running, inside, carried = decay_tables(decays, own_labels, label_before)
    weights = inside * scores[None, :, :] * steps.T[:, None, :]
    result = jnp.einsum("hij,jhp->ihp", weights, values, precision=HIGHEST)
    result = result + carried[:, :, None] * jnp.einsum(
        "hpn,in->ihp", carry_in, c_rows, precision=HIGHEST
    )
    return result + skip[None, :, None] * values


def block_state(values, b_rows, steps, decays, carry_in, own_labels, label_before):
    running = jnp.cumsum(decays, axis=0)
    living = (own_labels[-1] == label_before).astype(decays.dtype)
    tail = (own_labels == own_labels[-1]).astype(decays.dtype)
    weights = jnp.exp(running[-1][None, :] - running) * tail[:, None] * steps
    kept = (jnp.exp(running[-1]) * living)[:, None, None] * carry_in
    return kept + jnp.einsum("jh,jhp,jn->hpn", weights, values, b_rows, precision=HIGHEST)


DEAD = -1e30
GROUP = 4


def exchange_kernel(
    length,
    reverse,
    part_ref,
    log_ref,
    out_ref,
    parts,
    logs,
    edge_in,
    edge_out,
    given,
    part_send,
    part_recv,
    log_send,
    log_recv,
    edge_send,
    edge_recv,
    given_send,
    given_recv,
):
    me = lax.axis_index("seq")
    rank = lax.rem(me, GROUP)
    plane = me // GROUP
    first = me - rank
    mates = (
        rank + 1 - 2 * lax.rem(rank, 2),
        rank + 2 - 4 * (rank // 2),
        3 - rank,
    )
    micro = part_ref.shape[0]
    planes = length // GROUP
    begins, ends = plane == 0, plane == planes - 1
    if reverse:
        begins, ends = ends, begins
    step = -GROUP if reverse else GROUP

    barrier = pltpu.get_barrier_semaphore()
    for mate in mates:
        pl.semaphore_signal(
            barrier, inc=1, device_id={"seq": first + mate}, device_id_type=pl.DeviceIdType.MESH
        )

    @pl.when(plane > 0)
    def _():
        pl.semaphore_signal(
            barrier, inc=1, device_id={"seq": me - GROUP}, device_id_type=pl.DeviceIdType.MESH
        )

    @pl.when(plane < planes - 1)
    def _():
        pl.semaphore_signal(
            barrier, inc=1, device_id={"seq": me + GROUP}, device_id_type=pl.DeviceIdType.MESH
        )

    above = jnp.where(plane < planes - 1, 1, 0)
    below = jnp.where(plane > 0, 1, 0)
    pl.semaphore_wait(barrier, 3 + above + below)

    def remote(src, dst, send, recv, target):
        return pltpu.make_async_remote_copy(
            src_ref=src,
            dst_ref=dst,
            send_sem=send,
            recv_sem=recv,
            device_id={"seq": target},
            device_id_type=pl.DeviceIdType.MESH,
        )

    def log_copy(slot):
        mate = mates[slot]
        return remote(
            log_ref.at[mate], logs.at[rank], log_send.at[slot], log_recv.at[slot], first + mate
        )

    def part_copy(m, slot):
        mate = mates[slot]
        return remote(
            part_ref.at[m, mate],
            parts.at[m, rank],
            part_send.at[m, slot],
            part_recv.at[m, slot],
            first + mate,
        )

    def edge_copy(m):
        return remote(edge_out.at[m], edge_in.at[m], edge_send.at[m], edge_recv.at[m], me + step)

    def given_copy(m, slot):
        mate = mates[slot]
        return remote(
            given.at[m, mate],
            out_ref.at[m, rank],
            given_send.at[m, slot],
            given_recv.at[m, slot],
            first + mate,
        )

    for slot in range(3):
        log_copy(slot).start()
    for m in range(micro):
        for slot in range(3):
            part_copy(m, slot).start()
    logs[rank] = log_ref[rank]
    for m in range(micro):
        parts[m, rank] = part_ref[m, rank]

    @pl.when(begins)
    def _():
        edge_in[...] = jnp.zeros_like(edge_in)

    for slot in range(3):
        log_copy(slot).wait()
    order = tuple(reversed(range(GROUP))) if reverse else tuple(range(GROUP))
    for m in range(micro):
        for slot in range(3):
            part_copy(m, slot).wait()
        factors = [jnp.exp(logs[t, m])[:, None, :] for t in order]
        whole = jnp.exp(logs[0, m] + logs[1, m] + logs[2, m] + logs[3, m])[:, None, :]
        total = parts[m, order[0]]
        for t, factor in zip(order[1:], factors[1:]):
            total = total * factor + parts[m, t]

        @pl.when(jnp.logical_not(begins))
        def _():
            edge_copy(m).wait_recv()

        @pl.when(jnp.logical_not(ends))
        def _():
            edge_out[m] = total + whole * edge_in[m]
            edge_copy(m).start()

        running = edge_in[m]
        for place, (t, factor) in enumerate(zip(order, factors)):
            given[m, t] = running
            if place < GROUP - 1:
                running = running * factor + parts[m, t]
        for slot in range(3):
            given_copy(m, slot).start()
        out_ref[m, rank] = given[m, rank]
    for m in range(micro):
        for slot in range(3):
            given_copy(m, slot).wait()

        @pl.when(jnp.logical_not(ends))
        def _():
            edge_copy(m).wait_send()


def exchange(parts, logs, reverse):
    micro, heads, rows, columns = parts.shape
    quarter = heads // GROUP
    length = lax.axis_size("seq")
    spread = jnp.broadcast_to(logs[:, :, None], (micro, heads, columns))
    spread = spread.reshape(micro, GROUP, quarter, columns).transpose(1, 0, 2, 3)
    shape = (micro, GROUP, quarter, rows, columns)
    out = pl.pallas_call(
        functools.partial(exchange_kernel, length, reverse),
        out_shape=jax.ShapeDtypeStruct(shape, jnp.float32),
        in_specs=[pl.BlockSpec(memory_space=pltpu.VMEM)] * 2,
        out_specs=pl.BlockSpec(memory_space=pltpu.VMEM),
        scratch_shapes=[
            pltpu.VMEM(shape, jnp.float32),
            pltpu.VMEM((GROUP, micro, quarter, columns), jnp.float32),
            pltpu.VMEM((micro, quarter, rows, columns), jnp.float32),
            pltpu.VMEM((micro, quarter, rows, columns), jnp.float32),
            pltpu.VMEM(shape, jnp.float32),
            pltpu.SemaphoreType.DMA((micro, 3)),
            pltpu.SemaphoreType.DMA((micro, 3)),
            pltpu.SemaphoreType.DMA((3,)),
            pltpu.SemaphoreType.DMA((3,)),
            pltpu.SemaphoreType.DMA((micro,)),
            pltpu.SemaphoreType.DMA((micro,)),
            pltpu.SemaphoreType.DMA((micro, 3)),
            pltpu.SemaphoreType.DMA((micro, 3)),
        ],
        compiler_params=pltpu.CompilerParams(
            collective_id=1 if reverse else 0,
            has_side_effects=True,
            vmem_limit_bytes=40 * 1024 * 1024,
        ),
        name="exchange_back" if reverse else "exchange",
    )(parts.reshape(shape), spread)
    return out.reshape(micro, heads, rows, columns)


def xor_permute(value, axis, bit):
    size = lax.axis_size(axis)
    return lax.ppermute(value, axis, [(i, i ^ (1 << bit)) for i in range(size)])


def axis_bits(axis):
    return (lax.axis_size(axis) - 1).bit_length()


def own_bit(axis, bit):
    return lax.rem(lax.axis_index(axis) // (1 << bit), 2)


def pick(array, dim, index):
    return lax.dynamic_index_in_dim(array, index, dim, keepdims=False)


def all_sum(value, axis):
    for bit in range(axis_bits(axis)):
        value = value + xor_permute(value, axis, bit)
    return value


def scatter_product(left, right, order):
    bits = axis_bits("seq")
    tokens, rows = left.shape
    block = rows >> bits
    names = list(range(bits - 1, -1, -1))
    view = left.reshape((tokens,) + (2,) * bits + (block,))
    total = None
    for place, bit in enumerate(order):
        dim = names.index(bit)
        names.remove(bit)
        mine = own_bit("seq", bit)
        if place == 0:
            def product(index):
                chosen = pick(view, dim + 1, index).reshape(tokens, rows // 2)
                return lax.dot_general(
                    chosen, right, (((0,), (0,)), ((), ())), preferred_element_type=jnp.float32
                )

            arrived = xor_permute(product(1 - mine), "seq", bit)
            total = product(mine) + arrived
        else:
            cut = total.reshape((2,) * (len(names) + 1) + (block, right.shape[1]))
            arrived = xor_permute(pick(cut, dim, 1 - mine), "seq", bit)
            total = pick(cut, dim, mine) + arrived
        total = total.reshape((2,) * len(names) + (block, right.shape[1]))
    return total.reshape(block, right.shape[1])


def scatter_orders():
    bits = axis_bits("seq")
    if bits < 3:
        return [tuple(range(bits))]
    rest = tuple(range(3, bits))
    return [(0, 1, 2) + rest, (1, 0, 2) + rest, (2, 0, 1) + rest]


def scatter_all(left, right):
    orders = scatter_orders()
    columns = right.shape[1]
    unit = max(columns // 16, 128)
    shares = [5 * unit, 6 * unit, columns - 11 * unit] if columns >= 16 * 128 else [columns]
    if len(shares) > len(orders):
        shares = [columns]
    parts, first = [], 0
    for share, order in zip(shares, orders):
        parts.append(scatter_product(left, right[:, first : first + share], order))
        first += share
    return jnp.concatenate(parts, axis=1) if len(parts) > 1 else parts[0]


def gather_rows(block, axis):
    for bit in range(axis_bits(axis)):
        other = xor_permute(block, axis, bit)
        mine = own_bit(axis, bit)
        low = jnp.where(mine == 0, block, other)
        high = jnp.where(mine == 0, other, block)
        block = jnp.concatenate([low, high], axis=0)
    return block


def out_term(cot_flat, normed_gate):
    return lax.dot_general(
        cot_flat, normed_gate, (((0,), (0,)), ((), ())), preferred_element_type=jnp.float32
    )


def in_term(normed_low, grad_gate_x):
    return jnp.einsum("tr,tkc->rkc", normed_low, grad_gate_x, preferred_element_type=jnp.float32)


def body(
    tokens,
    norm_gain,
    in_weight,
    bc_weight,
    dt_weight,
    dt_bias,
    a_log,
    conv_weight,
    conv_bias,
    bc_conv_weight,
    bc_conv_bias,
    d_skip,
    gate_gain,
    out_weight,
    cotangent,
    seq_lengths,
):
    micro, length, width = tokens.shape
    heads = dt_bias.shape[0]
    inner = conv_bias.shape[0]
    head_dim = inner // heads
    state_size = bc_weight.shape[1] // 2
    taps = conv_weight.shape[0]
    span = min(BLOCK, length)
    pieces = length // span
    groups = micro * pieces
    total = micro * length
    full_inner = inner * lax.axis_size("head")
    labels = segment_ids(
        seq_lengths, lax.axis_index("seq") * length - (taps - 1), length + taps - 1, micro
    )
    own_labels = labels[:, taps - 1 :]
    before_labels = labels[:, taps - 2 :: span][:, :pieces].reshape(groups)
    flat = tokens.reshape(total, width).astype(jnp.float32)
    normed, norm_back = jax.vjp(rms_scale, flat, norm_gain)
    normed_low = normed.astype(jnp.bfloat16)
    gate_x = jnp.einsum("td,dkc->tkc", normed_low, in_weight, preferred_element_type=jnp.float32)
    gate_pre = gate_x[:, 0].reshape(micro, length, inner)
    x_pre = gate_x[:, 1].reshape(micro, length, inner)
    bc_pre = jnp.dot(normed_low, bc_weight, preferred_element_type=jnp.float32).reshape(
        micro, length, 2 * state_size
    )
    delta_pre = jnp.dot(normed_low, dt_weight, preferred_element_type=jnp.float32)
    left_x, left_bc = shifted(
        (x_pre[:, length - taps + 1 :], bc_pre[:, length - taps + 1 :]), "seq", 1
    )
    conv_many = jax.vmap(conv_silu, in_axes=(0, None, None, 0))
    x_act, x_conv_back = jax.vjp(
        lambda extended, weight, bias: conv_many(extended, weight, bias, labels),
        jnp.concatenate([left_x, x_pre], axis=1),
        conv_weight,
        conv_bias,
    )
    bc_act, bc_conv_back = jax.vjp(
        lambda extended, weight, bias: conv_many(extended, weight, bias, labels),
        jnp.concatenate([left_bc, bc_pre], axis=1),
        bc_conv_weight,
        bc_conv_bias,
    )
    x_low = x_act.astype(jnp.bfloat16)
    bc_low = bc_act.astype(jnp.bfloat16)
    (delta, decay), rate_back = jax.vjp(step_sizes, delta_pre, dt_bias, a_log)
    values = x_low.astype(jnp.float32).reshape(groups, span, heads, head_dim)
    b_low = bc_low[..., :state_size]
    c_low = bc_low[..., state_size:]
    b_rows = b_low.astype(jnp.float32)
    c_rows = c_low.astype(jnp.float32)
    scores = jnp.einsum("gin,gjn->gij", c_low, b_low, preferred_element_type=jnp.float32)
    steps = delta.reshape(groups, span, heads)
    decays = decay.reshape(groups, span, heads)
    zero_state = jnp.zeros((groups, heads, head_dim, state_size), jnp.float32)
    state_many = jax.vmap(block_state)
    own_states, state_back = jax.vjp(
        lambda block_values, block_b, block_steps, block_decays: state_many(
            block_values, block_b, block_steps, block_decays, zero_state, own_labels, before_labels
        ),
        values,
        b_rows,
        steps,
        decays,
    )
    living = (own_labels[:, -1] == before_labels).astype(jnp.float32)
    block_logs = jnp.sum(decays, axis=1)
    factor = (jnp.exp(block_logs) * living[:, None]).reshape(micro, pieces, heads)
    own_states = own_states.reshape(micro, pieces, heads, head_dim, state_size)
    device_state = jnp.zeros((micro, heads, head_dim, state_size), jnp.float32)
    piece = 0
    device_state = factor[:, piece, :, None, None] * device_state + own_states[:, piece]
    device_log = jnp.sum(block_logs.reshape(micro, pieces, heads), axis=1)
    device_live = jnp.prod(living.reshape(micro, pieces), axis=1)
    exchange_log = jnp.where(device_live[:, None] > 0.0, device_log, DEAD)
    incoming = exchange(device_state, exchange_log, False)
    current = incoming
    piece = 0
    starts = [current]
    block_starts = jnp.stack(starts, axis=1).reshape(groups, heads, head_dim, state_size)
    output_many = jax.vmap(block_output, in_axes=(0, 0, 0, 0, None, 0, 0, 0, 0))
    mixed, output_back = jax.vjp(
        lambda block_values, block_c, block_steps, block_decays, skip, carry, block_scores: output_many(
            block_values,
            block_c,
            block_steps,
            block_decays,
            skip,
            carry,
            block_scores,
            own_labels,
            before_labels,
        ),
        values,
        c_rows,
        steps,
        decays,
        d_skip,
        block_starts,
        scores,
    )
    mixed = mixed.reshape(micro, length, inner)
    gate_act = jax.nn.silu(gate_pre)
    gated = mixed * gate_act
    square_sum = all_sum(jnp.sum(gated * gated, axis=-1), "head")
    scale = lax.rsqrt(square_sum / full_inner + EPSILON)[:, :, None]
    normed_gate = (gated * scale * gate_gain).astype(jnp.bfloat16).reshape(total, inner)
    head_terms = lax.dot_general(
        normed_gate, out_weight, (((1,), (1,)), ((), ())), preferred_element_type=jnp.float32
    )
    summed = lax.psum_scatter(head_terms, "head", scatter_dimension=1, tiled=True)
    share = summed.shape[1]
    residual = lax.dynamic_slice_in_dim(flat, lax.axis_index("head") * share, share, 1)
    block_out = (residual + summed).astype(jnp.bfloat16).reshape(micro, length, share)
    cot_flat = cotangent.reshape(total, width)
    grad_gate_n = jnp.dot(cot_flat, out_weight, preferred_element_type=jnp.float32).reshape(
        micro, length, inner
    )
    grad_out_weight = scatter_all(cot_flat, normed_gate)
    grad_gate_gain = jnp.sum(grad_gate_n * gated * scale, axis=(0, 1))
    dot_total = all_sum(jnp.sum(grad_gate_n * gate_gain * gated, axis=-1), "head")
    grad_gated = (
        grad_gate_n * gate_gain * scale - gated * scale**3 * dot_total[:, :, None] / full_inner
    )
    sigma = jax.nn.sigmoid(gate_pre)
    grad_gate_pre = grad_gated * mixed * sigma * (1.0 + gate_pre * (1.0 - sigma))
    grad_mixed = (grad_gated * gate_act).astype(jnp.bfloat16).astype(jnp.float32)
    grad_rows = grad_mixed.reshape(groups, span, heads, head_dim)
    out_values, out_c, out_steps, out_decays, grad_d_skip, grad_starts, grad_scores = output_back(
        grad_rows
    )
    out_c = out_c + jnp.einsum("gij,gjn->gin", grad_scores, b_rows, precision=HIGHEST)
    out_b = jnp.einsum("gij,gin->gjn", grad_scores, c_rows, precision=HIGHEST)
    grad_starts = grad_starts.reshape(micro, pieces, heads, head_dim, state_size)
    device_grad = jnp.zeros_like(device_state)
    for piece in reversed(range(pieces)):
        device_grad = grad_starts[:, piece] + factor[:, piece, :, None, None] * device_grad
    outgoing = exchange(device_grad, exchange_log, True)
    ends = [outgoing] * pieces
    current = outgoing
    for piece in reversed(range(pieces)):
        ends[piece] = current
        current = grad_starts[:, piece] + factor[:, piece, :, None, None] * current
    end_grads = jnp.stack(ends, axis=1).reshape(groups, heads, head_dim, state_size)
    own_values, own_b, own_steps, own_decays = state_back(end_grads)
    carry_weight = jnp.sum(end_grads * block_starts, axis=(2, 3)) * factor.reshape(groups, heads)
    grad_values = (out_values + own_values).reshape(micro, length, inner)
    grad_bc_act = jnp.concatenate([out_b + own_b, out_c], axis=-1)
    grad_delta = (out_steps + own_steps).reshape(total, heads)
    grad_decay = (out_decays + own_decays + carry_weight[:, None, :]).reshape(total, heads)
    grad_delta_pre, grad_dt_bias, grad_a_log = rate_back((grad_delta, grad_decay))
    grad_x_ext, grad_conv_weight, grad_conv_bias = x_conv_back(grad_values)
    grad_bc_ext, grad_bc_conv_weight, grad_bc_conv_bias = bc_conv_back(grad_bc_act)
    right_x, right_bc = shifted((grad_x_ext[:, : taps - 1], grad_bc_ext[:, : taps - 1]), "seq", -1)
    grad_x_pre = grad_x_ext[:, taps - 1 :].at[:, length - taps + 1 :].add(right_x)
    grad_bc_pre = grad_bc_ext[:, taps - 1 :].at[:, length - taps + 1 :].add(right_bc)
    grad_gate_x = (
        jnp.stack([grad_gate_pre, grad_x_pre], axis=2).reshape(total, 2, inner).astype(jnp.bfloat16)
    )
    bc_flat = grad_bc_pre.reshape(total, 2 * state_size)
    row_part = jnp.einsum("tkc,dkc->td", grad_gate_x, in_weight, preferred_element_type=jnp.float32)
    row_part = row_part + jnp.einsum(
        "tc,dc->td", bc_flat, bc_weight, precision=HIGHEST, preferred_element_type=jnp.float32
    )
    row_part = row_part + jnp.einsum(
        "th,dh->td",
        grad_delta_pre,
        dt_weight,
        precision=HIGHEST,
        preferred_element_type=jnp.float32,
    )
    row_grads = all_sum(row_part, "head")
    grad_flat, grad_norm_gain = norm_back(row_grads)
    grad_tokens = (cot_flat.astype(jnp.float32) + grad_flat).reshape(micro, length, width)
    grad_in_weight = jnp.stack(
        [scatter_all(normed_low, grad_gate_x[:, 0]), scatter_all(normed_low, grad_gate_x[:, 1])],
        axis=1,
    )
    grad_bc_weight = jnp.einsum(
        "td,tc->dc", normed_low, bc_flat, precision=HIGHEST, preferred_element_type=jnp.float32
    )
    grad_dt_weight = jnp.einsum(
        "td,th->dh",
        normed_low,
        grad_delta_pre,
        precision=HIGHEST,
        preferred_element_type=jnp.float32,
    )
    bits = axis_bits("seq")
    rows = width >> bits
    narrow = jnp.concatenate([all_sum(grad_bc_weight, "head"), grad_dt_weight], axis=1)
    across = narrow.shape[1]
    for bit in range(bits):
        cut = narrow.reshape((2,) * (bits - bit) + (rows, across))
        mine = own_bit("seq", bit)
        dim = bits - bit - 1
        narrow = pick(cut, dim, mine) + xor_permute(pick(cut, dim, 1 - mine), "seq", bit)
    narrow = gather_rows(narrow.reshape(rows, across), "seq")
    grad_bc_weight = narrow[:, : 2 * state_size]
    grad_dt_weight = narrow[:, 2 * state_size :]
    shared = [grad_bc_conv_weight, grad_bc_conv_bias]
    shared_row = all_sum(jnp.concatenate([item.reshape(-1) for item in shared]), "head")
    small = [
        grad_norm_gain,
        grad_dt_bias,
        grad_a_log,
        grad_d_skip,
        grad_conv_weight,
        grad_conv_bias,
        grad_gate_gain,
    ]
    row = all_sum(jnp.concatenate([shared_row] + [item.reshape(-1) for item in small]), "seq")
    pieces_out, first = [], 0
    for item in shared + small:
        pieces_out.append(row[first : first + item.size].reshape(item.shape))
        first += item.size
    (
        grad_bc_conv_weight,
        grad_bc_conv_bias,
        grad_norm_gain,
        grad_dt_bias,
        grad_a_log,
        grad_d_skip,
        grad_conv_weight,
        grad_conv_bias,
        grad_gate_gain,
    ) = pieces_out
    return (
        block_out,
        grad_tokens,
        grad_norm_gain,
        grad_in_weight,
        grad_bc_weight,
        grad_dt_weight,
        grad_dt_bias,
        grad_a_log,
        grad_d_skip,
        grad_conv_weight,
        grad_conv_bias,
        grad_bc_conv_weight,
        grad_bc_conv_bias,
        grad_gate_gain,
        grad_out_weight,
    )


def solution(mesh):
    return jax.shard_map(
        body,
        mesh=mesh,
        in_specs=(
            P(None, "seq", None),
            P(),
            P(None, None, "head"),
            P(),
            P(None, "head"),
            P("head"),
            P("head"),
            P(None, "head"),
            P("head"),
            P(),
            P(),
            P("head"),
            P("head"),
            P(None, "head"),
            P(None, "seq", None),
            P(),
        ),
        out_specs=(
            P(None, "seq", "head"),
            P(None, "seq", None),
            P(),
            P("seq", None, "head"),
            P(),
            P(None, "head"),
            P("head"),
            P("head"),
            P("head"),
            P(None, "head"),
            P("head"),
            P(),
            P(),
            P("head"),
            P("seq", "head"),
        ),
        check_vma=False,
    )
```

```python
import functools
import math

import jax
import jax.numpy as jnp
from jax import lax
from jax.experimental import pallas as pl
from jax.experimental.pallas import tpu as pltpu
from jax.sharding import PartitionSpec as P

EPSILON = 1e-05
HIGHEST = lax.Precision.HIGHEST


def shifted(shard, axis, by):
    length = lax.axis_size(axis)
    pairs = [(i, i + by) for i in range(length) if 0 <= i + by < length]
    return lax.ppermute(shard, axis, pairs)


def segment_ids(seq_lengths, first, count, micro):
    places = first + jnp.arange(count, dtype=jnp.int32)
    starts = jnp.cumsum(seq_lengths, axis=-1) - seq_lengths
    short_ids = (
        jnp.sum((starts[:, None, :] <= places[None, :, None]).astype(jnp.int32), axis=-1) - 1
    )
    long_ids = jnp.zeros((micro - seq_lengths.shape[0], count), jnp.int32)
    labels = jnp.concatenate([short_ids, long_ids], axis=0)
    return jnp.where(places[None, :] >= 0, labels, -1)


def rms_scale(values, gain):
    return values * lax.rsqrt(jnp.mean(values * values, axis=-1, keepdims=True) + EPSILON) * gain


def conv_silu(extended, weight, bias, labels):
    taps = weight.shape[0]
    count = extended.shape[0] - taps + 1
    own = labels[taps - 1 :]
    total = bias + weight[0] * extended[taps - 1 :]
    for shift in range(1, taps):
        first = taps - 1 - shift
        mask = (labels[first : first + count] == own).astype(extended.dtype)
        total = total + weight[shift] * extended[first : first + count] * mask[:, None]
    return jax.nn.silu(total)


def step_sizes(delta_pre, dt_bias, a_log):
    delta = jax.nn.softplus(delta_pre + dt_bias[:, None])
    return (delta, -jnp.exp(a_log)[:, None] * delta)


DEAD = -1e30
EXCHANGE_COST = 100_000_000_000
FINISH_LIMIT = 60 * 1024 * 1024
GROUP = 4


def exchange_kernel(length, reverse, orders, part_ref, log_ref, *refs):
    refs = list(refs)
    sources = [refs.pop(0) for _ in range(2 if orders else 0)]
    out_ref = refs.pop(0)
    targets = [refs.pop(0) for _ in range(4 * len(orders))]
    (
        parts,
        logs,
        edge_in,
        edge_out,
        given,
        part_send,
        part_recv,
        log_send,
        log_recv,
        edge_send,
        edge_recv,
        given_send,
        given_recv,
        stage_sem,
        place_sem,
        staged,
    ) = refs
    me = lax.axis_index("seq")
    bits = (length - 1).bit_length()
    placed = arrange_copies(bits, orders, me, staged, targets, place_sem)
    stages = [
        pltpu.make_async_copy(source, staged.at[k], stage_sem.at[k])
        for k, source in enumerate(sources)
    ]
    for copy in stages:
        copy.start()
    rank = lax.rem(me, GROUP)
    plane = me // GROUP
    first = me - rank
    mates = (
        rank + 1 - 2 * lax.rem(rank, 2),
        rank + 2 - 4 * (rank // 2),
        3 - rank,
    )
    micro = part_ref.shape[0]
    planes = length // GROUP
    begins, ends = plane == 0, plane == planes - 1
    if reverse:
        begins, ends = ends, begins
    step = -GROUP if reverse else GROUP

    barrier = pltpu.get_barrier_semaphore()
    for mate in mates:
        pl.semaphore_signal(
            barrier, inc=1, device_id={"seq": first + mate}, device_id_type=pl.DeviceIdType.MESH
        )

    @pl.when(plane > 0)
    def _():
        pl.semaphore_signal(
            barrier, inc=1, device_id={"seq": me - GROUP}, device_id_type=pl.DeviceIdType.MESH
        )

    @pl.when(plane < planes - 1)
    def _():
        pl.semaphore_signal(
            barrier, inc=1, device_id={"seq": me + GROUP}, device_id_type=pl.DeviceIdType.MESH
        )

    above = jnp.where(plane < planes - 1, 1, 0)
    below = jnp.where(plane > 0, 1, 0)
    pl.semaphore_wait(barrier, 3 + above + below)

    def remote(src, dst, send, recv, target):
        return pltpu.make_async_remote_copy(
            src_ref=src,
            dst_ref=dst,
            send_sem=send,
            recv_sem=recv,
            device_id={"seq": target},
            device_id_type=pl.DeviceIdType.MESH,
        )

    def log_copy(slot):
        mate = mates[slot]
        return remote(
            log_ref.at[mate], logs.at[rank], log_send.at[slot], log_recv.at[slot], first + mate
        )

    def part_copy(m, slot):
        mate = mates[slot]
        return remote(
            part_ref.at[m, mate],
            parts.at[m, rank],
            part_send.at[m, slot],
            part_recv.at[m, slot],
            first + mate,
        )

    def edge_copy(m):
        return remote(edge_out.at[m], edge_in.at[m], edge_send.at[m], edge_recv.at[m], me + step)

    def given_copy(m, slot):
        mate = mates[slot]
        return remote(
            given.at[m, mate],
            out_ref.at[m, rank],
            given_send.at[m, slot],
            given_recv.at[m, slot],
            first + mate,
        )

    for slot in range(3):
        log_copy(slot).start()
    for m in range(micro):
        for slot in range(3):
            part_copy(m, slot).start()
    logs[rank] = log_ref[rank]
    for m in range(micro):
        parts[m, rank] = part_ref[m, rank]

    @pl.when(begins)
    def _():
        edge_in[...] = jnp.zeros_like(edge_in)

    for copy in stages:
        copy.wait()
    for copy in placed:
        copy.start()
    for slot in range(3):
        log_copy(slot).wait()
    order = tuple(reversed(range(GROUP))) if reverse else tuple(range(GROUP))
    for m in range(micro):
        for slot in range(3):
            part_copy(m, slot).wait()
        factors = [jnp.exp(logs[t, m])[:, None, :] for t in order]
        whole = jnp.exp(logs[0, m] + logs[1, m] + logs[2, m] + logs[3, m])[:, None, :]
        total = parts[m, order[0]]
        for t, factor in zip(order[1:], factors[1:]):
            total = total * factor + parts[m, t]

        @pl.when(jnp.logical_not(begins))
        def _():
            edge_copy(m).wait_recv()

        @pl.when(jnp.logical_not(ends))
        def _():
            edge_out[m] = total + whole * edge_in[m]
            edge_copy(m).start()

        running = edge_in[m]
        for place, (t, factor) in enumerate(zip(order, factors)):
            given[m, t] = running
            if place < GROUP - 1:
                running = running * factor + parts[m, t]
        for slot in range(3):
            given_copy(m, slot).start()
        out_ref[m, rank] = given[m, rank]
    for m in range(micro):
        for slot in range(3):
            given_copy(m, slot).wait()

        @pl.when(jnp.logical_not(ends))
        def _():
            edge_copy(m).wait_send()

    for copy in placed:
        copy.wait()


def exchange(parts, logs, reverse, sources=(), orders=()):
    micro, heads, rows, columns = parts.shape
    quarter = heads // GROUP
    length = lax.axis_size("seq")
    spread = jnp.broadcast_to(logs[:, :, None], (micro, heads, columns))
    spread = spread.reshape(micro, GROUP, quarter, columns).transpose(1, 0, 2, 3)
    shape = (micro, GROUP, quarter, rows, columns)
    arranged = []
    for source in sources:
        half = jax.ShapeDtypeStruct((source.shape[0], source.shape[1] // 2), source.dtype)
        arranged += [half] * (2 * len(orders))
    vmem = pl.BlockSpec(memory_space=pltpu.VMEM)
    hbm = pl.BlockSpec(memory_space=pl.ANY)
    out, *arranged = pl.pallas_call(
        functools.partial(exchange_kernel, length, reverse, orders),
        out_shape=[jax.ShapeDtypeStruct(shape, jnp.float32)] + arranged,
        in_specs=[vmem] * 2 + [hbm] * len(sources),
        out_specs=[vmem] + [hbm] * len(arranged),
        scratch_shapes=[
            pltpu.VMEM(shape, jnp.float32),
            pltpu.VMEM((GROUP, micro, quarter, columns), jnp.float32),
            pltpu.VMEM((micro, quarter, rows, columns), jnp.float32),
            pltpu.VMEM((micro, quarter, rows, columns), jnp.float32),
            pltpu.VMEM(shape, jnp.float32),
            pltpu.SemaphoreType.DMA((micro, 3)),
            pltpu.SemaphoreType.DMA((micro, 3)),
            pltpu.SemaphoreType.DMA((3,)),
            pltpu.SemaphoreType.DMA((3,)),
            pltpu.SemaphoreType.DMA((micro,)),
            pltpu.SemaphoreType.DMA((micro,)),
            pltpu.SemaphoreType.DMA((micro, 3)),
            pltpu.SemaphoreType.DMA((micro, 3)),
            pltpu.SemaphoreType.DMA((2,)),
            pltpu.SemaphoreType.DMA((max(len(arranged), 1) * max(length // 2, 1),)),
            pltpu.VMEM((2,) + sources[0].shape if sources else (2, 16, 128), jnp.bfloat16),
        ],
        compiler_params=pltpu.CompilerParams(
            collective_id=1 if reverse else 0,
            has_side_effects=True,
            vmem_limit_bytes=40 * 1024 * 1024,
        ),
        cost_estimate=pl.CostEstimate(
            flops=EXCHANGE_COST, bytes_accessed=0, transcendentals=0
        ),
        name="exchange_back" if reverse else "exchange",
    )(parts.reshape(shape), spread, *sources)
    return out.reshape(micro, heads, rows, columns), arranged


def xor_permute(value, axis, bit):
    size = lax.axis_size(axis)
    return lax.ppermute(value, axis, [(i, i ^ (1 << bit)) for i in range(size)])


def axis_bits(axis):
    return (lax.axis_size(axis) - 1).bit_length()


def own_bit(axis, bit):
    return lax.rem(lax.axis_index(axis) // (1 << bit), 2)


def all_sum(value, axis):
    for bit in range(axis_bits(axis)):
        value = value + xor_permute(value, axis, bit)
    return value


def scatter_parts(columns, bits):
    if bits < 3 or columns % 2048:
        return [(tuple(range(bits)), (columns,))]
    rest = tuple(range(3, bits))
    unit = columns // 16
    return [
        ((0, 1, 2) + rest, (3 * unit, 2 * unit)),
        ((1, 0, 2) + rest, (2 * unit, 3 * unit)),
        ((2, 0, 1) + rest, (3 * unit, 0)),
        ((2, 1, 0) + rest, (0, 3 * unit)),
    ]


def arranged_place(order, position, bits):
    return [(position >> (bits - 1 - t)) & 1 for t, _ in sorted(enumerate(order), key=lambda p: p[1])]


def arranged_block(order, position, bits, me):
    flips = arranged_place(order, position, bits)
    total = 0
    for bit, flip in enumerate(flips):
        mine = lax.rem(me // (1 << bit), 2)
        total = total + (1 << bit) * ((1 - mine) if flip else mine)
    return total


def arrange(left, orders):
    bits = axis_bits("seq")
    size = 1 << bits
    tokens, width = left.shape
    view = left.reshape(tokens, size, width // size)
    me = lax.axis_index("seq").astype(jnp.int32)
    results = []
    for order in orders:
        table = jnp.stack([arranged_block(order, j, bits, me) for j in range(size)])
        chosen = jnp.take(view, table, axis=1).reshape(tokens, width)
        results += [chosen[:, width // 2 :], chosen[:, : width // 2]]
    return results


def arrange_copies(bits, orders, me, staged, targets, sem):
    copies, number = [], 0
    half = 1 << (bits - 1)
    for source in range(len(targets) // (2 * len(orders)) if orders else 0):
        block = staged.shape[2] >> bits
        for order in orders:
            for begin in (half, 0):
                target = targets[number]
                for j in range(half):
                    place = arranged_block(order, begin + j, bits, me)
                    first = pl.multiple_of(place * block, block)
                    copies.append(
                        pltpu.make_async_copy(
                            staged.at[source, :, pl.ds(first, block)],
                            target.at[:, pl.ds(j * block, block)],
                            sem.at[number * half + j],
                        )
                    )
                number += 1
    return copies


def product(left, right):
    return lax.dot_general(left, right, (TN, ((), ())), preferred_element_type=jnp.float32)


def split_columns(array, parts):
    pieces, first = [], 0
    for _, widths in parts:
        pieces.append(array[:, first : first + sum(widths)])
        first += sum(widths)
    return pieces


def sent_products(lefts, right, parts):
    return [
        product(lefts[2 * k], piece) for k, piece in enumerate(split_columns(right, parts))
    ]


def send_parts(products, parts):
    return [xor_permute(item, "seq", order[0]) for item, (order, _) in zip(products, parts)]


def keep_parts(lefts, right, parts, arrived):
    return [
        product(lefts[2 * k + 1], piece) + arrived[k]
        for k, piece in enumerate(split_columns(right, parts))
    ]


def finish_kernel(parts, mats, bits, blocks, *refs):
    refs = list(refs)
    take = lambda count: [refs.pop(0) for _ in range(count)]
    ins = [take(len(parts)) for _ in range(mats)]
    narrow_ref, vector_ref = take(2)
    outs = take(mats)
    gathered_ref, vector_out_ref = take(2)
    me = lax.axis_index("seq")

    def partner(bit):
        return me + (1 << bit) * (1 - 2 * lax.rem(me // (1 << bit), 2))

    waves = []
    piece_count = len(parts[0][1])
    chain_count = 0
    for mat in range(mats):
        for piece in range(piece_count):
            wave, first = [], 0
            for k, (order, widths) in enumerate(parts):
                if widths[piece]:
                    within = sum(widths[:piece])
                    keep = refs.pop(0)
                    recvs = take(bits - 1)
                    wave.append(
                        (chain_count, ins[mat][k], within, outs[mat], first + within, order[1:], keep, recvs)
                    )
                    chain_count += 1
                first += sum(widths)
            waves.append(wave)
    narrow_order = parts[0][0]
    narrow = (chain_count, narrow_ref, 0, None, 0, narrow_order, refs.pop(0), take(bits))
    vector_sums, vector_recvs, local_sem, send_sem, recv_sem = refs

    barrier = pltpu.get_barrier_semaphore()
    for bit in range(bits):
        pl.semaphore_signal(
            barrier,
            inc=1,
            device_id={"seq": partner(bit)},
            device_id_type=pl.DeviceIdType.MESH,
        )
    pl.semaphore_wait(barrier, bits)

    numbers = {}

    def remote(key, src, dst, bit):
        number = numbers.setdefault(key, len(numbers))
        return pltpu.make_async_remote_copy(
            src_ref=src,
            dst_ref=dst,
            send_sem=send_sem.at[number],
            recv_sem=recv_sem.at[number],
            device_id={"seq": partner(bit)},
            device_id_type=pl.DeviceIdType.MESH,
        )

    def local_copy(chain):
        number, source, first, _, _, _, keep, _ = chain
        rows, columns = keep.shape
        return pltpu.make_async_copy(
            source.at[pl.ds(0, rows), pl.ds(first, columns)], keep, local_sem.at[number]
        )

    def chain_copy(chain, phase):
        number, source, first, _, _, order, keep, recvs = chain
        rows, columns = recvs[phase].shape
        if phase == 0:
            region = source.at[pl.ds(rows, rows), pl.ds(first, columns)]
        else:
            region = keep.at[pl.ds(rows, rows)]
        return remote((number, phase), region, recvs[phase], order[phase])

    def begin(wave):
        for chain in wave:
            chain_copy(chain, 0).start()
            local_copy(chain).start()

    def advance(chain, phase):
        if phase == 0:
            local_copy(chain).wait()
        chain_copy(chain, phase).wait_recv()
        number, _, _, out, place, order, keep, recvs = chain
        recv = recvs[phase]
        rows = recv.shape[0]
        slab = min(rows, 32)

        @pl.loop(0, rows // slab)
        def _(step):
            cut = pl.ds(pl.multiple_of(step * slab, slab), slab)
            keep[cut, :] = keep[cut, :] + recv[cut, :]

        if phase + 1 < len(order):
            chain_copy(chain, phase + 1).start()
        elif out is not None:
            out[:, place : place + keep.shape[1]] = keep[0:blocks, :]

    def vector_copy(phase):
        return remote(("vector", phase), vector_sums.at[phase], vector_recvs.at[phase], phase)

    def advance_vector(phase):
        vector_copy(phase).wait_recv()
        total = vector_sums[phase] + vector_recvs[phase]
        if phase + 1 < bits:
            vector_sums[phase + 1] = total
            vector_copy(phase + 1).start()
        else:
            vector_out_ref[...] = total

    def gather_copies(phase):
        bit = bits - 1 - phase
        copies = []
        for high in range(1 << phase):
            block = lax.rem(me, 2 << bit) + high * (2 << bit)
            region = gathered_ref.at[block]
            copies.append(remote(("gather", phase, high), region, region, bit))
        return copies

    narrow_steps = []

    def narrow_halving(phase):
        advance(narrow, phase)
        if phase + 1 == bits:
            gathered_ref[me] = narrow[6][0 : gathered_ref.shape[1], :]
            for copy in gather_copies(0):
                copy.start()

    def narrow_gather(phase):
        for copy in gather_copies(phase):
            copy.wait_recv()
        if phase + 1 < bits:
            for copy in gather_copies(phase + 1):
                copy.start()

    for phase in range(bits):
        narrow_steps.append(functools.partial(narrow_halving, phase))
    for phase in range(bits):
        narrow_steps.append(functools.partial(narrow_gather, phase))

    vector_sums[0] = vector_ref[...]
    vector_copy(0).start()
    chain_copy(narrow, 0).start()
    local_copy(narrow).start()
    for wave in waves[:2]:
        begin(wave)
    ticks = len(waves) + bits - 2
    for tick in range(max(ticks, 2 * bits)):
        if tick < bits:
            advance_vector(tick)
        if tick < len(narrow_steps):
            narrow_steps[tick]()
        for phase in range(bits - 1):
            number = tick - phase
            if 0 <= number < len(waves):
                for chain in waves[number]:
                    advance(chain, phase)
                if phase == 0 and number + 2 < len(waves):
                    begin(waves[number + 2])
    for wave in waves:
        for chain in wave:
            for phase in range(bits - 1):
                chain_copy(chain, phase).wait_send()
    for phase in range(bits):
        chain_copy(narrow, phase).wait_send()
        vector_copy(phase).wait_send()
        for copy in gather_copies(phase):
            copy.wait_send()


def finish(parts, mats, narrow, vector):
    bits = axis_bits("seq")
    size = 1 << bits
    blocks = mats[0][0].shape[0] // (size // 2)
    columns = sum(sum(widths) for _, widths in parts)
    scratch, copies, chains = [], 0, 0
    for _ in mats:
        for piece in range(len(parts[0][1])):
            for _, widths in parts:
                if widths[piece]:
                    rows = blocks * size // 4
                    scratch.append(pltpu.VMEM((rows, widths[piece]), jnp.float32))
                    for phase in range(bits - 1):
                        scratch.append(pltpu.VMEM((rows >> phase, widths[piece]), jnp.float32))
                    copies += bits - 1
                    chains += 1
    rows = narrow.shape[0] // 2
    scratch.append(pltpu.VMEM((rows, narrow.shape[1]), jnp.float32))
    for phase in range(bits):
        scratch.append(pltpu.VMEM((rows >> phase, narrow.shape[1]), jnp.float32))
    copies += 2 * bits + size - 1
    scratch += [pltpu.VMEM((bits,) + vector.shape, jnp.float32)] * 2
    scratch += [
        pltpu.SemaphoreType.DMA((chains + 1,)),
        pltpu.SemaphoreType.DMA((copies,)),
        pltpu.SemaphoreType.DMA((copies,)),
    ]
    shapes = [jax.ShapeDtypeStruct((blocks, columns), jnp.float32) for _ in mats]
    shapes.append(
        jax.ShapeDtypeStruct((size, narrow.shape[0] // size, narrow.shape[1]), jnp.float32)
    )
    shapes.append(jax.ShapeDtypeStruct(vector.shape, jnp.float32))
    flat = [item for mat in mats for item in mat]
    results = pl.pallas_call(
        functools.partial(finish_kernel, parts, len(mats), bits, blocks),
        out_shape=shapes,
        in_specs=[pl.BlockSpec(memory_space=pl.ANY)] * (len(flat) + 1)
        + [pl.BlockSpec(memory_space=pltpu.VMEM)],
        out_specs=[pl.BlockSpec(memory_space=pltpu.VMEM)] * len(shapes),
        scratch_shapes=scratch,
        compiler_params=pltpu.CompilerParams(
            collective_id=2, has_side_effects=True, vmem_limit_bytes=FINISH_LIMIT
        ),
        name="finish",
    )(*flat, narrow, vector)
    return results[:-2], results[-2], results[-1]


def head_gather(block):
    if lax.axis_size("head") != 2:
        return lax.all_gather(block, "head", axis=1, tiled=True)
    other = xor_permute(block, "head", 0)
    mine = lax.axis_index("head") == 0
    return jnp.concatenate(
        [jnp.where(mine, block, other), jnp.where(mine, other, block)], axis=1
    )


HEAD_GROUP = 8
VMEM_LIMIT = 56 * 1024 * 1024
FAR = 1 << 30
NN = ((1,), (0,))
NT = ((1,), (1,))
TN = ((0,), (0,))


def low_dot(left, right, dims):
    return lax.dot_general(
        left.astype(jnp.bfloat16),
        right.astype(jnp.bfloat16),
        (dims, ((), ())),
        preferred_element_type=jnp.float32,
    )


def halves_of(value):
    high = value.astype(jnp.bfloat16)
    return high, (value - high.astype(jnp.float32)).astype(jnp.bfloat16)


def thirds_of(value):
    first = value.astype(jnp.bfloat16).astype(jnp.float32)
    second = (value - first).astype(jnp.bfloat16).astype(jnp.float32)
    return first, second, value - first - second


def spread_matrix(heads, head_dim):
    shape = (heads, heads * head_dim)
    rows = lax.broadcasted_iota(jnp.int32, shape, 0)
    columns = lax.broadcasted_iota(jnp.int32, shape, 1)
    return (columns // head_dim == rows).astype(jnp.float32)


def turned(rows, matrix):
    return low_dot(
        jnp.concatenate(thirds_of(rows), axis=0), jnp.concatenate([matrix] * 3, axis=0), TN
    )


def head_sums(spread, value):
    high, low = halves_of(value)
    return low_dot(spread, high, NT) + low_dot(spread, low, NT)


def map_dot(left, right):
    high, low = halves_of(right)
    return low_dot(
        jnp.concatenate([left, left], axis=1), jnp.concatenate([high, low], axis=1), NT
    )


def fine_dot(left, right):
    left_high, left_low = halves_of(left)
    right_high, right_low = halves_of(right)
    return (
        low_dot(left_high, right_high, NN)
        + low_dot(left_high, right_low, NN)
        + low_dot(left_low, right_high, NN)
    )


def sigmoid(value):
    return 1.0 / (1.0 + jnp.exp(-value))


def segment_of(places, starts_ref, micro):
    label = jnp.zeros_like(places)
    for number in range(starts_ref.shape[1]):
        label = label + jnp.where(places >= starts_ref[micro, number], 1, 0)
    return label


def same_segment(count, base_ref, starts_ref, taps):
    micro = pl.program_id(0)
    places = base_ref[0] + lax.broadcasted_iota(jnp.int32, (count, 1), 0)
    own = segment_of(places, starts_ref, micro)
    return [
        jnp.where(segment_of(places - shift, starts_ref, micro) == own, 1.0, 0.0)
        for shift in range(1, taps)
    ]


def pair_labels(count, base_ref, starts_ref):
    micro = pl.program_id(0)
    column = base_ref[0] + lax.broadcasted_iota(jnp.int32, (count, 1), 0)
    row = base_ref[0] + lax.broadcasted_iota(jnp.int32, (1, count), 1)
    return segment_of(column, starts_ref, micro) == segment_of(row, starts_ref, micro)


def conv_sum(ext, value, halo, weight, bias, masks):
    count = value.shape[0]
    ext[0:8, :] = halo
    ext[8 : 8 + count, :] = value
    total = bias + weight[0:1] * value
    for shift in range(1, weight.shape[0]):
        total = (
            total
            + weight[shift : shift + 1]
            * ext[8 - shift : 8 - shift + count, :]
            * masks[shift - 1]
        )
    return total


def front_kernel(
    head_dim,
    base_ref,
    starts_ref,
    x_ref,
    halo_ref,
    weight_ref,
    bias_ref,
    b_ref,
    tail_ref,
    low_ref,
    state_ref,
    ext,
):
    heads = tail_ref.shape[1]
    weight = weight_ref[...]
    masks = same_segment(x_ref.shape[2], base_ref, starts_ref, weight.shape[0])
    total = conv_sum(ext, x_ref[0, 0], halo_ref[0], weight, bias_ref[...], masks)
    act = (total * sigmoid(total)).astype(jnp.bfloat16)
    low_ref[0] = act
    scale = turned(tail_ref[0], spread_matrix(heads, head_dim))
    high, low = halves_of(act.astype(jnp.float32) * scale)
    state_ref[0] = low_dot(high, b_ref[0], TN) + low_dot(low, b_ref[0], TN)


def mix_kernel(
    head_dim,
    base_ref,
    starts_ref,
    x_ref,
    b_ref,
    c_ref,
    run_ref,
    step_ref,
    carry_ref,
    start_ref,
    gate_ref,
    cot_ref,
    gain_ref,
    skip_ref,
    mixed_ref,
    sums_ref,
):
    heads = step_ref.shape[1]
    count = x_ref.shape[1]
    spread = spread_matrix(heads, head_dim)
    x = x_ref[0]
    b, c = b_ref[0], c_ref[0]
    rows = lax.broadcasted_iota(jnp.int32, (count, count), 0)
    columns = lax.broadcasted_iota(jnp.int32, (count, count), 1)
    valid = pair_labels(count, base_ref, starts_ref) & (rows >= columns)
    scores = jnp.where(valid, low_dot(c, b, NT), 0.0)
    wide = x.astype(jnp.float32)
    scaled = (wide * turned(step_ref[0], spread)).astype(jnp.bfloat16)
    inter = map_dot(c, start_ref[0]) * turned(carry_ref[0], spread)
    run_row = run_ref[0]
    run = turned(run_row, spread_matrix(heads, 1))
    pair = 2 * head_dim
    middle = count // 2
    lane = lax.broadcasted_iota(jnp.int32, (count, pair), 1)
    results = []
    for first in range(0, heads, 2):
        block = scaled[:, first * head_dim : first * head_dim + pair]
        halves = []
        for head in (first, first + 1):
            strips = []
            for top, cut in ((0, middle), (middle, count)):
                gap = run[top:cut, head : head + 1] - run_row[head : head + 1, :cut]
                weights = jnp.exp(jnp.minimum(gap, 0.0)) * scores[top:cut, :cut]
                strips.append(low_dot(weights, block[:cut], NN))
            halves.append(jnp.concatenate(strips, axis=0))
        results.append(jnp.where(lane < head_dim, halves[0], halves[1]))
    mixed = jnp.concatenate(results, axis=1) + inter + skip_ref[...] * wide
    mixed_ref[0] = mixed
    gate = gate_ref[0, 0]
    gated = mixed * (gate * sigmoid(gate))
    square = jnp.sum(gated * gated, axis=1, keepdims=True)
    cross = jnp.sum(cot_ref[0] * gain_ref[...] * gated, axis=1, keepdims=True)
    both = jnp.concatenate([square, cross], axis=1)

    @pl.when(pl.program_id(1) == 0)
    def _():
        sums_ref[0] = both

    @pl.when(pl.program_id(1) > 0)
    def _():
        sums_ref[0] = sums_ref[0] + both


def gate_kernel(
    head_dim,
    full,
    mixed_ref,
    gate_ref,
    cot_ref,
    sums_ref,
    gain_ref,
    carry_ref,
    c_ref,
    norm_ref,
    grad_gate_ref,
    both_ref,
    grad_mixed_ref,
    start_ref,
    rows_ref,
):
    heads = carry_ref.shape[1]
    mixed, gate, cot, gain = mixed_ref[0], gate_ref[0, 0], cot_ref[0], gain_ref[...]
    scale = lax.rsqrt(sums_ref[0, :, 0:1] / full + EPSILON)
    sigma = sigmoid(gate)
    act = gate * sigma
    gated = mixed * act
    unit = gated * scale
    norm_ref[0] = (unit * gain).astype(jnp.bfloat16)
    pull = scale * scale * scale * sums_ref[0, :, 1:2] / full
    grad_gated = cot * gain * scale - gated * pull
    grad_gate = (grad_gated * mixed * sigma * (1.0 + gate * (1.0 - sigma))).astype(jnp.bfloat16)
    grad_gate_ref[0] = grad_gate
    both_ref[0, 0] = grad_gate
    grad_mixed = (grad_gated * act).astype(jnp.bfloat16)
    grad_mixed_ref[0] = grad_mixed
    carried = grad_mixed.astype(jnp.float32) * turned(
        carry_ref[0], spread_matrix(heads, head_dim)
    )
    high, low = halves_of(carried)
    start_ref[0] = low_dot(high, c_ref[0], TN) + low_dot(low, c_ref[0], TN)
    gains = jnp.sum(cot * unit, axis=0, keepdims=True)
    rows_ref[0] = jnp.concatenate([gains, jnp.zeros((7, gains.shape[1]), jnp.float32)], axis=0)


def back_kernel(
    head_dim,
    base_ref,
    starts_ref,
    x_ref,
    g_ref,
    b_ref,
    c_ref,
    run_ref,
    step_ref,
    carry_ref,
    tail_ref,
    start_ref,
    end_ref,
    pre_ref,
    halo_ref,
    weight_ref,
    bias_ref,
    skip_ref,
    both_in_ref,
    both_ref,
    edge_ref,
    halo_out_ref,
    rows_ref,
    direct_ref,
    decay_ref,
    pair_ref,
    grad_b_ref,
    grad_c_ref,
    ext,
    moved,
):
    heads = step_ref.shape[1]
    count = x_ref.shape[1]
    spread = spread_matrix(heads, head_dim)
    x, g, b, c = x_ref[0], g_ref[0], b_ref[0], c_ref[0]
    x_wide, g_wide = x.astype(jnp.float32), g.astype(jnp.float32)
    rows = lax.broadcasted_iota(jnp.int32, (count, count), 0)
    columns = lax.broadcasted_iota(jnp.int32, (count, count), 1)
    valid = pair_labels(count, base_ref, starts_ref) & (columns >= rows)
    scores = jnp.where(valid, low_dot(b, c, NT), 0.0)
    upto = (rows >= columns).astype(jnp.bfloat16)
    before = (rows < columns).astype(jnp.float32)
    step = turned(step_ref[0], spread)
    carry = turned(carry_ref[0], spread)
    tail = turned(tail_ref[0], spread)
    scaled_wide = x_wide * step
    scaled, scaled_rest = halves_of(scaled_wide)
    start, end = start_ref[0], end_ref[0]
    run_row = run_ref[0]
    run = turned(run_row, spread_matrix(heads, 1))
    pair = 2 * head_dim
    lane = lax.broadcasted_iota(jnp.int32, (count, pair), 1)
    middle = count // 2
    score_grads = [
        jnp.zeros((middle, count), jnp.float32),
        jnp.zeros((count - middle, count - middle), jnp.float32),
    ]
    results, straddles = [], []
    for first in range(0, heads, 2):
        cut = slice(first * head_dim, first * head_dim + pair)
        g_block = g[:, cut]
        g_swap = jnp.concatenate([g_block[:, head_dim:], g_block[:, :head_dim]], axis=1)
        x_block, x_rest = scaled[:, cut], scaled_rest[:, cut]
        x_rest = jnp.concatenate([x_rest[:, head_dim:], x_rest[:, :head_dim]], axis=1)
        halves = []
        for head in (first, first + 1):
            own = (lane < head_dim) if head == first else (lane >= head_dim)
            x_own, g_own = jnp.where(own, x_block, x_rest), jnp.where(own, g_block, g_swap)
            strips, straddle = [], None
            for part, (top, cut) in enumerate(((0, middle), (middle, count))):
                gap = run_row[head : head + 1, top:] - run[top:cut, head : head + 1]
                fade = jnp.exp(jnp.minimum(gap, 0.0))
                weights = fade * scores[top:cut, top:]
                strips.append(low_dot(weights, g_block[top:], NN))
                inner = low_dot(x_own[top:cut], g_own[top:], NT)
                score_grads[part] = score_grads[part] + fade * inner
                sums = low_dot(weights * inner, upto[top:, top:], NN)
                sums = jnp.sum(sums * before[top:cut, top:], axis=0, keepdims=True)
                if part == 0:
                    straddle = sums
                else:
                    straddle = jnp.concatenate(
                        [straddle[:, :middle], straddle[:, middle:] + sums], axis=1
                    )
            straddles.append(straddle)
            halves.append(jnp.concatenate(strips, axis=0))
        results.append(jnp.where(lane < head_dim, halves[0], halves[1]))
    score_grad = jnp.concatenate(
        [
            score_grads[0],
            jnp.concatenate([jnp.zeros((count - middle, middle), jnp.float32), score_grads[1]], axis=1),
        ],
        axis=0,
    )
    score_grad = jnp.where(valid, score_grad, 0.0)
    later = map_dot(b, end) * tail
    values = jnp.concatenate(results, axis=1) + later
    inter = map_dot(c, start) * carry
    direct_ref[0] = head_sums(spread, x_wide * values)
    given = head_sums(spread, scaled_wide * later)
    taken = head_sums(spread, g_wide * inter)
    flows = jnp.concatenate([given, taken], axis=0)
    flow_pieces = [item.astype(jnp.bfloat16) for item in thirds_of(flows)]
    after = (rows < columns).astype(jnp.bfloat16)
    flow_later = sum(low_dot(item, after, NN) for item in flow_pieces)
    flow_sooner = sum(low_dot(item, upto, NN) for item in flow_pieces)
    decay_ref[0] = (
        jnp.concatenate(straddles, axis=0) + flow_later[:heads] + flow_sooner[heads:]
    )
    pair_high, pair_low = halves_of(start * end)
    pair_ref[0] = low_dot(spread, pair_high, NN) + low_dot(spread, pair_low, NN)
    grads_high, grads_low = halves_of(score_grad)
    grad_c = fine_dot(g_wide * carry, start) + low_dot(grads_high, b, TN) + low_dot(grads_low, b, TN)
    grad_b = fine_dot(scaled_wide * tail, end) + low_dot(grads_high, c, NN) + low_dot(grads_low, c, NN)

    @pl.when(pl.program_id(1) == 0)
    def _():
        grad_b_ref[0] = grad_b
        grad_c_ref[0] = grad_c

    @pl.when(pl.program_id(1) > 0)
    def _():
        grad_b_ref[0] = grad_b_ref[0] + grad_b
        grad_c_ref[0] = grad_c_ref[0] + grad_c

    weight, pre = weight_ref[...], pre_ref[0, 0]
    masks = same_segment(count, base_ref, starts_ref, weight.shape[0])
    total = conv_sum(ext, pre, halo_ref[0], weight, bias_ref[...], masks)
    sigma = sigmoid(total)
    grad_conv = (values * step + skip_ref[...] * g_wide) * (
        sigma * (1.0 + total * (1.0 - sigma))
    )
    moved[0:8, :] = jnp.zeros_like(moved[0:8, :])
    moved[8 + count :, :] = jnp.zeros_like(moved[8 + count :, :])
    sums = [jnp.sum(grad_conv * pre, axis=0, keepdims=True)]
    back = jnp.concatenate(
        [jnp.zeros((8, pre.shape[1]), jnp.float32), grad_conv * weight[0:1]], axis=0
    )
    for shift in range(1, weight.shape[0]):
        part = grad_conv * masks[shift - 1]
        sums.append(
            jnp.sum(part * ext[8 - shift : 8 - shift + count, :], axis=0, keepdims=True)
        )
        moved[8 : 8 + count, :] = part * weight[shift : shift + 1]
        back = back + moved[shift : shift + 8 + count, :]
    halo_out_ref[0] = back[:8]
    both_ref[0, 0] = back[8:].astype(jnp.bfloat16)
    edge_ref[0] = back[count:]
    sums.append(jnp.sum(grad_conv, axis=0, keepdims=True))
    sums.append(jnp.sum(g_wide * x_wide, axis=0, keepdims=True))
    sums.append(jnp.zeros((8 - len(sums), pre.shape[1]), jnp.float32))
    rows_ref[0] = jnp.concatenate(sums, axis=0)


def blocked(kernel, name, grid, ins, outs, scratch=(), micros=0, aliases=None):
    moved = sum(item[0].size * item[0].dtype.itemsize for item in ins if item[1] != "any")
    moved += sum(math.prod(item[2]) * grid[0] * grid[1] * jnp.dtype(item[1]).itemsize for item in outs)

    def spec(item):
        if item[1] is None:
            return pl.BlockSpec(memory_space=pltpu.SMEM)
        if item[1] == "any":
            return pl.BlockSpec(memory_space=pl.ANY)
        return pl.BlockSpec(item[1], item[2])

    return pl.pallas_call(
        kernel,
        grid=grid,
        in_specs=[spec(item) for item in ins],
        out_specs=[pl.BlockSpec(item[2], item[3]) for item in outs],
        out_shape=[jax.ShapeDtypeStruct(item[0], item[1]) for item in outs],
        scratch_shapes=list(scratch),
        input_output_aliases=aliases or {},
        compiler_params=pltpu.CompilerParams(
            dimension_semantics=("arbitrary",) * len(grid), vmem_limit_bytes=VMEM_LIMIT
        ),
        cost_estimate=pl.CostEstimate(
            flops=micros * 1_000_000_000, bytes_accessed=moved, transcendentals=0
        ),
        name=name,
    )(*[item[0] for item in ins])


def body(
    tokens,
    norm_gain,
    in_weight,
    bc_weight,
    dt_weight,
    dt_bias,
    a_log,
    conv_weight,
    conv_bias,
    bc_conv_weight,
    bc_conv_bias,
    d_skip,
    gate_gain,
    out_weight,
    cotangent,
    seq_lengths,
):
    micro, length, width = tokens.shape
    heads = dt_bias.shape[0]
    inner = conv_bias.shape[0]
    head_dim = inner // heads
    state_size = bc_weight.shape[1] // 2
    taps = conv_weight.shape[0]
    total = micro * length
    head_count = lax.axis_size("head")
    full_inner = inner * head_count
    group = min(HEAD_GROUP, heads)
    groups = heads // group
    wide = group * head_dim
    base = lax.axis_index("seq").astype(jnp.int32) * length
    labels = segment_ids(seq_lengths, base - (taps - 1), length + taps - 1, micro)
    own_labels = labels[:, taps - 1 :]
    before_labels = labels[:, taps - 2]
    starts = jnp.cumsum(seq_lengths, axis=-1).astype(jnp.int32) - seq_lengths
    long_starts = jnp.full((micro - starts.shape[0], starts.shape[1]), FAR, jnp.int32)
    starts = jnp.concatenate([starts, long_starts.at[:, 0].set(0)], axis=0)
    base_item, starts_item = (base[None], None), (starts, None)

    flat = tokens.reshape(total, width).astype(jnp.float32)
    cot_flat = cotangent.reshape(total, width)
    normed, norm_back = jax.vjp(rms_scale, flat, norm_gain)
    normed_low = normed.astype(jnp.bfloat16)
    gate_x = jnp.einsum(
        "td,dkc->ktc", normed_low, in_weight, preferred_element_type=jnp.float32
    ).reshape(2, micro, length, inner)
    bc_pre = jnp.dot(normed_low, bc_weight, preferred_element_type=jnp.float32).reshape(
        micro, length, 2 * state_size
    )
    delta_pre = lax.dot_general(
        dt_weight, normed_low, (((0,), (1,)), ((), ())), preferred_element_type=jnp.float32
    )
    left = shifted(
        jnp.concatenate(
            [gate_x[1, :, length - taps + 1 :], bc_pre[:, length - taps + 1 :]], axis=-1
        ),
        "seq",
        1,
    )
    left_x, left_bc = left[..., :inner], left[..., inner:]
    halo = jnp.pad(left_x, ((0, 0), (9 - taps, 0), (0, 0)))
    conv_many = jax.vmap(conv_silu, in_axes=(0, None, None, 0))
    bc_act, bc_conv_back = jax.vjp(
        lambda extended, weight, bias: conv_many(extended, weight, bias, labels),
        jnp.concatenate([left_bc, bc_pre], axis=1),
        bc_conv_weight,
        bc_conv_bias,
    )
    bc_low = bc_act.astype(jnp.bfloat16)
    b_low, c_low = bc_low[..., :state_size], bc_low[..., state_size:]
    (delta, decay), rate_back = jax.vjp(step_sizes, delta_pre, dt_bias, a_log)

    def by_micro(array):
        return array.reshape(heads, micro, length).transpose(1, 0, 2)

    def by_head(array):
        return array.transpose(1, 0, 2).reshape(heads, total)

    delta, decay = by_micro(delta), by_micro(decay)
    order = jnp.arange(length)
    running = jnp.einsum(
        "mhj,ji->mhi",
        decay,
        (order[:, None] <= order[None, :]).astype(jnp.float32),
        precision=HIGHEST,
    )
    device_log = running[:, :, -1]
    live = (own_labels == before_labels[:, None]).astype(jnp.float32)
    last = (own_labels == own_labels[:, -1:]).astype(jnp.float32)
    carried = jnp.exp(running) * live[:, None]
    tail = jnp.exp(device_log[:, :, None] - running) * last[:, None]
    device_live = live[:, -1]
    gain_row, skip_row = gate_gain[None], jnp.repeat(d_skip, head_dim)[None]
    conv_row = conv_bias[None]

    grid = (micro, groups)
    token_block = (1, length, wide)
    in_token = lambda m, k: (m, 0, k)
    half_block = (1, 1, length, wide)
    in_gate, in_x = lambda m, k: (0, m, 0, k), lambda m, k: (1, m, 0, k)
    row_block, in_row = (1, group, length), lambda m, k: (m, k, 0)
    map_block, in_map = (1, length, state_size), lambda m, k: (m, 0, 0)
    state_block, in_state = (1, wide, state_size), lambda m, k: (m, k, 0)
    halo_block = (1, 8, wide)
    flat_block, in_flat = (1, wide), lambda m, k: (0, k)
    conv_item = (conv_weight, (taps, wide), in_flat)
    whole = (micro, length, inner)
    state_shape = (micro, inner, state_size)
    row_shape = (micro, heads, length)

    x_low, device_state = blocked(
        functools.partial(front_kernel, head_dim),
        "front",
        grid,
        [
            base_item,
            starts_item,
            (gate_x, half_block, in_x),
            (halo, halo_block, in_token),
            conv_item,
            (conv_row, flat_block, in_flat),
            (b_low, map_block, in_map),
            (tail * delta, row_block, in_row),
        ],
        [
            (whole, jnp.bfloat16, token_block, in_token),
            (state_shape, jnp.float32, state_block, in_state),
        ],
        [pltpu.VMEM((length + 8, wide), jnp.float32)],
        20,
    )
    exchange_log = jnp.where(device_live[:, None] > 0.0, device_log, DEAD)
    exchange_shape = (micro, heads, head_dim, state_size)
    parts = scatter_parts(inner, axis_bits("seq"))
    orders = tuple(order for order, _ in parts)
    tiled = (width >> axis_bits("seq")) % 128 == 0
    incoming, arranged = exchange(
        device_state.reshape(exchange_shape),
        exchange_log,
        False,
        (cot_flat, normed_low) if tiled else (),
        orders if tiled else (),
    )
    if not tiled:
        arranged = arrange(cot_flat, orders) + arrange(normed_low, orders)
    cot_parts, normed_parts = arranged[: 2 * len(parts)], arranged[2 * len(parts) :]
    incoming = incoming.reshape(state_shape)

    grad_gate_n = jnp.dot(cot_flat, out_weight, preferred_element_type=jnp.float32).reshape(whole)
    mixed, sums = blocked(
        functools.partial(mix_kernel, head_dim),
        "mix",
        grid,
        [
            base_item,
            starts_item,
            (x_low, token_block, in_token),
            (b_low, map_block, in_map),
            (c_low, map_block, in_map),
            (running, row_block, in_row),
            (delta, row_block, in_row),
            (carried, row_block, in_row),
            (incoming, state_block, in_state),
            (gate_x, half_block, in_gate),
            (grad_gate_n, token_block, in_token),
            (gain_row, flat_block, in_flat),
            (skip_row, flat_block, in_flat),
        ],
        [
            (whole, jnp.float32, token_block, in_token),
            ((micro, length, 2), jnp.float32, (1, length, 2), in_map),
        ],
        (),
        25,
    )
    sums = all_sum(sums, "head")
    normed_gate, grad_gate_pre, grad_gate_x, grad_mixed, device_grad, gate_rows = blocked(
        functools.partial(gate_kernel, head_dim, float(full_inner)),
        "gate",
        grid,
        [
            (mixed, token_block, in_token),
            (gate_x, half_block, in_gate),
            (grad_gate_n, token_block, in_token),
            (sums, (1, length, 2), in_map),
            (gain_row, flat_block, in_flat),
            (carried, row_block, in_row),
            (c_low, map_block, in_map),
        ],
        [
            (whole, jnp.bfloat16, token_block, in_token),
            (whole, jnp.bfloat16, token_block, in_token),
            ((2,) + whole, jnp.bfloat16, half_block, in_gate),
            (whole, jnp.bfloat16, token_block, in_token),
            (state_shape, jnp.float32, state_block, in_state),
            ((micro, 8, inner), jnp.float32, halo_block, in_token),
        ],
        (),
        20,
    )
    normed_gate = normed_gate.reshape(total, inner)
    grad_gate_pre = grad_gate_pre.reshape(total, inner)
    grad_gate_gain = jnp.sum(gate_rows[:, 0], axis=0)

    out_sent = sent_products(cot_parts, normed_gate, parts)
    gate_sent = sent_products(normed_parts, grad_gate_pre, parts)
    outgoing, _ = exchange(device_grad.reshape(exchange_shape), exchange_log, True)
    outgoing, out_sent, gate_sent = lax.optimization_barrier((outgoing, out_sent, gate_sent))
    out_arrived = send_parts(out_sent, parts)
    gate_arrived = send_parts(gate_sent, parts)
    outgoing = outgoing.reshape(state_shape)
    grad_gate_x, edge, halo_grad, conv_rows, direct, fading, pairs, grad_b, grad_c = blocked(
        functools.partial(back_kernel, head_dim),
        "back",
        grid,
        [
            base_item,
            starts_item,
            (x_low, token_block, in_token),
            (grad_mixed, token_block, in_token),
            (b_low, map_block, in_map),
            (c_low, map_block, in_map),
            (running, row_block, in_row),
            (delta, row_block, in_row),
            (carried, row_block, in_row),
            (tail, row_block, in_row),
            (incoming, state_block, in_state),
            (outgoing, state_block, in_state),
            (gate_x, half_block, in_x),
            (halo, halo_block, in_token),
            conv_item,
            (conv_row, flat_block, in_flat),
            (skip_row, flat_block, in_flat),
            (grad_gate_x, "any"),
        ],
        [
            ((2,) + whole, jnp.bfloat16, half_block, in_x),
            ((micro, 8, inner), jnp.float32, halo_block, in_token),
            ((micro, 8, inner), jnp.float32, halo_block, in_token),
            ((micro, 8, inner), jnp.float32, halo_block, in_token),
            (row_shape, jnp.float32, row_block, in_row),
            (row_shape, jnp.float32, row_block, in_row),
            ((micro, heads, state_size), jnp.float32, (1, group, state_size), in_state),
            ((micro, length, state_size), jnp.float32, map_block, in_map),
            ((micro, length, state_size), jnp.float32, map_block, in_map),
        ],
        [
            pltpu.VMEM((length + 8, wide), jnp.float32),
            pltpu.VMEM((length + 16, wide), jnp.float32),
        ],
        80,
        {17: 0},
    )
    halo_grad, grad_b, grad_gate_x, out_arrived, gate_arrived = lax.optimization_barrier(
        (halo_grad, grad_b, grad_gate_x, out_arrived, gate_arrived)
    )
    grad_bc = all_sum(jnp.concatenate([grad_b, grad_c], axis=-1), "head")
    kept = jnp.sum(pairs, axis=-1) * jnp.exp(device_log) * device_live[:, None]
    grad_decay = by_head(fading + kept[:, :, None])
    grad_delta_pre, grad_dt_bias, grad_a_log = rate_back((by_head(direct), grad_decay))
    conv_rows = jnp.sum(conv_rows, axis=0)
    grad_conv_weight, grad_conv_bias = conv_rows[:taps], conv_rows[taps]
    grad_d_skip = jnp.sum(conv_rows[taps + 1].reshape(heads, head_dim), axis=-1)
    grad_bc_ext, grad_bc_conv_weight, grad_bc_conv_bias = bc_conv_back(grad_bc)
    right = shifted(
        jnp.concatenate([halo_grad[:, 9 - taps :], grad_bc_ext[:, : taps - 1]], axis=-1), "seq", -1
    )
    right_x, right_bc = right[..., :inner], right[..., inner:]
    grad_gate_x = lax.dynamic_update_slice(
        grad_gate_x,
        (edge[:, 9 - taps :] + right_x).astype(jnp.bfloat16)[None],
        (1, 0, length - taps + 1, 0),
    )
    grad_bc_pre = grad_bc_ext[:, taps - 1 :].at[:, length - taps + 1 :].add(right_bc)
    bc_flat = grad_bc_pre.reshape(total, 2 * state_size)
    grad_gate_x = grad_gate_x.reshape(2, total, inner)
    x_sent = sent_products(normed_parts, grad_gate_x[1], parts)
    grad_gate_x, x_sent = lax.optimization_barrier((grad_gate_x, x_sent))
    x_arrived = send_parts(x_sent, parts)

    row_part = jnp.einsum(
        "ktc,dkc->td", grad_gate_x, in_weight, preferred_element_type=jnp.float32
    )
    bc_high, bc_rest = halves_of(bc_flat * (1.0 / head_count))
    delta_high, delta_rest = halves_of(grad_delta_pre.T)
    narrow_left = jnp.concatenate([bc_high, bc_rest, delta_high, delta_rest], axis=1)
    narrow_right = jnp.concatenate([bc_weight, bc_weight, dt_weight, dt_weight], axis=1)
    row_part = row_part + lax.dot_general(
        narrow_left, narrow_right, (NT, ((), ())), preferred_element_type=jnp.float32
    )
    row_grads = all_sum(row_part, "head")
    grad_flat, grad_norm_gain = norm_back(row_grads)
    grad_tokens = (cot_flat.astype(jnp.float32) + grad_flat).reshape(micro, length, width)

    share_bc = 2 * state_size // head_count
    own_bc = lax.dynamic_slice_in_dim(bc_flat, lax.axis_index("head") * share_bc, share_bc, 1)
    across = share_bc + heads
    narrow_high, narrow_rest = halves_of(jnp.concatenate([own_bc, grad_delta_pre.T], axis=1))
    both = jnp.concatenate([narrow_high, narrow_rest], axis=1)
    narrow = jnp.concatenate(
        [product(normed_parts[1], both), product(normed_parts[0], both)], axis=0
    )
    narrow = narrow[:, :across] + narrow[:, across:]
    size = lax.axis_size("seq")
    row_count = width // size
    narrow = narrow.reshape(size, row_count, across)
    beside = 128 // heads
    narrow_bc = jnp.pad(narrow[:, :, :share_bc], ((0, 0), (0, 0), (0, -share_bc % 128)))
    narrow_steps = narrow[:, :, share_bc:].reshape(size, row_count // beside, 128)
    narrow_steps = jnp.pad(narrow_steps, ((0, 0), (0, 0), (0, narrow_bc.shape[2] - 128)))
    narrow = jnp.concatenate([narrow_bc, narrow_steps], axis=1)
    narrow_rows = narrow.shape[1]
    narrow = jnp.pad(narrow, ((0, 0), (0, -narrow_rows % 8), (0, 0)))
    narrow = narrow.reshape(-1, narrow.shape[2])

    small = [
        grad_bc_conv_weight,
        grad_bc_conv_bias,
        grad_norm_gain,
        grad_dt_bias,
        grad_a_log,
        grad_d_skip,
        grad_conv_weight,
        grad_conv_bias,
        grad_gate_gain,
    ]
    row = jnp.concatenate([item.reshape(-1) for item in small])
    count = row.size
    row = jnp.pad(row, (0, -count % 1024)).reshape(-1, 128)

    mats = [
        keep_parts(cot_parts, normed_gate, parts, out_arrived),
        keep_parts(normed_parts, grad_gate_pre, parts, gate_arrived),
        keep_parts(normed_parts, grad_gate_x[1], parts, x_arrived),
    ]
    (grad_out_weight, gate_block, x_block), gathered, row = finish(parts, mats, narrow, row)
    grad_in_weight = jnp.stack([gate_block, x_block], axis=1)
    grad_bc_weight = head_gather(gathered[:, :row_count, :share_bc].reshape(width, share_bc))
    grad_dt_weight = gathered[:, row_count:narrow_rows, :128].reshape(width, heads)
    row = row.reshape(-1)
    sizes, first = [], 0
    for item in small:
        sizes.append(row[first : first + item.size].reshape(item.shape))
        first += item.size
    (
        grad_bc_conv_weight,
        grad_bc_conv_bias,
        grad_norm_gain,
        grad_dt_bias,
        grad_a_log,
        grad_d_skip,
        grad_conv_weight,
        grad_conv_bias,
        grad_gate_gain,
    ) = sizes

    share = width // head_count
    if head_count == 2:
        first = lax.axis_index("head") * share
        own_rows = lax.dynamic_slice_in_dim(out_weight, first, share, 0)
        other_rows = lax.dynamic_slice_in_dim(out_weight, share - first, share, 0)
        summed = lax.dot_general(
            normed_gate, own_rows, (NT, ((), ())), preferred_element_type=jnp.float32
        ) + xor_permute(
            lax.dot_general(
                normed_gate, other_rows, (NT, ((), ())), preferred_element_type=jnp.float32
            ),
            "head",
            0,
        )
    else:
        head_terms = lax.dot_general(
            normed_gate, out_weight, (NT, ((), ())), preferred_element_type=jnp.float32
        )
        summed = lax.psum_scatter(head_terms, "head", scatter_dimension=1, tiled=True)
    residual = lax.dynamic_slice_in_dim(flat, lax.axis_index("head") * share, share, 1)
    block_out = (residual + summed).astype(jnp.bfloat16).reshape(micro, length, share)
    return (
        block_out,
        grad_tokens,
        grad_norm_gain,
        grad_in_weight,
        grad_bc_weight,
        grad_dt_weight,
        grad_dt_bias,
        grad_a_log,
        grad_d_skip,
        grad_conv_weight,
        grad_conv_bias,
        grad_bc_conv_weight,
        grad_bc_conv_bias,
        grad_gate_gain,
        grad_out_weight,
    )


def solution(mesh):
    return jax.shard_map(
        body,
        mesh=mesh,
        in_specs=(
            P(None, "seq", None),
            P(),
            P(None, None, "head"),
            P(),
            P(None, "head"),
            P("head"),
            P("head"),
            P(None, "head"),
            P("head"),
            P(),
            P(),
            P("head"),
            P("head"),
            P(None, "head"),
            P(None, "seq", None),
            P(),
        ),
        out_specs=(
            P(None, "seq", "head"),
            P(None, "seq", None),
            P(),
            P("seq", None, "head"),
            P(),
            P(None, "head"),
            P("head"),
            P("head"),
            P("head"),
            P(None, "head"),
            P("head"),
            P(),
            P(),
            P("head"),
            P("seq", "head"),
        ),
        check_vma=False,
    )
```

```python
import functools
import math

import jax
import jax.numpy as jnp
from jax import lax
from jax.experimental import pallas as pl
from jax.experimental.pallas import tpu as pltpu
from jax.sharding import PartitionSpec as P

EPSILON = 1e-05
HIGHEST = lax.Precision.HIGHEST


def shifted(shard, axis, by):
    length = lax.axis_size(axis)
    pairs = [(i, i + by) for i in range(length) if 0 <= i + by < length]
    return lax.ppermute(shard, axis, pairs)


def segment_ids(seq_lengths, first, count, micro):
    places = first + jnp.arange(count, dtype=jnp.int32)
    starts = jnp.cumsum(seq_lengths, axis=-1) - seq_lengths
    short_ids = (
        jnp.sum((starts[:, None, :] <= places[None, :, None]).astype(jnp.int32), axis=-1) - 1
    )
    long_ids = jnp.zeros((micro - seq_lengths.shape[0], count), jnp.int32)
    labels = jnp.concatenate([short_ids, long_ids], axis=0)
    return jnp.where(places[None, :] >= 0, labels, -1)


def rms_scale(values, gain):
    return values * lax.rsqrt(jnp.mean(values * values, axis=-1, keepdims=True) + EPSILON) * gain


def conv_silu(extended, weight, bias, labels):
    taps = weight.shape[0]
    count = extended.shape[0] - taps + 1
    own = labels[taps - 1 :]
    total = bias + weight[0] * extended[taps - 1 :]
    for shift in range(1, taps):
        first = taps - 1 - shift
        mask = (labels[first : first + count] == own).astype(extended.dtype)
        total = total + weight[shift] * extended[first : first + count] * mask[:, None]
    return jax.nn.silu(total)


def step_sizes(delta_pre, dt_bias, a_log):
    delta = jax.nn.softplus(delta_pre + dt_bias[:, None])
    return (delta, -jnp.exp(a_log)[:, None] * delta)


DEAD = -1e30
EXCHANGE_COST = 100_000_000_000
FINISH_LIMIT = 60 * 1024 * 1024
GROUP = 4


def exchange_kernel(length, reverse, orders, jobs, part_ref, log_ref, *refs):
    refs = list(refs)
    sources = [refs.pop(0) for _ in range(2 if orders else 0)]
    job_refs = [[refs.pop(0) for _ in range(count)] for _, _, count in jobs]
    out_ref = refs.pop(0)
    steps = []
    for (make, parts, _), inputs in zip(jobs, job_refs):
        steps += make(inputs, refs.pop(0), parts)
    targets = [refs.pop(0) for _ in range(4 * len(orders))]
    (
        parts,
        logs,
        edge_in,
        edge_out,
        given,
        part_send,
        part_recv,
        log_send,
        log_recv,
        edge_send,
        edge_recv,
        given_send,
        given_recv,
        stage_sem,
        place_sem,
        staged,
    ) = refs
    me = lax.axis_index("seq")
    bits = (length - 1).bit_length()
    placed = arrange_copies(bits, orders, me, staged, targets, place_sem)
    stages = [
        pltpu.make_async_copy(source, staged.at[k], stage_sem.at[k])
        for k, source in enumerate(sources)
    ]
    for copy in stages:
        copy.start()
    rank = lax.rem(me, GROUP)
    plane = me // GROUP
    first = me - rank
    mates = (
        rank + 1 - 2 * lax.rem(rank, 2),
        rank + 2 - 4 * (rank // 2),
        3 - rank,
    )
    micro = part_ref.shape[0]
    planes = length // GROUP
    begins, ends = plane == 0, plane == planes - 1
    if reverse:
        begins, ends = ends, begins
    onward = -GROUP if reverse else GROUP

    barrier = pltpu.get_barrier_semaphore()
    for mate in mates:
        pl.semaphore_signal(
            barrier, inc=1, device_id={"seq": first + mate}, device_id_type=pl.DeviceIdType.MESH
        )

    @pl.when(plane > 0)
    def _():
        pl.semaphore_signal(
            barrier, inc=1, device_id={"seq": me - GROUP}, device_id_type=pl.DeviceIdType.MESH
        )

    @pl.when(plane < planes - 1)
    def _():
        pl.semaphore_signal(
            barrier, inc=1, device_id={"seq": me + GROUP}, device_id_type=pl.DeviceIdType.MESH
        )

    above = jnp.where(plane < planes - 1, 1, 0)
    below = jnp.where(plane > 0, 1, 0)
    pl.semaphore_wait(barrier, 3 + above + below)

    def remote(src, dst, send, recv, target):
        return pltpu.make_async_remote_copy(
            src_ref=src,
            dst_ref=dst,
            send_sem=send,
            recv_sem=recv,
            device_id={"seq": target},
            device_id_type=pl.DeviceIdType.MESH,
        )

    def log_copy(slot):
        mate = mates[slot]
        return remote(
            log_ref.at[mate], logs.at[rank], log_send.at[slot], log_recv.at[slot], first + mate
        )

    def part_copy(m, slot):
        mate = mates[slot]
        return remote(
            part_ref.at[m, mate],
            parts.at[m, rank],
            part_send.at[m, slot],
            part_recv.at[m, slot],
            first + mate,
        )

    def edge_copy(m):
        return remote(edge_out.at[m], edge_in.at[m], edge_send.at[m], edge_recv.at[m], me + onward)

    def given_copy(m, slot):
        mate = mates[slot]
        return remote(
            given.at[m, mate],
            out_ref.at[m, rank],
            given_send.at[m, slot],
            given_recv.at[m, slot],
            first + mate,
        )

    for slot in range(3):
        log_copy(slot).start()
    for m in range(micro):
        for slot in range(3):
            part_copy(m, slot).start()
    logs[rank] = log_ref[rank]
    for m in range(micro):
        parts[m, rank] = part_ref[m, rank]

    @pl.when(begins)
    def _():
        edge_in[...] = jnp.zeros_like(edge_in)

    for copy in stages:
        copy.wait()
    for copy in placed:
        copy.start()
    for slot in range(3):
        log_copy(slot).wait()
    order = tuple(reversed(range(GROUP))) if reverse else tuple(range(GROUP))
    for m in range(micro):
        for step in steps[m * len(steps) // micro : (m + 1) * len(steps) // micro]:
            step()
        for slot in range(3):
            part_copy(m, slot).wait()
        factors = [jnp.exp(logs[t, m])[:, None, :] for t in order]
        whole = jnp.exp(logs[0, m] + logs[1, m] + logs[2, m] + logs[3, m])[:, None, :]
        total = parts[m, order[0]]
        for t, factor in zip(order[1:], factors[1:]):
            total = total * factor + parts[m, t]

        @pl.when(jnp.logical_not(begins))
        def _():
            edge_copy(m).wait_recv()

        @pl.when(jnp.logical_not(ends))
        def _():
            edge_out[m] = total + whole * edge_in[m]
            edge_copy(m).start()

        running = edge_in[m]
        for place, (t, factor) in enumerate(zip(order, factors)):
            given[m, t] = running
            if place < GROUP - 1:
                running = running * factor + parts[m, t]
        for slot in range(3):
            given_copy(m, slot).start()
        out_ref[m, rank] = given[m, rank]
    for m in range(micro):
        for slot in range(3):
            given_copy(m, slot).wait()

        @pl.when(jnp.logical_not(ends))
        def _():
            edge_copy(m).wait_send()

    for copy in placed:
        copy.wait()


def exchange(parts, logs, reverse, sources=(), orders=(), jobs=()):
    micro, heads, rows, columns = parts.shape
    quarter = heads // GROUP
    length = lax.axis_size("seq")
    spread = jnp.broadcast_to(logs[:, :, None], (micro, heads, columns))
    spread = spread.reshape(micro, GROUP, quarter, columns).transpose(1, 0, 2, 3)
    shape = (micro, GROUP, quarter, rows, columns)
    arranged = []
    for source in sources:
        half = jax.ShapeDtypeStruct((source.shape[0], source.shape[1] // 2), source.dtype)
        arranged += [half] * (2 * len(orders))
    vmem = pl.BlockSpec(memory_space=pltpu.VMEM)
    hbm = pl.BlockSpec(memory_space=pl.ANY)
    made = [jax.ShapeDtypeStruct(job[3], jnp.float32) for job in jobs]
    count = len(arranged)
    arranged = made + arranged
    job_inputs = [item for job in jobs for item in job[2]]
    plans = tuple((job[0], job[1], len(job[2])) for job in jobs)
    out, *arranged = pl.pallas_call(
        functools.partial(exchange_kernel, length, reverse, orders, plans),
        out_shape=[jax.ShapeDtypeStruct(shape, jnp.float32)] + arranged,
        in_specs=[vmem] * 2 + [hbm] * (len(sources) + len(job_inputs)),
        out_specs=[vmem] + [hbm] * len(arranged),
        scratch_shapes=[
            pltpu.VMEM(shape, jnp.float32),
            pltpu.VMEM((GROUP, micro, quarter, columns), jnp.float32),
            pltpu.VMEM((micro, quarter, rows, columns), jnp.float32),
            pltpu.VMEM((micro, quarter, rows, columns), jnp.float32),
            pltpu.VMEM(shape, jnp.float32),
            pltpu.SemaphoreType.DMA((micro, 3)),
            pltpu.SemaphoreType.DMA((micro, 3)),
            pltpu.SemaphoreType.DMA((3,)),
            pltpu.SemaphoreType.DMA((3,)),
            pltpu.SemaphoreType.DMA((micro,)),
            pltpu.SemaphoreType.DMA((micro,)),
            pltpu.SemaphoreType.DMA((micro, 3)),
            pltpu.SemaphoreType.DMA((micro, 3)),
            pltpu.SemaphoreType.DMA((2,)),
            pltpu.SemaphoreType.DMA((max(count, 1) * max(length // 2, 1),)),
            pltpu.VMEM((2,) + sources[0].shape if sources else (2, 16, 128), jnp.bfloat16),
        ],
        compiler_params=pltpu.CompilerParams(
            collective_id=1 if reverse else 0,
            has_side_effects=True,
            vmem_limit_bytes=FINISH_LIMIT,
        ),
        cost_estimate=pl.CostEstimate(
            flops=EXCHANGE_COST, bytes_accessed=0, transcendentals=0
        ),
        name="exchange_back" if reverse else "exchange",
    )(parts.reshape(shape), spread, *sources, *job_inputs)
    out = out.reshape(micro, heads, rows, columns)
    return out, arranged[: len(jobs)], arranged[len(jobs) :]


def xor_permute(value, axis, bit):
    size = lax.axis_size(axis)
    return lax.ppermute(value, axis, [(i, i ^ (1 << bit)) for i in range(size)])


def axis_bits(axis):
    return (lax.axis_size(axis) - 1).bit_length()


def own_bit(axis, bit):
    return lax.rem(lax.axis_index(axis) // (1 << bit), 2)


def all_sum(value, axis):
    for bit in range(axis_bits(axis)):
        value = value + xor_permute(value, axis, bit)
    return value


def scatter_parts(columns, bits):
    if bits < 3 or columns % 2048:
        return [(tuple(range(bits)), (columns,))]
    rest = tuple(range(3, bits))
    unit = columns // 16
    return [
        ((0, 1, 2) + rest, (3 * unit, 2 * unit)),
        ((1, 0, 2) + rest, (2 * unit, 3 * unit)),
        ((2, 0, 1) + rest, (3 * unit, 0)),
        ((2, 1, 0) + rest, (0, 3 * unit)),
    ]


def arranged_place(order, position, bits):
    return [(position >> (bits - 1 - t)) & 1 for t, _ in sorted(enumerate(order), key=lambda p: p[1])]


def arranged_block(order, position, bits, me):
    flips = arranged_place(order, position, bits)
    total = 0
    for bit, flip in enumerate(flips):
        mine = lax.rem(me // (1 << bit), 2)
        total = total + (1 << bit) * ((1 - mine) if flip else mine)
    return total


def arrange(left, orders):
    bits = axis_bits("seq")
    size = 1 << bits
    tokens, width = left.shape
    view = left.reshape(tokens, size, width // size)
    me = lax.axis_index("seq").astype(jnp.int32)
    results = []
    for order in orders:
        table = jnp.stack([arranged_block(order, j, bits, me) for j in range(size)])
        chosen = jnp.take(view, table, axis=1).reshape(tokens, width)
        results += [chosen[:, width // 2 :], chosen[:, : width // 2]]
    return results


def arrange_copies(bits, orders, me, staged, targets, sem):
    copies, number = [], 0
    half = 1 << (bits - 1)
    for source in range(len(targets) // (2 * len(orders)) if orders else 0):
        block = staged.shape[2] >> bits
        for order in orders:
            for begin in (half, 0):
                target = targets[number]
                for j in range(half):
                    place = arranged_block(order, begin + j, bits, me)
                    first = pl.multiple_of(place * block, block)
                    copies.append(
                        pltpu.make_async_copy(
                            staged.at[source, :, pl.ds(first, block)],
                            target.at[:, pl.ds(j * block, block)],
                            sem.at[number * half + j],
                        )
                    )
                number += 1
    return copies


def product(left, right):
    return lax.dot_general(left, right, (TN, ((), ())), preferred_element_type=jnp.float32)


def product_steps(inputs, out_ref, parts):
    lefts, right_ref, more = inputs[: len(parts)], inputs[len(parts)], inputs[len(parts) + 1 :]
    steps, first = [], 0
    for left_ref, (_, widths) in zip(lefts, parts):
        steps.append(
            functools.partial(product_step, left_ref, right_ref, more, out_ref, first, sum(widths))
        )
        first += sum(widths)
    return steps


def product_step(left_ref, right_ref, more, out_ref, first, width):
    tokens, rows = left_ref.shape
    tile = min(rows, 256)
    columns = pl.ds(first, width)

    def body(left, right, *rest):
        value = product(left[...], right[...])
        for item in rest[:-1]:
            value = value + item[...]
        rest[-1][...] = value

    tiled = pl.BlockSpec((tile, width), lambda i: (i, 0))
    pltpu.emit_pipeline(
        body,
        grid=(rows // tile,),
        in_specs=[
            pl.BlockSpec((tokens, tile), lambda i: (0, i)),
            pl.BlockSpec((tokens, width), lambda i: (0, 0)),
        ]
        + [tiled] * len(more),
        out_specs=[tiled],
    )(
        left_ref,
        right_ref.at[:, columns],
        *[item.at[:, columns] for item in more],
        out_ref.at[:, columns],
    )


def plain_steps(inputs, out_ref, parts):
    left_ref, right_ref = inputs
    width = min(right_ref.shape[1], 512)
    return [
        functools.partial(plain_step, left_ref, right_ref, out_ref, first, width)
        for first in range(0, right_ref.shape[1], width)
    ]


def plain_step(left_ref, right_ref, out_ref, first, width):
    rows, depth = left_ref.shape
    tile = min(rows, 256)
    columns = pl.ds(first, width)

    def body(left, right, out):
        out[...] = low_dot(left[...], right[...], NN)

    pltpu.emit_pipeline(
        body,
        grid=(rows // tile,),
        in_specs=[
            pl.BlockSpec((tile, depth), lambda i: (i, 0)),
            pl.BlockSpec((depth, width), lambda i: (0, 0)),
        ],
        out_specs=[pl.BlockSpec((tile, width), lambda i: (i, 0))],
    )(left_ref, right_ref.at[:, columns], out_ref.at[:, columns])


def split_columns(array, parts):
    pieces, first = [], 0
    for _, widths in parts:
        pieces.append(array[:, first : first + sum(widths)])
        first += sum(widths)
    return pieces


def sent_products(lefts, right, parts):
    return [
        product(lefts[2 * k], piece) for k, piece in enumerate(split_columns(right, parts))
    ]


def send_parts(products, parts):
    return [xor_permute(item, "seq", order[0]) for item, (order, _) in zip(products, parts)]


def keep_parts(lefts, right, parts, arrived):
    return [
        product(lefts[2 * k + 1], piece) + arrived[k]
        for k, piece in enumerate(split_columns(right, parts))
    ]


def finish_kernel(parts, kinds, bits, blocks, *refs):
    refs = list(refs)
    take = lambda count: [refs.pop(0) for _ in range(count)]
    mats = len(kinds)
    ins = [take(len(parts) + (2 if made else 0)) for made in kinds]
    narrow_ref, vector_ref = take(2)
    outs = take(mats)
    gathered_ref, vector_out_ref = take(2)
    made_refs = [take(1)[0] if made else None for made in kinds]
    me = lax.axis_index("seq")

    def partner(bit):
        return me + (1 << bit) * (1 - 2 * lax.rem(me // (1 << bit), 2))

    waves = []
    piece_count = len(parts[0][1])
    chain_count = 0
    for mat in range(mats):
        for piece in range(piece_count):
            wave, first = [], 0
            for k, (order, widths) in enumerate(parts):
                if widths[piece]:
                    within = sum(widths[:piece])
                    keep = refs.pop(0)
                    recvs = take(bits - 1)
                    source, start = ins[mat][k], within
                    if kinds[mat]:
                        source, start = made_refs[mat], first + within
                    wave.append(
                        (chain_count, source, start, outs[mat], first + within, order[1:], keep, recvs)
                    )
                    chain_count += 1
                first += sum(widths)
            waves.append(wave)
    narrow_order = parts[0][0]
    narrow = (chain_count, narrow_ref, 0, None, 0, narrow_order, refs.pop(0), take(bits))
    vector_sums, vector_recvs, local_sem, send_sem, recv_sem = refs

    barrier = pltpu.get_barrier_semaphore()
    for bit in range(bits):
        pl.semaphore_signal(
            barrier,
            inc=1,
            device_id={"seq": partner(bit)},
            device_id_type=pl.DeviceIdType.MESH,
        )
    pl.semaphore_wait(barrier, bits)

    numbers = {}

    def remote(key, src, dst, bit):
        number = numbers.setdefault(key, len(numbers))
        return pltpu.make_async_remote_copy(
            src_ref=src,
            dst_ref=dst,
            send_sem=send_sem.at[number],
            recv_sem=recv_sem.at[number],
            device_id={"seq": partner(bit)},
            device_id_type=pl.DeviceIdType.MESH,
        )

    def local_copy(chain):
        number, source, first, _, _, _, keep, _ = chain
        rows, columns = keep.shape
        return pltpu.make_async_copy(
            source.at[pl.ds(0, rows), pl.ds(first, columns)], keep, local_sem.at[number]
        )

    def chain_copy(chain, phase):
        number, source, first, _, _, order, keep, recvs = chain
        rows, columns = recvs[phase].shape
        if phase == 0:
            region = source.at[pl.ds(rows, rows), pl.ds(first, columns)]
        else:
            region = keep.at[pl.ds(rows, rows)]
        return remote((number, phase), region, recvs[phase], order[phase])

    def begin(wave):
        for chain in wave:
            chain_copy(chain, 0).start()
            local_copy(chain).start()

    def advance(chain, phase):
        if phase == 0:
            local_copy(chain).wait()
        chain_copy(chain, phase).wait_recv()
        number, _, _, out, place, order, keep, recvs = chain
        recv = recvs[phase]
        rows = recv.shape[0]
        slab = min(rows, 32)

        @pl.loop(0, rows // slab)
        def _(step):
            cut = pl.ds(pl.multiple_of(step * slab, slab), slab)
            keep[cut, :] = keep[cut, :] + recv[cut, :]

        if phase + 1 < len(order):
            chain_copy(chain, phase + 1).start()
        elif out is not None:
            out[:, place : place + keep.shape[1]] = keep[0:blocks, :]

    def vector_copy(phase):
        return remote(("vector", phase), vector_sums.at[phase], vector_recvs.at[phase], phase)

    def advance_vector(phase):
        vector_copy(phase).wait_recv()
        total = vector_sums[phase] + vector_recvs[phase]
        if phase + 1 < bits:
            vector_sums[phase + 1] = total
            vector_copy(phase + 1).start()
        else:
            vector_out_ref[...] = total

    def gather_copies(phase):
        bit = bits - 1 - phase
        copies = []
        for high in range(1 << phase):
            block = lax.rem(me, 2 << bit) + high * (2 << bit)
            region = gathered_ref.at[block]
            copies.append(remote(("gather", phase, high), region, region, bit))
        return copies

    narrow_steps = []

    def narrow_halving(phase):
        advance(narrow, phase)
        if phase + 1 == bits:
            gathered_ref[me] = narrow[6][0 : gathered_ref.shape[1], :]
            for copy in gather_copies(0):
                copy.start()

    def narrow_gather(phase):
        for copy in gather_copies(phase):
            copy.wait_recv()
        if phase + 1 < bits:
            for copy in gather_copies(phase + 1):
                copy.start()

    for phase in range(bits):
        narrow_steps.append(functools.partial(narrow_halving, phase))
    for phase in range(bits):
        narrow_steps.append(functools.partial(narrow_gather, phase))

    vector_sums[0] = vector_ref[...]
    vector_copy(0).start()
    chain_copy(narrow, 0).start()
    local_copy(narrow).start()
    makes = [
        product_steps(items, made_refs[mat], parts) if kinds[mat] else []
        for mat, items in enumerate(ins)
    ]
    begun = min(2, len(waves))
    for number in range(begun):
        if number % piece_count == 0:
            for step in makes[number // piece_count]:
                step()
        begin(waves[number])
    ticks = len(waves) + bits - 2
    if len(waves) > begun:
        for step in makes[begun // piece_count]:
            step()
    for tick in range(max(ticks, 2 * bits)):
        if tick < bits:
            advance_vector(tick)
        if tick < len(narrow_steps):
            narrow_steps[tick]()
        for phase in range(bits - 1):
            number = tick - phase
            if 0 <= number < len(waves):
                for chain in waves[number]:
                    advance(chain, phase)
                if phase == 0 and number + 2 < len(waves):
                    begin(waves[number + 2])
                    ahead = number + 3
                    if ahead < len(waves) and ahead % piece_count == 0:
                        for step in makes[ahead // piece_count]:
                            step()
    for wave in waves:
        for chain in wave:
            for phase in range(bits - 1):
                chain_copy(chain, phase).wait_send()
    for phase in range(bits):
        chain_copy(narrow, phase).wait_send()
        vector_copy(phase).wait_send()
        for copy in gather_copies(phase):
            copy.wait_send()


def finish(parts, mats, narrow, vector):
    bits = axis_bits("seq")
    size = 1 << bits
    kinds = tuple(len(mat) > len(parts) for mat in mats)
    blocks = mats[-1][-1].shape[0] // (size // 2)
    columns = sum(sum(widths) for _, widths in parts)
    scratch, copies, chains = [], 0, 0
    for _ in mats:
        for piece in range(len(parts[0][1])):
            for _, widths in parts:
                if widths[piece]:
                    rows = blocks * size // 4
                    scratch.append(pltpu.VMEM((rows, widths[piece]), jnp.float32))
                    for phase in range(bits - 1):
                        scratch.append(pltpu.VMEM((rows >> phase, widths[piece]), jnp.float32))
                    copies += bits - 1
                    chains += 1
    rows = narrow.shape[0] // 2
    scratch.append(pltpu.VMEM((rows, narrow.shape[1]), jnp.float32))
    for phase in range(bits):
        scratch.append(pltpu.VMEM((rows >> phase, narrow.shape[1]), jnp.float32))
    copies += 2 * bits + size - 1
    scratch += [pltpu.VMEM((bits,) + vector.shape, jnp.float32)] * 2
    scratch += [
        pltpu.SemaphoreType.DMA((chains + 1,)),
        pltpu.SemaphoreType.DMA((copies,)),
        pltpu.SemaphoreType.DMA((copies,)),
    ]
    shapes = [jax.ShapeDtypeStruct((blocks, columns), jnp.float32) for _ in mats]
    shapes.append(
        jax.ShapeDtypeStruct((size, narrow.shape[0] // size, narrow.shape[1]), jnp.float32)
    )
    shapes.append(jax.ShapeDtypeStruct(vector.shape, jnp.float32))
    flat = [item for mat in mats for item in mat]
    outputs = len(shapes)
    made = sum(kinds)
    shapes += [jax.ShapeDtypeStruct((blocks * size // 2, columns), jnp.float32)] * made
    results = pl.pallas_call(
        functools.partial(finish_kernel, parts, kinds, bits, blocks),
        out_shape=shapes,
        in_specs=[pl.BlockSpec(memory_space=pl.ANY)] * (len(flat) + 1)
        + [pl.BlockSpec(memory_space=pltpu.VMEM)],
        out_specs=[pl.BlockSpec(memory_space=pltpu.VMEM)] * outputs
        + [pl.BlockSpec(memory_space=pl.ANY)] * made,
        scratch_shapes=scratch,
        compiler_params=pltpu.CompilerParams(
            collective_id=2, has_side_effects=True, vmem_limit_bytes=FINISH_LIMIT
        ),
        name="finish",
    )(*flat, narrow, vector)
    return results[: outputs - 2], results[outputs - 2], results[outputs - 1]


def head_gather(block):
    if lax.axis_size("head") != 2:
        return lax.all_gather(block, "head", axis=1, tiled=True)
    other = xor_permute(block, "head", 0)
    mine = lax.axis_index("head") == 0
    return jnp.concatenate(
        [jnp.where(mine, block, other), jnp.where(mine, other, block)], axis=1
    )


HEAD_GROUP = 8
VMEM_LIMIT = 56 * 1024 * 1024
FAR = 1 << 30
NN = ((1,), (0,))
NT = ((1,), (1,))
TN = ((0,), (0,))


def low_dot(left, right, dims):
    return lax.dot_general(
        left.astype(jnp.bfloat16),
        right.astype(jnp.bfloat16),
        (dims, ((), ())),
        preferred_element_type=jnp.float32,
    )


def halves_of(value):
    high = value.astype(jnp.bfloat16)
    return high, (value - high.astype(jnp.float32)).astype(jnp.bfloat16)


def thirds_of(value):
    first = value.astype(jnp.bfloat16).astype(jnp.float32)
    second = (value - first).astype(jnp.bfloat16).astype(jnp.float32)
    return first, second, value - first - second


def spread_matrix(heads, head_dim):
    shape = (heads, heads * head_dim)
    rows = lax.broadcasted_iota(jnp.int32, shape, 0)
    columns = lax.broadcasted_iota(jnp.int32, shape, 1)
    return (columns // head_dim == rows).astype(jnp.float32)


def turned(rows, matrix):
    return low_dot(
        jnp.concatenate(thirds_of(rows), axis=0), jnp.concatenate([matrix] * 3, axis=0), TN
    )


def head_sums(spread, value):
    high, low = halves_of(value)
    return low_dot(spread, high, NT) + low_dot(spread, low, NT)


def map_dot(left, right):
    high, low = halves_of(right)
    return low_dot(
        jnp.concatenate([left, left], axis=1), jnp.concatenate([high, low], axis=1), NT
    )


def fine_dot(left, right):
    left_high, left_low = halves_of(left)
    right_high, right_low = halves_of(right)
    return (
        low_dot(left_high, right_high, NN)
        + low_dot(left_high, right_low, NN)
        + low_dot(left_low, right_high, NN)
    )


def sigmoid(value):
    return 1.0 / (1.0 + jnp.exp(-value))


def segment_of(places, starts_ref, micro):
    label = jnp.zeros_like(places)
    for number in range(starts_ref.shape[1]):
        label = label + jnp.where(places >= starts_ref[micro, number], 1, 0)
    return label


def same_segment(count, base_ref, starts_ref, taps):
    micro = pl.program_id(0)
    places = base_ref[0] + lax.broadcasted_iota(jnp.int32, (count, 1), 0)
    own = segment_of(places, starts_ref, micro)
    return [
        jnp.where(segment_of(places - shift, starts_ref, micro) == own, 1.0, 0.0)
        for shift in range(1, taps)
    ]


def pair_labels(count, base_ref, starts_ref):
    micro = pl.program_id(0)
    column = base_ref[0] + lax.broadcasted_iota(jnp.int32, (count, 1), 0)
    row = base_ref[0] + lax.broadcasted_iota(jnp.int32, (1, count), 1)
    return segment_of(column, starts_ref, micro) == segment_of(row, starts_ref, micro)


def conv_sum(ext, value, halo, weight, bias, masks):
    count = value.shape[0]
    ext[0:8, :] = halo
    ext[8 : 8 + count, :] = value
    total = bias + weight[0:1] * value
    for shift in range(1, weight.shape[0]):
        total = (
            total
            + weight[shift : shift + 1]
            * ext[8 - shift : 8 - shift + count, :]
            * masks[shift - 1]
        )
    return total


def front_kernel(
    head_dim,
    base_ref,
    starts_ref,
    x_ref,
    halo_ref,
    weight_ref,
    bias_ref,
    b_ref,
    tail_ref,
    low_ref,
    state_ref,
    ext,
):
    heads = tail_ref.shape[1]
    weight = weight_ref[...]
    masks = same_segment(x_ref.shape[2], base_ref, starts_ref, weight.shape[0])
    total = conv_sum(ext, x_ref[0, 0], halo_ref[0], weight, bias_ref[...], masks)
    act = (total * sigmoid(total)).astype(jnp.bfloat16)
    low_ref[0] = act
    scale = turned(tail_ref[0], spread_matrix(heads, head_dim))
    high, low = halves_of(act.astype(jnp.float32) * scale)
    state_ref[0] = low_dot(high, b_ref[0], TN) + low_dot(low, b_ref[0], TN)


def mix_kernel(
    head_dim,
    base_ref,
    starts_ref,
    x_ref,
    b_ref,
    c_ref,
    run_ref,
    step_ref,
    carry_ref,
    start_ref,
    gate_ref,
    cot_ref,
    gain_ref,
    skip_ref,
    mixed_ref,
    sums_ref,
):
    heads = step_ref.shape[1]
    count = x_ref.shape[1]
    spread = spread_matrix(heads, head_dim)
    x = x_ref[0]
    b, c = b_ref[0], c_ref[0]
    rows = lax.broadcasted_iota(jnp.int32, (count, count), 0)
    columns = lax.broadcasted_iota(jnp.int32, (count, count), 1)
    valid = pair_labels(count, base_ref, starts_ref) & (rows >= columns)
    scores = jnp.where(valid, low_dot(c, b, NT), 0.0)
    wide = x.astype(jnp.float32)
    scaled = (wide * turned(step_ref[0], spread)).astype(jnp.bfloat16)
    inter = map_dot(c, start_ref[0]) * turned(carry_ref[0], spread)
    run_row = run_ref[0]
    run = turned(run_row, spread_matrix(heads, 1))
    pair = 2 * head_dim
    middle = count // 2
    lane = lax.broadcasted_iota(jnp.int32, (count, pair), 1)
    results = []
    for first in range(0, heads, 2):
        block = scaled[:, first * head_dim : first * head_dim + pair]
        halves = []
        for head in (first, first + 1):
            strips = []
            for top, cut in ((0, middle), (middle, count)):
                gap = run[top:cut, head : head + 1] - run_row[head : head + 1, :cut]
                weights = jnp.exp(jnp.minimum(gap, 0.0)) * scores[top:cut, :cut]
                strips.append(low_dot(weights, block[:cut], NN))
            halves.append(jnp.concatenate(strips, axis=0))
        results.append(jnp.where(lane < head_dim, halves[0], halves[1]))
    mixed = jnp.concatenate(results, axis=1) + inter + skip_ref[...] * wide
    mixed_ref[0] = mixed
    gate = gate_ref[0, 0]
    gated = mixed * (gate * sigmoid(gate))
    square = jnp.sum(gated * gated, axis=1, keepdims=True)
    cross = jnp.sum(cot_ref[0] * gain_ref[...] * gated, axis=1, keepdims=True)
    both = jnp.concatenate([square, cross], axis=1)

    @pl.when(pl.program_id(1) == 0)
    def _():
        sums_ref[0] = both

    @pl.when(pl.program_id(1) > 0)
    def _():
        sums_ref[0] = sums_ref[0] + both


def gate_kernel(
    head_dim,
    full,
    mixed_ref,
    gate_ref,
    cot_ref,
    sums_ref,
    gain_ref,
    carry_ref,
    c_ref,
    norm_ref,
    grad_gate_ref,
    both_ref,
    grad_mixed_ref,
    start_ref,
    rows_ref,
):
    heads = carry_ref.shape[1]
    mixed, gate, cot, gain = mixed_ref[0], gate_ref[0, 0], cot_ref[0], gain_ref[...]
    scale = lax.rsqrt(sums_ref[0, :, 0:1] / full + EPSILON)
    sigma = sigmoid(gate)
    act = gate * sigma
    gated = mixed * act
    unit = gated * scale
    norm_ref[0] = (unit * gain).astype(jnp.bfloat16)
    pull = scale * scale * scale * sums_ref[0, :, 1:2] / full
    grad_gated = cot * gain * scale - gated * pull
    grad_gate = (grad_gated * mixed * sigma * (1.0 + gate * (1.0 - sigma))).astype(jnp.bfloat16)
    grad_gate_ref[0] = grad_gate
    both_ref[0, 0] = grad_gate
    grad_mixed = (grad_gated * act).astype(jnp.bfloat16)
    grad_mixed_ref[0] = grad_mixed
    carried = grad_mixed.astype(jnp.float32) * turned(
        carry_ref[0], spread_matrix(heads, head_dim)
    )
    high, low = halves_of(carried)
    start_ref[0] = low_dot(high, c_ref[0], TN) + low_dot(low, c_ref[0], TN)
    gains = jnp.sum(cot * unit, axis=0, keepdims=True)
    rows_ref[0] = jnp.concatenate([gains, jnp.zeros((7, gains.shape[1]), jnp.float32)], axis=0)


def back_kernel(
    head_dim,
    parts,
    bits,
    base_ref,
    starts_ref,
    x_ref,
    g_ref,
    b_ref,
    c_ref,
    run_ref,
    step_ref,
    carry_ref,
    tail_ref,
    start_ref,
    end_ref,
    pre_ref,
    halo_ref,
    weight_ref,
    bias_ref,
    skip_ref,
    both_in_ref,
    out_sent_ref,
    gate_sent_ref,
    both_ref,
    edge_ref,
    halo_out_ref,
    rows_ref,
    direct_ref,
    decay_ref,
    pair_ref,
    grad_b_ref,
    grad_c_ref,
    out_arrived_ref,
    gate_arrived_ref,
    ext,
    moved,
    send_sem,
    recv_sem,
):
    me = lax.axis_index("seq")

    def partner(bit):
        return me + (1 << bit) * (1 - 2 * lax.rem(me // (1 << bit), 2))

    def sends():
        copies = []
        for source, target in (
            (out_sent_ref, out_arrived_ref),
            (gate_sent_ref, gate_arrived_ref),
        ):
            first = 0
            for order, widths in parts:
                columns = pl.ds(first, sum(widths))
                first += sum(widths)
                copies.append(
                    pltpu.make_async_remote_copy(
                        src_ref=source.at[:, columns],
                        dst_ref=target.at[:, columns],
                        send_sem=send_sem.at[len(copies)],
                        recv_sem=recv_sem.at[len(copies)],
                        device_id={"seq": partner(order[0])},
                        device_id_type=pl.DeviceIdType.MESH,
                    )
                )
        return copies

    at_first = (pl.program_id(0) == 0) & (pl.program_id(1) == 0)
    at_last = (pl.program_id(0) == pl.num_programs(0) - 1) & (
        pl.program_id(1) == pl.num_programs(1) - 1
    )
    used = sorted({order[0] for order, _ in parts})

    @pl.when(at_first)
    def _():
        barrier = pltpu.get_barrier_semaphore()
        for bit in used:
            pl.semaphore_signal(
                barrier,
                inc=1,
                device_id={"seq": partner(bit)},
                device_id_type=pl.DeviceIdType.MESH,
            )
        pl.semaphore_wait(barrier, len(used))
        for copy in sends():
            copy.start()

    heads = step_ref.shape[1]
    count = x_ref.shape[1]
    spread = spread_matrix(heads, head_dim)
    x, g, b, c = x_ref[0], g_ref[0], b_ref[0], c_ref[0]
    x_wide, g_wide = x.astype(jnp.float32), g.astype(jnp.float32)
    rows = lax.broadcasted_iota(jnp.int32, (count, count), 0)
    columns = lax.broadcasted_iota(jnp.int32, (count, count), 1)
    valid = pair_labels(count, base_ref, starts_ref) & (columns >= rows)
    scores = jnp.where(valid, low_dot(b, c, NT), 0.0)
    upto = (rows >= columns).astype(jnp.bfloat16)
    before = (rows < columns).astype(jnp.float32)
    step = turned(step_ref[0], spread)
    carry = turned(carry_ref[0], spread)
    tail = turned(tail_ref[0], spread)
    scaled_wide = x_wide * step
    scaled, scaled_rest = halves_of(scaled_wide)
    start, end = start_ref[0], end_ref[0]
    run_row = run_ref[0]
    run = turned(run_row, spread_matrix(heads, 1))
    pair = 2 * head_dim
    lane = lax.broadcasted_iota(jnp.int32, (count, pair), 1)
    middle = count // 2
    score_grads = [
        jnp.zeros((middle, count), jnp.float32),
        jnp.zeros((count - middle, count - middle), jnp.float32),
    ]
    results, straddles = [], []
    for first in range(0, heads, 2):
        cut = slice(first * head_dim, first * head_dim + pair)
        g_block = g[:, cut]
        g_swap = jnp.concatenate([g_block[:, head_dim:], g_block[:, :head_dim]], axis=1)
        x_block, x_rest = scaled[:, cut], scaled_rest[:, cut]
        x_rest = jnp.concatenate([x_rest[:, head_dim:], x_rest[:, :head_dim]], axis=1)
        halves = []
        for head in (first, first + 1):
            own = (lane < head_dim) if head == first else (lane >= head_dim)
            x_own, g_own = jnp.where(own, x_block, x_rest), jnp.where(own, g_block, g_swap)
            strips, straddle = [], None
            for part, (top, cut) in enumerate(((0, middle), (middle, count))):
                gap = run_row[head : head + 1, top:] - run[top:cut, head : head + 1]
                fade = jnp.exp(jnp.minimum(gap, 0.0))
                weights = fade * scores[top:cut, top:]
                strips.append(low_dot(weights, g_block[top:], NN))
                inner = low_dot(x_own[top:cut], g_own[top:], NT)
                score_grads[part] = score_grads[part] + fade * inner
                sums = low_dot(weights * inner, upto[top:, top:], NN)
                sums = jnp.sum(sums * before[top:cut, top:], axis=0, keepdims=True)
                if part == 0:
                    straddle = sums
                else:
                    straddle = jnp.concatenate(
                        [straddle[:, :middle], straddle[:, middle:] + sums], axis=1
                    )
            straddles.append(straddle)
            halves.append(jnp.concatenate(strips, axis=0))
        results.append(jnp.where(lane < head_dim, halves[0], halves[1]))
    score_grad = jnp.concatenate(
        [
            score_grads[0],
            jnp.concatenate([jnp.zeros((count - middle, middle), jnp.float32), score_grads[1]], axis=1),
        ],
        axis=0,
    )
    score_grad = jnp.where(valid, score_grad, 0.0)
    later = map_dot(b, end) * tail
    values = jnp.concatenate(results, axis=1) + later
    inter = map_dot(c, start) * carry
    direct_ref[0] = head_sums(spread, x_wide * values)
    given = head_sums(spread, scaled_wide * later)
    taken = head_sums(spread, g_wide * inter)
    flows = jnp.concatenate([given, taken], axis=0)
    flow_pieces = [item.astype(jnp.bfloat16) for item in thirds_of(flows)]
    after = (rows < columns).astype(jnp.bfloat16)
    flow_later = sum(low_dot(item, after, NN) for item in flow_pieces)
    flow_sooner = sum(low_dot(item, upto, NN) for item in flow_pieces)
    decay_ref[0] = (
        jnp.concatenate(straddles, axis=0) + flow_later[:heads] + flow_sooner[heads:]
    )
    pair_high, pair_low = halves_of(start * end)
    pair_ref[0] = low_dot(spread, pair_high, NN) + low_dot(spread, pair_low, NN)
    grads_high, grads_low = halves_of(score_grad)
    grad_c = fine_dot(g_wide * carry, start) + low_dot(grads_high, b, TN) + low_dot(grads_low, b, TN)
    grad_b = fine_dot(scaled_wide * tail, end) + low_dot(grads_high, c, NN) + low_dot(grads_low, c, NN)

    @pl.when(pl.program_id(1) == 0)
    def _():
        grad_b_ref[0] = grad_b
        grad_c_ref[0] = grad_c

    @pl.when(pl.program_id(1) > 0)
    def _():
        grad_b_ref[0] = grad_b_ref[0] + grad_b
        grad_c_ref[0] = grad_c_ref[0] + grad_c

    weight, pre = weight_ref[...], pre_ref[0, 0]
    masks = same_segment(count, base_ref, starts_ref, weight.shape[0])
    total = conv_sum(ext, pre, halo_ref[0], weight, bias_ref[...], masks)
    sigma = sigmoid(total)
    grad_conv = (values * step + skip_ref[...] * g_wide) * (
        sigma * (1.0 + total * (1.0 - sigma))
    )
    moved[0:8, :] = jnp.zeros_like(moved[0:8, :])
    moved[8 + count :, :] = jnp.zeros_like(moved[8 + count :, :])
    sums = [jnp.sum(grad_conv * pre, axis=0, keepdims=True)]
    back = jnp.concatenate(
        [jnp.zeros((8, pre.shape[1]), jnp.float32), grad_conv * weight[0:1]], axis=0
    )
    for shift in range(1, weight.shape[0]):
        part = grad_conv * masks[shift - 1]
        sums.append(
            jnp.sum(part * ext[8 - shift : 8 - shift + count, :], axis=0, keepdims=True)
        )
        moved[8 : 8 + count, :] = part * weight[shift : shift + 1]
        back = back + moved[shift : shift + 8 + count, :]
    halo_out_ref[0] = back[:8]
    both_ref[0, 0] = back[8:].astype(jnp.bfloat16)
    edge_ref[0] = back[count:]
    sums.append(jnp.sum(grad_conv, axis=0, keepdims=True))
    sums.append(jnp.sum(g_wide * x_wide, axis=0, keepdims=True))
    sums.append(jnp.zeros((8 - len(sums), pre.shape[1]), jnp.float32))
    rows_ref[0] = jnp.concatenate(sums, axis=0)

    @pl.when(at_last)
    def _():
        for copy in sends():
            copy.wait()


def blocked(kernel, name, grid, ins, outs, scratch=(), micros=0, aliases=None, remote=None):
    moved = sum(item[0].size * item[0].dtype.itemsize for item in ins if item[1] != "any")
    moved += sum(
        math.prod(item[2]) * grid[0] * grid[1] * jnp.dtype(item[1]).itemsize
        for item in outs
        if item[2] != "any"
    )

    def spec(item):
        if item[1] is None:
            return pl.BlockSpec(memory_space=pltpu.SMEM)
        if item[1] == "any":
            return pl.BlockSpec(memory_space=pl.ANY)
        return pl.BlockSpec(item[1], item[2])

    return pl.pallas_call(
        kernel,
        grid=grid,
        in_specs=[spec(item) for item in ins],
        out_specs=[spec(item[1:]) for item in outs],
        out_shape=[jax.ShapeDtypeStruct(item[0], item[1]) for item in outs],
        scratch_shapes=list(scratch),
        input_output_aliases=aliases or {},
        compiler_params=pltpu.CompilerParams(
            dimension_semantics=("arbitrary",) * len(grid),
            vmem_limit_bytes=VMEM_LIMIT,
            collective_id=remote,
            has_side_effects=remote is not None,
        ),
        cost_estimate=pl.CostEstimate(
            flops=micros * 1_000_000_000, bytes_accessed=moved, transcendentals=0
        ),
        name=name,
    )(*[item[0] for item in ins])


def body(
    tokens,
    norm_gain,
    in_weight,
    bc_weight,
    dt_weight,
    dt_bias,
    a_log,
    conv_weight,
    conv_bias,
    bc_conv_weight,
    bc_conv_bias,
    d_skip,
    gate_gain,
    out_weight,
    cotangent,
    seq_lengths,
):
    micro, length, width = tokens.shape
    heads = dt_bias.shape[0]
    inner = conv_bias.shape[0]
    head_dim = inner // heads
    state_size = bc_weight.shape[1] // 2
    taps = conv_weight.shape[0]
    total = micro * length
    head_count = lax.axis_size("head")
    full_inner = inner * head_count
    group = min(HEAD_GROUP, heads)
    groups = heads // group
    wide = group * head_dim
    base = lax.axis_index("seq").astype(jnp.int32) * length
    labels = segment_ids(seq_lengths, base - (taps - 1), length + taps - 1, micro)
    own_labels = labels[:, taps - 1 :]
    before_labels = labels[:, taps - 2]
    starts = jnp.cumsum(seq_lengths, axis=-1).astype(jnp.int32) - seq_lengths
    long_starts = jnp.full((micro - starts.shape[0], starts.shape[1]), FAR, jnp.int32)
    starts = jnp.concatenate([starts, long_starts.at[:, 0].set(0)], axis=0)
    base_item, starts_item = (base[None], None), (starts, None)

    flat = tokens.reshape(total, width).astype(jnp.float32)
    cot_flat = cotangent.reshape(total, width)
    normed, norm_back = jax.vjp(rms_scale, flat, norm_gain)
    normed_low = normed.astype(jnp.bfloat16)
    gate_x = jnp.einsum(
        "td,dkc->ktc", normed_low, in_weight, preferred_element_type=jnp.float32
    ).reshape(2, micro, length, inner)
    bc_pre = jnp.dot(normed_low, bc_weight, preferred_element_type=jnp.float32).reshape(
        micro, length, 2 * state_size
    )
    delta_pre = lax.dot_general(
        dt_weight, normed_low, (((0,), (1,)), ((), ())), preferred_element_type=jnp.float32
    )
    left = shifted(
        jnp.concatenate(
            [gate_x[1, :, length - taps + 1 :], bc_pre[:, length - taps + 1 :]], axis=-1
        ),
        "seq",
        1,
    )
    left_x, left_bc = left[..., :inner], left[..., inner:]
    halo = jnp.pad(left_x, ((0, 0), (9 - taps, 0), (0, 0)))
    conv_many = jax.vmap(conv_silu, in_axes=(0, None, None, 0))
    bc_act, bc_conv_back = jax.vjp(
        lambda extended, weight, bias: conv_many(extended, weight, bias, labels),
        jnp.concatenate([left_bc, bc_pre], axis=1),
        bc_conv_weight,
        bc_conv_bias,
    )
    bc_low = bc_act.astype(jnp.bfloat16)
    b_low, c_low = bc_low[..., :state_size], bc_low[..., state_size:]
    (delta, decay), rate_back = jax.vjp(step_sizes, delta_pre, dt_bias, a_log)

    def by_micro(array):
        return array.reshape(heads, micro, length).transpose(1, 0, 2)

    def by_head(array):
        return array.transpose(1, 0, 2).reshape(heads, total)

    delta, decay = by_micro(delta), by_micro(decay)
    order = jnp.arange(length)
    running = jnp.einsum(
        "mhj,ji->mhi",
        decay,
        (order[:, None] <= order[None, :]).astype(jnp.float32),
        precision=HIGHEST,
    )
    device_log = running[:, :, -1]
    live = (own_labels == before_labels[:, None]).astype(jnp.float32)
    last = (own_labels == own_labels[:, -1:]).astype(jnp.float32)
    carried = jnp.exp(running) * live[:, None]
    tail = jnp.exp(device_log[:, :, None] - running) * last[:, None]
    device_live = live[:, -1]
    gain_row, skip_row = gate_gain[None], jnp.repeat(d_skip, head_dim)[None]
    conv_row = conv_bias[None]

    grid = (micro, groups)
    token_block = (1, length, wide)
    in_token = lambda m, k: (m, 0, k)
    half_block = (1, 1, length, wide)
    in_gate, in_x = lambda m, k: (0, m, 0, k), lambda m, k: (1, m, 0, k)
    row_block, in_row = (1, group, length), lambda m, k: (m, k, 0)
    map_block, in_map = (1, length, state_size), lambda m, k: (m, 0, 0)
    state_block, in_state = (1, wide, state_size), lambda m, k: (m, k, 0)
    halo_block = (1, 8, wide)
    flat_block, in_flat = (1, wide), lambda m, k: (0, k)
    conv_item = (conv_weight, (taps, wide), in_flat)
    whole = (micro, length, inner)
    state_shape = (micro, inner, state_size)
    row_shape = (micro, heads, length)

    x_low, device_state = blocked(
        functools.partial(front_kernel, head_dim),
        "front",
        grid,
        [
            base_item,
            starts_item,
            (gate_x, half_block, in_x),
            (halo, halo_block, in_token),
            conv_item,
            (conv_row, flat_block, in_flat),
            (b_low, map_block, in_map),
            (tail * delta, row_block, in_row),
        ],
        [
            (whole, jnp.bfloat16, token_block, in_token),
            (state_shape, jnp.float32, state_block, in_state),
        ],
        [pltpu.VMEM((length + 8, wide), jnp.float32)],
        20,
    )
    exchange_log = jnp.where(device_live[:, None] > 0.0, device_log, DEAD)
    exchange_shape = (micro, heads, head_dim, state_size)
    parts = scatter_parts(inner, axis_bits("seq"))
    orders = tuple(order for order, _ in parts)
    tiled = (width >> axis_bits("seq")) % 128 == 0
    incoming, (grad_gate_n,), arranged = exchange(
        device_state.reshape(exchange_shape),
        exchange_log,
        False,
        (cot_flat, normed_low) if tiled else (),
        orders if tiled else (),
        [(plain_steps, (), (cot_flat, out_weight), (total, inner))],
    )
    grad_gate_n = grad_gate_n.reshape(whole)
    if not tiled:
        arranged = arrange(cot_flat, orders) + arrange(normed_low, orders)
    cot_parts, normed_parts = arranged[: 2 * len(parts)], arranged[2 * len(parts) :]
    incoming = incoming.reshape(state_shape)

    mixed, sums = blocked(
        functools.partial(mix_kernel, head_dim),
        "mix",
        grid,
        [
            base_item,
            starts_item,
            (x_low, token_block, in_token),
            (b_low, map_block, in_map),
            (c_low, map_block, in_map),
            (running, row_block, in_row),
            (delta, row_block, in_row),
            (carried, row_block, in_row),
            (incoming, state_block, in_state),
            (gate_x, half_block, in_gate),
            (grad_gate_n, token_block, in_token),
            (gain_row, flat_block, in_flat),
            (skip_row, flat_block, in_flat),
        ],
        [
            (whole, jnp.float32, token_block, in_token),
            ((micro, length, 2), jnp.float32, (1, length, 2), in_map),
        ],
        (),
        25,
    )
    sums = all_sum(sums, "head")
    normed_gate, grad_gate_pre, grad_gate_x, grad_mixed, device_grad, gate_rows = blocked(
        functools.partial(gate_kernel, head_dim, float(full_inner)),
        "gate",
        grid,
        [
            (mixed, token_block, in_token),
            (gate_x, half_block, in_gate),
            (grad_gate_n, token_block, in_token),
            (sums, (1, length, 2), in_map),
            (gain_row, flat_block, in_flat),
            (carried, row_block, in_row),
            (c_low, map_block, in_map),
        ],
        [
            (whole, jnp.bfloat16, token_block, in_token),
            (whole, jnp.bfloat16, token_block, in_token),
            ((2,) + whole, jnp.bfloat16, half_block, in_gate),
            (whole, jnp.bfloat16, token_block, in_token),
            (state_shape, jnp.float32, state_block, in_state),
            ((micro, 8, inner), jnp.float32, halo_block, in_token),
        ],
        (),
        20,
    )
    normed_gate = normed_gate.reshape(total, inner)
    grad_gate_pre = grad_gate_pre.reshape(total, inner)
    grad_gate_gain = jnp.sum(gate_rows[:, 0], axis=0)

    half_shape = (width // 2, inner)
    outgoing, (out_sent, gate_sent), _ = exchange(
        device_grad.reshape(exchange_shape),
        exchange_log,
        True,
        jobs=[
            (product_steps, parts, cot_parts[::2] + [normed_gate], half_shape),
            (product_steps, parts, normed_parts[::2] + [grad_gate_pre], half_shape),
        ],
    )
    outgoing = outgoing.reshape(state_shape)
    (
        grad_gate_x,
        edge,
        halo_grad,
        conv_rows,
        direct,
        fading,
        pairs,
        grad_b,
        grad_c,
        out_arrived,
        gate_arrived,
    ) = blocked(
        functools.partial(back_kernel, head_dim, parts, axis_bits("seq")),
        "back",
        grid,
        [
            base_item,
            starts_item,
            (x_low, token_block, in_token),
            (grad_mixed, token_block, in_token),
            (b_low, map_block, in_map),
            (c_low, map_block, in_map),
            (running, row_block, in_row),
            (delta, row_block, in_row),
            (carried, row_block, in_row),
            (tail, row_block, in_row),
            (incoming, state_block, in_state),
            (outgoing, state_block, in_state),
            (gate_x, half_block, in_x),
            (halo, halo_block, in_token),
            conv_item,
            (conv_row, flat_block, in_flat),
            (skip_row, flat_block, in_flat),
            (grad_gate_x, "any"),
            (out_sent, "any"),
            (gate_sent, "any"),
        ],
        [
            ((2,) + whole, jnp.bfloat16, half_block, in_x),
            ((micro, 8, inner), jnp.float32, halo_block, in_token),
            ((micro, 8, inner), jnp.float32, halo_block, in_token),
            ((micro, 8, inner), jnp.float32, halo_block, in_token),
            (row_shape, jnp.float32, row_block, in_row),
            (row_shape, jnp.float32, row_block, in_row),
            ((micro, heads, state_size), jnp.float32, (1, group, state_size), in_state),
            ((micro, length, state_size), jnp.float32, map_block, in_map),
            ((micro, length, state_size), jnp.float32, map_block, in_map),
            (half_shape, jnp.float32, "any"),
            (half_shape, jnp.float32, "any"),
        ],
        [
            pltpu.VMEM((length + 8, wide), jnp.float32),
            pltpu.VMEM((length + 16, wide), jnp.float32),
            pltpu.SemaphoreType.DMA((2 * len(parts),)),
            pltpu.SemaphoreType.DMA((2 * len(parts),)),
        ],
        80,
        {17: 0},
        3,
    )
    grad_bc = all_sum(jnp.concatenate([grad_b, grad_c], axis=-1), "head")
    kept = jnp.sum(pairs, axis=-1) * jnp.exp(device_log) * device_live[:, None]
    grad_decay = by_head(fading + kept[:, :, None])
    grad_delta_pre, grad_dt_bias, grad_a_log = rate_back((by_head(direct), grad_decay))
    conv_rows = jnp.sum(conv_rows, axis=0)
    grad_conv_weight, grad_conv_bias = conv_rows[:taps], conv_rows[taps]
    grad_d_skip = jnp.sum(conv_rows[taps + 1].reshape(heads, head_dim), axis=-1)
    grad_bc_ext, grad_bc_conv_weight, grad_bc_conv_bias = bc_conv_back(grad_bc)
    right = shifted(
        jnp.concatenate([halo_grad[:, 9 - taps :], grad_bc_ext[:, : taps - 1]], axis=-1), "seq", -1
    )
    right_x, right_bc = right[..., :inner], right[..., inner:]
    grad_gate_x = lax.dynamic_update_slice(
        grad_gate_x,
        (edge[:, 9 - taps :] + right_x).astype(jnp.bfloat16)[None],
        (1, 0, length - taps + 1, 0),
    )
    grad_bc_pre = grad_bc_ext[:, taps - 1 :].at[:, length - taps + 1 :].add(right_bc)
    bc_flat = grad_bc_pre.reshape(total, 2 * state_size)
    grad_gate_x = grad_gate_x.reshape(2, total, inner)
    x_sent = sent_products(normed_parts, grad_gate_x[1], parts)
    grad_gate_x, x_sent = lax.optimization_barrier((grad_gate_x, x_sent))
    x_arrived = send_parts(x_sent, parts)

    row_part = jnp.einsum(
        "ktc,dkc->td", grad_gate_x, in_weight, preferred_element_type=jnp.float32
    )
    bc_high, bc_rest = halves_of(bc_flat * (1.0 / head_count))
    delta_high, delta_rest = halves_of(grad_delta_pre.T)
    narrow_left = jnp.concatenate([bc_high, bc_rest, delta_high, delta_rest], axis=1)
    narrow_right = jnp.concatenate([bc_weight, bc_weight, dt_weight, dt_weight], axis=1)
    row_part = row_part + lax.dot_general(
        narrow_left, narrow_right, (NT, ((), ())), preferred_element_type=jnp.float32
    )
    row_grads = all_sum(row_part, "head")
    grad_flat, grad_norm_gain = norm_back(row_grads)
    grad_tokens = (cot_flat.astype(jnp.float32) + grad_flat).reshape(micro, length, width)

    share_bc = 2 * state_size // head_count
    own_bc = lax.dynamic_slice_in_dim(bc_flat, lax.axis_index("head") * share_bc, share_bc, 1)
    across = share_bc + heads
    narrow_high, narrow_rest = halves_of(jnp.concatenate([own_bc, grad_delta_pre.T], axis=1))
    both = jnp.concatenate([narrow_high, narrow_rest], axis=1)
    narrow = jnp.concatenate(
        [product(normed_parts[1], both), product(normed_parts[0], both)], axis=0
    )
    narrow = narrow[:, :across] + narrow[:, across:]
    size = lax.axis_size("seq")
    row_count = width // size
    narrow = narrow.reshape(size, row_count, across)
    beside = 128 // heads
    narrow_bc = jnp.pad(narrow[:, :, :share_bc], ((0, 0), (0, 0), (0, -share_bc % 128)))
    narrow_steps = narrow[:, :, share_bc:].reshape(size, row_count // beside, 128)
    narrow_steps = jnp.pad(narrow_steps, ((0, 0), (0, 0), (0, narrow_bc.shape[2] - 128)))
    narrow = jnp.concatenate([narrow_bc, narrow_steps], axis=1)
    narrow_rows = narrow.shape[1]
    narrow = jnp.pad(narrow, ((0, 0), (0, -narrow_rows % 8), (0, 0)))
    narrow = narrow.reshape(-1, narrow.shape[2])

    small = [
        grad_bc_conv_weight,
        grad_bc_conv_bias,
        grad_norm_gain,
        grad_dt_bias,
        grad_a_log,
        grad_d_skip,
        grad_conv_weight,
        grad_conv_bias,
        grad_gate_gain,
    ]
    row = jnp.concatenate([item.reshape(-1) for item in small])
    count = row.size
    row = jnp.pad(row, (0, -count % 1024)).reshape(-1, 128)

    mats = [
        keep_parts(normed_parts, grad_gate_x[1], parts, x_arrived),
        cot_parts[1::2] + [normed_gate, out_arrived],
        normed_parts[1::2] + [grad_gate_pre, gate_arrived],
    ]
    (x_block, grad_out_weight, gate_block), gathered, row = finish(parts, mats, narrow, row)
    grad_in_weight = jnp.stack([gate_block, x_block], axis=1)
    grad_bc_weight = head_gather(gathered[:, :row_count, :share_bc].reshape(width, share_bc))
    grad_dt_weight = gathered[:, row_count:narrow_rows, :128].reshape(width, heads)
    row = row.reshape(-1)
    sizes, first = [], 0
    for item in small:
        sizes.append(row[first : first + item.size].reshape(item.shape))
        first += item.size
    (
        grad_bc_conv_weight,
        grad_bc_conv_bias,
        grad_norm_gain,
        grad_dt_bias,
        grad_a_log,
        grad_d_skip,
        grad_conv_weight,
        grad_conv_bias,
        grad_gate_gain,
    ) = sizes

    share = width // head_count
    if head_count == 2:
        first = lax.axis_index("head") * share
        own_rows = lax.dynamic_slice_in_dim(out_weight, first, share, 0)
        other_rows = lax.dynamic_slice_in_dim(out_weight, share - first, share, 0)
        summed = lax.dot_general(
            normed_gate, own_rows, (NT, ((), ())), preferred_element_type=jnp.float32
        ) + xor_permute(
            lax.dot_general(
                normed_gate, other_rows, (NT, ((), ())), preferred_element_type=jnp.float32
            ),
            "head",
            0,
        )
    else:
        head_terms = lax.dot_general(
            normed_gate, out_weight, (NT, ((), ())), preferred_element_type=jnp.float32
        )
        summed = lax.psum_scatter(head_terms, "head", scatter_dimension=1, tiled=True)
    residual = lax.dynamic_slice_in_dim(flat, lax.axis_index("head") * share, share, 1)
    block_out = (residual + summed).astype(jnp.bfloat16).reshape(micro, length, share)
    return (
        block_out,
        grad_tokens,
        grad_norm_gain,
        grad_in_weight,
        grad_bc_weight,
        grad_dt_weight,
        grad_dt_bias,
        grad_a_log,
        grad_d_skip,
        grad_conv_weight,
        grad_conv_bias,
        grad_bc_conv_weight,
        grad_bc_conv_bias,
        grad_gate_gain,
        grad_out_weight,
    )


def solution(mesh):
    return jax.shard_map(
        body,
        mesh=mesh,
        in_specs=(
            P(None, "seq", None),
            P(),
            P(None, None, "head"),
            P(),
            P(None, "head"),
            P("head"),
            P("head"),
            P(None, "head"),
            P("head"),
            P(),
            P(),
            P("head"),
            P("head"),
            P(None, "head"),
            P(None, "seq", None),
            P(),
        ),
        out_specs=(
            P(None, "seq", "head"),
            P(None, "seq", None),
            P(),
            P("seq", None, "head"),
            P(),
            P(None, "head"),
            P("head"),
            P("head"),
            P("head"),
            P(None, "head"),
            P("head"),
            P(),
            P(),
            P("head"),
            P("seq", "head"),
        ),
        check_vma=False,
    )
```

```python
import functools
import math

import jax
import jax.numpy as jnp
from jax import lax
from jax.experimental import pallas as pl
from jax.experimental.pallas import tpu as pltpu
from jax.sharding import PartitionSpec as P

EPSILON = 1e-05
HIGHEST = lax.Precision.HIGHEST


def shifted(shard, axis, by):
    length = lax.axis_size(axis)
    pairs = [(i, i + by) for i in range(length) if 0 <= i + by < length]
    return lax.ppermute(shard, axis, pairs)


def segment_ids(seq_lengths, first, count, micro):
    places = first + jnp.arange(count, dtype=jnp.int32)
    starts = jnp.cumsum(seq_lengths, axis=-1) - seq_lengths
    short_ids = (
        jnp.sum((starts[:, None, :] <= places[None, :, None]).astype(jnp.int32), axis=-1) - 1
    )
    long_ids = jnp.zeros((micro - seq_lengths.shape[0], count), jnp.int32)
    labels = jnp.concatenate([short_ids, long_ids], axis=0)
    return jnp.where(places[None, :] >= 0, labels, -1)


def rms_scale(values, gain):
    return values * lax.rsqrt(jnp.mean(values * values, axis=-1, keepdims=True) + EPSILON) * gain


def conv_silu(extended, weight, bias, labels):
    taps = weight.shape[0]
    count = extended.shape[0] - taps + 1
    own = labels[taps - 1 :]
    total = bias + weight[0] * extended[taps - 1 :]
    for shift in range(1, taps):
        first = taps - 1 - shift
        mask = (labels[first : first + count] == own).astype(extended.dtype)
        total = total + weight[shift] * extended[first : first + count] * mask[:, None]
    return jax.nn.silu(total)


def step_sizes(delta_pre, dt_bias, a_log):
    delta = jax.nn.softplus(delta_pre + dt_bias[:, None])
    return (delta, -jnp.exp(a_log)[:, None] * delta)


DEAD = -1e30
EXCHANGE_COST = 100_000_000_000
FINISH_LIMIT = 60 * 1024 * 1024
GROUP = 4


def exchange_kernel(length, reverse, orders, jobs, tail, part_ref, log_ref, *refs):
    refs = list(refs)
    sources = [refs.pop(0) for _ in range(2 if orders else 0)]
    job_refs = [[refs.pop(0) for _ in range(job[2])] for job in jobs]
    out_ref = refs.pop(0)
    steps, made = [], []
    for (make, plan, _, results), inputs in zip(jobs, job_refs):
        made.append(refs.pop(0))
        steps += make(inputs, made[-1], plan)
    tail_ref = refs.pop(0) if tail is not None else None
    targets = [refs.pop(0) for _ in range(4 * len(orders))]
    (
        parts,
        logs,
        edge_in,
        edge_out,
        given,
        part_send,
        part_recv,
        log_send,
        log_recv,
        edge_send,
        edge_recv,
        given_send,
        given_recv,
        stage_sem,
        place_sem,
        tail_sem,
        staged,
    ) = refs
    me = lax.axis_index("seq")
    bits = (length - 1).bit_length()
    placed = arrange_copies(bits, orders, me, staged, targets, place_sem)
    stages = [
        pltpu.make_async_copy(source, staged.at[k], stage_sem.at[k])
        for k, source in enumerate(sources)
    ]
    for copy in stages:
        copy.start()
    rank = lax.rem(me, GROUP)
    plane = me // GROUP
    first = me - rank
    mates = (
        rank + 1 - 2 * lax.rem(rank, 2),
        rank + 2 - 4 * (rank // 2),
        3 - rank,
    )
    micro = part_ref.shape[0]
    planes = length // GROUP
    begins, ends = plane == 0, plane == planes - 1
    if reverse:
        begins, ends = ends, begins
    onward = -GROUP if reverse else GROUP

    barrier = pltpu.get_barrier_semaphore()
    for mate in mates:
        pl.semaphore_signal(
            barrier, inc=1, device_id={"seq": first + mate}, device_id_type=pl.DeviceIdType.MESH
        )

    @pl.when(plane > 0)
    def _():
        pl.semaphore_signal(
            barrier, inc=1, device_id={"seq": me - GROUP}, device_id_type=pl.DeviceIdType.MESH
        )

    @pl.when(plane < planes - 1)
    def _():
        pl.semaphore_signal(
            barrier, inc=1, device_id={"seq": me + GROUP}, device_id_type=pl.DeviceIdType.MESH
        )

    above = jnp.where(plane < planes - 1, 1, 0)
    below = jnp.where(plane > 0, 1, 0)
    pl.semaphore_wait(barrier, 3 + above + below)

    def remote(src, dst, send, recv, target):
        return pltpu.make_async_remote_copy(
            src_ref=src,
            dst_ref=dst,
            send_sem=send,
            recv_sem=recv,
            device_id={"seq": target},
            device_id_type=pl.DeviceIdType.MESH,
        )

    def log_copy(slot):
        mate = mates[slot]
        return remote(
            log_ref.at[mate], logs.at[rank], log_send.at[slot], log_recv.at[slot], first + mate
        )

    def part_copy(m, slot):
        mate = mates[slot]
        return remote(
            part_ref.at[m, mate],
            parts.at[m, rank],
            part_send.at[m, slot],
            part_recv.at[m, slot],
            first + mate,
        )

    def edge_copy(m):
        return remote(edge_out.at[m], edge_in.at[m], edge_send.at[m], edge_recv.at[m], me + onward)

    def given_copy(m, slot):
        mate = mates[slot]
        return remote(
            given.at[m, mate],
            out_ref.at[m, rank],
            given_send.at[m, slot],
            given_recv.at[m, slot],
            first + mate,
        )

    for slot in range(3):
        log_copy(slot).start()
    for m in range(micro):
        for slot in range(3):
            part_copy(m, slot).start()
    logs[rank] = log_ref[rank]
    for m in range(micro):
        parts[m, rank] = part_ref[m, rank]

    @pl.when(begins)
    def _():
        edge_in[...] = jnp.zeros_like(edge_in)

    for copy in stages:
        copy.wait()
    for copy in placed:
        copy.start()
    for slot in range(3):
        log_copy(slot).wait()
    order = tuple(reversed(range(GROUP))) if reverse else tuple(range(GROUP))
    for m in range(micro):
        for step in steps[m * len(steps) // micro : (m + 1) * len(steps) // micro]:
            step()
        for slot in range(3):
            part_copy(m, slot).wait()
        factors = [jnp.exp(logs[t, m])[:, None, :] for t in order]
        whole = jnp.exp(logs[0, m] + logs[1, m] + logs[2, m] + logs[3, m])[:, None, :]
        total = parts[m, order[0]]
        for t, factor in zip(order[1:], factors[1:]):
            total = total * factor + parts[m, t]

        @pl.when(jnp.logical_not(begins))
        def _():
            edge_copy(m).wait_recv()

        @pl.when(jnp.logical_not(ends))
        def _():
            edge_out[m] = total + whole * edge_in[m]
            edge_copy(m).start()

        running = edge_in[m]
        for place, (t, factor) in enumerate(zip(order, factors)):
            given[m, t] = running
            if place < GROUP - 1:
                running = running * factor + parts[m, t]
        for slot in range(3):
            given_copy(m, slot).start()
        out_ref[m, rank] = given[m, rank]
    if tail is not None:
        columns = part_columns(jobs[0][1])[tail]
        bit = jobs[0][1][tail][0][0]
        tail_copy = remote(
            made[0].at[:, columns],
            tail_ref,
            tail_sem.at[0],
            tail_sem.at[1],
            me + (1 << bit) * (1 - 2 * lax.rem(me // (1 << bit), 2)),
        )
        tail_copy.start()
    for m in range(micro):
        for slot in range(3):
            given_copy(m, slot).wait()

        @pl.when(jnp.logical_not(ends))
        def _():
            edge_copy(m).wait_send()

    if tail is not None:
        tail_copy.wait()
    for copy in placed:
        copy.wait()


def exchange(parts, logs, reverse, sources=(), orders=(), jobs=(), tail=None):
    micro, heads, rows, columns = parts.shape
    quarter = heads // GROUP
    length = lax.axis_size("seq")
    spread = jnp.broadcast_to(logs[:, :, None], (micro, heads, columns))
    spread = spread.reshape(micro, GROUP, quarter, columns).transpose(1, 0, 2, 3)
    shape = (micro, GROUP, quarter, rows, columns)
    arranged = []
    for source in sources:
        half = jax.ShapeDtypeStruct((source.shape[0], source.shape[1] // 2), source.dtype)
        arranged += [half] * (2 * len(orders))
    vmem = pl.BlockSpec(memory_space=pltpu.VMEM)
    hbm = pl.BlockSpec(memory_space=pl.ANY)
    made = [jax.ShapeDtypeStruct(job[3], jnp.float32) for job in jobs]
    if tail is not None:
        made.append(
            jax.ShapeDtypeStruct((jobs[0][3][0], sum(jobs[0][1][tail][1])), jnp.float32)
        )
    results = len(made)
    count = len(arranged)
    arranged = made + arranged
    job_inputs = [item for job in jobs for item in job[2]]
    plans = tuple((job[0], job[1], len(job[2]), 1) for job in jobs)
    out, *arranged = pl.pallas_call(
        functools.partial(exchange_kernel, length, reverse, orders, plans, tail),
        out_shape=[jax.ShapeDtypeStruct(shape, jnp.float32)] + arranged,
        in_specs=[vmem] * 2 + [hbm] * (len(sources) + len(job_inputs)),
        out_specs=[vmem] + [hbm] * len(arranged),
        scratch_shapes=[
            pltpu.VMEM(shape, jnp.float32),
            pltpu.VMEM((GROUP, micro, quarter, columns), jnp.float32),
            pltpu.VMEM((micro, quarter, rows, columns), jnp.float32),
            pltpu.VMEM((micro, quarter, rows, columns), jnp.float32),
            pltpu.VMEM(shape, jnp.float32),
            pltpu.SemaphoreType.DMA((micro, 3)),
            pltpu.SemaphoreType.DMA((micro, 3)),
            pltpu.SemaphoreType.DMA((3,)),
            pltpu.SemaphoreType.DMA((3,)),
            pltpu.SemaphoreType.DMA((micro,)),
            pltpu.SemaphoreType.DMA((micro,)),
            pltpu.SemaphoreType.DMA((micro, 3)),
            pltpu.SemaphoreType.DMA((micro, 3)),
            pltpu.SemaphoreType.DMA((2,)),
            pltpu.SemaphoreType.DMA((max(count, 1) * max(length // 2, 1),)),
            pltpu.SemaphoreType.DMA((2,)),
            pltpu.VMEM((2,) + sources[0].shape if sources else (2, 16, 128), jnp.bfloat16),
        ],
        compiler_params=pltpu.CompilerParams(
            collective_id=1 if reverse else 0,
            has_side_effects=True,
            vmem_limit_bytes=FINISH_LIMIT,
        ),
        cost_estimate=pl.CostEstimate(
            flops=EXCHANGE_COST, bytes_accessed=0, transcendentals=0
        ),
        name="exchange_back" if reverse else "exchange",
    )(parts.reshape(shape), spread, *sources, *job_inputs)
    out = out.reshape(micro, heads, rows, columns)
    return out, arranged[:results], arranged[results:]


def xor_permute(value, axis, bit):
    size = lax.axis_size(axis)
    return lax.ppermute(value, axis, [(i, i ^ (1 << bit)) for i in range(size)])


def axis_bits(axis):
    return (lax.axis_size(axis) - 1).bit_length()


def own_bit(axis, bit):
    return lax.rem(lax.axis_index(axis) // (1 << bit), 2)


def all_sum(value, axis):
    for bit in range(axis_bits(axis)):
        value = value + xor_permute(value, axis, bit)
    return value


def scatter_parts(columns, bits):
    if bits < 3 or columns % 2048:
        return [(tuple(range(bits)), (columns,))]
    rest = tuple(range(3, bits))
    unit = columns // 16
    return [
        ((0, 1, 2) + rest, (3 * unit, 2 * unit)),
        ((1, 0, 2) + rest, (2 * unit, 3 * unit)),
        ((2, 0, 1) + rest, (3 * unit, 0)),
        ((2, 1, 0) + rest, (0, 3 * unit)),
    ]


def arranged_place(order, position, bits):
    return [(position >> (bits - 1 - t)) & 1 for t, _ in sorted(enumerate(order), key=lambda p: p[1])]


def arranged_block(order, position, bits, me):
    flips = arranged_place(order, position, bits)
    total = 0
    for bit, flip in enumerate(flips):
        mine = lax.rem(me // (1 << bit), 2)
        total = total + (1 << bit) * ((1 - mine) if flip else mine)
    return total


def arrange(left, orders):
    bits = axis_bits("seq")
    size = 1 << bits
    tokens, width = left.shape
    view = left.reshape(tokens, size, width // size)
    me = lax.axis_index("seq").astype(jnp.int32)
    results = []
    for order in orders:
        table = jnp.stack([arranged_block(order, j, bits, me) for j in range(size)])
        chosen = jnp.take(view, table, axis=1).reshape(tokens, width)
        results += [chosen[:, width // 2 :], chosen[:, : width // 2]]
    return results


def arrange_copies(bits, orders, me, staged, targets, sem):
    copies, number = [], 0
    half = 1 << (bits - 1)
    for source in range(len(targets) // (2 * len(orders)) if orders else 0):
        block = staged.shape[2] >> bits
        for order in orders:
            for begin in (half, 0):
                target = targets[number]
                for j in range(half):
                    place = arranged_block(order, begin + j, bits, me)
                    first = pl.multiple_of(place * block, block)
                    copies.append(
                        pltpu.make_async_copy(
                            staged.at[source, :, pl.ds(first, block)],
                            target.at[:, pl.ds(j * block, block)],
                            sem.at[number * half + j],
                        )
                    )
                number += 1
    return copies


def product(left, right):
    return lax.dot_general(left, right, (TN, ((), ())), preferred_element_type=jnp.float32)


def part_columns(parts):
    first, columns = 0, []
    for _, widths in parts:
        columns.append(pl.ds(first, sum(widths)))
        first += sum(widths)
    return columns


def product_steps(inputs, out_ref, parts):
    count = len(parts)
    lefts, right_ref, more = inputs[:count], inputs[count], inputs[count + 1 :]
    return [
        functools.partial(
            product_step, lefts[k], right_ref, more[k : k + 1], out_ref, columns.start, columns.size
        )
        for k, columns in enumerate(part_columns(parts))
    ]


def product_step(left_ref, right_ref, more, out_ref, first, width):
    tokens, rows = left_ref.shape
    tile = min(rows, 256)
    columns = pl.ds(first, width)

    def body(left, right, *rest):
        value = product(left[...], right[...])
        for item in rest[:-1]:
            value = value + item[...]
        rest[-1][...] = value

    tiled = pl.BlockSpec((tile, width), lambda i: (i, 0))
    pltpu.emit_pipeline(
        body,
        grid=(rows // tile,),
        in_specs=[
            pl.BlockSpec((tokens, tile), lambda i: (0, i)),
            pl.BlockSpec((tokens, width), lambda i: (0, 0)),
        ]
        + [tiled] * len(more),
        out_specs=[tiled],
    )(
        left_ref,
        right_ref.at[:, columns],
        *more,
        out_ref.at[:, columns],
    )


def plain_steps(inputs, out_ref, parts):
    left_ref, right_ref = inputs
    width = min(right_ref.shape[1], 512)
    return [
        functools.partial(plain_step, left_ref, right_ref, out_ref, first, width)
        for first in range(0, right_ref.shape[1], width)
    ]


def plain_step(left_ref, right_ref, out_ref, first, width):
    rows, depth = left_ref.shape
    tile = min(rows, 256)
    columns = pl.ds(first, width)

    def body(left, right, out):
        out[...] = low_dot(left[...], right[...], NN)

    pltpu.emit_pipeline(
        body,
        grid=(rows // tile,),
        in_specs=[
            pl.BlockSpec((tile, depth), lambda i: (i, 0)),
            pl.BlockSpec((depth, width), lambda i: (0, 0)),
        ],
        out_specs=[pl.BlockSpec((tile, width), lambda i: (i, 0))],
    )(left_ref, right_ref.at[:, columns], out_ref.at[:, columns])


def share_steps(inputs, out_refs, parts):
    left_ref, right_ref = inputs
    share = right_ref.shape[0] // 2
    mine = lax.axis_index("head") * share
    return [
        functools.partial(share_step, left_ref, right_ref, out_ref, first, share)
        for out_ref, first in zip(out_refs, (share - mine, mine))
    ]


def share_step(left_ref, right_ref, out_ref, first, share):
    rows, depth = left_ref.shape
    tile = min(rows, 256)
    width = min(share, 512)
    chosen = right_ref.at[pl.ds(pl.multiple_of(first, share), share)]

    def body(left, right, out):
        out[...] = low_dot(left[...], right[...], NT)

    pltpu.emit_pipeline(
        body,
        grid=(share // width, rows // tile),
        in_specs=[
            pl.BlockSpec((tile, depth), lambda j, i: (i, 0)),
            pl.BlockSpec((width, depth), lambda j, i: (j, 0)),
        ],
        out_specs=[pl.BlockSpec((tile, width), lambda j, i: (i, j))],
    )(left_ref, chosen, out_ref)


def row_step(grad_ref, weight_ref, narrow_left_ref, narrow_right_ref, out_ref, first, rows):
    depth, halves, width = weight_ref.shape
    tile = min(depth, 256)

    def inner(held, sem):
        copy = pltpu.make_async_copy(grad_ref.at[:, pl.ds(first, rows)], held, sem)
        copy.start()
        copy.wait()

        def body(weight, narrow_left, narrow_right, out):
            turned_weight = jnp.swapaxes(weight[...], 0, 1)
            total = low_dot(narrow_left[...], narrow_right[...], NT)
            for half in range(halves):
                total = total + low_dot(held[half], turned_weight[half], NT)
            out[...] = total

        pltpu.emit_pipeline(
            body,
            grid=(depth // tile,),
            in_specs=[
                pl.BlockSpec((tile, halves, width), lambda j: (j, 0, 0)),
                pl.BlockSpec((rows, narrow_left_ref.shape[1]), lambda j: (0, 0)),
                pl.BlockSpec((tile, narrow_left_ref.shape[1]), lambda j: (j, 0)),
            ],
            out_specs=[pl.BlockSpec((rows, tile), lambda j: (0, j))],
        )(
            weight_ref,
            narrow_left_ref.at[pl.ds(first, rows)],
            narrow_right_ref,
            out_ref.at[pl.ds(first, rows)],
        )

    pl.run_scoped(
        inner,
        pltpu.VMEM((halves, rows, width), jnp.bfloat16),
        pltpu.SemaphoreType.DMA,
    )


def token_step(
    gain_ref, gain_sum, tokens_ref, cot_ref, rows_refs, kept_ref, other_ref, grad_ref, block_ref
):
    count, width = tokens_ref.shape
    share = width // 2
    tile = min(count, 128)
    mine = lax.axis_index("head") == 0
    gain_sum[...] = jnp.zeros_like(gain_sum)

    def body(tokens, cot, own, other, kept, arrived, grad, block):
        values = tokens[...].astype(jnp.float32)
        pulls = own[...] + other[...]
        scale = lax.rsqrt(jnp.mean(values * values, axis=1, keepdims=True) + EPSILON)
        gained = pulls * gain_ref[...]
        cross = jnp.sum(gained * values, axis=1, keepdims=True)
        grad[...] = (
            cot[...].astype(jnp.float32)
            + gained * scale
            - values * (scale * scale * scale * cross * (1.0 / width))
        )
        parts = (pulls * values * scale).reshape(tile // 8, 8, width)
        gain_sum[...] = gain_sum[...] + jnp.sum(parts, axis=0)
        residual = jnp.where(mine, values[:, :share], values[:, share:])
        block[...] = (residual + kept[...] + arrived[...]).astype(jnp.bfloat16)

    full = pl.BlockSpec((tile, width), lambda i: (i, 0))
    half = pl.BlockSpec((tile, share), lambda i: (i, 0))
    pltpu.emit_pipeline(
        body,
        grid=(count // tile,),
        in_specs=[full] * 4 + [half] * 2,
        out_specs=[full, half],
    )(tokens_ref, cot_ref, *rows_refs, kept_ref, other_ref, grad_ref, block_ref)


def finish_kernel(parts, mats, paired, bits, blocks, *refs):
    refs = list(refs)
    take = lambda count: [refs.pop(0) for _ in range(count)]
    ins = [take(2 * len(parts) + 1) for _ in range(mats - 1)]
    last_sent, last_kept = take(len(parts)), take(len(parts))
    grad_ref, narrow_ref, vector_ref = take(3)
    if paired:
        weight_ref, gain_ref, tokens_ref, cot_ref = take(4)
        narrow_left_ref, narrow_right_ref, gated_ref, out_weight_ref = take(4)
    outs = take(mats)
    gathered_ref, vector_out_ref = take(2)
    if paired:
        token_grad_ref, block_ref, row_ref, row_other_ref = take(4)
        share_sent_ref, share_kept_ref, share_other_ref = take(3)
    sent_ref, arrived_ref = take(2)
    made_refs = take(mats)
    me = lax.axis_index("seq")
    last_right = grad_ref.at[grad_ref.shape[0] - 1]
    columns_of = part_columns(parts)
    ins.append(last_kept + [last_right] + [arrived_ref.at[:, columns] for columns in columns_of])

    def partner(bit):
        return me + (1 << bit) * (1 - 2 * lax.rem(me // (1 << bit), 2))

    waves = []
    piece_count = len(parts[0][1])
    chain_count = 0
    for mat in range(mats):
        for piece in range(piece_count):
            wave, first = [], 0
            for order, widths in parts:
                if widths[piece]:
                    place = first + sum(widths[:piece])
                    keep = refs.pop(0)
                    recvs = take(bits - 1)
                    wave.append(
                        (chain_count, made_refs[mat], place, outs[mat], place, order[1:], keep, recvs)
                    )
                    chain_count += 1
                first += sum(widths)
            waves.append(wave)
    narrow_order = parts[0][0]
    narrow = (chain_count, narrow_ref, 0, None, 0, narrow_order, refs.pop(0), take(bits))
    vector_sums, vector_recvs, gain_sum, local_sem, send_sem, recv_sem = refs

    barrier = pltpu.get_barrier_semaphore()
    for bit in range(bits):
        pl.semaphore_signal(
            barrier,
            inc=1,
            device_id={"seq": partner(bit)},
            device_id_type=pl.DeviceIdType.MESH,
        )
    if paired:
        pl.semaphore_signal(
            barrier,
            inc=1,
            device_id={"head": 1 - lax.axis_index("head")},
            device_id_type=pl.DeviceIdType.MESH,
        )
    pl.semaphore_wait(barrier, bits + (1 if paired else 0))

    numbers = {}

    def remote_to(key, src, dst, target):
        number = numbers.setdefault(key, len(numbers))
        return pltpu.make_async_remote_copy(
            src_ref=src,
            dst_ref=dst,
            send_sem=send_sem.at[number],
            recv_sem=recv_sem.at[number],
            device_id=target,
            device_id_type=pl.DeviceIdType.MESH,
        )

    def remote(key, src, dst, bit):
        return remote_to(key, src, dst, {"seq": partner(bit)})

    def first_copy(k):
        region = (slice(None), columns_of[k])
        return remote(("first", k), sent_ref.at[region], arrived_ref.at[region], parts[k][0][0])

    def share_copy():
        return remote_to(
            "share", share_sent_ref, share_other_ref, {"head": 1 - lax.axis_index("head")}
        )

    def shares(part):
        share_steps(
            (gated_ref, out_weight_ref), (share_sent_ref, share_kept_ref), ()
        )[part]()
        if part == 0:
            share_copy().start()

    def row_copy():
        return remote_to("row", row_ref, row_other_ref, {"head": 1 - lax.axis_index("head")})

    def local_copy(chain):
        number, source, first, _, _, _, keep, _ = chain
        rows, columns = keep.shape
        return pltpu.make_async_copy(
            source.at[pl.ds(0, rows), pl.ds(first, columns)], keep, local_sem.at[number]
        )

    def chain_copy(chain, phase):
        number, source, first, _, _, order, keep, recvs = chain
        rows, columns = recvs[phase].shape
        if phase == 0:
            region = source.at[pl.ds(rows, rows), pl.ds(first, columns)]
        else:
            region = keep.at[pl.ds(rows, rows)]
        return remote((number, phase), region, recvs[phase], order[phase])

    made = set()

    def make(mat):
        if mat in made:
            return
        made.add(mat)
        if mat == mats - 1:
            for k in range(len(parts)):
                first_copy(k).wait_recv()
        for step in product_steps(ins[mat], made_refs[mat], parts):
            step()

    def begin(number):
        make(number // piece_count)
        for chain in waves[number]:
            chain_copy(chain, 0).start()
            local_copy(chain).start()

    def advance(chain, phase):
        if phase == 0:
            local_copy(chain).wait()
        chain_copy(chain, phase).wait_recv()
        number, _, _, out, place, order, keep, recvs = chain
        recv = recvs[phase]
        rows = recv.shape[0]
        slab = min(rows, 32)

        @pl.loop(0, rows // slab)
        def _(step):
            cut = pl.ds(pl.multiple_of(step * slab, slab), slab)
            keep[cut, :] = keep[cut, :] + recv[cut, :]

        if phase + 1 < len(order):
            chain_copy(chain, phase + 1).start()
        elif out is not None:
            out[:, place : place + keep.shape[1]] = keep[0:blocks, :]

    def vector_copy(phase):
        return remote(("vector", phase), vector_sums.at[phase], vector_recvs.at[phase], phase)

    def begin_vector():
        vector_sums[0] = vector_ref[...]
        if paired:
            total = jnp.sum(gain_sum[...], axis=0, keepdims=True)
            for place in range(total.shape[1] // 128):
                vector_sums[0, place : place + 1, :] = total[:, place * 128 : place * 128 + 128]
        vector_copy(0).start()

    def advance_vector(phase):
        vector_copy(phase).wait_recv()
        total = vector_sums[phase] + vector_recvs[phase]
        if phase + 1 < bits:
            vector_sums[phase + 1] = total
            vector_copy(phase + 1).start()
        else:
            vector_out_ref[...] = total

    def gather_copies(phase):
        bit = bits - 1 - phase
        copies = []
        for high in range(1 << phase):
            block = lax.rem(me, 2 << bit) + high * (2 << bit)
            region = gathered_ref.at[block]
            copies.append(remote(("gather", phase, high), region, region, bit))
        return copies

    def narrow_halving(phase):
        advance(narrow, phase)
        if phase + 1 == bits:
            gathered_ref[me] = narrow[6][0 : gathered_ref.shape[1], :]
            for copy in gather_copies(0):
                copy.start()

    def narrow_gather(phase):
        for copy in gather_copies(phase):
            copy.wait_recv()
        if phase + 1 < bits:
            for copy in gather_copies(phase + 1):
                copy.start()

    def rows(part):
        count = row_ref.shape[0] // 2
        row_step(
            grad_ref, weight_ref, narrow_left_ref, narrow_right_ref, row_ref, part * count, count
        )
        if part == 1:
            row_copy().start()

    def token_rows():
        row_copy().wait()
        share_copy().wait()
        token_step(
            gain_ref,
            gain_sum,
            tokens_ref,
            cot_ref,
            (row_ref, row_other_ref),
            share_kept_ref,
            share_other_ref,
            token_grad_ref,
            block_ref,
        )

    narrow_steps = [functools.partial(narrow_halving, phase) for phase in range(bits)]
    narrow_steps += [functools.partial(narrow_gather, phase) for phase in range(bits)]
    fills = {}
    vector_tick = 0
    if paired:
        fills = {
            0: [functools.partial(rows, 0)],
            1: [functools.partial(rows, 1), functools.partial(shares, 0)],
            2: [functools.partial(shares, 1)],
            3: [token_rows],
        }
        vector_tick = 4

    chain_copy(narrow, 0).start()
    local_copy(narrow).start()
    sent_steps = product_steps(last_sent + [last_right], sent_ref, parts)
    for k, step in enumerate(sent_steps):
        step()
        first_copy(k).start()
    begun = min(2, len(waves))
    for number in range(begun):
        begin(number)
    if len(waves) > begun:
        make(begun // piece_count)
    ticks = max(len(waves) + bits - 2, 2 * bits, vector_tick + bits)
    for tick in range(ticks):
        if tick < len(narrow_steps):
            narrow_steps[tick]()
        for phase in range(bits - 1):
            number = tick - phase
            if 0 <= number < len(waves):
                for chain in waves[number]:
                    advance(chain, phase)
                if phase == 0 and number + 2 < len(waves):
                    begin(number + 2)
        if tick + 3 < len(waves):
            make((tick + 3) // piece_count)
        for step in fills.get(tick, ()):
            step()
        if tick == vector_tick:
            begin_vector()
        if 0 <= tick - vector_tick < bits:
            advance_vector(tick - vector_tick)
    for k in range(len(parts)):
        first_copy(k).wait_send()
    for wave in waves:
        for chain in wave:
            for phase in range(bits - 1):
                chain_copy(chain, phase).wait_send()
    for phase in range(bits):
        chain_copy(narrow, phase).wait_send()
        vector_copy(phase).wait_send()
        for copy in gather_copies(phase):
            copy.wait_send()


def finish(parts, mats, last_sent, last_kept, grad, narrow, vector, row_inputs):
    bits = axis_bits("seq")
    size = 1 << bits
    count = len(mats) + 1
    paired = bool(row_inputs)
    rows = last_kept[0].shape[1]
    blocks = rows // (size // 2)
    columns = sum(sum(widths) for _, widths in parts)
    scratch, copies, chains = [], 0, 0
    for _ in range(count):
        for piece in range(len(parts[0][1])):
            for _, widths in parts:
                if widths[piece]:
                    scratch.append(pltpu.VMEM((rows // 2, widths[piece]), jnp.float32))
                    for phase in range(bits - 1):
                        scratch.append(
                            pltpu.VMEM(((rows // 2) >> phase, widths[piece]), jnp.float32)
                        )
                    copies += bits - 1
                    chains += 1
    narrow_rows = narrow.shape[0] // 2
    scratch.append(pltpu.VMEM((narrow_rows, narrow.shape[1]), jnp.float32))
    for phase in range(bits):
        scratch.append(pltpu.VMEM((narrow_rows >> phase, narrow.shape[1]), jnp.float32))
    copies += 2 * bits + size - 1 + len(parts) + 2
    scratch += [pltpu.VMEM((bits,) + vector.shape, jnp.float32)] * 2
    scratch += [
        pltpu.VMEM((8, row_inputs[1].shape[1] if paired else 128), jnp.float32),
        pltpu.SemaphoreType.DMA((chains + 1,)),
        pltpu.SemaphoreType.DMA((copies,)),
        pltpu.SemaphoreType.DMA((copies,)),
    ]
    vmem, hbm = pl.BlockSpec(memory_space=pltpu.VMEM), pl.BlockSpec(memory_space=pl.ANY)
    shapes = [jax.ShapeDtypeStruct((blocks, columns), jnp.float32) for _ in range(count)]
    shapes.append(
        jax.ShapeDtypeStruct((size, narrow.shape[0] // size, narrow.shape[1]), jnp.float32)
    )
    shapes.append(jax.ShapeDtypeStruct(vector.shape, jnp.float32))
    specs = [vmem] * len(shapes)
    if paired:
        tokens = row_inputs[2]
        token_shape = jax.ShapeDtypeStruct(tokens.shape, jnp.float32)
        block_shape = jax.ShapeDtypeStruct((tokens.shape[0], tokens.shape[1] // 2), jnp.bfloat16)
        share_shape = jax.ShapeDtypeStruct(block_shape.shape, jnp.float32)
        shapes += [token_shape, block_shape, token_shape, token_shape] + [share_shape] * 3
    half = jax.ShapeDtypeStruct((rows, columns), jnp.float32)
    shapes += [half] * (2 + count)
    specs += [hbm] * (len(shapes) - len(specs))
    flat = [item for mat in mats for item in mat] + last_sent + last_kept + [grad, narrow]
    row_specs = [hbm, vmem] + [hbm] * 6 if paired else []
    results = pl.pallas_call(
        functools.partial(finish_kernel, parts, count, paired, bits, blocks),
        out_shape=shapes,
        in_specs=[hbm] * len(flat) + [vmem] + row_specs,
        out_specs=specs,
        scratch_shapes=scratch,
        compiler_params=pltpu.CompilerParams(
            collective_id=2, has_side_effects=True, vmem_limit_bytes=FINISH_LIMIT
        ),
        name="finish",
    )(*flat, vector, *row_inputs)
    return (
        results[:count],
        results[count],
        results[count + 1],
        *(results[count + 2 : count + 4] if paired else ()),
    )


def head_gather(block):
    if lax.axis_size("head") != 2:
        return lax.all_gather(block, "head", axis=1, tiled=True)
    other = xor_permute(block, "head", 0)
    mine = lax.axis_index("head") == 0
    return jnp.concatenate(
        [jnp.where(mine, block, other), jnp.where(mine, other, block)], axis=1
    )


HEAD_GROUP = 8
VMEM_LIMIT = 56 * 1024 * 1024
FAR = 1 << 30
NN = ((1,), (0,))
NT = ((1,), (1,))
TN = ((0,), (0,))


def low_dot(left, right, dims):
    return lax.dot_general(
        left.astype(jnp.bfloat16),
        right.astype(jnp.bfloat16),
        (dims, ((), ())),
        preferred_element_type=jnp.float32,
    )


def halves_of(value):
    high = value.astype(jnp.bfloat16)
    return high, (value - high.astype(jnp.float32)).astype(jnp.bfloat16)


def thirds_of(value):
    first = value.astype(jnp.bfloat16).astype(jnp.float32)
    second = (value - first).astype(jnp.bfloat16).astype(jnp.float32)
    return first, second, value - first - second


def spread_matrix(heads, head_dim):
    shape = (heads, heads * head_dim)
    rows = lax.broadcasted_iota(jnp.int32, shape, 0)
    columns = lax.broadcasted_iota(jnp.int32, shape, 1)
    return (columns // head_dim == rows).astype(jnp.float32)


def turned(rows, matrix):
    return low_dot(
        jnp.concatenate(thirds_of(rows), axis=0), jnp.concatenate([matrix] * 3, axis=0), TN
    )


def head_sums(spread, value):
    high, low = halves_of(value)
    return low_dot(spread, high, NT) + low_dot(spread, low, NT)


def map_dot(left, right):
    high, low = halves_of(right)
    return low_dot(
        jnp.concatenate([left, left], axis=1), jnp.concatenate([high, low], axis=1), NT
    )


def fine_dot(left, right):
    left_high, left_low = halves_of(left)
    right_high, right_low = halves_of(right)
    return (
        low_dot(left_high, right_high, NN)
        + low_dot(left_high, right_low, NN)
        + low_dot(left_low, right_high, NN)
    )


def sigmoid(value):
    return 1.0 / (1.0 + jnp.exp(-value))


def segment_of(places, starts_ref, micro):
    label = jnp.zeros_like(places)
    for number in range(starts_ref.shape[1]):
        label = label + jnp.where(places >= starts_ref[micro, number], 1, 0)
    return label


def same_segment(count, base_ref, starts_ref, taps):
    micro = pl.program_id(0)
    places = base_ref[0] + lax.broadcasted_iota(jnp.int32, (count, 1), 0)
    own = segment_of(places, starts_ref, micro)
    return [
        jnp.where(segment_of(places - shift, starts_ref, micro) == own, 1.0, 0.0)
        for shift in range(1, taps)
    ]


def pair_labels(count, base_ref, starts_ref):
    micro = pl.program_id(0)
    column = base_ref[0] + lax.broadcasted_iota(jnp.int32, (count, 1), 0)
    row = base_ref[0] + lax.broadcasted_iota(jnp.int32, (1, count), 1)
    return segment_of(column, starts_ref, micro) == segment_of(row, starts_ref, micro)


def conv_sum(ext, value, halo, weight, bias, masks):
    count = value.shape[0]
    ext[0:8, :] = halo
    ext[8 : 8 + count, :] = value
    total = bias + weight[0:1] * value
    for shift in range(1, weight.shape[0]):
        total = (
            total
            + weight[shift : shift + 1]
            * ext[8 - shift : 8 - shift + count, :]
            * masks[shift - 1]
        )
    return total


def project_kernel(tokens_ref, gain_ref, weight_ref, normed_ref, out_ref):
    count = tokens_ref.shape[0]
    slab = min(count, 64)

    @pl.when(pl.program_id(0) == 0)
    def _():
        @pl.loop(0, count // slab)
        def _(step):
            cut = pl.ds(pl.multiple_of(step * slab, slab), slab)
            values = tokens_ref[cut, :].astype(jnp.float32)
            scale = lax.rsqrt(jnp.mean(values * values, axis=1, keepdims=True) + EPSILON)
            normed_ref[cut, :] = (values * scale * gain_ref[...]).astype(jnp.bfloat16)

    weight = jnp.swapaxes(weight_ref[...], 0, 1)
    for half in range(weight.shape[0]):
        out_ref[half] = low_dot(normed_ref[...], weight[half], NN)


def project(tokens, gain, weight):
    count, width = tokens.shape
    _, halves, columns = weight.shape
    tile = min(columns, 256)
    return pl.pallas_call(
        project_kernel,
        grid=(columns // tile,),
        in_specs=[
            pl.BlockSpec((count, width), lambda j: (0, 0)),
            pl.BlockSpec((1, width), lambda j: (0, 0)),
            pl.BlockSpec((width, halves, tile), lambda j: (0, 0, j)),
        ],
        out_specs=[
            pl.BlockSpec((count, width), lambda j: (0, 0)),
            pl.BlockSpec((halves, count, tile), lambda j: (0, 0, j)),
        ],
        out_shape=[
            jax.ShapeDtypeStruct((count, width), jnp.bfloat16),
            jax.ShapeDtypeStruct((halves, count, columns), jnp.float32),
        ],
        compiler_params=pltpu.CompilerParams(vmem_limit_bytes=VMEM_LIMIT),
        cost_estimate=pl.CostEstimate(
            flops=2 * count * width * columns * halves, bytes_accessed=0, transcendentals=0
        ),
        name="project",
    )(tokens, gain[None], weight)


def front_kernel(
    head_dim,
    base_ref,
    starts_ref,
    x_ref,
    halo_ref,
    weight_ref,
    bias_ref,
    b_ref,
    tail_ref,
    low_ref,
    state_ref,
    ext,
):
    heads = tail_ref.shape[1]
    weight = weight_ref[...]
    masks = same_segment(x_ref.shape[2], base_ref, starts_ref, weight.shape[0])
    total = conv_sum(ext, x_ref[0, 0], halo_ref[0], weight, bias_ref[...], masks)
    act = (total * sigmoid(total)).astype(jnp.bfloat16)
    low_ref[0] = act
    scale = turned(tail_ref[0], spread_matrix(heads, head_dim))
    high, low = halves_of(act.astype(jnp.float32) * scale)
    state_ref[0] = low_dot(high, b_ref[0], TN) + low_dot(low, b_ref[0], TN)


def mix_kernel(
    head_dim,
    base_ref,
    starts_ref,
    x_ref,
    b_ref,
    c_ref,
    run_ref,
    step_ref,
    carry_ref,
    start_ref,
    gate_ref,
    cot_ref,
    gain_ref,
    skip_ref,
    mixed_ref,
    sums_ref,
):
    heads = step_ref.shape[1]
    count = x_ref.shape[1]
    spread = spread_matrix(heads, head_dim)
    x = x_ref[0]
    b, c = b_ref[0], c_ref[0]
    rows = lax.broadcasted_iota(jnp.int32, (count, count), 0)
    columns = lax.broadcasted_iota(jnp.int32, (count, count), 1)
    valid = pair_labels(count, base_ref, starts_ref) & (rows >= columns)
    scores = jnp.where(valid, low_dot(c, b, NT), 0.0)
    wide = x.astype(jnp.float32)
    scaled = (wide * turned(step_ref[0], spread)).astype(jnp.bfloat16)
    inter = map_dot(c, start_ref[0]) * turned(carry_ref[0], spread)
    run_row = run_ref[0]
    run = turned(run_row, spread_matrix(heads, 1))
    pair = 2 * head_dim
    middle = count // 2
    lane = lax.broadcasted_iota(jnp.int32, (count, pair), 1)
    results = []
    for first in range(0, heads, 2):
        block = scaled[:, first * head_dim : first * head_dim + pair]
        halves = []
        for head in (first, first + 1):
            strips = []
            for top, cut in ((0, middle), (middle, count)):
                gap = run[top:cut, head : head + 1] - run_row[head : head + 1, :cut]
                weights = jnp.exp(jnp.minimum(gap, 0.0)) * scores[top:cut, :cut]
                strips.append(low_dot(weights, block[:cut], NN))
            halves.append(jnp.concatenate(strips, axis=0))
        results.append(jnp.where(lane < head_dim, halves[0], halves[1]))
    mixed = jnp.concatenate(results, axis=1) + inter + skip_ref[...] * wide
    mixed_ref[0] = mixed
    gate = gate_ref[0, 0]
    gated = mixed * (gate * sigmoid(gate))
    square = jnp.sum(gated * gated, axis=1, keepdims=True)
    cross = jnp.sum(cot_ref[0] * gain_ref[...] * gated, axis=1, keepdims=True)
    both = jnp.concatenate([square, cross], axis=1)

    @pl.when(pl.program_id(1) == 0)
    def _():
        sums_ref[0] = both

    @pl.when(pl.program_id(1) > 0)
    def _():
        sums_ref[0] = sums_ref[0] + both


def gate_kernel(
    head_dim,
    full,
    mixed_ref,
    gate_ref,
    cot_ref,
    sums_ref,
    gain_ref,
    carry_ref,
    c_ref,
    norm_ref,
    grad_gate_ref,
    both_ref,
    grad_mixed_ref,
    start_ref,
    rows_ref,
):
    heads = carry_ref.shape[1]
    mixed, gate, cot, gain = mixed_ref[0], gate_ref[0, 0], cot_ref[0], gain_ref[...]
    scale = lax.rsqrt(sums_ref[0, :, 0:1] / full + EPSILON)
    sigma = sigmoid(gate)
    act = gate * sigma
    gated = mixed * act
    unit = gated * scale
    norm_ref[0] = (unit * gain).astype(jnp.bfloat16)
    pull = scale * scale * scale * sums_ref[0, :, 1:2] / full
    grad_gated = cot * gain * scale - gated * pull
    grad_gate = (grad_gated * mixed * sigma * (1.0 + gate * (1.0 - sigma))).astype(jnp.bfloat16)
    grad_gate_ref[0] = grad_gate
    both_ref[0, 0] = grad_gate
    grad_mixed = (grad_gated * act).astype(jnp.bfloat16)
    grad_mixed_ref[0] = grad_mixed
    carried = grad_mixed.astype(jnp.float32) * turned(
        carry_ref[0], spread_matrix(heads, head_dim)
    )
    high, low = halves_of(carried)
    start_ref[0] = low_dot(high, c_ref[0], TN) + low_dot(low, c_ref[0], TN)
    gains = jnp.sum(cot * unit, axis=0, keepdims=True)
    rows_ref[0] = jnp.concatenate([gains, jnp.zeros((7, gains.shape[1]), jnp.float32)], axis=0)


def back_kernel(
    head_dim,
    parts,
    skipped,
    base_ref,
    starts_ref,
    x_ref,
    g_ref,
    b_ref,
    c_ref,
    run_ref,
    step_ref,
    carry_ref,
    tail_ref,
    start_ref,
    end_ref,
    pre_ref,
    halo_ref,
    weight_ref,
    bias_ref,
    skip_ref,
    both_in_ref,
    out_sent_ref,
    gate_sent_ref,
    both_ref,
    edge_ref,
    halo_out_ref,
    rows_ref,
    direct_ref,
    decay_ref,
    pair_ref,
    grad_b_ref,
    grad_c_ref,
    *refs,
):
    refs = list(refs)
    ext, moved, send_sem, recv_sem = refs[-4:]
    me = lax.axis_index("seq")

    def partner(bit):
        return me + (1 << bit) * (1 - 2 * lax.rem(me // (1 << bit), 2))

    def sends():
        copies = []
        for mat, source in enumerate((out_sent_ref, gate_sent_ref)):
            for k, columns in enumerate(part_columns(parts)):
                if (mat, k) not in skipped:
                    copies.append(
                        pltpu.make_async_remote_copy(
                            src_ref=source.at[:, columns],
                            dst_ref=refs[len(copies)],
                            send_sem=send_sem.at[len(copies)],
                            recv_sem=recv_sem.at[len(copies)],
                            device_id={"seq": partner(parts[k][0][0])},
                            device_id_type=pl.DeviceIdType.MESH,
                        )
                    )
        return copies

    at_first = (pl.program_id(0) == 0) & (pl.program_id(1) == 0)
    at_last = (pl.program_id(0) == pl.num_programs(0) - 1) & (
        pl.program_id(1) == pl.num_programs(1) - 1
    )
    used = sorted({order[0] for order, _ in parts})

    @pl.when(at_first)
    def _():
        barrier = pltpu.get_barrier_semaphore()
        for bit in used:
            pl.semaphore_signal(
                barrier,
                inc=1,
                device_id={"seq": partner(bit)},
                device_id_type=pl.DeviceIdType.MESH,
            )
        pl.semaphore_wait(barrier, len(used))
        for copy in sends():
            copy.start()

    heads = step_ref.shape[1]
    count = x_ref.shape[1]
    spread = spread_matrix(heads, head_dim)
    x, g, b, c = x_ref[0], g_ref[0], b_ref[0], c_ref[0]
    x_wide, g_wide = x.astype(jnp.float32), g.astype(jnp.float32)
    rows = lax.broadcasted_iota(jnp.int32, (count, count), 0)
    columns = lax.broadcasted_iota(jnp.int32, (count, count), 1)
    valid = pair_labels(count, base_ref, starts_ref) & (columns >= rows)
    scores = jnp.where(valid, low_dot(b, c, NT), 0.0)
    upto = (rows >= columns).astype(jnp.bfloat16)
    before = (rows < columns).astype(jnp.float32)
    step = turned(step_ref[0], spread)
    carry = turned(carry_ref[0], spread)
    tail = turned(tail_ref[0], spread)
    scaled_wide = x_wide * step
    scaled, scaled_rest = halves_of(scaled_wide)
    start, end = start_ref[0], end_ref[0]
    run_row = run_ref[0]
    run = turned(run_row, spread_matrix(heads, 1))
    pair = 2 * head_dim
    lane = lax.broadcasted_iota(jnp.int32, (count, pair), 1)
    middle = count // 2
    score_grads = [
        jnp.zeros((middle, count), jnp.float32),
        jnp.zeros((count - middle, count - middle), jnp.float32),
    ]
    results, straddles = [], []
    for first in range(0, heads, 2):
        cut = slice(first * head_dim, first * head_dim + pair)
        g_block = g[:, cut]
        g_swap = jnp.concatenate([g_block[:, head_dim:], g_block[:, :head_dim]], axis=1)
        x_block, x_rest = scaled[:, cut], scaled_rest[:, cut]
        x_rest = jnp.concatenate([x_rest[:, head_dim:], x_rest[:, :head_dim]], axis=1)
        halves = []
        for head in (first, first + 1):
            own = (lane < head_dim) if head == first else (lane >= head_dim)
            x_own, g_own = jnp.where(own, x_block, x_rest), jnp.where(own, g_block, g_swap)
            strips, straddle = [], None
            for part, (top, cut) in enumerate(((0, middle), (middle, count))):
                gap = run_row[head : head + 1, top:] - run[top:cut, head : head + 1]
                fade = jnp.exp(jnp.minimum(gap, 0.0))
                weights = fade * scores[top:cut, top:]
                strips.append(low_dot(weights, g_block[top:], NN))
                inner = low_dot(x_own[top:cut], g_own[top:], NT)
                score_grads[part] = score_grads[part] + fade * inner
                sums = low_dot(weights * inner, upto[top:, top:], NN)
                sums = jnp.sum(sums * before[top:cut, top:], axis=0, keepdims=True)
                if part == 0:
                    straddle = sums
                else:
                    straddle = jnp.concatenate(
                        [straddle[:, :middle], straddle[:, middle:] + sums], axis=1
                    )
            straddles.append(straddle)
            halves.append(jnp.concatenate(strips, axis=0))
        results.append(jnp.where(lane < head_dim, halves[0], halves[1]))
    score_grad = jnp.concatenate(
        [
            score_grads[0],
            jnp.concatenate([jnp.zeros((count - middle, middle), jnp.float32), score_grads[1]], axis=1),
        ],
        axis=0,
    )
    score_grad = jnp.where(valid, score_grad, 0.0)
    later = map_dot(b, end) * tail
    values = jnp.concatenate(results, axis=1) + later
    inter = map_dot(c, start) * carry
    direct_ref[0] = head_sums(spread, x_wide * values)
    given = head_sums(spread, scaled_wide * later)
    taken = head_sums(spread, g_wide * inter)
    flows = jnp.concatenate([given, taken], axis=0)
    flow_pieces = [item.astype(jnp.bfloat16) for item in thirds_of(flows)]
    after = (rows < columns).astype(jnp.bfloat16)
    flow_later = sum(low_dot(item, after, NN) for item in flow_pieces)
    flow_sooner = sum(low_dot(item, upto, NN) for item in flow_pieces)
    decay_ref[0] = (
        jnp.concatenate(straddles, axis=0) + flow_later[:heads] + flow_sooner[heads:]
    )
    pair_high, pair_low = halves_of(start * end)
    pair_ref[0] = low_dot(spread, pair_high, NN) + low_dot(spread, pair_low, NN)
    grads_high, grads_low = halves_of(score_grad)
    grad_c = fine_dot(g_wide * carry, start) + low_dot(grads_high, b, TN) + low_dot(grads_low, b, TN)
    grad_b = fine_dot(scaled_wide * tail, end) + low_dot(grads_high, c, NN) + low_dot(grads_low, c, NN)

    @pl.when(pl.program_id(1) == 0)
    def _():
        grad_b_ref[0] = grad_b
        grad_c_ref[0] = grad_c

    @pl.when(pl.program_id(1) > 0)
    def _():
        grad_b_ref[0] = grad_b_ref[0] + grad_b
        grad_c_ref[0] = grad_c_ref[0] + grad_c

    weight, pre = weight_ref[...], pre_ref[0, 0]
    masks = same_segment(count, base_ref, starts_ref, weight.shape[0])
    total = conv_sum(ext, pre, halo_ref[0], weight, bias_ref[...], masks)
    sigma = sigmoid(total)
    grad_conv = (values * step + skip_ref[...] * g_wide) * (
        sigma * (1.0 + total * (1.0 - sigma))
    )
    moved[0:8, :] = jnp.zeros_like(moved[0:8, :])
    moved[8 + count :, :] = jnp.zeros_like(moved[8 + count :, :])
    sums = [jnp.sum(grad_conv * pre, axis=0, keepdims=True)]
    back = jnp.concatenate(
        [jnp.zeros((8, pre.shape[1]), jnp.float32), grad_conv * weight[0:1]], axis=0
    )
    for shift in range(1, weight.shape[0]):
        part = grad_conv * masks[shift - 1]
        sums.append(
            jnp.sum(part * ext[8 - shift : 8 - shift + count, :], axis=0, keepdims=True)
        )
        moved[8 : 8 + count, :] = part * weight[shift : shift + 1]
        back = back + moved[shift : shift + 8 + count, :]
    halo_out_ref[0] = back[:8]
    both_ref[0, 0] = back[8:].astype(jnp.bfloat16)
    edge_ref[0] = back[count:]
    sums.append(jnp.sum(grad_conv, axis=0, keepdims=True))
    sums.append(jnp.sum(g_wide * x_wide, axis=0, keepdims=True))
    sums.append(jnp.zeros((8 - len(sums), pre.shape[1]), jnp.float32))
    rows_ref[0] = jnp.concatenate(sums, axis=0)

    @pl.when(at_last)
    def _():
        for copy in sends():
            copy.wait()


def blocked(kernel, name, grid, ins, outs, scratch=(), micros=0, aliases=None, remote=None):
    moved = sum(item[0].size * item[0].dtype.itemsize for item in ins if item[1] != "any")
    moved += sum(
        math.prod(item[2]) * grid[0] * grid[1] * jnp.dtype(item[1]).itemsize
        for item in outs
        if item[2] != "any"
    )

    def spec(item):
        if item[1] is None:
            return pl.BlockSpec(memory_space=pltpu.SMEM)
        if item[1] == "any":
            return pl.BlockSpec(memory_space=pl.ANY)
        return pl.BlockSpec(item[1], item[2])

    return pl.pallas_call(
        kernel,
        grid=grid,
        in_specs=[spec(item) for item in ins],
        out_specs=[spec(item[1:]) for item in outs],
        out_shape=[jax.ShapeDtypeStruct(item[0], item[1]) for item in outs],
        scratch_shapes=list(scratch),
        input_output_aliases=aliases or {},
        compiler_params=pltpu.CompilerParams(
            dimension_semantics=("arbitrary",) * len(grid),
            vmem_limit_bytes=VMEM_LIMIT,
            collective_id=remote,
            has_side_effects=remote is not None,
        ),
        cost_estimate=pl.CostEstimate(
            flops=micros * 1_000_000_000, bytes_accessed=moved, transcendentals=0
        ),
        name=name,
    )(*[item[0] for item in ins])


def body(
    tokens,
    norm_gain,
    in_weight,
    bc_weight,
    dt_weight,
    dt_bias,
    a_log,
    conv_weight,
    conv_bias,
    bc_conv_weight,
    bc_conv_bias,
    d_skip,
    gate_gain,
    out_weight,
    cotangent,
    seq_lengths,
):
    micro, length, width = tokens.shape
    heads = dt_bias.shape[0]
    inner = conv_bias.shape[0]
    head_dim = inner // heads
    state_size = bc_weight.shape[1] // 2
    taps = conv_weight.shape[0]
    total = micro * length
    head_count = lax.axis_size("head")
    full_inner = inner * head_count
    group = min(HEAD_GROUP, heads)
    groups = heads // group
    wide = group * head_dim
    base = lax.axis_index("seq").astype(jnp.int32) * length
    labels = segment_ids(seq_lengths, base - (taps - 1), length + taps - 1, micro)
    own_labels = labels[:, taps - 1 :]
    before_labels = labels[:, taps - 2]
    starts = jnp.cumsum(seq_lengths, axis=-1).astype(jnp.int32) - seq_lengths
    long_starts = jnp.full((micro - starts.shape[0], starts.shape[1]), FAR, jnp.int32)
    starts = jnp.concatenate([starts, long_starts.at[:, 0].set(0)], axis=0)
    base_item, starts_item = (base[None], None), (starts, None)

    flat = tokens.reshape(total, width).astype(jnp.float32)
    cot_flat = cotangent.reshape(total, width)
    _, norm_back = jax.vjp(rms_scale, flat, norm_gain)
    normed_low, gate_x = project(tokens.reshape(total, width), norm_gain, in_weight)
    gate_x = gate_x.reshape(2, micro, length, inner)
    bc_pre = jnp.dot(normed_low, bc_weight, preferred_element_type=jnp.float32).reshape(
        micro, length, 2 * state_size
    )
    delta_pre = lax.dot_general(
        dt_weight, normed_low, (((0,), (1,)), ((), ())), preferred_element_type=jnp.float32
    )
    left = shifted(
        jnp.concatenate(
            [gate_x[1, :, length - taps + 1 :], bc_pre[:, length - taps + 1 :]], axis=-1
        ),
        "seq",
        1,
    )
    left_x, left_bc = left[..., :inner], left[..., inner:]
    halo = jnp.pad(left_x, ((0, 0), (9 - taps, 0), (0, 0)))
    conv_many = jax.vmap(conv_silu, in_axes=(0, None, None, 0))
    bc_act, bc_conv_back = jax.vjp(
        lambda extended, weight, bias: conv_many(extended, weight, bias, labels),
        jnp.concatenate([left_bc, bc_pre], axis=1),
        bc_conv_weight,
        bc_conv_bias,
    )
    bc_low = bc_act.astype(jnp.bfloat16)
    b_low, c_low = bc_low[..., :state_size], bc_low[..., state_size:]
    (delta, decay), rate_back = jax.vjp(step_sizes, delta_pre, dt_bias, a_log)

    def by_micro(array):
        return array.reshape(heads, micro, length).transpose(1, 0, 2)

    def by_head(array):
        return array.transpose(1, 0, 2).reshape(heads, total)

    delta, decay = by_micro(delta), by_micro(decay)
    order = jnp.arange(length)
    running = jnp.einsum(
        "mhj,ji->mhi",
        decay,
        (order[:, None] <= order[None, :]).astype(jnp.float32),
        precision=HIGHEST,
    )
    device_log = running[:, :, -1]
    live = (own_labels == before_labels[:, None]).astype(jnp.float32)
    last = (own_labels == own_labels[:, -1:]).astype(jnp.float32)
    carried = jnp.exp(running) * live[:, None]
    tail = jnp.exp(device_log[:, :, None] - running) * last[:, None]
    device_live = live[:, -1]
    gain_row, skip_row = gate_gain[None], jnp.repeat(d_skip, head_dim)[None]
    conv_row = conv_bias[None]

    grid = (micro, groups)
    token_block = (1, length, wide)
    in_token = lambda m, k: (m, 0, k)
    half_block = (1, 1, length, wide)
    in_gate, in_x = lambda m, k: (0, m, 0, k), lambda m, k: (1, m, 0, k)
    row_block, in_row = (1, group, length), lambda m, k: (m, k, 0)
    map_block, in_map = (1, length, state_size), lambda m, k: (m, 0, 0)
    state_block, in_state = (1, wide, state_size), lambda m, k: (m, k, 0)
    halo_block = (1, 8, wide)
    flat_block, in_flat = (1, wide), lambda m, k: (0, k)
    conv_item = (conv_weight, (taps, wide), in_flat)
    whole = (micro, length, inner)
    state_shape = (micro, inner, state_size)
    row_shape = (micro, heads, length)

    x_low, device_state = blocked(
        functools.partial(front_kernel, head_dim),
        "front",
        grid,
        [
            base_item,
            starts_item,
            (gate_x, half_block, in_x),
            (halo, halo_block, in_token),
            conv_item,
            (conv_row, flat_block, in_flat),
            (b_low, map_block, in_map),
            (tail * delta, row_block, in_row),
        ],
        [
            (whole, jnp.bfloat16, token_block, in_token),
            (state_shape, jnp.float32, state_block, in_state),
        ],
        [pltpu.VMEM((length + 8, wide), jnp.float32)],
        20,
    )
    exchange_log = jnp.where(device_live[:, None] > 0.0, device_log, DEAD)
    exchange_shape = (micro, heads, head_dim, state_size)
    parts = scatter_parts(inner, axis_bits("seq"))
    orders = tuple(order for order, _ in parts)
    tiled = (width >> axis_bits("seq")) % 128 == 0
    incoming, (grad_gate_n,), arranged = exchange(
        device_state.reshape(exchange_shape),
        exchange_log,
        False,
        (cot_flat, normed_low) if tiled else (),
        orders if tiled else (),
        [(plain_steps, (), (cot_flat, out_weight), (total, inner))],
    )
    grad_gate_n = grad_gate_n.reshape(whole)
    if not tiled:
        arranged = arrange(cot_flat, orders) + arrange(normed_low, orders)
    cot_parts, normed_parts = arranged[: 2 * len(parts)], arranged[2 * len(parts) :]
    incoming = incoming.reshape(state_shape)

    mixed, sums = blocked(
        functools.partial(mix_kernel, head_dim),
        "mix",
        grid,
        [
            base_item,
            starts_item,
            (x_low, token_block, in_token),
            (b_low, map_block, in_map),
            (c_low, map_block, in_map),
            (running, row_block, in_row),
            (delta, row_block, in_row),
            (carried, row_block, in_row),
            (incoming, state_block, in_state),
            (gate_x, half_block, in_gate),
            (grad_gate_n, token_block, in_token),
            (gain_row, flat_block, in_flat),
            (skip_row, flat_block, in_flat),
        ],
        [
            (whole, jnp.float32, token_block, in_token),
            ((micro, length, 2), jnp.float32, (1, length, 2), in_map),
        ],
        (),
        25,
    )
    sums = all_sum(sums, "head")
    normed_gate, grad_gate_pre, grad_gate_x, grad_mixed, device_grad, gate_rows = blocked(
        functools.partial(gate_kernel, head_dim, float(full_inner)),
        "gate",
        grid,
        [
            (mixed, token_block, in_token),
            (gate_x, half_block, in_gate),
            (grad_gate_n, token_block, in_token),
            (sums, (1, length, 2), in_map),
            (gain_row, flat_block, in_flat),
            (carried, row_block, in_row),
            (c_low, map_block, in_map),
        ],
        [
            (whole, jnp.bfloat16, token_block, in_token),
            (whole, jnp.bfloat16, token_block, in_token),
            ((2,) + whole, jnp.bfloat16, half_block, in_gate),
            (whole, jnp.bfloat16, token_block, in_token),
            (state_shape, jnp.float32, state_block, in_state),
            ((micro, 8, inner), jnp.float32, halo_block, in_token),
        ],
        (),
        20,
    )
    normed_gate = normed_gate.reshape(total, inner)
    grad_gate_pre = grad_gate_pre.reshape(total, inner)
    grad_gate_gain = jnp.sum(gate_rows[:, 0], axis=0)

    half_shape = (width // 2, inner)
    paired = head_count == 2
    share = width // head_count
    far = [k for k, (order, _) in enumerate(parts) if order[0] == 2 and len(parts) > 1]
    skipped = {(0, far[0])} if far else set()
    outgoing, (out_sent, gate_sent, *early), _ = exchange(
        device_grad.reshape(exchange_shape),
        exchange_log,
        True,
        jobs=[
            (product_steps, parts, cot_parts[::2] + [normed_gate], half_shape),
            (product_steps, parts, normed_parts[::2] + [grad_gate_pre], half_shape),
        ],
        tail=far[0] if far else None,
    )
    outgoing = outgoing.reshape(state_shape)
    (
        grad_gate_x,
        edge,
        halo_grad,
        conv_rows,
        direct,
        fading,
        pairs,
        grad_b,
        grad_c,
        *arrivals,
    ) = blocked(
        functools.partial(back_kernel, head_dim, parts, skipped),
        "back",
        grid,
        [
            base_item,
            starts_item,
            (x_low, token_block, in_token),
            (grad_mixed, token_block, in_token),
            (b_low, map_block, in_map),
            (c_low, map_block, in_map),
            (running, row_block, in_row),
            (delta, row_block, in_row),
            (carried, row_block, in_row),
            (tail, row_block, in_row),
            (incoming, state_block, in_state),
            (outgoing, state_block, in_state),
            (gate_x, half_block, in_x),
            (halo, halo_block, in_token),
            conv_item,
            (conv_row, flat_block, in_flat),
            (skip_row, flat_block, in_flat),
            (grad_gate_x, "any"),
            (out_sent, "any"),
            (gate_sent, "any"),
        ],
        [
            ((2,) + whole, jnp.bfloat16, half_block, in_x),
            ((micro, 8, inner), jnp.float32, halo_block, in_token),
            ((micro, 8, inner), jnp.float32, halo_block, in_token),
            ((micro, 8, inner), jnp.float32, halo_block, in_token),
            (row_shape, jnp.float32, row_block, in_row),
            (row_shape, jnp.float32, row_block, in_row),
            ((micro, heads, state_size), jnp.float32, (1, group, state_size), in_state),
            ((micro, length, state_size), jnp.float32, map_block, in_map),
            ((micro, length, state_size), jnp.float32, map_block, in_map),
        ]
        + [
            ((width // 2, sum(widths)), jnp.float32, "any")
            for mat in range(2)
            for k, (_, widths) in enumerate(parts)
            if (mat, k) not in skipped
        ],
        [
            pltpu.VMEM((length + 8, wide), jnp.float32),
            pltpu.VMEM((length + 16, wide), jnp.float32),
            pltpu.SemaphoreType.DMA((2 * len(parts),)),
            pltpu.SemaphoreType.DMA((2 * len(parts),)),
        ],
        80,
        {17: 0},
        3,
    )
    arrived = [
        [early[0] if (mat, k) in skipped else arrivals.pop(0) for k in range(len(parts))]
        for mat in range(2)
    ]
    grad_bc = all_sum(jnp.concatenate([grad_b, grad_c], axis=-1), "head")
    kept = jnp.sum(pairs, axis=-1) * jnp.exp(device_log) * device_live[:, None]
    grad_decay = by_head(fading + kept[:, :, None])
    grad_delta_pre, grad_dt_bias, grad_a_log = rate_back((by_head(direct), grad_decay))
    conv_rows = jnp.sum(conv_rows, axis=0)
    grad_conv_weight, grad_conv_bias = conv_rows[:taps], conv_rows[taps]
    grad_d_skip = jnp.sum(conv_rows[taps + 1].reshape(heads, head_dim), axis=-1)
    grad_bc_ext, grad_bc_conv_weight, grad_bc_conv_bias = bc_conv_back(grad_bc)
    right = shifted(
        jnp.concatenate([halo_grad[:, 9 - taps :], grad_bc_ext[:, : taps - 1]], axis=-1), "seq", -1
    )
    right_x, right_bc = right[..., :inner], right[..., inner:]
    grad_gate_x = lax.dynamic_update_slice(
        grad_gate_x,
        (edge[:, 9 - taps :] + right_x).astype(jnp.bfloat16)[None],
        (1, 0, length - taps + 1, 0),
    )
    grad_bc_pre = grad_bc_ext[:, taps - 1 :].at[:, length - taps + 1 :].add(right_bc)
    bc_flat = grad_bc_pre.reshape(total, 2 * state_size)
    grad_gate_x = grad_gate_x.reshape(2, total, inner)
    bc_high, bc_rest = halves_of(bc_flat * (1.0 / head_count))
    delta_high, delta_rest = halves_of(grad_delta_pre.T)
    narrow_left = jnp.concatenate([bc_high, bc_rest, delta_high, delta_rest], axis=1)
    narrow_right = jnp.concatenate([bc_weight, bc_weight, dt_weight, dt_weight], axis=1)
    if paired:
        row_inputs = (
            in_weight,
            norm_gain[None],
            tokens.reshape(total, width),
            cot_flat,
            narrow_left,
            narrow_right,
            normed_gate,
            out_weight,
        )
        gain_grad = jnp.zeros_like(norm_gain)
    else:
        row_inputs = ()
        row_part = lax.dot_general(
            narrow_left, narrow_right, (NT, ((), ())), preferred_element_type=jnp.float32
        ) + jnp.einsum(
            "ktc,dkc->td", grad_gate_x, in_weight, preferred_element_type=jnp.float32
        )
        grad_flat, gain_grad = norm_back(all_sum(row_part, "head"))
        grad_tokens = cot_flat.astype(jnp.float32) + grad_flat
        head_terms = lax.dot_general(
            normed_gate, out_weight, (NT, ((), ())), preferred_element_type=jnp.float32
        )
        summed = lax.psum_scatter(head_terms, "head", scatter_dimension=1, tiled=True)
        residual = lax.dynamic_slice_in_dim(flat, lax.axis_index("head") * share, share, 1)
        block_out = (residual + summed).astype(jnp.bfloat16)

    share_bc = 2 * state_size // head_count
    own_bc = lax.dynamic_slice_in_dim(bc_flat, lax.axis_index("head") * share_bc, share_bc, 1)
    across = share_bc + heads
    narrow_high, narrow_rest = halves_of(jnp.concatenate([own_bc, grad_delta_pre.T], axis=1))
    both = jnp.concatenate([narrow_high, narrow_rest], axis=1)
    narrow = jnp.concatenate(
        [product(normed_parts[1], both), product(normed_parts[0], both)], axis=0
    )
    narrow = narrow[:, :across] + narrow[:, across:]
    size = lax.axis_size("seq")
    row_count = width // size
    narrow = narrow.reshape(size, row_count, across)
    beside = 128 // heads
    narrow_bc = jnp.pad(narrow[:, :, :share_bc], ((0, 0), (0, 0), (0, -share_bc % 128)))
    narrow_steps = narrow[:, :, share_bc:].reshape(size, row_count // beside, 128)
    narrow_steps = jnp.pad(narrow_steps, ((0, 0), (0, 0), (0, narrow_bc.shape[2] - 128)))
    narrow = jnp.concatenate([narrow_bc, narrow_steps], axis=1)
    narrow_rows = narrow.shape[1]
    narrow = jnp.pad(narrow, ((0, 0), (0, -narrow_rows % 8), (0, 0)))
    narrow = narrow.reshape(-1, narrow.shape[2])

    small = [
        gain_grad,
        grad_bc_conv_weight,
        grad_bc_conv_bias,
        grad_dt_bias,
        grad_a_log,
        grad_d_skip,
        grad_conv_weight,
        grad_conv_bias,
        grad_gate_gain,
    ]
    row = jnp.concatenate([item.reshape(-1) for item in small])
    count = row.size
    row = jnp.pad(row, (0, -count % 1024)).reshape(-1, 128)

    (grad_out_weight, gate_block, x_block), gathered, row, *token_grads = finish(
        parts,
        [
            cot_parts[1::2] + [normed_gate] + arrived[0],
            normed_parts[1::2] + [grad_gate_pre] + arrived[1],
        ],
        normed_parts[::2],
        normed_parts[1::2],
        grad_gate_x,
        narrow,
        row,
        row_inputs,
    )
    if paired:
        grad_tokens, block_out = token_grads
    grad_tokens = grad_tokens.reshape(micro, length, width)
    block_out = block_out.reshape(micro, length, share)
    grad_in_weight = jnp.stack([gate_block, x_block], axis=1)
    grad_bc_weight = head_gather(gathered[:, :row_count, :share_bc].reshape(width, share_bc))
    grad_dt_weight = gathered[:, row_count:narrow_rows, :128].reshape(width, heads)
    row = row.reshape(-1)
    sizes, first = [], 0
    for item in small:
        sizes.append(row[first : first + item.size].reshape(item.shape))
        first += item.size
    (
        grad_norm_gain,
        grad_bc_conv_weight,
        grad_bc_conv_bias,
        grad_dt_bias,
        grad_a_log,
        grad_d_skip,
        grad_conv_weight,
        grad_conv_bias,
        grad_gate_gain,
    ) = sizes

    return (
        block_out,
        grad_tokens,
        grad_norm_gain,
        grad_in_weight,
        grad_bc_weight,
        grad_dt_weight,
        grad_dt_bias,
        grad_a_log,
        grad_d_skip,
        grad_conv_weight,
        grad_conv_bias,
        grad_bc_conv_weight,
        grad_bc_conv_bias,
        grad_gate_gain,
        grad_out_weight,
    )


def solution(mesh):
    return jax.shard_map(
        body,
        mesh=mesh,
        in_specs=(
            P(None, "seq", None),
            P(),
            P(None, None, "head"),
            P(),
            P(None, "head"),
            P("head"),
            P("head"),
            P(None, "head"),
            P("head"),
            P(),
            P(),
            P("head"),
            P("head"),
            P(None, "head"),
            P(None, "seq", None),
            P(),
        ),
        out_specs=(
            P(None, "seq", "head"),
            P(None, "seq", None),
            P(),
            P("seq", None, "head"),
            P(),
            P(None, "head"),
            P("head"),
            P("head"),
            P("head"),
            P(None, "head"),
            P("head"),
            P(),
            P(),
            P("head"),
            P("seq", "head"),
        ),
        check_vma=False,
    )
```

```python
import functools
import math

import jax
import jax.numpy as jnp
from jax import lax
from jax.experimental import pallas as pl
from jax.experimental.pallas import tpu as pltpu
from jax.sharding import PartitionSpec as P

EPSILON = 1e-05
HIGHEST = lax.Precision.HIGHEST


def shifted(shard, axis, by):
    length = lax.axis_size(axis)
    pairs = [(i, i + by) for i in range(length) if 0 <= i + by < length]
    return lax.ppermute(shard, axis, pairs)


def segment_ids(seq_lengths, first, count, micro):
    places = first + jnp.arange(count, dtype=jnp.int32)
    starts = jnp.cumsum(seq_lengths, axis=-1) - seq_lengths
    short_ids = (
        jnp.sum((starts[:, None, :] <= places[None, :, None]).astype(jnp.int32), axis=-1) - 1
    )
    long_ids = jnp.zeros((micro - seq_lengths.shape[0], count), jnp.int32)
    labels = jnp.concatenate([short_ids, long_ids], axis=0)
    return jnp.where(places[None, :] >= 0, labels, -1)


def rms_scale(values, gain):
    return values * lax.rsqrt(jnp.mean(values * values, axis=-1, keepdims=True) + EPSILON) * gain


def conv_silu(extended, weight, bias, labels):
    taps = weight.shape[0]
    count = extended.shape[0] - taps + 1
    own = labels[taps - 1 :]
    total = bias + weight[0] * extended[taps - 1 :]
    for shift in range(1, taps):
        first = taps - 1 - shift
        mask = (labels[first : first + count] == own).astype(extended.dtype)
        total = total + weight[shift] * extended[first : first + count] * mask[:, None]
    return jax.nn.silu(total)


def step_sizes(delta_pre, dt_bias, a_log):
    delta = jax.nn.softplus(delta_pre + dt_bias[:, None])
    return (delta, -jnp.exp(a_log)[:, None] * delta)


DEAD = -1e30
EXCHANGE_COST = 100_000_000_000
FINISH_LIMIT = 60 * 1024 * 1024
GROUP = 4


def exchange_kernel(length, reverse, orders, jobs, part_ref, log_ref, *refs):
    refs = list(refs)
    sources = [refs.pop(0) for _ in range(2 if orders else 0)]
    job_refs = [[refs.pop(0) for _ in range(job[2])] for job in jobs]
    out_ref = refs.pop(0)
    steps = []
    for (make, plan, _), inputs in zip(jobs, job_refs):
        steps += make(inputs, refs.pop(0), plan)
    targets = [refs.pop(0) for _ in range(4 * len(orders))]
    (
        parts,
        logs,
        edge_in,
        edge_out,
        given,
        part_send,
        part_recv,
        log_send,
        log_recv,
        edge_send,
        edge_recv,
        given_send,
        given_recv,
        stage_sem,
        place_sem,
        staged,
    ) = refs
    me = lax.axis_index("seq")
    bits = (length - 1).bit_length()
    placed = arrange_copies(bits, orders, me, staged, targets, place_sem)
    stages = [
        pltpu.make_async_copy(source, staged.at[k], stage_sem.at[k])
        for k, source in enumerate(sources)
    ]
    for copy in stages:
        copy.start()
    rank = lax.rem(me, GROUP)
    plane = me // GROUP
    first = me - rank
    mates = (
        rank + 1 - 2 * lax.rem(rank, 2),
        rank + 2 - 4 * (rank // 2),
        3 - rank,
    )
    micro = part_ref.shape[0]
    planes = length // GROUP
    begins, ends = plane == 0, plane == planes - 1
    if reverse:
        begins, ends = ends, begins
    onward = -GROUP if reverse else GROUP

    barrier = pltpu.get_barrier_semaphore()
    for mate in mates:
        pl.semaphore_signal(
            barrier, inc=1, device_id={"seq": first + mate}, device_id_type=pl.DeviceIdType.MESH
        )

    @pl.when(plane > 0)
    def _():
        pl.semaphore_signal(
            barrier, inc=1, device_id={"seq": me - GROUP}, device_id_type=pl.DeviceIdType.MESH
        )

    @pl.when(plane < planes - 1)
    def _():
        pl.semaphore_signal(
            barrier, inc=1, device_id={"seq": me + GROUP}, device_id_type=pl.DeviceIdType.MESH
        )

    above = jnp.where(plane < planes - 1, 1, 0)
    below = jnp.where(plane > 0, 1, 0)
    pl.semaphore_wait(barrier, 3 + above + below)

    def remote(src, dst, send, recv, target):
        return pltpu.make_async_remote_copy(
            src_ref=src,
            dst_ref=dst,
            send_sem=send,
            recv_sem=recv,
            device_id={"seq": target},
            device_id_type=pl.DeviceIdType.MESH,
        )

    def log_copy(slot):
        mate = mates[slot]
        return remote(
            log_ref.at[mate], logs.at[rank], log_send.at[slot], log_recv.at[slot], first + mate
        )

    quarter = edge_in.shape[2]

    def own_columns(place):
        return pl.ds(pl.multiple_of(place * quarter, quarter), quarter)

    def part_copy(m, slot):
        mate = mates[slot]
        return remote(
            part_ref.at[m, :, own_columns(mate)],
            parts.at[m, rank],
            part_send.at[m, slot],
            part_recv.at[m, slot],
            first + mate,
        )

    def edge_copy(m):
        return remote(edge_out.at[m], edge_in.at[m], edge_send.at[m], edge_recv.at[m], me + onward)

    def given_copy(m, slot):
        mate = mates[slot]
        return remote(
            given.at[m, mate],
            out_ref.at[m, :, own_columns(rank)],
            given_send.at[m, slot],
            given_recv.at[m, slot],
            first + mate,
        )

    for slot in range(3):
        log_copy(slot).start()
    for m in range(micro):
        for slot in range(3):
            part_copy(m, slot).start()
    logs[rank] = log_ref[rank]
    for m in range(micro):
        parts[m, rank] = part_ref[m, :, own_columns(rank)]

    @pl.when(begins)
    def _():
        edge_in[...] = jnp.zeros_like(edge_in)

    for copy in stages:
        copy.wait()
    for copy in placed:
        copy.start()
    for slot in range(3):
        log_copy(slot).wait()
    order = tuple(reversed(range(GROUP))) if reverse else tuple(range(GROUP))
    for m in range(micro):
        for step in steps[m * len(steps) // micro : (m + 1) * len(steps) // micro]:
            step()
        for slot in range(3):
            part_copy(m, slot).wait()
        factors = [jnp.exp(logs[t, m : m + 1, :]) for t in order]
        whole = jnp.exp(sum(logs[t, m : m + 1, :] for t in order))
        total = parts[m, order[0]]
        for t, factor in zip(order[1:], factors[1:]):
            total = total * factor + parts[m, t]

        @pl.when(jnp.logical_not(begins))
        def _():
            edge_copy(m).wait_recv()

        @pl.when(jnp.logical_not(ends))
        def _():
            edge_out[m] = total + whole * edge_in[m]
            edge_copy(m).start()

        running = edge_in[m]
        for place, (t, factor) in enumerate(zip(order, factors)):
            given[m, t] = running
            if place < GROUP - 1:
                running = running * factor + parts[m, t]
        for slot in range(3):
            given_copy(m, slot).start()
        out_ref[m, :, own_columns(rank)] = given[m, rank]
    for m in range(micro):
        for slot in range(3):
            given_copy(m, slot).wait()

        @pl.when(jnp.logical_not(ends))
        def _():
            edge_copy(m).wait_send()

    for copy in placed:
        copy.wait()


def exchange(parts, logs, reverse, sources=(), orders=(), jobs=()):
    micro, rows, columns = parts.shape
    quarter = columns // GROUP
    length = lax.axis_size("seq")
    spread = logs.reshape(micro, GROUP, quarter).transpose(1, 0, 2)
    shape = (micro, GROUP, rows, quarter)
    arranged = []
    for source in sources:
        half = jax.ShapeDtypeStruct((source.shape[0], source.shape[1] // 2), source.dtype)
        arranged += [half] * (2 * len(orders))
    vmem = pl.BlockSpec(memory_space=pltpu.VMEM)
    hbm = pl.BlockSpec(memory_space=pl.ANY)
    made = [jax.ShapeDtypeStruct(job[3], jnp.float32) for job in jobs]
    results = len(made)
    count = len(arranged)
    arranged = made + arranged
    job_inputs = [item for job in jobs for item in job[2]]
    plans = tuple((job[0], job[1], len(job[2])) for job in jobs)
    smem = pl.BlockSpec(memory_space=pltpu.SMEM)
    job_specs = [smem if item.dtype == jnp.int32 else hbm for item in job_inputs]
    out, *arranged = pl.pallas_call(
        functools.partial(exchange_kernel, length, reverse, orders, plans),
        out_shape=[jax.ShapeDtypeStruct(parts.shape, jnp.float32)] + arranged,
        in_specs=[vmem] * 2 + [hbm] * len(sources) + job_specs,
        out_specs=[vmem] + [hbm] * len(arranged),
        scratch_shapes=[
            pltpu.VMEM(shape, jnp.float32),
            pltpu.VMEM((GROUP, micro, quarter), jnp.float32),
            pltpu.VMEM((micro, rows, quarter), jnp.float32),
            pltpu.VMEM((micro, rows, quarter), jnp.float32),
            pltpu.VMEM(shape, jnp.float32),
            pltpu.SemaphoreType.DMA((micro, 3)),
            pltpu.SemaphoreType.DMA((micro, 3)),
            pltpu.SemaphoreType.DMA((3,)),
            pltpu.SemaphoreType.DMA((3,)),
            pltpu.SemaphoreType.DMA((micro,)),
            pltpu.SemaphoreType.DMA((micro,)),
            pltpu.SemaphoreType.DMA((micro, 3)),
            pltpu.SemaphoreType.DMA((micro, 3)),
            pltpu.SemaphoreType.DMA((2,)),
            pltpu.SemaphoreType.DMA((max(count, 1) * max(length // 2, 1),)),
            pltpu.VMEM((2,) + sources[0].shape if sources else (2, 16, 128), jnp.bfloat16),
        ],
        compiler_params=pltpu.CompilerParams(
            collective_id=1 if reverse else 0,
            has_side_effects=True,
            vmem_limit_bytes=FINISH_LIMIT,
        ),
        cost_estimate=pl.CostEstimate(
            flops=EXCHANGE_COST, bytes_accessed=0, transcendentals=0
        ),
        name="exchange_back" if reverse else "exchange",
    )(parts, spread, *sources, *job_inputs)
    return out, arranged[:results], arranged[results:]


def xor_permute(value, axis, bit):
    size = lax.axis_size(axis)
    return lax.ppermute(value, axis, [(i, i ^ (1 << bit)) for i in range(size)])


def axis_bits(axis):
    return (lax.axis_size(axis) - 1).bit_length()


def own_bit(axis, bit):
    return lax.rem(lax.axis_index(axis) // (1 << bit), 2)


def all_sum(value, axis):
    for bit in range(axis_bits(axis)):
        value = value + xor_permute(value, axis, bit)
    return value


def scatter_plans(columns, bits):
    if bits < 3 or columns % 2048:
        return [[(tuple(range(bits)), (columns,))]] * 3
    rest = tuple(range(3, bits))
    unit = columns // 16
    orders = ((0, 1, 2), (1, 0, 2), (2, 0, 1), (2, 1, 0))
    shares = (
        ((3, 3), (2, 3), (3, 0), (0, 2)),
        ((3, 2), (3, 3), (3, 0), (0, 2)),
        ((3, 2), (2, 3), (3, 0), (0, 3)),
    )
    return [
        [
            (order + rest, tuple(unit * count for count in counts))
            for order, counts in zip(orders, share)
        ]
        for share in shares
    ]


def arranged_place(order, position, bits):
    return [(position >> (bits - 1 - t)) & 1 for t, _ in sorted(enumerate(order), key=lambda p: p[1])]


def arranged_block(order, position, bits, me):
    flips = arranged_place(order, position, bits)
    total = 0
    for bit, flip in enumerate(flips):
        mine = lax.rem(me // (1 << bit), 2)
        total = total + (1 << bit) * ((1 - mine) if flip else mine)
    return total


def arrange(left, orders):
    bits = axis_bits("seq")
    size = 1 << bits
    tokens, width = left.shape
    view = left.reshape(tokens, size, width // size)
    me = lax.axis_index("seq").astype(jnp.int32)
    results = []
    for order in orders:
        table = jnp.stack([arranged_block(order, j, bits, me) for j in range(size)])
        chosen = jnp.take(view, table, axis=1).reshape(tokens, width)
        results += [chosen[:, width // 2 :], chosen[:, : width // 2]]
    return results


def arrange_copies(bits, orders, me, staged, targets, sem):
    copies, number = [], 0
    half = 1 << (bits - 1)
    for source in range(len(targets) // (2 * len(orders)) if orders else 0):
        block = staged.shape[2] >> bits
        for order in orders:
            for begin in (half, 0):
                target = targets[number]
                for j in range(half):
                    place = arranged_block(order, begin + j, bits, me)
                    first = pl.multiple_of(place * block, block)
                    copies.append(
                        pltpu.make_async_copy(
                            staged.at[source, :, pl.ds(first, block)],
                            target.at[:, pl.ds(j * block, block)],
                            sem.at[number * half + j],
                        )
                    )
                number += 1
    return copies


def product(left, right):
    return lax.dot_general(left, right, (TN, ((), ())), preferred_element_type=jnp.float32)


def part_columns(parts):
    first, columns = 0, []
    for _, widths in parts:
        columns.append(pl.ds(first, sum(widths)))
        first += sum(widths)
    return columns


def product_steps(inputs, out_ref, parts):
    count = len(parts)
    lefts, right_ref, more = inputs[:count], inputs[count], inputs[count + 1 :]
    return [
        functools.partial(
            product_step, lefts[k], right_ref, more[k : k + 1], out_ref, columns.start, columns.size
        )
        for k, columns in enumerate(part_columns(parts))
    ]


def product_step(left_ref, right_ref, more, out_ref, first, width):
    tokens, rows = left_ref.shape
    tile = min(rows, 256)
    columns = pl.ds(first, width)

    def body(left, right, *rest):
        value = product(left[...], right[...])
        for item in rest[:-1]:
            value = value + item[...]
        rest[-1][...] = value

    tiled = pl.BlockSpec((tile, width), lambda i: (i, 0))
    pltpu.emit_pipeline(
        body,
        grid=(rows // tile,),
        in_specs=[
            pl.BlockSpec((tokens, tile), lambda i: (0, i)),
            pl.BlockSpec((tokens, width), lambda i: (0, 0)),
        ]
        + [tiled] * len(more),
        out_specs=[tiled],
    )(
        left_ref,
        right_ref.at[:, columns],
        *more,
        out_ref.at[:, columns],
    )


def plain_steps(inputs, out_ref, parts):
    left_ref, right_ref = inputs
    width = min(right_ref.shape[1], 512)
    return [
        functools.partial(plain_step, left_ref, right_ref, out_ref, first, width)
        for first in range(0, right_ref.shape[1], width)
    ]


def plain_step(left_ref, right_ref, out_ref, first, width):
    rows, depth = left_ref.shape
    tile = min(rows, 256)
    columns = pl.ds(first, width)

    def body(left, right, out):
        out[...] = low_dot(left[...], right[...], NN)

    pltpu.emit_pipeline(
        body,
        grid=(rows // tile,),
        in_specs=[
            pl.BlockSpec((tile, depth), lambda i: (i, 0)),
            pl.BlockSpec((depth, width), lambda i: (0, 0)),
        ],
        out_specs=[pl.BlockSpec((tile, width), lambda i: (i, 0))],
    )(left_ref, right_ref.at[:, columns], out_ref.at[:, columns])


def share_steps(inputs, out_refs, parts):
    left_ref, right_ref = inputs
    share = right_ref.shape[0] // 2
    mine = lax.axis_index("head") * share
    return [
        functools.partial(share_step, left_ref, right_ref, out_ref, first, share)
        for out_ref, first in zip(out_refs, (share - mine, mine))
    ]


def share_step(left_ref, right_ref, out_ref, first, share):
    rows, depth = left_ref.shape
    tile = min(rows, 256)
    width = min(share, 512)
    chosen = right_ref.at[pl.ds(pl.multiple_of(first, share), share)]

    def body(left, right, out):
        out[...] = low_dot(left[...], right[...], NT)

    pltpu.emit_pipeline(
        body,
        grid=(share // width, rows // tile),
        in_specs=[
            pl.BlockSpec((tile, depth), lambda j, i: (i, 0)),
            pl.BlockSpec((width, depth), lambda j, i: (j, 0)),
        ],
        out_specs=[pl.BlockSpec((tile, width), lambda j, i: (i, j))],
    )(left_ref, chosen, out_ref)


def row_step(grad_ref, weight_ref, narrow_ref, map_ref, step_ref, out_ref, first, rows):
    depth, halves, width = weight_ref.shape
    tile = min(depth, 256)

    def inner(held, sem):
        copy = pltpu.make_async_copy(grad_ref.at[:, pl.ds(first, rows)], held, sem)
        copy.start()
        copy.wait()

        def body(weight, narrow, map_weight, step_weight, out):
            turned_weight = jnp.swapaxes(weight[...], 0, 1)
            maps = map_weight.shape[1]
            high, rest = halves_of(narrow[...])
            total = low_dot(high[:, :maps], map_weight[...], NT) + low_dot(
                rest[:, :maps], map_weight[...], NT
            )
            total = total + low_dot(high[:, maps:], step_weight[...], NT)
            total = total + low_dot(rest[:, maps:], step_weight[...], NT)
            for half in range(halves):
                total = total + low_dot(held[half], turned_weight[half], NT)
            out[...] = total

        pltpu.emit_pipeline(
            body,
            grid=(depth // tile,),
            in_specs=[
                pl.BlockSpec((tile, halves, width), lambda j: (j, 0, 0)),
                pl.BlockSpec((rows, narrow_ref.shape[1]), lambda j: (0, 0)),
                pl.BlockSpec((tile, map_ref.shape[1]), lambda j: (j, 0)),
                pl.BlockSpec((tile, step_ref.shape[1]), lambda j: (j, 0)),
            ],
            out_specs=[pl.BlockSpec((rows, tile), lambda j: (0, j))],
        )(
            weight_ref,
            narrow_ref.at[pl.ds(first, rows)],
            map_ref,
            step_ref,
            out_ref.at[pl.ds(first, rows)],
        )

    pl.run_scoped(
        inner,
        pltpu.VMEM((halves, rows, width), jnp.bfloat16),
        pltpu.SemaphoreType.DMA,
    )


def token_step(
    gain_ref, gain_sum, tokens_ref, cot_ref, rows_refs, kept_ref, other_ref, grad_ref, block_ref
):
    count, width = tokens_ref.shape
    share = width // 2
    tile = min(count, 128)
    mine = lax.axis_index("head") == 0
    gain_sum[...] = jnp.zeros_like(gain_sum)

    def body(tokens, cot, own, other, kept, arrived, grad, block):
        values = tokens[...].astype(jnp.float32)
        pulls = own[...] + other[...]
        scale = lax.rsqrt(jnp.mean(values * values, axis=1, keepdims=True) + EPSILON)
        gained = pulls * gain_ref[...]
        cross = jnp.sum(gained * values, axis=1, keepdims=True)
        grad[...] = (
            cot[...].astype(jnp.float32)
            + gained * scale
            - values * (scale * scale * scale * cross * (1.0 / width))
        )
        parts = (pulls * values * scale).reshape(tile // 8, 8, width)
        gain_sum[...] = gain_sum[...] + jnp.sum(parts, axis=0)
        residual = jnp.where(mine, values[:, :share], values[:, share:])
        block[...] = (residual + kept[...] + arrived[...]).astype(jnp.bfloat16)

    full = pl.BlockSpec((tile, width), lambda i: (i, 0))
    half = pl.BlockSpec((tile, share), lambda i: (i, 0))
    pltpu.emit_pipeline(
        body,
        grid=(count // tile,),
        in_specs=[full] * 4 + [half] * 2,
        out_specs=[full, half],
    )(tokens_ref, cot_ref, *rows_refs, kept_ref, other_ref, grad_ref, block_ref)


def finish_kernel(plans, paired, bits, blocks, *refs):
    refs = list(refs)
    mats, parts = len(plans), plans[-1]
    take = lambda count: [refs.pop(0) for _ in range(count)]
    ins = [take(2 * len(parts) + 1) for _ in range(mats - 1)]
    last_sent, last_kept = take(len(parts)), take(len(parts))
    grad_ref, narrow_ref, vector_ref = take(3)
    if paired:
        weight_ref, gain_ref, tokens_ref, cot_ref = take(4)
        narrow_row_ref, map_ref, step_ref, gated_ref, out_weight_ref = take(5)
    outs = take(mats)
    gathered_ref, vector_out_ref = take(2)
    if paired:
        token_grad_ref, block_ref, row_ref, row_other_ref = take(4)
        share_sent_ref, share_kept_ref, share_other_ref = take(3)
    sent_ref, arrived_ref = take(2)
    made_refs = take(mats)
    me = lax.axis_index("seq")
    last_right = grad_ref.at[grad_ref.shape[0] - 1]
    columns_of = part_columns(parts)
    ins.append(last_kept + [last_right] + [arrived_ref.at[:, columns] for columns in columns_of])

    def partner(bit):
        return me + (1 << bit) * (1 - 2 * lax.rem(me // (1 << bit), 2))

    waves = []
    piece_count = len(parts[0][1])
    chain_count = 0
    for mat in range(mats):
        for piece in range(piece_count):
            wave, first = [], 0
            for order, widths in plans[mat]:
                if widths[piece]:
                    place = first + sum(widths[:piece])
                    keep = refs.pop(0)
                    recvs = take(bits - 1)
                    wave.append(
                        (chain_count, made_refs[mat], place, outs[mat], place, order[1:], keep, recvs)
                    )
                    chain_count += 1
                first += sum(widths)
            waves.append(wave)
    narrow_order = parts[min(1, len(parts) - 1)][0]
    narrow = (chain_count, narrow_ref, 0, None, 0, narrow_order, refs.pop(0), take(bits))
    vector_sums, vector_recvs, gain_sum, local_sem, send_sem, recv_sem = refs

    barrier = pltpu.get_barrier_semaphore()
    for bit in range(bits):
        pl.semaphore_signal(
            barrier,
            inc=1,
            device_id={"seq": partner(bit)},
            device_id_type=pl.DeviceIdType.MESH,
        )
    if paired:
        pl.semaphore_signal(
            barrier,
            inc=1,
            device_id={"head": 1 - lax.axis_index("head")},
            device_id_type=pl.DeviceIdType.MESH,
        )
    pl.semaphore_wait(barrier, bits + (1 if paired else 0))

    numbers = {}

    def remote_to(key, src, dst, target):
        number = numbers.setdefault(key, len(numbers))
        return pltpu.make_async_remote_copy(
            src_ref=src,
            dst_ref=dst,
            send_sem=send_sem.at[number],
            recv_sem=recv_sem.at[number],
            device_id=target,
            device_id_type=pl.DeviceIdType.MESH,
        )

    def remote(key, src, dst, bit):
        return remote_to(key, src, dst, {"seq": partner(bit)})

    def first_copy(k):
        region = (slice(None), columns_of[k])
        return remote(("first", k), sent_ref.at[region], arrived_ref.at[region], parts[k][0][0])

    def share_copy():
        return remote_to(
            "share", share_sent_ref, share_other_ref, {"head": 1 - lax.axis_index("head")}
        )

    def shares(part):
        share_steps(
            (gated_ref, out_weight_ref), (share_sent_ref, share_kept_ref), ()
        )[part]()
        if part == 0:
            share_copy().start()

    def row_copy():
        return remote_to("row", row_ref, row_other_ref, {"head": 1 - lax.axis_index("head")})

    def local_copy(chain):
        number, source, first, _, _, _, keep, _ = chain
        rows, columns = keep.shape
        return pltpu.make_async_copy(
            source.at[pl.ds(0, rows), pl.ds(first, columns)], keep, local_sem.at[number]
        )

    def chain_copy(chain, phase):
        number, source, first, _, _, order, keep, recvs = chain
        rows, columns = recvs[phase].shape
        if phase == 0:
            region = source.at[pl.ds(rows, rows), pl.ds(first, columns)]
        else:
            region = keep.at[pl.ds(rows, rows)]
        return remote((number, phase), region, recvs[phase], order[phase])

    made = set()

    def make(mat):
        if mat in made:
            return
        made.add(mat)
        if mat == mats - 1:
            for k in range(len(parts)):
                first_copy(k).wait_recv()
        for step in product_steps(ins[mat], made_refs[mat], plans[mat]):
            step()

    def begin(number):
        make(number // piece_count)
        for chain in waves[number]:
            chain_copy(chain, 0).start()
            local_copy(chain).start()

    def advance(chain, phase):
        if phase == 0:
            local_copy(chain).wait()
        chain_copy(chain, phase).wait_recv()
        number, _, _, out, place, order, keep, recvs = chain
        recv = recvs[phase]
        rows = recv.shape[0]
        slab = min(rows, 32)

        @pl.loop(0, rows // slab)
        def _(step):
            cut = pl.ds(pl.multiple_of(step * slab, slab), slab)
            keep[cut, :] = keep[cut, :] + recv[cut, :]

        if phase + 1 < len(order):
            chain_copy(chain, phase + 1).start()
        elif out is not None:
            out[:, place : place + keep.shape[1]] = keep[0:blocks, :]

    def vector_copy(phase):
        return remote(("vector", phase), vector_sums.at[phase], vector_recvs.at[phase], phase)

    def begin_vector():
        vector_sums[0] = vector_ref[...]
        if paired:
            total = jnp.sum(gain_sum[...], axis=0, keepdims=True)
            for place in range(total.shape[1] // 128):
                vector_sums[0, place : place + 1, :] = total[:, place * 128 : place * 128 + 128]
        vector_copy(0).start()

    def advance_vector(phase):
        vector_copy(phase).wait_recv()
        total = vector_sums[phase] + vector_recvs[phase]
        if phase + 1 < bits:
            vector_sums[phase + 1] = total
            vector_copy(phase + 1).start()
        else:
            vector_out_ref[...] = total

    gather_bits = tuple(range(bits - 1, 1, -1)) + tuple(range(min(bits, 2)))

    def gather_copies(phase):
        free = gather_bits[:phase]
        fixed = sum(
            (1 << bit) * lax.rem(me // (1 << bit), 2) for bit in range(bits) if bit not in free
        )
        copies = []
        for number in range(1 << phase):
            block = fixed + sum(
                (1 << bit) * ((number >> place) & 1) for place, bit in enumerate(free)
            )
            region = gathered_ref.at[block]
            copies.append(remote(("gather", phase, number), region, region, gather_bits[phase]))
        return copies

    def narrow_halving(phase):
        advance(narrow, phase)
        if phase + 1 == bits:
            gathered_ref[me] = narrow[6][0 : gathered_ref.shape[1], :]
            for copy in gather_copies(0):
                copy.start()

    def narrow_gather(phase):
        for copy in gather_copies(phase):
            copy.wait_recv()
        if phase + 1 < bits:
            for copy in gather_copies(phase + 1):
                copy.start()

    def rows(part):
        count = row_ref.shape[0] // 2
        row_step(
            grad_ref,
            weight_ref,
            narrow_row_ref,
            map_ref,
            step_ref,
            row_ref,
            part * count,
            count,
        )
        if part == 1:
            row_copy().start()

    def token_rows():
        row_copy().wait()
        share_copy().wait()
        token_step(
            gain_ref,
            gain_sum,
            tokens_ref,
            cot_ref,
            (row_ref, row_other_ref),
            share_kept_ref,
            share_other_ref,
            token_grad_ref,
            block_ref,
        )

    narrow_steps = [functools.partial(narrow_halving, phase) for phase in range(bits)]
    narrow_steps += [functools.partial(narrow_gather, phase) for phase in range(bits)]
    fills = {}
    vector_tick = 0
    if paired:
        fills = {
            0: [functools.partial(rows, 0)],
            1: [functools.partial(rows, 1), functools.partial(shares, 0)],
            2: [functools.partial(shares, 1)],
            3: [token_rows],
        }
        vector_tick = 4

    chain_copy(narrow, 0).start()
    local_copy(narrow).start()
    sent_steps = product_steps(last_sent + [last_right], sent_ref, parts)
    for k, step in enumerate(sent_steps):
        step()
        first_copy(k).start()
    begun = min(2, len(waves))
    for number in range(begun):
        begin(number)
    if len(waves) > begun:
        make(begun // piece_count)
    ticks = max(len(waves) + bits - 2, 2 * bits, vector_tick + bits)
    for tick in range(ticks):
        if tick < len(narrow_steps):
            narrow_steps[tick]()
        for phase in range(bits - 1):
            number = tick - phase
            if 0 <= number < len(waves):
                for chain in waves[number]:
                    advance(chain, phase)
                if phase == 0 and number + 2 < len(waves):
                    begin(number + 2)
        if tick + 3 < len(waves):
            make((tick + 3) // piece_count)
        for step in fills.get(tick, ()):
            step()
        if tick == vector_tick:
            begin_vector()
        if 0 <= tick - vector_tick < bits:
            advance_vector(tick - vector_tick)
    for k in range(len(parts)):
        first_copy(k).wait_send()
    for wave in waves:
        for chain in wave:
            for phase in range(bits - 1):
                chain_copy(chain, phase).wait_send()
    for phase in range(bits):
        chain_copy(narrow, phase).wait_send()
        vector_copy(phase).wait_send()
        for copy in gather_copies(phase):
            copy.wait_send()


def finish(plans, mats, last_sent, last_kept, grad, narrow, vector, row_inputs):
    bits = axis_bits("seq")
    size = 1 << bits
    count, parts = len(plans), plans[-1]
    paired = bool(row_inputs)
    rows = last_kept[0].shape[1]
    blocks = rows // (size // 2)
    columns = sum(sum(widths) for _, widths in parts)
    scratch, copies, chains = [], 0, 0
    for plan in plans:
        for piece in range(len(parts[0][1])):
            for _, widths in plan:
                if widths[piece]:
                    scratch.append(pltpu.VMEM((rows // 2, widths[piece]), jnp.float32))
                    for phase in range(bits - 1):
                        scratch.append(
                            pltpu.VMEM(((rows // 2) >> phase, widths[piece]), jnp.float32)
                        )
                    copies += bits - 1
                    chains += 1
    narrow_rows = narrow.shape[0] // 2
    scratch.append(pltpu.VMEM((narrow_rows, narrow.shape[1]), jnp.float32))
    for phase in range(bits):
        scratch.append(pltpu.VMEM((narrow_rows >> phase, narrow.shape[1]), jnp.float32))
    copies += 2 * bits + size - 1 + len(parts) + 2
    scratch += [pltpu.VMEM((bits,) + vector.shape, jnp.float32)] * 2
    scratch += [
        pltpu.VMEM((8, row_inputs[1].shape[1] if paired else 128), jnp.float32),
        pltpu.SemaphoreType.DMA((chains + 1,)),
        pltpu.SemaphoreType.DMA((copies,)),
        pltpu.SemaphoreType.DMA((copies,)),
    ]
    vmem, hbm = pl.BlockSpec(memory_space=pltpu.VMEM), pl.BlockSpec(memory_space=pl.ANY)
    shapes = [jax.ShapeDtypeStruct((blocks, columns), jnp.float32) for _ in range(count)]
    shapes.append(
        jax.ShapeDtypeStruct((size, narrow.shape[0] // size, narrow.shape[1]), jnp.float32)
    )
    shapes.append(jax.ShapeDtypeStruct(vector.shape, jnp.float32))
    specs = [vmem] * len(shapes)
    if paired:
        tokens = row_inputs[2]
        token_shape = jax.ShapeDtypeStruct(tokens.shape, jnp.float32)
        block_shape = jax.ShapeDtypeStruct((tokens.shape[0], tokens.shape[1] // 2), jnp.bfloat16)
        share_shape = jax.ShapeDtypeStruct(block_shape.shape, jnp.float32)
        shapes += [token_shape, block_shape, token_shape, token_shape] + [share_shape] * 3
    half = jax.ShapeDtypeStruct((rows, columns), jnp.float32)
    shapes += [half] * (2 + count)
    specs += [hbm] * (len(shapes) - len(specs))
    flat = [item for mat in mats for item in mat] + last_sent + last_kept + [grad, narrow]
    row_specs = [hbm, vmem] + [hbm] * 7 if paired else []
    results = pl.pallas_call(
        functools.partial(finish_kernel, plans, paired, bits, blocks),
        out_shape=shapes,
        in_specs=[hbm] * len(flat) + [vmem] + row_specs,
        out_specs=specs,
        scratch_shapes=scratch,
        compiler_params=pltpu.CompilerParams(
            collective_id=2, has_side_effects=True, vmem_limit_bytes=FINISH_LIMIT
        ),
        name="finish",
    )(*flat, vector, *row_inputs)
    return (
        results[:count],
        results[count],
        results[count + 1],
        *(results[count + 2 : count + 4] if paired else ()),
    )


def head_gather(block):
    if lax.axis_size("head") != 2:
        return lax.all_gather(block, "head", axis=1, tiled=True)
    other = xor_permute(block, "head", 0)
    mine = lax.axis_index("head") == 0
    return jnp.concatenate(
        [jnp.where(mine, block, other), jnp.where(mine, other, block)], axis=1
    )


HEAD_GROUP = 8
BROAD_GROUP = 32
SLAB = 16
VMEM_LIMIT = 56 * 1024 * 1024
FAR = 1 << 30
NN = ((1,), (0,))
NT = ((1,), (1,))
TN = ((0,), (0,))


def low_dot(left, right, dims):
    return lax.dot_general(
        left.astype(jnp.bfloat16),
        right.astype(jnp.bfloat16),
        (dims, ((), ())),
        preferred_element_type=jnp.float32,
    )


def halves_of(value):
    high = value.astype(jnp.bfloat16)
    return high, (value - high.astype(jnp.float32)).astype(jnp.bfloat16)


def thirds_of(value):
    first = value.astype(jnp.bfloat16).astype(jnp.float32)
    second = (value - first).astype(jnp.bfloat16).astype(jnp.float32)
    return first, second, value - first - second


def spread_matrix(heads, head_dim):
    shape = (heads, heads * head_dim)
    rows = lax.broadcasted_iota(jnp.int32, shape, 0)
    columns = lax.broadcasted_iota(jnp.int32, shape, 1)
    return (columns // head_dim == rows).astype(jnp.float32)


def turned(rows, matrix):
    return low_dot(
        jnp.concatenate(thirds_of(rows), axis=0), jnp.concatenate([matrix] * 3, axis=0), TN
    )


def head_sums(spread, value):
    high, low = halves_of(value)
    return low_dot(spread, high, NT) + low_dot(spread, low, NT)


def map_dot(left, right):
    return low_dot(
        jnp.concatenate([left, left], axis=1), jnp.concatenate(halves_of(right), axis=0), NN
    )


def fine_dot(left, right):
    left_high, left_low = halves_of(left)
    right_high, right_low = halves_of(right)
    return (
        low_dot(left_high, right_high, NT)
        + low_dot(left_high, right_low, NT)
        + low_dot(left_low, right_high, NT)
    )


def sigmoid(value):
    return 0.5 + 0.5 * jnp.tanh(0.5 * value)


def segment_of(places, starts_ref, micro):
    label = jnp.zeros_like(places)
    for number in range(starts_ref.shape[1]):
        label = label + jnp.where(places >= starts_ref[micro, number], 1, 0)
    return label


def same_segment(count, base_ref, starts_ref, taps):
    micro = pl.program_id(0)
    places = base_ref[0] + lax.broadcasted_iota(jnp.int32, (count, 1), 0)
    own = segment_of(places, starts_ref, micro)
    return [
        jnp.where(segment_of(places - shift, starts_ref, micro) == own, 1.0, 0.0)
        for shift in range(1, taps)
    ]


def pair_labels(count, base_ref, starts_ref, micro):
    column = base_ref[0] + lax.broadcasted_iota(jnp.int32, (count, 1), 0)
    row = base_ref[0] + lax.broadcasted_iota(jnp.int32, (1, count), 1)
    return segment_of(column, starts_ref, micro) == segment_of(row, starts_ref, micro)


def conv_sum(ext, value, halo, weight, bias, masks):
    count = value.shape[0]
    ext[0:8, :] = halo
    ext[8 : 8 + count, :] = value
    total = bias + weight[0:1] * value
    for shift in range(1, weight.shape[0]):
        total = (
            total
            + weight[shift : shift + 1]
            * ext[8 - shift : 8 - shift + count, :]
            * masks[shift - 1]
        )
    return total


def project_kernel(
    tokens_ref, gain_ref, weight_ref, map_ref, step_ref, normed_ref, out_ref, map_out_ref, step_out_ref
):
    count = tokens_ref.shape[0]
    slab = min(count, 64)

    @pl.when(pl.program_id(0) == 0)
    def _():
        @pl.loop(0, count // slab)
        def _(step):
            cut = pl.ds(pl.multiple_of(step * slab, slab), slab)
            values = tokens_ref[cut, :].astype(jnp.float32)
            scale = lax.rsqrt(jnp.mean(values * values, axis=1, keepdims=True) + EPSILON)
            normed_ref[cut, :] = (values * scale * gain_ref[...]).astype(jnp.bfloat16)

        map_out_ref[...] = low_dot(normed_ref[...], map_ref[...], NN)
        step_out_ref[...] = low_dot(normed_ref[...], step_ref[...], NN)

    weight = jnp.swapaxes(weight_ref[...], 0, 1)
    for half in range(weight.shape[0]):
        out_ref[half] = low_dot(normed_ref[...], weight[half], NN)


def project(tokens, gain, weight, map_weight, step_weight):
    count, width = tokens.shape
    _, halves, columns = weight.shape
    tile = min(columns, 256)
    return pl.pallas_call(
        project_kernel,
        grid=(columns // tile,),
        in_specs=[
            pl.BlockSpec((count, width), lambda j: (0, 0)),
            pl.BlockSpec((1, width), lambda j: (0, 0)),
            pl.BlockSpec((width, halves, tile), lambda j: (0, 0, j)),
            pl.BlockSpec(map_weight.shape, lambda j: (0, 0)),
            pl.BlockSpec(step_weight.shape, lambda j: (0, 0)),
        ],
        out_specs=[
            pl.BlockSpec((count, width), lambda j: (0, 0)),
            pl.BlockSpec((halves, count, tile), lambda j: (0, 0, j)),
            pl.BlockSpec((count, map_weight.shape[1]), lambda j: (0, 0)),
            pl.BlockSpec((count, step_weight.shape[1]), lambda j: (0, 0)),
        ],
        out_shape=[
            jax.ShapeDtypeStruct((count, width), jnp.bfloat16),
            jax.ShapeDtypeStruct((halves, count, columns), jnp.float32),
            jax.ShapeDtypeStruct((count, map_weight.shape[1]), jnp.float32),
            jax.ShapeDtypeStruct((count, step_weight.shape[1]), jnp.float32),
        ],
        compiler_params=pltpu.CompilerParams(vmem_limit_bytes=VMEM_LIMIT),
        cost_estimate=pl.CostEstimate(
            flops=2 * count * width * columns * halves, bytes_accessed=0, transcendentals=0
        ),
        name="project",
    )(tokens, gain[None], weight, map_weight, step_weight)


def front_kernel(
    head_dim,
    base_ref,
    starts_ref,
    x_ref,
    halo_ref,
    weight_ref,
    bias_ref,
    b_ref,
    tail_ref,
    low_ref,
    state_ref,
    ext,
    high_keep,
    rest_keep,
):
    heads = tail_ref.shape[1]
    count = x_ref.shape[2]
    weight, bias = weight_ref[...], bias_ref[...]
    masks = same_segment(count, base_ref, starts_ref, weight.shape[0])
    scale = turned(tail_ref[0], spread_matrix(heads, head_dim))
    ext[0:8, :] = halo_ref[0]
    ext[8 : 8 + count, :] = x_ref[0, 0]
    for top in range(0, count, SLAB):
        cut = slice(top, top + SLAB)
        total = bias + weight[0:1] * ext[8 + top : 8 + top + SLAB, :]
        for shift in range(1, weight.shape[0]):
            first = 8 - shift + top
            total = (
                total
                + weight[shift : shift + 1] * ext[first : first + SLAB, :] * masks[shift - 1][cut]
            )
        act = (total * sigmoid(total)).astype(jnp.bfloat16)
        low_ref[0, cut, :] = act
        high, rest = halves_of(act.astype(jnp.float32) * scale[cut])
        high_keep[cut, :] = high
        rest_keep[cut, :] = rest
    state_ref[0] = low_dot(b_ref[0], high_keep[...], TN) + low_dot(b_ref[0], rest_keep[...], TN)


def intra_block(head_dim, valid, x, b, c, run_row, step_row, skip):
    heads, count = run_row.shape
    spread = spread_matrix(heads, head_dim)
    scores = jnp.where(valid, low_dot(c, b, NT), 0.0)
    wide = x.astype(jnp.float32)
    scaled = (wide * turned(step_row, spread)).astype(jnp.bfloat16)
    run = turned(run_row, spread_matrix(heads, 1))
    pair = 2 * head_dim
    middle = count // 2
    lane = lax.broadcasted_iota(jnp.int32, (count, pair), 1)
    results = []
    for first in range(0, heads, 2):
        block = scaled[:, first * head_dim : first * head_dim + pair]
        halves = []
        for head in (first, first + 1):
            strips = []
            for top, cut in ((0, middle), (middle, count)):
                gap = run[top:cut, head : head + 1] - run_row[head : head + 1, :cut]
                weights = jnp.exp2(jnp.minimum(gap, 0.0)) * scores[top:cut, :cut]
                strips.append(low_dot(weights, block[:cut], NN))
            halves.append(jnp.concatenate(strips, axis=0))
        results.append(jnp.where(lane < head_dim, halves[0], halves[1]))
    return jnp.concatenate(results, axis=1) + skip * wide


def intra_steps(inputs, out_ref, head_dim):
    return [
        functools.partial(intra_step, inputs, out_ref, head_dim, micro)
        for micro in range(out_ref.shape[0])
    ]


def intra_step(inputs, out_ref, head_dim, micro):
    base_ref, starts_ref, x_ref, b_ref, c_ref, run_ref, step_ref, skip_ref = inputs
    _, count, inner = x_ref.shape
    heads = run_ref.shape[1]
    group = min(HEAD_GROUP, heads)
    wide = group * head_dim

    def body(x, b, c, run, step, skip, out):
        rows = lax.broadcasted_iota(jnp.int32, (count, count), 0)
        columns = lax.broadcasted_iota(jnp.int32, (count, count), 1)
        valid = pair_labels(count, base_ref, starts_ref, micro) & (rows >= columns)
        out[...] = intra_block(
            head_dim, valid, x[...], b[...], c[...], run[...], step[...], skip[...]
        )

    token = pl.BlockSpec((count, wide), lambda k: (0, k))
    maps = pl.BlockSpec((count, b_ref.shape[2]), lambda k: (0, 0))
    row = pl.BlockSpec((group, count), lambda k: (k, 0))
    pltpu.emit_pipeline(
        body,
        grid=(inner // wide,),
        in_specs=[token, maps, maps, row, row, pl.BlockSpec((1, wide), lambda k: (0, k))],
        out_specs=[token],
    )(
        x_ref.at[micro],
        b_ref.at[micro],
        c_ref.at[micro],
        run_ref.at[micro],
        step_ref.at[micro],
        skip_ref,
        out_ref.at[micro],
    )


def gate_kernel(
    head_dim,
    full,
    bits,
    intra_ref,
    c_ref,
    carry_ref,
    begin_ref,
    gate_ref,
    cot_ref,
    gain_ref,
    norm_ref,
    grad_gate_ref,
    both_ref,
    grad_mixed_ref,
    start_ref,
    rows_ref,
    mixed_keep,
    gate_keep,
    cot_keep,
    high_keep,
    rest_keep,
    both_keep,
    sums,
    sums_in,
    send_sem,
    recv_sem,
):
    stage, micro, number = pl.program_id(0), pl.program_id(1), pl.program_id(2)
    groups = pl.num_programs(2)
    heads = carry_ref.shape[1]
    place = micro * groups + number
    carry = turned(carry_ref[0], spread_matrix(heads, head_dim))
    mine = lax.axis_index("head")

    def partner(bit):
        return {"head": mine + (1 << bit) * (1 - 2 * lax.rem(mine // (1 << bit), 2))}

    @pl.when((stage == 0) & (place == 0))
    def _():
        barrier = pltpu.get_barrier_semaphore()
        for bit in range(bits):
            pl.semaphore_signal(
                barrier, inc=1, device_id=partner(bit), device_id_type=pl.DeviceIdType.MESH
            )
        pl.semaphore_wait(barrier, bits)

    @pl.when(stage == 0)
    def _():
        inter = map_dot(c_ref[0], begin_ref[0])
        gain = gain_ref[...]
        for top in range(0, inter.shape[0], SLAB):
            cut = slice(top, top + SLAB)
            mixed = intra_ref[0, cut, :] + inter[cut] * carry[cut]
            gate, cot = gate_ref[0, 0, cut, :], cot_ref[0, cut, :]
            mixed_keep[place, cut, :] = mixed
            gate_keep[place, cut, :] = gate
            cot_keep[place, cut, :] = cot
            gated = mixed * (gate * sigmoid(gate))
            square = jnp.sum(gated * gated, axis=1, keepdims=True)
            cross = jnp.sum(cot * gain * gated, axis=1, keepdims=True)
            lane = lax.broadcasted_iota(jnp.int32, (SLAB, 128), 1)
            both_keep[cut, :] = jnp.where(lane == 0, square, jnp.where(lane == 1, cross, 0.0))

        @pl.when(number == 0)
        def _():
            sums[0, micro] = both_keep[...]

        @pl.when(number > 0)
        def _():
            sums[0, micro] = sums[0, micro] + both_keep[...]

    @pl.when((stage == 1) & (place == 0))
    def _():
        for bit in range(bits):
            copy = pltpu.make_async_remote_copy(
                src_ref=sums.at[bit],
                dst_ref=sums_in.at[bit],
                send_sem=send_sem.at[bit],
                recv_sem=recv_sem.at[bit],
                device_id=partner(bit),
                device_id_type=pl.DeviceIdType.MESH,
            )
            copy.start()
            copy.wait()
            sums[bit + 1] = sums[bit] + sums_in[bit]

    @pl.when(stage == 1)
    def _():
        gain = gain_ref[...]
        gains = jnp.zeros((8, gain.shape[1]), jnp.float32)
        for top in range(0, carry.shape[0], SLAB):
            cut = slice(top, top + SLAB)
            mixed, gate = mixed_keep[place, cut, :], gate_keep[place, cut, :]
            cot = cot_keep[place, cut, :]
            total = sums[bits, micro, cut, :]
            scale = lax.rsqrt(total[:, 0:1] / full + EPSILON)
            pull = scale * scale * scale * total[:, 1:2] / full
            sigma = sigmoid(gate)
            act = gate * sigma
            gated = mixed * act
            unit = gated * scale
            norm_ref[0, cut, :] = (unit * gain).astype(jnp.bfloat16)
            grad_gated = cot * gain * scale - gated * pull
            grad_gate = grad_gated * mixed * sigma * (1.0 + gate * (1.0 - sigma))
            grad_gate = grad_gate.astype(jnp.bfloat16)
            grad_gate_ref[0, cut, :] = grad_gate
            both_ref[0, 0, cut, :] = grad_gate
            grad_mixed = (grad_gated * act).astype(jnp.bfloat16)
            grad_mixed_ref[0, cut, :] = grad_mixed
            high, rest = halves_of(grad_mixed.astype(jnp.float32) * carry[cut])
            high_keep[cut, :] = high
            rest_keep[cut, :] = rest
            parts = (cot * unit).reshape(SLAB // 8, 8, cot.shape[1])
            gains = gains + jnp.sum(parts, axis=0)
        c = c_ref[0]
        start_ref[0] = low_dot(c, high_keep[...], TN) + low_dot(c, rest_keep[...], TN)
        rows_ref[0] = gains


def back_kernel(
    head_dim,
    plans,
    base_ref,
    starts_ref,
    x_ref,
    g_ref,
    b_ref,
    c_ref,
    run_ref,
    step_ref,
    carry_ref,
    tail_ref,
    start_ref,
    end_ref,
    pre_ref,
    halo_ref,
    weight_ref,
    bias_ref,
    skip_ref,
    both_in_ref,
    out_sent_ref,
    gate_sent_ref,
    both_ref,
    edge_ref,
    halo_out_ref,
    rows_ref,
    direct_ref,
    decay_ref,
    grad_b_ref,
    grad_c_ref,
    *refs,
):
    refs = list(refs)
    ext, moved, send_sem, recv_sem = refs[-4:]
    me = lax.axis_index("seq")

    def partner(bit):
        return me + (1 << bit) * (1 - 2 * lax.rem(me // (1 << bit), 2))

    def sends():
        copies = []
        for plan, source in zip(plans, (out_sent_ref, gate_sent_ref)):
            for (order, _), columns in zip(plan, part_columns(plan)):
                copies.append(
                    pltpu.make_async_remote_copy(
                        src_ref=source.at[:, columns],
                        dst_ref=refs[len(copies)],
                        send_sem=send_sem.at[len(copies)],
                        recv_sem=recv_sem.at[len(copies)],
                        device_id={"seq": partner(order[0])},
                        device_id_type=pl.DeviceIdType.MESH,
                    )
                )
        return copies

    at_first = (pl.program_id(0) == 0) & (pl.program_id(1) == 0)
    at_last = (pl.program_id(0) == pl.num_programs(0) - 1) & (
        pl.program_id(1) == pl.num_programs(1) - 1
    )
    used = sorted({order[0] for order, _ in plans[0]})

    @pl.when(at_first)
    def _():
        barrier = pltpu.get_barrier_semaphore()
        for bit in used:
            pl.semaphore_signal(
                barrier,
                inc=1,
                device_id={"seq": partner(bit)},
                device_id_type=pl.DeviceIdType.MESH,
            )
        pl.semaphore_wait(barrier, len(used))
        for copy in sends():
            copy.start()

    heads = step_ref.shape[1]
    count = x_ref.shape[1]
    spread = spread_matrix(heads, head_dim)
    x, g, b, c = x_ref[0], g_ref[0], b_ref[0], c_ref[0]
    x_wide, g_wide = x.astype(jnp.float32), g.astype(jnp.float32)
    rows = lax.broadcasted_iota(jnp.int32, (count, count), 0)
    columns = lax.broadcasted_iota(jnp.int32, (count, count), 1)
    valid = pair_labels(count, base_ref, starts_ref, pl.program_id(0)) & (
        columns >= rows
    )
    scores = jnp.where(valid, low_dot(b, c, NT), 0.0)
    upto = (rows >= columns).astype(jnp.bfloat16)
    before = (rows < columns).astype(jnp.float32)
    step = turned(step_ref[0], spread)
    carry = turned(carry_ref[0], spread)
    tail = turned(tail_ref[0], spread)
    scaled_wide = x_wide * step
    scaled, scaled_rest = halves_of(scaled_wide)
    start, end = start_ref[0], end_ref[0]
    run_row = run_ref[0]
    run = turned(run_row, spread_matrix(heads, 1))
    pair = 2 * head_dim
    lane = lax.broadcasted_iota(jnp.int32, (count, pair), 1)
    middle = count // 2
    score_grads = [
        jnp.zeros((middle, count), jnp.float32),
        jnp.zeros((count - middle, count - middle), jnp.float32),
    ]
    results, straddles = [], []
    for first in range(0, heads, 2):
        cut = slice(first * head_dim, first * head_dim + pair)
        g_block = g[:, cut]
        g_swap = jnp.concatenate([g_block[:, head_dim:], g_block[:, :head_dim]], axis=1)
        x_block, x_rest = scaled[:, cut], scaled_rest[:, cut]
        x_rest = jnp.concatenate([x_rest[:, head_dim:], x_rest[:, :head_dim]], axis=1)
        halves = []
        for head in (first, first + 1):
            own = (lane < head_dim) if head == first else (lane >= head_dim)
            x_own, g_own = jnp.where(own, x_block, x_rest), jnp.where(own, g_block, g_swap)
            strips, straddle = [], None
            for part, (top, cut) in enumerate(((0, middle), (middle, count))):
                gap = run_row[head : head + 1, top:] - run[top:cut, head : head + 1]
                fade = jnp.exp2(jnp.minimum(gap, 0.0))
                weights = fade * scores[top:cut, top:]
                strips.append(low_dot(weights, g_block[top:], NN))
                inner = low_dot(x_own[top:cut], g_own[top:], NT)
                score_grads[part] = score_grads[part] + fade * inner
                sums = low_dot(weights * inner, upto[top:, top:], NN)
                sums = jnp.sum(sums * before[top:cut, top:], axis=0, keepdims=True)
                if part == 0:
                    straddle = sums
                else:
                    straddle = jnp.concatenate(
                        [straddle[:, :middle], straddle[:, middle:] + sums], axis=1
                    )
            straddles.append(straddle)
            halves.append(jnp.concatenate(strips, axis=0))
        results.append(jnp.where(lane < head_dim, halves[0], halves[1]))
    score_grad = jnp.concatenate(
        [
            score_grads[0],
            jnp.concatenate([jnp.zeros((count - middle, middle), jnp.float32), score_grads[1]], axis=1),
        ],
        axis=0,
    )
    score_grad = jnp.where(valid, score_grad, 0.0)
    later = map_dot(b, end) * tail
    values = jnp.concatenate(results, axis=1) + later
    inter = map_dot(c, start) * carry
    direct_ref[0] = head_sums(spread, x_wide * values)
    given = head_sums(spread, scaled_wide * later)
    taken = head_sums(spread, g_wide * inter)
    flows = jnp.concatenate([given, taken], axis=0)
    flow_pieces = [item.astype(jnp.bfloat16) for item in thirds_of(flows)]
    after = (rows < columns).astype(jnp.bfloat16)
    flow_later = sum(low_dot(item, after, NN) for item in flow_pieces)
    flow_sooner = sum(low_dot(item, upto, NN) for item in flow_pieces)
    decay_ref[0] = (
        jnp.concatenate(straddles, axis=0) + flow_later[:heads] + flow_sooner[heads:]
    )
    grads_high, grads_low = halves_of(score_grad)
    grad_c = fine_dot(g_wide * carry, start) + low_dot(grads_high, b, TN) + low_dot(grads_low, b, TN)
    grad_b = fine_dot(scaled_wide * tail, end) + low_dot(grads_high, c, NN) + low_dot(grads_low, c, NN)

    @pl.when(pl.program_id(1) == 0)
    def _():
        grad_b_ref[0] = grad_b
        grad_c_ref[0] = grad_c

    @pl.when(pl.program_id(1) > 0)
    def _():
        grad_b_ref[0] = grad_b_ref[0] + grad_b
        grad_c_ref[0] = grad_c_ref[0] + grad_c

    weight, pre = weight_ref[...], pre_ref[0, 0]
    masks = same_segment(count, base_ref, starts_ref, weight.shape[0])
    total = conv_sum(ext, pre, halo_ref[0], weight, bias_ref[...], masks)
    sigma = sigmoid(total)
    grad_conv = (values * step + skip_ref[...] * g_wide) * (
        sigma * (1.0 + total * (1.0 - sigma))
    )
    moved[0:8, :] = jnp.zeros_like(moved[0:8, :])
    moved[8 + count :, :] = jnp.zeros_like(moved[8 + count :, :])
    sums = [jnp.sum(grad_conv * pre, axis=0, keepdims=True)]
    back = jnp.concatenate(
        [jnp.zeros((8, pre.shape[1]), jnp.float32), grad_conv * weight[0:1]], axis=0
    )
    for shift in range(1, weight.shape[0]):
        part = grad_conv * masks[shift - 1]
        sums.append(
            jnp.sum(part * ext[8 - shift : 8 - shift + count, :], axis=0, keepdims=True)
        )
        moved[8 : 8 + count, :] = part * weight[shift : shift + 1]
        back = back + moved[shift : shift + 8 + count, :]
    halo_out_ref[0] = back[:8]
    both_ref[0, 0] = back[8:].astype(jnp.bfloat16)
    edge_ref[0] = back[count:]
    sums.append(jnp.sum(grad_conv, axis=0, keepdims=True))
    sums.append(jnp.sum(g_wide * x_wide, axis=0, keepdims=True))
    sums.append(jnp.sum(start * end, axis=0, keepdims=True))
    sums.append(jnp.zeros((8 - len(sums), pre.shape[1]), jnp.float32))
    rows_ref[0] = jnp.concatenate(sums, axis=0)

    @pl.when(at_last)
    def _():
        for copy in sends():
            copy.wait()


def blocked(kernel, name, grid, ins, outs, scratch=(), micros=0, aliases=None, remote=None):
    moved = sum(item[0].size * item[0].dtype.itemsize for item in ins if item[1] != "any")
    moved += sum(
        math.prod(item[2]) * math.prod(grid) * jnp.dtype(item[1]).itemsize
        for item in outs
        if item[2] != "any"
    )

    def spec(item):
        if item[1] is None:
            return pl.BlockSpec(memory_space=pltpu.SMEM)
        if item[1] == "any":
            return pl.BlockSpec(memory_space=pl.ANY)
        return pl.BlockSpec(item[1], item[2])

    return pl.pallas_call(
        kernel,
        grid=grid,
        in_specs=[spec(item) for item in ins],
        out_specs=[spec(item[1:]) for item in outs],
        out_shape=[jax.ShapeDtypeStruct(item[0], item[1]) for item in outs],
        scratch_shapes=list(scratch),
        input_output_aliases=aliases or {},
        compiler_params=pltpu.CompilerParams(
            dimension_semantics=("arbitrary",) * len(grid),
            vmem_limit_bytes=VMEM_LIMIT,
            collective_id=remote,
            has_side_effects=remote is not None,
        ),
        cost_estimate=pl.CostEstimate(
            flops=micros * 1_000_000_000, bytes_accessed=moved, transcendentals=0
        ),
        name=name,
    )(*[item[0] for item in ins])


def body(
    tokens,
    norm_gain,
    in_weight,
    bc_weight,
    dt_weight,
    dt_bias,
    a_log,
    conv_weight,
    conv_bias,
    bc_conv_weight,
    bc_conv_bias,
    d_skip,
    gate_gain,
    out_weight,
    cotangent,
    seq_lengths,
):
    micro, length, width = tokens.shape
    heads = dt_bias.shape[0]
    inner = conv_bias.shape[0]
    head_dim = inner // heads
    state_size = bc_weight.shape[1] // 2
    taps = conv_weight.shape[0]
    total = micro * length
    head_count = lax.axis_size("head")
    full_inner = inner * head_count
    group = min(HEAD_GROUP, heads)
    groups = heads // group
    wide = group * head_dim
    base = lax.axis_index("seq").astype(jnp.int32) * length
    labels = segment_ids(seq_lengths, base - (taps - 1), length + taps - 1, micro)
    own_labels = labels[:, taps - 1 :]
    before_labels = labels[:, taps - 2]
    starts = jnp.cumsum(seq_lengths, axis=-1).astype(jnp.int32) - seq_lengths
    long_starts = jnp.full((micro - starts.shape[0], starts.shape[1]), FAR, jnp.int32)
    starts = jnp.concatenate([starts, long_starts.at[:, 0].set(0)], axis=0)
    base_item, starts_item = (base[None], None), (starts, None)

    flat = tokens.reshape(total, width).astype(jnp.float32)
    cot_flat = cotangent.reshape(total, width)
    _, norm_back = jax.vjp(rms_scale, flat, norm_gain)
    normed_low, gate_x, bc_pre, delta_pre = project(
        tokens.reshape(total, width), norm_gain, in_weight, bc_weight, dt_weight
    )
    gate_x = gate_x.reshape(2, micro, length, inner)
    bc_pre = bc_pre.reshape(micro, length, 2 * state_size)
    delta_pre = delta_pre.T
    left = shifted(
        jnp.concatenate(
            [gate_x[1, :, length - taps + 1 :], bc_pre[:, length - taps + 1 :]], axis=-1
        ),
        "seq",
        1,
    )
    left_x, left_bc = left[..., :inner], left[..., inner:]
    halo = jnp.pad(left_x, ((0, 0), (9 - taps, 0), (0, 0)))
    conv_many = jax.vmap(conv_silu, in_axes=(0, None, None, 0))
    bc_act, bc_conv_back = jax.vjp(
        lambda extended, weight, bias: conv_many(extended, weight, bias, labels),
        jnp.concatenate([left_bc, bc_pre], axis=1),
        bc_conv_weight,
        bc_conv_bias,
    )
    bc_low = bc_act.astype(jnp.bfloat16)
    b_low, c_low = bc_low[..., :state_size], bc_low[..., state_size:]
    (delta, decay), rate_back = jax.vjp(step_sizes, delta_pre, dt_bias, a_log)

    def by_micro(array):
        return array.reshape(heads, micro, length).transpose(1, 0, 2)

    def by_head(array):
        return array.transpose(1, 0, 2).reshape(heads, total)

    delta, decay = by_micro(delta), by_micro(decay)
    order = jnp.arange(length)
    running = jnp.einsum(
        "mhj,ji->mhi",
        decay,
        (order[:, None] <= order[None, :]).astype(jnp.float32),
        precision=HIGHEST,
    )
    device_log = running[:, :, -1]
    running_two = running * math.log2(math.e)
    live = (own_labels == before_labels[:, None]).astype(jnp.float32)
    last = (own_labels == own_labels[:, -1:]).astype(jnp.float32)
    carried = jnp.exp(running) * live[:, None]
    tail = jnp.exp(device_log[:, :, None] - running) * last[:, None]
    device_live = live[:, -1]
    gain_row, skip_row = gate_gain[None], jnp.repeat(d_skip, head_dim)[None]
    conv_row = conv_bias[None]

    grid = (micro, groups)
    token_block = (1, length, wide)
    in_token = lambda m, k: (m, 0, k)
    half_block = (1, 1, length, wide)
    in_gate, in_x = lambda m, k: (0, m, 0, k), lambda m, k: (1, m, 0, k)
    row_block, in_row = (1, group, length), lambda m, k: (m, k, 0)
    map_block, in_map = (1, length, state_size), lambda m, k: (m, 0, 0)
    state_block, in_state = (1, state_size, wide), in_token
    halo_block = (1, 8, wide)
    flat_block, in_flat = (1, wide), lambda m, k: (0, k)
    conv_item = (conv_weight, (taps, wide), in_flat)
    whole = (micro, length, inner)
    state_shape = (micro, state_size, inner)
    row_shape = (micro, heads, length)

    broad_group = min(BROAD_GROUP, heads)
    broad_groups, broad = heads // broad_group, broad_group * head_dim
    broad_token, broad_half = (1, length, broad), (1, 1, length, broad)
    broad_row, broad_state = (1, broad_group, length), (1, state_size, broad)
    x_low, device_state = blocked(
        functools.partial(front_kernel, head_dim),
        "front",
        (micro, broad_groups),
        [
            base_item,
            starts_item,
            (gate_x, broad_half, in_x),
            (halo, (1, 8, broad), in_token),
            (conv_weight, (taps, broad), in_flat),
            (conv_row, (1, broad), in_flat),
            (b_low, map_block, in_map),
            (tail * delta, broad_row, in_row),
        ],
        [
            (whole, jnp.bfloat16, broad_token, in_token),
            (state_shape, jnp.float32, broad_state, in_state),
        ],
        [
            pltpu.VMEM((length + 8, broad), jnp.float32),
            pltpu.VMEM((length, broad), jnp.bfloat16),
            pltpu.VMEM((length, broad), jnp.bfloat16),
        ],
        20,
    )
    exchange_log = jnp.where(device_live[:, None] > 0.0, device_log, DEAD)
    exchange_log = jnp.repeat(exchange_log, head_dim, axis=1)
    plans = scatter_plans(inner, axis_bits("seq"))
    parts = plans[-1]
    orders = tuple(order for order, _ in parts)
    tiled = (width >> axis_bits("seq")) % 128 == 0
    incoming, (grad_gate_n, intra), arranged = exchange(
        device_state,
        exchange_log,
        False,
        (cot_flat, normed_low) if tiled else (),
        orders if tiled else (),
        [
            (plain_steps, (), (cot_flat, out_weight), (total, inner)),
            (
                intra_steps,
                head_dim,
                (base[None], starts, x_low, b_low, c_low, running_two, delta, skip_row),
                whole,
            ),
        ],
    )
    grad_gate_n = grad_gate_n.reshape(whole)
    if not tiled:
        arranged = arrange(cot_flat, orders) + arrange(normed_low, orders)
    cot_parts, normed_parts = arranged[: 2 * len(parts)], arranged[2 * len(parts) :]


    def first_stage(index):
        return lambda p, m, k: index(m + p * (micro - 1 - m), k + p * (broad_groups - 1 - k))

    def second_stage(index):
        return lambda p, m, k: index(m * p, k * p)

    def both_stages(index):
        return lambda p, m, k: index(m, k)

    head_bits = axis_bits("head")
    kept_shape = (micro * broad_groups, length, broad)
    sums_shape = (micro, length, 128)
    normed_gate, grad_gate_pre, grad_gate_x, grad_mixed, device_grad, gate_rows = blocked(
        functools.partial(gate_kernel, head_dim, float(full_inner), head_bits),
        "gate",
        (2, micro, broad_groups),
        [
            (intra, broad_token, first_stage(in_token)),
            (c_low, map_block, both_stages(in_map)),
            (carried, broad_row, both_stages(in_row)),
            (incoming, broad_state, first_stage(in_state)),
            (gate_x, broad_half, first_stage(in_gate)),
            (grad_gate_n, broad_token, first_stage(in_token)),
            (gain_row, (1, broad), both_stages(in_flat)),
        ],
        [
            (whole, jnp.bfloat16, broad_token, second_stage(in_token)),
            (whole, jnp.bfloat16, broad_token, second_stage(in_token)),
            ((2,) + whole, jnp.bfloat16, broad_half, second_stage(in_gate)),
            (whole, jnp.bfloat16, broad_token, second_stage(in_token)),
            (state_shape, jnp.float32, broad_state, second_stage(in_state)),
            ((micro, 8, inner), jnp.float32, (1, 8, broad), second_stage(in_token)),
        ],
        [
            pltpu.VMEM(kept_shape, jnp.float32),
            pltpu.VMEM(kept_shape, jnp.float32),
            pltpu.VMEM(kept_shape, jnp.float32),
            pltpu.VMEM((length, broad), jnp.bfloat16),
            pltpu.VMEM((length, broad), jnp.bfloat16),
            pltpu.VMEM((length, 128), jnp.float32),
            pltpu.VMEM((head_bits + 1,) + sums_shape, jnp.float32),
            pltpu.VMEM((head_bits,) + sums_shape, jnp.float32),
            pltpu.SemaphoreType.DMA((head_bits,)),
            pltpu.SemaphoreType.DMA((head_bits,)),
        ],
        30,
        None,
        4,
    )
    normed_gate = normed_gate.reshape(total, inner)
    grad_gate_pre = grad_gate_pre.reshape(total, inner)
    grad_gate_gain = jnp.sum(gate_rows, axis=(0, 1))

    half_shape = (width // 2, inner)
    paired = head_count == 2
    share = width // head_count
    outgoing, (out_sent, gate_sent), _ = exchange(
        device_grad,
        exchange_log,
        True,
        jobs=[
            (product_steps, plans[0], cot_parts[::2] + [normed_gate], half_shape),
            (product_steps, plans[1], normed_parts[::2] + [grad_gate_pre], half_shape),
        ],
    )
    (
        grad_gate_x,
        edge,
        halo_grad,
        conv_rows,
        direct,
        fading,
        grad_b,
        grad_c,
        *arrivals,
    ) = blocked(
        functools.partial(back_kernel, head_dim, plans),
        "back",
        grid,
        [
            base_item,
            starts_item,
            (x_low, token_block, in_token),
            (grad_mixed, token_block, in_token),
            (b_low, map_block, in_map),
            (c_low, map_block, in_map),
            (running_two, row_block, in_row),
            (delta, row_block, in_row),
            (carried, row_block, in_row),
            (tail, row_block, in_row),
            (incoming, state_block, in_state),
            (outgoing, state_block, in_state),
            (gate_x, half_block, in_x),
            (halo, halo_block, in_token),
            conv_item,
            (conv_row, flat_block, in_flat),
            (skip_row, flat_block, in_flat),
            (grad_gate_x, "any"),
            (out_sent, "any"),
            (gate_sent, "any"),
        ],
        [
            ((2,) + whole, jnp.bfloat16, half_block, in_x),
            ((micro, 8, inner), jnp.float32, halo_block, in_token),
            ((micro, 8, inner), jnp.float32, halo_block, in_token),
            ((micro, 8, inner), jnp.float32, halo_block, in_token),
            (row_shape, jnp.float32, row_block, in_row),
            (row_shape, jnp.float32, row_block, in_row),
            ((micro, length, state_size), jnp.float32, map_block, in_map),
            ((micro, length, state_size), jnp.float32, map_block, in_map),
        ]
        + [
            ((width // 2, sum(widths)), jnp.float32, "any")
            for plan in plans[:2]
            for _, widths in plan
        ],
        [
            pltpu.VMEM((length + 8, wide), jnp.float32),
            pltpu.VMEM((length + 16, wide), jnp.float32),
            pltpu.SemaphoreType.DMA((2 * len(parts),)),
            pltpu.SemaphoreType.DMA((2 * len(parts),)),
        ],
        80,
        {17: 0},
        3,
    )
    arrived = [arrivals[: len(parts)], arrivals[len(parts) :]]
    grad_bc = all_sum(jnp.concatenate([grad_b, grad_c], axis=-1), "head")
    pairs = conv_rows[:, taps + 2].reshape(micro, heads, head_dim)
    kept = jnp.sum(pairs, axis=-1) * jnp.exp(device_log) * device_live[:, None]
    grad_decay = by_head(fading + kept[:, :, None])
    grad_delta_pre, grad_dt_bias, grad_a_log = rate_back((by_head(direct), grad_decay))
    conv_rows = jnp.sum(conv_rows, axis=0)
    grad_conv_weight, grad_conv_bias = conv_rows[:taps], conv_rows[taps]
    grad_d_skip = jnp.sum(conv_rows[taps + 1].reshape(heads, head_dim), axis=-1)
    grad_bc_ext, grad_bc_conv_weight, grad_bc_conv_bias = bc_conv_back(grad_bc)
    right = shifted(
        jnp.concatenate([halo_grad[:, 9 - taps :], grad_bc_ext[:, : taps - 1]], axis=-1), "seq", -1
    )
    right_x, right_bc = right[..., :inner], right[..., inner:]
    grad_gate_x = lax.dynamic_update_slice(
        grad_gate_x,
        (edge[:, 9 - taps :] + right_x).astype(jnp.bfloat16)[None],
        (1, 0, length - taps + 1, 0),
    )
    grad_bc_pre = grad_bc_ext[:, taps - 1 :].at[:, length - taps + 1 :].add(right_bc)
    bc_flat = grad_bc_pre.reshape(total, 2 * state_size)
    grad_gate_x = grad_gate_x.reshape(2, total, inner)
    grad_steps = grad_delta_pre.T
    narrow_row = jnp.concatenate([bc_flat * (1.0 / head_count), grad_steps], axis=1)
    if paired:
        row_inputs = (
            in_weight,
            norm_gain[None],
            tokens.reshape(total, width),
            cot_flat,
            narrow_row,
            bc_weight,
            dt_weight,
            normed_gate,
            out_weight,
        )
        gain_grad = jnp.zeros_like(norm_gain)
    else:
        row_inputs = ()
        row_part = lax.dot_general(
            narrow_row,
            jnp.concatenate([bc_weight, dt_weight], axis=1),
            (NT, ((), ())),
            precision=HIGHEST,
            preferred_element_type=jnp.float32,
        ) + jnp.einsum(
            "ktc,dkc->td", grad_gate_x, in_weight, preferred_element_type=jnp.float32
        )
        grad_flat, gain_grad = norm_back(all_sum(row_part, "head"))
        grad_tokens = cot_flat.astype(jnp.float32) + grad_flat
        head_terms = lax.dot_general(
            normed_gate, out_weight, (NT, ((), ())), preferred_element_type=jnp.float32
        )
        summed = lax.psum_scatter(head_terms, "head", scatter_dimension=1, tiled=True)
        residual = lax.dynamic_slice_in_dim(flat, lax.axis_index("head") * share, share, 1)
        block_out = (residual + summed).astype(jnp.bfloat16)

    share_bc = 2 * state_size // head_count
    own_bc = lax.dynamic_slice_in_dim(bc_flat, lax.axis_index("head") * share_bc, share_bc, 1)
    across = share_bc + heads
    side = min(1, len(parts) - 1)
    narrow_high, narrow_rest = halves_of(jnp.concatenate([own_bc, grad_steps], axis=1))
    both = jnp.concatenate([narrow_high, narrow_rest], axis=1)
    narrow = jnp.concatenate(
        [product(normed_parts[2 * side + 1], both), product(normed_parts[2 * side], both)], axis=0
    )
    narrow = narrow[:, :across] + narrow[:, across:]
    size = lax.axis_size("seq")
    row_count = width // size
    narrow = narrow.reshape(size, row_count, across)
    beside = 128 // heads
    narrow_bc = jnp.pad(narrow[:, :, :share_bc], ((0, 0), (0, 0), (0, -share_bc % 128)))
    narrow_steps = narrow[:, :, share_bc:].reshape(size, row_count // beside, 128)
    narrow_steps = jnp.pad(narrow_steps, ((0, 0), (0, 0), (0, narrow_bc.shape[2] - 128)))
    narrow = jnp.concatenate([narrow_bc, narrow_steps], axis=1)
    narrow_rows = narrow.shape[1]
    narrow = jnp.pad(narrow, ((0, 0), (0, -narrow_rows % 8), (0, 0)))
    narrow = narrow.reshape(-1, narrow.shape[2])

    small = [
        gain_grad,
        grad_bc_conv_weight,
        grad_bc_conv_bias,
        grad_dt_bias,
        grad_a_log,
        grad_d_skip,
        grad_conv_weight,
        grad_conv_bias,
        grad_gate_gain,
    ]
    row = jnp.concatenate([item.reshape(-1) for item in small])
    count = row.size
    row = jnp.pad(row, (0, -count % 1024)).reshape(-1, 128)

    (grad_out_weight, gate_block, x_block), gathered, row, *token_grads = finish(
        plans,
        [
            cot_parts[1::2] + [normed_gate] + arrived[0],
            normed_parts[1::2] + [grad_gate_pre] + arrived[1],
        ],
        normed_parts[::2],
        normed_parts[1::2],
        grad_gate_x,
        narrow,
        row,
        row_inputs,
    )
    if paired:
        grad_tokens, block_out = token_grads
    grad_tokens = grad_tokens.reshape(micro, length, width)
    block_out = block_out.reshape(micro, length, share)
    grad_in_weight = jnp.stack([gate_block, x_block], axis=1)
    grad_bc_weight = head_gather(gathered[:, :row_count, :share_bc].reshape(width, share_bc))
    grad_dt_weight = gathered[:, row_count:narrow_rows, :128].reshape(width, heads)
    row = row.reshape(-1)
    sizes, first = [], 0
    for item in small:
        sizes.append(row[first : first + item.size].reshape(item.shape))
        first += item.size
    (
        grad_norm_gain,
        grad_bc_conv_weight,
        grad_bc_conv_bias,
        grad_dt_bias,
        grad_a_log,
        grad_d_skip,
        grad_conv_weight,
        grad_conv_bias,
        grad_gate_gain,
    ) = sizes

    return (
        block_out,
        grad_tokens,
        grad_norm_gain,
        grad_in_weight,
        grad_bc_weight,
        grad_dt_weight,
        grad_dt_bias,
        grad_a_log,
        grad_d_skip,
        grad_conv_weight,
        grad_conv_bias,
        grad_bc_conv_weight,
        grad_bc_conv_bias,
        grad_gate_gain,
        grad_out_weight,
    )


def solution(mesh):
    return jax.shard_map(
        body,
        mesh=mesh,
        in_specs=(
            P(None, "seq", None),
            P(),
            P(None, None, "head"),
            P(),
            P(None, "head"),
            P("head"),
            P("head"),
            P(None, "head"),
            P("head"),
            P(),
            P(),
            P("head"),
            P("head"),
            P(None, "head"),
            P(None, "seq", None),
            P(),
        ),
        out_specs=(
            P(None, "seq", "head"),
            P(None, "seq", None),
            P(),
            P("seq", None, "head"),
            P(),
            P(None, "head"),
            P("head"),
            P("head"),
            P("head"),
            P(None, "head"),
            P("head"),
            P(),
            P(),
            P("head"),
            P("seq", "head"),
        ),
        check_vma=False,
    )
```

```python
import functools
import math

import jax
import jax.numpy as jnp
from jax import lax
from jax.experimental import pallas as pl
from jax.experimental.pallas import tpu as pltpu
from jax.sharding import PartitionSpec as P

EPSILON = 1e-05
HIGHEST = lax.Precision.HIGHEST


def shifted(shard, axis, by):
    length = lax.axis_size(axis)
    pairs = [(i, i + by) for i in range(length) if 0 <= i + by < length]
    return lax.ppermute(shard, axis, pairs)


def segment_ids(seq_lengths, first, count, micro):
    places = first + jnp.arange(count, dtype=jnp.int32)
    starts = jnp.cumsum(seq_lengths, axis=-1) - seq_lengths
    short_ids = (
        jnp.sum((starts[:, None, :] <= places[None, :, None]).astype(jnp.int32), axis=-1) - 1
    )
    long_ids = jnp.zeros((micro - seq_lengths.shape[0], count), jnp.int32)
    labels = jnp.concatenate([short_ids, long_ids], axis=0)
    return jnp.where(places[None, :] >= 0, labels, -1)


def rms_scale(values, gain):
    return values * lax.rsqrt(jnp.mean(values * values, axis=-1, keepdims=True) + EPSILON) * gain


def conv_silu(extended, weight, bias, labels):
    taps = weight.shape[0]
    count = extended.shape[0] - taps + 1
    own = labels[taps - 1 :]
    total = bias + weight[0] * extended[taps - 1 :]
    for shift in range(1, taps):
        first = taps - 1 - shift
        mask = (labels[first : first + count] == own).astype(extended.dtype)
        total = total + weight[shift] * extended[first : first + count] * mask[:, None]
    return jax.nn.silu(total)


def step_sizes(delta_pre, dt_bias, a_log):
    delta = jax.nn.softplus(delta_pre + dt_bias[:, None])
    return (delta, -jnp.exp(a_log)[:, None] * delta)


DEAD = -1e30
EXCHANGE_COST = 100_000_000_000
FINISH_LIMIT = 60 * 1024 * 1024
GROUP = 4


def exchange_kernel(length, reverse, orders, jobs, head_dim, log_ref, *refs):
    refs = list(refs)
    if head_dim:
        front_ins = [refs.pop(0) for _ in range(8)]
    else:
        part_ref = refs.pop(0)
    sources = [refs.pop(0) for _ in range(2 if orders else 0)]
    job_refs = [[refs.pop(0) for _ in range(job[2])] for job in jobs]
    out_ref = refs.pop(0)
    if head_dim:
        low_ref = refs.pop(0)
    steps = []
    for (make, plan, _), inputs in zip(jobs, job_refs):
        more = [low_ref] if make is intra_steps else []
        steps += make(inputs + more, refs.pop(0), plan)
    targets = [refs.pop(0) for _ in range(4 * len(orders))]
    (
        parts,
        logs,
        edge_in,
        edge_out,
        given,
        part_send,
        part_recv,
        log_send,
        log_recv,
        edge_send,
        edge_recv,
        given_send,
        given_recv,
        stage_sem,
        place_sem,
        staged,
        *front_keeps,
    ) = refs
    if head_dim:
        part_ref = front_keeps.pop(0)
    me = lax.axis_index("seq")
    bits = (length - 1).bit_length()
    placed = arrange_copies(bits, orders, me, staged, targets, place_sem)
    stages = [
        pltpu.make_async_copy(source, staged.at[k], stage_sem.at[k])
        for k, source in enumerate(sources)
    ]
    for copy in stages:
        copy.start()
    rank = lax.rem(me, GROUP)
    plane = me // GROUP
    first = me - rank
    mates = (
        rank + 1 - 2 * lax.rem(rank, 2),
        rank + 2 - 4 * (rank // 2),
        3 - rank,
    )
    micro = parts.shape[0]
    planes = length // GROUP
    begins, ends = plane == 0, plane == planes - 1
    if reverse:
        begins, ends = ends, begins
    onward = -GROUP if reverse else GROUP

    barrier = pltpu.get_barrier_semaphore()
    for mate in mates:
        pl.semaphore_signal(
            barrier, inc=1, device_id={"seq": first + mate}, device_id_type=pl.DeviceIdType.MESH
        )

    @pl.when(plane > 0)
    def _():
        pl.semaphore_signal(
            barrier, inc=1, device_id={"seq": me - GROUP}, device_id_type=pl.DeviceIdType.MESH
        )

    @pl.when(plane < planes - 1)
    def _():
        pl.semaphore_signal(
            barrier, inc=1, device_id={"seq": me + GROUP}, device_id_type=pl.DeviceIdType.MESH
        )

    above = jnp.where(plane < planes - 1, 1, 0)
    below = jnp.where(plane > 0, 1, 0)
    pl.semaphore_wait(barrier, 3 + above + below)

    def remote(src, dst, send, recv, target):
        return pltpu.make_async_remote_copy(
            src_ref=src,
            dst_ref=dst,
            send_sem=send,
            recv_sem=recv,
            device_id={"seq": target},
            device_id_type=pl.DeviceIdType.MESH,
        )

    def log_copy(slot):
        mate = mates[slot]
        return remote(
            log_ref.at[mate], logs.at[rank], log_send.at[slot], log_recv.at[slot], first + mate
        )

    quarter = edge_in.shape[2]

    def own_columns(place):
        return pl.ds(pl.multiple_of(place * quarter, quarter), quarter)

    def part_copy(m, slot):
        mate = mates[slot]
        return remote(
            part_ref.at[m, :, own_columns(mate)],
            parts.at[m, rank],
            part_send.at[m, slot],
            part_recv.at[m, slot],
            first + mate,
        )

    def edge_copy(m):
        return remote(edge_out.at[m], edge_in.at[m], edge_send.at[m], edge_recv.at[m], me + onward)

    def given_copy(m, slot):
        mate = mates[slot]
        return remote(
            given.at[m, mate],
            out_ref.at[m, :, own_columns(rank)],
            given_send.at[m, slot],
            given_recv.at[m, slot],
            first + mate,
        )

    for slot in range(3):
        log_copy(slot).start()
    def front_body(x, halo, weight, bias, b, tail, low):
        m = pl.program_id(0)
        front_kernel(
            head_dim,
            front_ins[0],
            front_ins[1],
            x,
            halo,
            weight,
            bias,
            b,
            tail,
            low,
            part_ref.at[pl.ds(m, 1)],
            *front_keeps,
        )
        for slot in range(3):
            part_copy(m, slot).start()

    if head_dim:
        x_ref, halo_ref, weight_ref, bias_ref, b_ref, tail_ref = front_ins[2:]
        by_micro = lambda shape: pl.BlockSpec((1,) + shape[1:], lambda m: (m, 0, 0))
        fixed = lambda shape: pl.BlockSpec(shape, lambda m: (0, 0))
        pltpu.emit_pipeline(
            front_body,
            grid=(micro,),
            in_specs=[
                pl.BlockSpec((1, 1) + x_ref.shape[2:], lambda m: (1, m, 0, 0)),
                by_micro(halo_ref.shape),
                fixed(weight_ref.shape),
                fixed(bias_ref.shape),
                by_micro(b_ref.shape),
                by_micro(tail_ref.shape),
            ],
            out_specs=[by_micro(low_ref.shape)],
        )(x_ref, halo_ref, weight_ref, bias_ref, b_ref, tail_ref, low_ref)
    else:
        for m in range(micro):
            for slot in range(3):
                part_copy(m, slot).start()
    logs[rank] = log_ref[rank]
    for m in range(micro):
        parts[m, rank] = part_ref[m, :, own_columns(rank)]

    @pl.when(begins)
    def _():
        edge_in[...] = jnp.zeros_like(edge_in)

    for copy in stages:
        copy.wait()
    for copy in placed:
        copy.start()
    for slot in range(3):
        log_copy(slot).wait()
    order = tuple(reversed(range(GROUP))) if reverse else tuple(range(GROUP))
    for m in range(micro):
        for step in steps[m * len(steps) // micro : (m + 1) * len(steps) // micro]:
            step()
        for slot in range(3):
            part_copy(m, slot).wait()
        factors = [jnp.exp(logs[t, m : m + 1, :]) for t in order]
        whole = jnp.exp(sum(logs[t, m : m + 1, :] for t in order))
        total = parts[m, order[0]]
        for t, factor in zip(order[1:], factors[1:]):
            total = total * factor + parts[m, t]

        @pl.when(jnp.logical_not(begins))
        def _():
            edge_copy(m).wait_recv()

        @pl.when(jnp.logical_not(ends))
        def _():
            edge_out[m] = total + whole * edge_in[m]
            edge_copy(m).start()

        running = edge_in[m]
        for place, (t, factor) in enumerate(zip(order, factors)):
            given[m, t] = running
            if place < GROUP - 1:
                running = running * factor + parts[m, t]
        for slot in range(3):
            given_copy(m, slot).start()
        out_ref[m, :, own_columns(rank)] = given[m, rank]
    for m in range(micro):
        for slot in range(3):
            given_copy(m, slot).wait()

        @pl.when(jnp.logical_not(ends))
        def _():
            edge_copy(m).wait_send()

    for copy in placed:
        copy.wait()


def exchange(parts, logs, reverse, sources=(), orders=(), jobs=(), head_dim=0):
    if head_dim:
        state_shape = (parts[6].shape[0], parts[6].shape[2], parts[2].shape[3])
        low_shape = parts[2].shape[1:]
    else:
        state_shape = parts.shape
    micro, rows, columns = state_shape
    quarter = columns // GROUP
    length = lax.axis_size("seq")
    spread = logs.reshape(micro, GROUP, quarter).transpose(1, 0, 2)
    shape = (micro, GROUP, rows, quarter)
    arranged = []
    for source in sources:
        half = jax.ShapeDtypeStruct((source.shape[0], source.shape[1] // 2), source.dtype)
        arranged += [half] * (2 * len(orders))
    vmem = pl.BlockSpec(memory_space=pltpu.VMEM)
    hbm = pl.BlockSpec(memory_space=pl.ANY)
    made = [jax.ShapeDtypeStruct(job[3], jnp.float32) for job in jobs]
    results = len(made)
    count = len(arranged)
    arranged = made + arranged
    job_inputs = [item for job in jobs for item in job[2]]
    plans = tuple((job[0], job[1], len(job[2])) for job in jobs)
    smem = pl.BlockSpec(memory_space=pltpu.SMEM)
    job_specs = [smem if item.dtype == jnp.int32 else hbm for item in job_inputs]
    out, *arranged = pl.pallas_call(
        functools.partial(exchange_kernel, length, reverse, orders, plans, head_dim),
        out_shape=[jax.ShapeDtypeStruct(state_shape, jnp.float32)]
        + ([jax.ShapeDtypeStruct(low_shape, jnp.bfloat16)] if head_dim else [])
        + arranged,
        in_specs=[vmem]
        + ([smem, smem] + [hbm] * 6 if head_dim else [vmem])
        + [hbm] * len(sources)
        + job_specs,
        out_specs=[vmem] + [hbm] * (len(arranged) + (1 if head_dim else 0)),
        scratch_shapes=[
            pltpu.VMEM(shape, jnp.float32),
            pltpu.VMEM((GROUP, micro, quarter), jnp.float32),
            pltpu.VMEM((micro, rows, quarter), jnp.float32),
            pltpu.VMEM((micro, rows, quarter), jnp.float32),
            pltpu.VMEM(shape, jnp.float32),
            pltpu.SemaphoreType.DMA((micro, 3)),
            pltpu.SemaphoreType.DMA((micro, 3)),
            pltpu.SemaphoreType.DMA((3,)),
            pltpu.SemaphoreType.DMA((3,)),
            pltpu.SemaphoreType.DMA((micro,)),
            pltpu.SemaphoreType.DMA((micro,)),
            pltpu.SemaphoreType.DMA((micro, 3)),
            pltpu.SemaphoreType.DMA((micro, 3)),
            pltpu.SemaphoreType.DMA((2,)),
            pltpu.SemaphoreType.DMA((max(count, 1) * max(length // 2, 1),)),
            pltpu.VMEM((2,) + sources[0].shape if sources else (2, 16, 128), jnp.bfloat16),
        ]
        + (
            [
                pltpu.VMEM(state_shape, jnp.float32),
                pltpu.VMEM((low_shape[1] + 8, columns), jnp.float32),
                pltpu.VMEM(low_shape[1:], jnp.bfloat16),
                pltpu.VMEM(low_shape[1:], jnp.bfloat16),
            ]
            if head_dim
            else []
        ),
        compiler_params=pltpu.CompilerParams(
            collective_id=1 if reverse else 0,
            has_side_effects=True,
            vmem_limit_bytes=FINISH_LIMIT,
        ),
        cost_estimate=pl.CostEstimate(
            flops=EXCHANGE_COST, bytes_accessed=0, transcendentals=0
        ),
        name="exchange_back" if reverse else "exchange",
    )(spread, *(parts if head_dim else (parts,)), *sources, *job_inputs)
    if head_dim:
        out = (out, arranged.pop(0))
    return out, arranged[:results], arranged[results:]


def xor_permute(value, axis, bit):
    size = lax.axis_size(axis)
    return lax.ppermute(value, axis, [(i, i ^ (1 << bit)) for i in range(size)])


def axis_bits(axis):
    return (lax.axis_size(axis) - 1).bit_length()


def own_bit(axis, bit):
    return lax.rem(lax.axis_index(axis) // (1 << bit), 2)


def all_sum(value, axis):
    for bit in range(axis_bits(axis)):
        value = value + xor_permute(value, axis, bit)
    return value


def scatter_plans(columns, bits):
    if bits < 3 or columns % 2048:
        return [[(tuple(range(bits)), (columns,))]] * 3
    rest = tuple(range(3, bits))
    unit = columns // 16
    orders = ((0, 1, 2), (1, 0, 2), (2, 0, 1), (2, 1, 0))
    shares = (
        ((3, 3), (2, 3), (3, 0), (0, 2)),
        ((3, 2), (3, 3), (3, 0), (0, 2)),
        ((4, 1), (2, 2), (3, 1), (2, 1)),
    )
    return [
        [
            (order + rest, tuple(unit * count for count in counts))
            for order, counts in zip(orders, share)
        ]
        for share in shares
    ]


def arranged_place(order, position, bits):
    return [(position >> (bits - 1 - t)) & 1 for t, _ in sorted(enumerate(order), key=lambda p: p[1])]


def arranged_block(order, position, bits, me):
    flips = arranged_place(order, position, bits)
    total = 0
    for bit, flip in enumerate(flips):
        mine = lax.rem(me // (1 << bit), 2)
        total = total + (1 << bit) * ((1 - mine) if flip else mine)
    return total


def arrange(left, orders):
    bits = axis_bits("seq")
    size = 1 << bits
    tokens, width = left.shape
    view = left.reshape(tokens, size, width // size)
    me = lax.axis_index("seq").astype(jnp.int32)
    results = []
    for order in orders:
        table = jnp.stack([arranged_block(order, j, bits, me) for j in range(size)])
        chosen = jnp.take(view, table, axis=1).reshape(tokens, width)
        results += [chosen[:, width // 2 :], chosen[:, : width // 2]]
    return results


def arrange_copies(bits, orders, me, staged, targets, sem):
    copies, number = [], 0
    half = 1 << (bits - 1)
    for source in range(len(targets) // (2 * len(orders)) if orders else 0):
        block = staged.shape[2] >> bits
        for order in orders:
            for begin in (half, 0):
                target = targets[number]
                for j in range(half):
                    place = arranged_block(order, begin + j, bits, me)
                    first = pl.multiple_of(place * block, block)
                    copies.append(
                        pltpu.make_async_copy(
                            staged.at[source, :, pl.ds(first, block)],
                            target.at[:, pl.ds(j * block, block)],
                            sem.at[number * half + j],
                        )
                    )
                number += 1
    return copies


def product(left, right):
    return lax.dot_general(left, right, (TN, ((), ())), preferred_element_type=jnp.float32)


def part_columns(parts):
    first, columns = 0, []
    for _, widths in parts:
        columns.append(pl.ds(first, sum(widths)))
        first += sum(widths)
    return columns


def product_steps(inputs, out_ref, parts):
    count = len(parts)
    lefts, right_ref, more = inputs[:count], inputs[count], inputs[count + 1 :]
    return [
        functools.partial(
            product_step, lefts[k], right_ref, more[k : k + 1], out_ref, columns.start, columns.size
        )
        for k, columns in enumerate(part_columns(parts))
    ]


def product_step(left_ref, right_ref, more, out_ref, first, width):
    tokens, rows = left_ref.shape
    tile = min(rows, 256)
    columns = pl.ds(first, width)

    def body(left, right, *rest):
        value = product(left[...], right[...])
        for item in rest[:-1]:
            value = value + item[...]
        rest[-1][...] = value

    tiled = pl.BlockSpec((tile, width), lambda i: (i, 0))
    pltpu.emit_pipeline(
        body,
        grid=(rows // tile,),
        in_specs=[
            pl.BlockSpec((tokens, tile), lambda i: (0, i)),
            pl.BlockSpec((tokens, width), lambda i: (0, 0)),
        ]
        + [tiled] * len(more),
        out_specs=[tiled],
    )(
        left_ref,
        right_ref.at[:, columns],
        *more,
        out_ref.at[:, columns],
    )


def plain_steps(inputs, out_ref, parts):
    left_ref, right_ref = inputs
    width = min(right_ref.shape[1], 512)
    return [
        functools.partial(plain_step, left_ref, right_ref, out_ref, first, width)
        for first in range(0, right_ref.shape[1], width)
    ]


def plain_step(left_ref, right_ref, out_ref, first, width):
    rows, depth = left_ref.shape
    tile = min(rows, 256)
    columns = pl.ds(first, width)

    def body(left, right, out):
        out[...] = low_dot(left[...], right[...], NN)

    pltpu.emit_pipeline(
        body,
        grid=(rows // tile,),
        in_specs=[
            pl.BlockSpec((tile, depth), lambda i: (i, 0)),
            pl.BlockSpec((depth, width), lambda i: (0, 0)),
        ],
        out_specs=[pl.BlockSpec((tile, width), lambda i: (i, 0))],
    )(left_ref, right_ref.at[:, columns], out_ref.at[:, columns])


def share_steps(inputs, out_refs, parts):
    left_ref, right_ref = inputs
    share = right_ref.shape[0] // 2
    mine = lax.axis_index("head") * share
    return [
        functools.partial(share_step, left_ref, right_ref, out_ref, first, share)
        for out_ref, first in zip(out_refs, (share - mine, mine))
    ]


def share_step(left_ref, right_ref, out_ref, first, share):
    rows, depth = left_ref.shape
    tile = min(rows, 256)
    width = min(share, 512)
    chosen = right_ref.at[pl.ds(pl.multiple_of(first, share), share)]

    def body(left, right, out):
        out[...] = low_dot(left[...], right[...], NT)

    pltpu.emit_pipeline(
        body,
        grid=(share // width, rows // tile),
        in_specs=[
            pl.BlockSpec((tile, depth), lambda j, i: (i, 0)),
            pl.BlockSpec((width, depth), lambda j, i: (j, 0)),
        ],
        out_specs=[pl.BlockSpec((tile, width), lambda j, i: (i, j))],
    )(left_ref, chosen, out_ref)


def row_step(grad_ref, weight_ref, narrow_ref, map_ref, step_ref, out_ref, first, rows):
    depth, halves, width = weight_ref.shape
    tile = min(depth, 256)

    def inner(held, sem):
        copy = pltpu.make_async_copy(grad_ref.at[:, pl.ds(first, rows)], held, sem)
        copy.start()
        copy.wait()

        def body(weight, narrow, map_weight, step_weight, out):
            turned_weight = jnp.swapaxes(weight[...], 0, 1)
            maps = map_weight.shape[1]
            high, rest = halves_of(narrow[...])
            total = low_dot(high[:, :maps], map_weight[...], NT) + low_dot(
                rest[:, :maps], map_weight[...], NT
            )
            total = total + low_dot(high[:, maps:], step_weight[...], NT)
            total = total + low_dot(rest[:, maps:], step_weight[...], NT)
            for half in range(halves):
                total = total + low_dot(held[half], turned_weight[half], NT)
            out[...] = total

        pltpu.emit_pipeline(
            body,
            grid=(depth // tile,),
            in_specs=[
                pl.BlockSpec((tile, halves, width), lambda j: (j, 0, 0)),
                pl.BlockSpec((rows, narrow_ref.shape[1]), lambda j: (0, 0)),
                pl.BlockSpec((tile, map_ref.shape[1]), lambda j: (j, 0)),
                pl.BlockSpec((tile, step_ref.shape[1]), lambda j: (j, 0)),
            ],
            out_specs=[pl.BlockSpec((rows, tile), lambda j: (0, j))],
        )(
            weight_ref,
            narrow_ref.at[pl.ds(first, rows)],
            map_ref,
            step_ref,
            out_ref.at[pl.ds(first, rows)],
        )

    pl.run_scoped(
        inner,
        pltpu.VMEM((halves, rows, width), jnp.bfloat16),
        pltpu.SemaphoreType.DMA,
    )


def token_step(
    gain_ref, gain_sum, tokens_ref, cot_ref, rows_refs, kept_ref, other_ref, grad_ref, block_ref
):
    count, width = tokens_ref.shape
    share = width // 2
    tile = min(count, 128)
    mine = lax.axis_index("head") == 0
    gain_sum[...] = jnp.zeros_like(gain_sum)

    def body(tokens, cot, own, other, kept, arrived, grad, block):
        values = tokens[...].astype(jnp.float32)
        pulls = own[...] + other[...]
        scale = lax.rsqrt(jnp.mean(values * values, axis=1, keepdims=True) + EPSILON)
        gained = pulls * gain_ref[...]
        cross = jnp.sum(gained * values, axis=1, keepdims=True)
        grad[...] = (
            cot[...].astype(jnp.float32)
            + gained * scale
            - values * (scale * scale * scale * cross * (1.0 / width))
        )
        parts = (pulls * values * scale).reshape(tile // 8, 8, width)
        gain_sum[...] = gain_sum[...] + jnp.sum(parts, axis=0)
        residual = jnp.where(mine, values[:, :share], values[:, share:])
        block[...] = (residual + kept[...] + arrived[...]).astype(jnp.bfloat16)

    full = pl.BlockSpec((tile, width), lambda i: (i, 0))
    half = pl.BlockSpec((tile, share), lambda i: (i, 0))
    pltpu.emit_pipeline(
        body,
        grid=(count // tile,),
        in_specs=[full] * 4 + [half] * 2,
        out_specs=[full, half],
    )(tokens_ref, cot_ref, *rows_refs, kept_ref, other_ref, grad_ref, block_ref)


def finish_kernel(plans, paired, bits, blocks, *refs):
    refs = list(refs)
    mats, parts = len(plans), plans[-1]
    take = lambda count: [refs.pop(0) for _ in range(count)]
    ins = [take(2 * len(parts) + 1) for _ in range(mats - 1)]
    last_sent, last_kept = take(len(parts)), take(len(parts))
    grad_ref, narrow_ref, vector_ref = take(3)
    if paired:
        weight_ref, gain_ref, tokens_ref, cot_ref = take(4)
        narrow_row_ref, map_ref, step_ref, gated_ref, out_weight_ref = take(5)
    outs = take(mats)
    gathered_ref, vector_out_ref = take(2)
    if paired:
        token_grad_ref, block_ref, row_ref, row_other_ref = take(4)
        share_sent_ref, share_kept_ref, share_other_ref = take(3)
    sent_ref, arrived_ref = take(2)
    made_refs = take(mats)
    me = lax.axis_index("seq")
    last_right = grad_ref.at[grad_ref.shape[0] - 1]
    columns_of = part_columns(parts)
    ins.append(last_kept + [last_right] + [arrived_ref.at[:, columns] for columns in columns_of])

    def partner(bit):
        return me + (1 << bit) * (1 - 2 * lax.rem(me // (1 << bit), 2))

    waves = []
    piece_count = len(parts[0][1])
    chain_count = 0
    for mat in range(mats):
        for piece in range(piece_count):
            wave, first = [], 0
            for order, widths in plans[mat]:
                if widths[piece]:
                    place = first + sum(widths[:piece])
                    keep = refs.pop(0)
                    recvs = take(bits - 1)
                    wave.append(
                        (chain_count, made_refs[mat], place, outs[mat], place, order[1:], keep, recvs)
                    )
                    chain_count += 1
                first += sum(widths)
            waves.append(wave)
    narrow_order = parts[0][0]
    narrow = (chain_count, narrow_ref, 0, None, 0, narrow_order, refs.pop(0), take(bits))
    vector_sums, vector_recvs, gain_sum, local_sem, send_sem, recv_sem = refs

    barrier = pltpu.get_barrier_semaphore()
    for bit in range(bits):
        pl.semaphore_signal(
            barrier,
            inc=1,
            device_id={"seq": partner(bit)},
            device_id_type=pl.DeviceIdType.MESH,
        )
    if paired:
        pl.semaphore_signal(
            barrier,
            inc=1,
            device_id={"head": 1 - lax.axis_index("head")},
            device_id_type=pl.DeviceIdType.MESH,
        )
    pl.semaphore_wait(barrier, bits + (1 if paired else 0))

    numbers = {}

    def remote_to(key, src, dst, target):
        number = numbers.setdefault(key, len(numbers))
        return pltpu.make_async_remote_copy(
            src_ref=src,
            dst_ref=dst,
            send_sem=send_sem.at[number],
            recv_sem=recv_sem.at[number],
            device_id=target,
            device_id_type=pl.DeviceIdType.MESH,
        )

    def remote(key, src, dst, bit):
        return remote_to(key, src, dst, {"seq": partner(bit)})

    def first_copy(k):
        region = (slice(None), columns_of[k])
        return remote(("first", k), sent_ref.at[region], arrived_ref.at[region], parts[k][0][0])

    def share_copy():
        return remote_to(
            "share", share_sent_ref, share_other_ref, {"head": 1 - lax.axis_index("head")}
        )

    def shares(part):
        share_steps(
            (gated_ref, out_weight_ref), (share_sent_ref, share_kept_ref), ()
        )[part]()
        if part == 0:
            share_copy().start()

    def row_copy():
        return remote_to("row", row_ref, row_other_ref, {"head": 1 - lax.axis_index("head")})

    def local_copy(chain):
        number, source, first, _, _, _, keep, _ = chain
        rows, columns = keep.shape
        return pltpu.make_async_copy(
            source.at[pl.ds(0, rows), pl.ds(first, columns)], keep, local_sem.at[number]
        )

    def chain_copy(chain, phase):
        number, source, first, _, _, order, keep, recvs = chain
        rows, columns = recvs[phase].shape
        if phase == 0:
            region = source.at[pl.ds(rows, rows), pl.ds(first, columns)]
        else:
            region = keep.at[pl.ds(rows, rows)]
        return remote((number, phase), region, recvs[phase], order[phase])

    made = set()

    def make(mat):
        if mat in made:
            return
        made.add(mat)
        if mat == mats - 1:
            for k in range(len(parts)):
                first_copy(k).wait_recv()
        for step in product_steps(ins[mat], made_refs[mat], plans[mat]):
            step()

    def begin(number):
        make(number // piece_count)
        for chain in waves[number]:
            chain_copy(chain, 0).start()
            local_copy(chain).start()

    def advance(chain, phase):
        if phase == 0:
            local_copy(chain).wait()
        chain_copy(chain, phase).wait_recv()
        number, _, _, out, place, order, keep, recvs = chain
        recv = recvs[phase]
        rows = recv.shape[0]
        slab = min(rows, 32)

        @pl.loop(0, rows // slab)
        def _(step):
            cut = pl.ds(pl.multiple_of(step * slab, slab), slab)
            keep[cut, :] = keep[cut, :] + recv[cut, :]

        if phase + 1 < len(order):
            chain_copy(chain, phase + 1).start()
        elif out is not None:
            out[:, place : place + keep.shape[1]] = keep[0:blocks, :]

    def vector_copy(phase):
        return remote(("vector", phase), vector_sums.at[phase], vector_recvs.at[phase], phase)

    def begin_vector():
        vector_sums[0] = vector_ref[...]
        if paired:
            total = jnp.sum(gain_sum[...], axis=0, keepdims=True)
            for place in range(total.shape[1] // 128):
                vector_sums[0, place : place + 1, :] = total[:, place * 128 : place * 128 + 128]
        vector_copy(0).start()

    def advance_vector(phase):
        vector_copy(phase).wait_recv()
        total = vector_sums[phase] + vector_recvs[phase]
        if phase + 1 < bits:
            vector_sums[phase + 1] = total
            vector_copy(phase + 1).start()
        else:
            vector_out_ref[...] = total

    gather_bits = tuple(reversed(range(bits)))

    def gather_copies(phase):
        free = gather_bits[:phase]
        fixed = sum(
            (1 << bit) * lax.rem(me // (1 << bit), 2) for bit in range(bits) if bit not in free
        )
        copies = []
        for number in range(1 << phase):
            block = fixed + sum(
                (1 << bit) * ((number >> place) & 1) for place, bit in enumerate(free)
            )
            region = gathered_ref.at[block]
            copies.append(remote(("gather", phase, number), region, region, gather_bits[phase]))
        return copies

    def narrow_halving(phase):
        advance(narrow, phase)
        if phase + 1 == bits:
            gathered_ref[me] = narrow[6][0 : gathered_ref.shape[1], :]
            for copy in gather_copies(0):
                copy.start()

    def narrow_gather(phase):
        for copy in gather_copies(phase):
            copy.wait_recv()
        if phase + 1 < bits:
            for copy in gather_copies(phase + 1):
                copy.start()

    def rows(part):
        count = row_ref.shape[0] // 2
        row_step(
            grad_ref,
            weight_ref,
            narrow_row_ref,
            map_ref,
            step_ref,
            row_ref,
            part * count,
            count,
        )
        if part == 1:
            row_copy().start()

    def token_rows():
        row_copy().wait()
        share_copy().wait()
        token_step(
            gain_ref,
            gain_sum,
            tokens_ref,
            cot_ref,
            (row_ref, row_other_ref),
            share_kept_ref,
            share_other_ref,
            token_grad_ref,
            block_ref,
        )

    narrow_steps = [functools.partial(narrow_halving, phase) for phase in range(bits)]
    narrow_steps += [functools.partial(narrow_gather, phase) for phase in range(bits)]
    fills = {}
    vector_tick = 0
    if paired:
        fills = {
            0: [functools.partial(rows, 0)],
            1: [functools.partial(rows, 1), functools.partial(shares, 0)],
            2: [functools.partial(shares, 1)],
            3: [token_rows],
        }
        vector_tick = 4

    chain_copy(narrow, 0).start()
    local_copy(narrow).start()
    sent_steps = product_steps(last_sent + [last_right], sent_ref, parts)
    for k, step in enumerate(sent_steps):
        step()
        first_copy(k).start()
    begun = min(2, len(waves))
    for number in range(begun):
        begin(number)
    if len(waves) > begun:
        make(begun // piece_count)
    ticks = max(len(waves) + bits - 2, 2 * bits, vector_tick + bits)
    for tick in range(ticks):
        if tick < len(narrow_steps):
            narrow_steps[tick]()
        for phase in range(bits - 1):
            number = tick - phase
            if 0 <= number < len(waves):
                for chain in waves[number]:
                    advance(chain, phase)
                if phase == 0 and number + 2 < len(waves):
                    begin(number + 2)
        if tick + 3 < len(waves):
            make((tick + 3) // piece_count)
        for step in fills.get(tick, ()):
            step()
        if tick == vector_tick:
            begin_vector()
        if 0 <= tick - vector_tick < bits:
            advance_vector(tick - vector_tick)
    for k in range(len(parts)):
        first_copy(k).wait_send()
    for wave in waves:
        for chain in wave:
            for phase in range(bits - 1):
                chain_copy(chain, phase).wait_send()
    for phase in range(bits):
        chain_copy(narrow, phase).wait_send()
        vector_copy(phase).wait_send()
        for copy in gather_copies(phase):
            copy.wait_send()


def finish(plans, mats, last_sent, last_kept, grad, narrow, vector, row_inputs):
    bits = axis_bits("seq")
    size = 1 << bits
    count, parts = len(plans), plans[-1]
    paired = bool(row_inputs)
    rows = last_kept[0].shape[1]
    blocks = rows // (size // 2)
    columns = sum(sum(widths) for _, widths in parts)
    scratch, copies, chains = [], 0, 0
    for plan in plans:
        for piece in range(len(parts[0][1])):
            for _, widths in plan:
                if widths[piece]:
                    scratch.append(pltpu.VMEM((rows // 2, widths[piece]), jnp.float32))
                    for phase in range(bits - 1):
                        scratch.append(
                            pltpu.VMEM(((rows // 2) >> phase, widths[piece]), jnp.float32)
                        )
                    copies += bits - 1
                    chains += 1
    narrow_rows = narrow.shape[0] // 2
    scratch.append(pltpu.VMEM((narrow_rows, narrow.shape[1]), jnp.float32))
    for phase in range(bits):
        scratch.append(pltpu.VMEM((narrow_rows >> phase, narrow.shape[1]), jnp.float32))
    copies += 2 * bits + size - 1 + len(parts) + 2
    scratch += [pltpu.VMEM((bits,) + vector.shape, jnp.float32)] * 2
    scratch += [
        pltpu.VMEM((8, row_inputs[1].shape[1] if paired else 128), jnp.float32),
        pltpu.SemaphoreType.DMA((chains + 1,)),
        pltpu.SemaphoreType.DMA((copies,)),
        pltpu.SemaphoreType.DMA((copies,)),
    ]
    vmem, hbm = pl.BlockSpec(memory_space=pltpu.VMEM), pl.BlockSpec(memory_space=pl.ANY)
    shapes = [jax.ShapeDtypeStruct((blocks, columns), jnp.float32) for _ in range(count)]
    shapes.append(
        jax.ShapeDtypeStruct((size, narrow.shape[0] // size, narrow.shape[1]), jnp.float32)
    )
    shapes.append(jax.ShapeDtypeStruct(vector.shape, jnp.float32))
    specs = [vmem] * len(shapes)
    if paired:
        tokens = row_inputs[2]
        token_shape = jax.ShapeDtypeStruct(tokens.shape, jnp.float32)
        block_shape = jax.ShapeDtypeStruct((tokens.shape[0], tokens.shape[1] // 2), jnp.bfloat16)
        share_shape = jax.ShapeDtypeStruct(block_shape.shape, jnp.float32)
        shapes += [token_shape, block_shape, token_shape, token_shape] + [share_shape] * 3
    half = jax.ShapeDtypeStruct((rows, columns), jnp.float32)
    shapes += [half] * (2 + count)
    specs += [hbm] * (len(shapes) - len(specs))
    flat = [item for mat in mats for item in mat] + last_sent + last_kept + [grad, narrow]
    row_specs = [hbm, vmem] + [hbm] * 7 if paired else []
    results = pl.pallas_call(
        functools.partial(finish_kernel, plans, paired, bits, blocks),
        out_shape=shapes,
        in_specs=[hbm] * len(flat) + [vmem] + row_specs,
        out_specs=specs,
        scratch_shapes=scratch,
        compiler_params=pltpu.CompilerParams(
            collective_id=2, has_side_effects=True, vmem_limit_bytes=FINISH_LIMIT
        ),
        name="finish",
    )(*flat, vector, *row_inputs)
    return (
        results[:count],
        results[count],
        results[count + 1],
        *(results[count + 2 : count + 4] if paired else ()),
    )


def head_gather(block):
    if lax.axis_size("head") != 2:
        return lax.all_gather(block, "head", axis=1, tiled=True)
    other = xor_permute(block, "head", 0)
    mine = lax.axis_index("head") == 0
    return jnp.concatenate(
        [jnp.where(mine, block, other), jnp.where(mine, other, block)], axis=1
    )


HEAD_GROUP = 8
BROAD_GROUP = 32
SLAB = 16
VMEM_LIMIT = 56 * 1024 * 1024
FAR = 1 << 30
NN = ((1,), (0,))
NT = ((1,), (1,))
TN = ((0,), (0,))


def low_dot(left, right, dims):
    return lax.dot_general(
        left.astype(jnp.bfloat16),
        right.astype(jnp.bfloat16),
        (dims, ((), ())),
        preferred_element_type=jnp.float32,
    )


def halves_of(value):
    high = value.astype(jnp.bfloat16)
    return high, (value - high.astype(jnp.float32)).astype(jnp.bfloat16)


def thirds_of(value):
    first = value.astype(jnp.bfloat16).astype(jnp.float32)
    second = (value - first).astype(jnp.bfloat16).astype(jnp.float32)
    return first, second, value - first - second


def spread_matrix(heads, head_dim):
    shape = (heads, heads * head_dim)
    rows = lax.broadcasted_iota(jnp.int32, shape, 0)
    columns = lax.broadcasted_iota(jnp.int32, shape, 1)
    return (columns // head_dim == rows).astype(jnp.float32)


def turned(rows, matrix):
    return low_dot(
        jnp.concatenate(thirds_of(rows), axis=0), jnp.concatenate([matrix] * 3, axis=0), TN
    )


def head_sums(spread, value):
    high, low = halves_of(value)
    return low_dot(spread, high, NT) + low_dot(spread, low, NT)


def map_dot(left, right):
    return low_dot(
        jnp.concatenate([left, left], axis=1), jnp.concatenate(halves_of(right), axis=0), NN
    )


def fine_dot(left, right):
    left_high, left_low = halves_of(left)
    right_high, right_low = halves_of(right)
    return (
        low_dot(left_high, right_high, NT)
        + low_dot(left_high, right_low, NT)
        + low_dot(left_low, right_high, NT)
    )


def sigmoid(value):
    return 0.5 + 0.5 * jnp.tanh(0.5 * value)


def segment_of(places, starts_ref, micro):
    label = jnp.zeros_like(places)
    for number in range(starts_ref.shape[1]):
        label = label + jnp.where(places >= starts_ref[micro, number], 1, 0)
    return label


def same_segment(count, base_ref, starts_ref, taps):
    micro = pl.program_id(0)
    places = base_ref[0] + lax.broadcasted_iota(jnp.int32, (count, 1), 0)
    own = segment_of(places, starts_ref, micro)
    return [
        jnp.where(segment_of(places - shift, starts_ref, micro) == own, 1.0, 0.0)
        for shift in range(1, taps)
    ]


def pair_labels(count, base_ref, starts_ref, micro):
    column = base_ref[0] + lax.broadcasted_iota(jnp.int32, (count, 1), 0)
    row = base_ref[0] + lax.broadcasted_iota(jnp.int32, (1, count), 1)
    return segment_of(column, starts_ref, micro) == segment_of(row, starts_ref, micro)


def conv_sum(ext, value, halo, weight, bias, masks):
    count = value.shape[0]
    ext[0:8, :] = halo
    ext[8 : 8 + count, :] = value
    total = bias + weight[0:1] * value
    for shift in range(1, weight.shape[0]):
        total = (
            total
            + weight[shift : shift + 1]
            * ext[8 - shift : 8 - shift + count, :]
            * masks[shift - 1]
        )
    return total


def project_kernel(
    tokens_ref, gain_ref, weight_ref, map_ref, step_ref, normed_ref, out_ref, map_out_ref, step_out_ref
):
    count = tokens_ref.shape[0]
    slab = min(count, 64)

    @pl.when(pl.program_id(0) == 0)
    def _():
        @pl.loop(0, count // slab)
        def _(step):
            cut = pl.ds(pl.multiple_of(step * slab, slab), slab)
            values = tokens_ref[cut, :].astype(jnp.float32)
            scale = lax.rsqrt(jnp.mean(values * values, axis=1, keepdims=True) + EPSILON)
            normed_ref[cut, :] = (values * scale * gain_ref[...]).astype(jnp.bfloat16)

        map_out_ref[...] = low_dot(normed_ref[...], map_ref[...], NN)
        step_out_ref[...] = low_dot(normed_ref[...], step_ref[...], NN)

    weight = jnp.swapaxes(weight_ref[...], 0, 1)
    for half in range(weight.shape[0]):
        out_ref[half] = low_dot(normed_ref[...], weight[half], NN)


def project(tokens, gain, weight, map_weight, step_weight):
    count, width = tokens.shape
    _, halves, columns = weight.shape
    tile = min(columns, 256)
    return pl.pallas_call(
        project_kernel,
        grid=(columns // tile,),
        in_specs=[
            pl.BlockSpec((count, width), lambda j: (0, 0)),
            pl.BlockSpec((1, width), lambda j: (0, 0)),
            pl.BlockSpec((width, halves, tile), lambda j: (0, 0, j)),
            pl.BlockSpec(map_weight.shape, lambda j: (0, 0)),
            pl.BlockSpec(step_weight.shape, lambda j: (0, 0)),
        ],
        out_specs=[
            pl.BlockSpec((count, width), lambda j: (0, 0)),
            pl.BlockSpec((halves, count, tile), lambda j: (0, 0, j)),
            pl.BlockSpec((count, map_weight.shape[1]), lambda j: (0, 0)),
            pl.BlockSpec((count, step_weight.shape[1]), lambda j: (0, 0)),
        ],
        out_shape=[
            jax.ShapeDtypeStruct((count, width), jnp.bfloat16),
            jax.ShapeDtypeStruct((halves, count, columns), jnp.float32),
            jax.ShapeDtypeStruct((count, map_weight.shape[1]), jnp.float32),
            jax.ShapeDtypeStruct((count, step_weight.shape[1]), jnp.float32),
        ],
        compiler_params=pltpu.CompilerParams(vmem_limit_bytes=VMEM_LIMIT),
        cost_estimate=pl.CostEstimate(
            flops=2 * count * width * columns * halves, bytes_accessed=0, transcendentals=0
        ),
        name="project",
    )(tokens, gain[None], weight, map_weight, step_weight)


def front_kernel(
    head_dim,
    base_ref,
    starts_ref,
    x_ref,
    halo_ref,
    weight_ref,
    bias_ref,
    b_ref,
    tail_ref,
    low_ref,
    state_ref,
    ext,
    high_keep,
    rest_keep,
):
    heads = tail_ref.shape[1]
    count = x_ref.shape[2]
    weight, bias = weight_ref[...], bias_ref[...]
    masks = same_segment(count, base_ref, starts_ref, weight.shape[0])
    scale = turned(tail_ref[0], spread_matrix(heads, head_dim))
    ext[0:8, :] = halo_ref[0]
    ext[8 : 8 + count, :] = x_ref[0, 0]
    for top in range(0, count, SLAB):
        cut = slice(top, top + SLAB)
        total = bias + weight[0:1] * ext[8 + top : 8 + top + SLAB, :]
        for shift in range(1, weight.shape[0]):
            first = 8 - shift + top
            total = (
                total
                + weight[shift : shift + 1] * ext[first : first + SLAB, :] * masks[shift - 1][cut]
            )
        act = (total * sigmoid(total)).astype(jnp.bfloat16)
        low_ref[0, cut, :] = act
        high, rest = halves_of(act.astype(jnp.float32) * scale[cut])
        high_keep[cut, :] = high
        rest_keep[cut, :] = rest
    state_ref[0] = low_dot(b_ref[0], high_keep[...], TN) + low_dot(b_ref[0], rest_keep[...], TN)


def intra_block(head_dim, valid, x, b, c, run_row, step_row, skip):
    heads, count = run_row.shape
    spread = spread_matrix(heads, head_dim)
    scores = jnp.where(valid, low_dot(c, b, NT), 0.0)
    wide = x.astype(jnp.float32)
    scaled = (wide * turned(step_row, spread)).astype(jnp.bfloat16)
    run = turned(run_row, spread_matrix(heads, 1))
    pair = 2 * head_dim
    middle = count // 2
    lane = lax.broadcasted_iota(jnp.int32, (count, pair), 1)
    results = []
    for first in range(0, heads, 2):
        block = scaled[:, first * head_dim : first * head_dim + pair]
        halves = []
        for head in (first, first + 1):
            strips = []
            for top, cut in ((0, middle), (middle, count)):
                gap = run[top:cut, head : head + 1] - run_row[head : head + 1, :cut]
                weights = jnp.exp2(jnp.minimum(gap, 0.0)) * scores[top:cut, :cut]
                strips.append(low_dot(weights, block[:cut], NN))
            halves.append(jnp.concatenate(strips, axis=0))
        results.append(jnp.where(lane < head_dim, halves[0], halves[1]))
    return jnp.concatenate(results, axis=1) + skip * wide


def intra_steps(inputs, out_ref, head_dim):
    return [
        functools.partial(intra_step, inputs, out_ref, head_dim, micro)
        for micro in range(out_ref.shape[0])
    ]


def intra_step(inputs, out_ref, head_dim, micro):
    base_ref, starts_ref, b_ref, c_ref, run_ref, step_ref, skip_ref, x_ref = inputs
    _, count, inner = x_ref.shape
    heads = run_ref.shape[1]
    group = min(HEAD_GROUP, heads)
    wide = group * head_dim

    def body(x, b, c, run, step, skip, out):
        rows = lax.broadcasted_iota(jnp.int32, (count, count), 0)
        columns = lax.broadcasted_iota(jnp.int32, (count, count), 1)
        valid = pair_labels(count, base_ref, starts_ref, micro) & (rows >= columns)
        out[...] = intra_block(
            head_dim, valid, x[...], b[...], c[...], run[...], step[...], skip[...]
        )

    token = pl.BlockSpec((count, wide), lambda k: (0, k))
    maps = pl.BlockSpec((count, b_ref.shape[2]), lambda k: (0, 0))
    row = pl.BlockSpec((group, count), lambda k: (k, 0))
    pltpu.emit_pipeline(
        body,
        grid=(inner // wide,),
        in_specs=[token, maps, maps, row, row, pl.BlockSpec((1, wide), lambda k: (0, k))],
        out_specs=[token],
    )(
        x_ref.at[micro],
        b_ref.at[micro],
        c_ref.at[micro],
        run_ref.at[micro],
        step_ref.at[micro],
        skip_ref,
        out_ref.at[micro],
    )


def gate_kernel(
    head_dim,
    full,
    bits,
    intra_ref,
    c_ref,
    carry_ref,
    begin_ref,
    gate_ref,
    cot_ref,
    gain_ref,
    norm_ref,
    grad_gate_ref,
    both_ref,
    grad_mixed_ref,
    start_ref,
    rows_ref,
    mixed_keep,
    gate_keep,
    cot_keep,
    high_keep,
    rest_keep,
    both_keep,
    sums,
    sums_in,
    send_sem,
    recv_sem,
):
    stage, micro, number = pl.program_id(0), pl.program_id(1), pl.program_id(2)
    groups = pl.num_programs(2)
    heads = carry_ref.shape[1]
    place = micro * groups + number
    carry = turned(carry_ref[0], spread_matrix(heads, head_dim))
    mine = lax.axis_index("head")

    def partner(bit):
        return {"head": mine + (1 << bit) * (1 - 2 * lax.rem(mine // (1 << bit), 2))}

    @pl.when((stage == 0) & (place == 0))
    def _():
        barrier = pltpu.get_barrier_semaphore()
        for bit in range(bits):
            pl.semaphore_signal(
                barrier, inc=1, device_id=partner(bit), device_id_type=pl.DeviceIdType.MESH
            )
        pl.semaphore_wait(barrier, bits)

    @pl.when(stage == 0)
    def _():
        inter = map_dot(c_ref[0], begin_ref[0])
        gain = gain_ref[...]
        for top in range(0, inter.shape[0], SLAB):
            cut = slice(top, top + SLAB)
            mixed = intra_ref[0, cut, :] + inter[cut] * carry[cut]
            gate, cot = gate_ref[0, 0, cut, :], cot_ref[0, cut, :]
            mixed_keep[place, cut, :] = mixed
            gate_keep[place, cut, :] = gate
            cot_keep[place, cut, :] = cot
            gated = mixed * (gate * sigmoid(gate))
            square = jnp.sum(gated * gated, axis=1, keepdims=True)
            cross = jnp.sum(cot * gain * gated, axis=1, keepdims=True)
            lane = lax.broadcasted_iota(jnp.int32, (SLAB, 128), 1)
            both_keep[cut, :] = jnp.where(lane == 0, square, jnp.where(lane == 1, cross, 0.0))

        @pl.when(number == 0)
        def _():
            sums[0, micro] = both_keep[...]

        @pl.when(number > 0)
        def _():
            sums[0, micro] = sums[0, micro] + both_keep[...]

    @pl.when((stage == 1) & (place == 0))
    def _():
        for bit in range(bits):
            copy = pltpu.make_async_remote_copy(
                src_ref=sums.at[bit],
                dst_ref=sums_in.at[bit],
                send_sem=send_sem.at[bit],
                recv_sem=recv_sem.at[bit],
                device_id=partner(bit),
                device_id_type=pl.DeviceIdType.MESH,
            )
            copy.start()
            copy.wait()
            sums[bit + 1] = sums[bit] + sums_in[bit]

    @pl.when(stage == 1)
    def _():
        gain = gain_ref[...]
        gains = jnp.zeros((8, gain.shape[1]), jnp.float32)
        for top in range(0, carry.shape[0], SLAB):
            cut = slice(top, top + SLAB)
            mixed, gate = mixed_keep[place, cut, :], gate_keep[place, cut, :]
            cot = cot_keep[place, cut, :]
            total = sums[bits, micro, cut, :]
            scale = lax.rsqrt(total[:, 0:1] / full + EPSILON)
            pull = scale * scale * scale * total[:, 1:2] / full
            sigma = sigmoid(gate)
            act = gate * sigma
            gated = mixed * act
            unit = gated * scale
            norm_ref[0, cut, :] = (unit * gain).astype(jnp.bfloat16)
            grad_gated = cot * gain * scale - gated * pull
            grad_gate = grad_gated * mixed * sigma * (1.0 + gate * (1.0 - sigma))
            grad_gate = grad_gate.astype(jnp.bfloat16)
            grad_gate_ref[0, cut, :] = grad_gate
            both_ref[0, 0, cut, :] = grad_gate
            grad_mixed = (grad_gated * act).astype(jnp.bfloat16)
            grad_mixed_ref[0, cut, :] = grad_mixed
            high, rest = halves_of(grad_mixed.astype(jnp.float32) * carry[cut])
            high_keep[cut, :] = high
            rest_keep[cut, :] = rest
            parts = (cot * unit).reshape(SLAB // 8, 8, cot.shape[1])
            gains = gains + jnp.sum(parts, axis=0)
        c = c_ref[0]
        start_ref[0] = low_dot(c, high_keep[...], TN) + low_dot(c, rest_keep[...], TN)
        rows_ref[0] = gains


def back_kernel(
    head_dim,
    plans,
    base_ref,
    starts_ref,
    x_ref,
    g_ref,
    b_ref,
    c_ref,
    run_ref,
    step_ref,
    carry_ref,
    tail_ref,
    start_ref,
    end_ref,
    pre_ref,
    halo_ref,
    weight_ref,
    bias_ref,
    skip_ref,
    both_in_ref,
    out_sent_ref,
    gate_sent_ref,
    both_ref,
    edge_ref,
    halo_out_ref,
    rows_ref,
    direct_ref,
    decay_ref,
    grad_b_ref,
    grad_c_ref,
    *refs,
):
    refs = list(refs)
    ext, moved, send_sem, recv_sem = refs[-4:]
    me = lax.axis_index("seq")

    def partner(bit):
        return me + (1 << bit) * (1 - 2 * lax.rem(me // (1 << bit), 2))

    def sends():
        copies = []
        for plan, source in zip(plans, (out_sent_ref, gate_sent_ref)):
            for (order, _), columns in zip(plan, part_columns(plan)):
                copies.append(
                    pltpu.make_async_remote_copy(
                        src_ref=source.at[:, columns],
                        dst_ref=refs[len(copies)],
                        send_sem=send_sem.at[len(copies)],
                        recv_sem=recv_sem.at[len(copies)],
                        device_id={"seq": partner(order[0])},
                        device_id_type=pl.DeviceIdType.MESH,
                    )
                )
        return copies

    at_first = (pl.program_id(0) == 0) & (pl.program_id(1) == 0)
    at_last = (pl.program_id(0) == pl.num_programs(0) - 1) & (
        pl.program_id(1) == pl.num_programs(1) - 1
    )
    used = sorted({order[0] for order, _ in plans[0]})

    @pl.when(at_first)
    def _():
        barrier = pltpu.get_barrier_semaphore()
        for bit in used:
            pl.semaphore_signal(
                barrier,
                inc=1,
                device_id={"seq": partner(bit)},
                device_id_type=pl.DeviceIdType.MESH,
            )
        pl.semaphore_wait(barrier, len(used))
        for copy in sends():
            copy.start()

    heads = step_ref.shape[1]
    count = x_ref.shape[1]
    spread = spread_matrix(heads, head_dim)
    x, g, b, c = x_ref[0], g_ref[0], b_ref[0], c_ref[0]
    x_wide, g_wide = x.astype(jnp.float32), g.astype(jnp.float32)
    rows = lax.broadcasted_iota(jnp.int32, (count, count), 0)
    columns = lax.broadcasted_iota(jnp.int32, (count, count), 1)
    valid = pair_labels(count, base_ref, starts_ref, pl.program_id(0)) & (
        columns >= rows
    )
    scores = jnp.where(valid, low_dot(b, c, NT), 0.0)
    upto = (rows >= columns).astype(jnp.bfloat16)
    before = (rows < columns).astype(jnp.float32)
    step = turned(step_ref[0], spread)
    carry = turned(carry_ref[0], spread)
    tail = turned(tail_ref[0], spread)
    scaled_wide = x_wide * step
    scaled, scaled_rest = halves_of(scaled_wide)
    start, end = start_ref[0], end_ref[0]
    run_row = run_ref[0]
    run = turned(run_row, spread_matrix(heads, 1))
    pair = 2 * head_dim
    lane = lax.broadcasted_iota(jnp.int32, (count, pair), 1)
    middle = count // 2
    score_grads = [
        jnp.zeros((middle, count), jnp.float32),
        jnp.zeros((count - middle, count - middle), jnp.float32),
    ]
    results, straddles = [], []
    for first in range(0, heads, 2):
        cut = slice(first * head_dim, first * head_dim + pair)
        g_block = g[:, cut]
        g_swap = jnp.concatenate([g_block[:, head_dim:], g_block[:, :head_dim]], axis=1)
        x_block, x_rest = scaled[:, cut], scaled_rest[:, cut]
        x_rest = jnp.concatenate([x_rest[:, head_dim:], x_rest[:, :head_dim]], axis=1)
        halves = []
        for head in (first, first + 1):
            own = (lane < head_dim) if head == first else (lane >= head_dim)
            x_own, g_own = jnp.where(own, x_block, x_rest), jnp.where(own, g_block, g_swap)
            strips, straddle = [], None
            for part, (top, cut) in enumerate(((0, middle), (middle, count))):
                gap = run_row[head : head + 1, top:] - run[top:cut, head : head + 1]
                fade = jnp.exp2(jnp.minimum(gap, 0.0))
                weights = fade * scores[top:cut, top:]
                strips.append(low_dot(weights, g_block[top:], NN))
                inner = low_dot(x_own[top:cut], g_own[top:], NT)
                score_grads[part] = score_grads[part] + fade * inner
                sums = low_dot(weights * inner, upto[top:, top:], NN)
                sums = jnp.sum(sums * before[top:cut, top:], axis=0, keepdims=True)
                if part == 0:
                    straddle = sums
                else:
                    straddle = jnp.concatenate(
                        [straddle[:, :middle], straddle[:, middle:] + sums], axis=1
                    )
            straddles.append(straddle)
            halves.append(jnp.concatenate(strips, axis=0))
        results.append(jnp.where(lane < head_dim, halves[0], halves[1]))
    score_grad = jnp.concatenate(
        [
            score_grads[0],
            jnp.concatenate([jnp.zeros((count - middle, middle), jnp.float32), score_grads[1]], axis=1),
        ],
        axis=0,
    )
    score_grad = jnp.where(valid, score_grad, 0.0)
    later = map_dot(b, end) * tail
    values = jnp.concatenate(results, axis=1) + later
    inter = map_dot(c, start) * carry
    direct_ref[0] = head_sums(spread, x_wide * values)
    given = head_sums(spread, scaled_wide * later)
    taken = head_sums(spread, g_wide * inter)
    flows = jnp.concatenate([given, taken], axis=0)
    flow_pieces = [item.astype(jnp.bfloat16) for item in thirds_of(flows)]
    after = (rows < columns).astype(jnp.bfloat16)
    flow_later = sum(low_dot(item, after, NN) for item in flow_pieces)
    flow_sooner = sum(low_dot(item, upto, NN) for item in flow_pieces)
    decay_ref[0] = (
        jnp.concatenate(straddles, axis=0) + flow_later[:heads] + flow_sooner[heads:]
    )
    grads_high, grads_low = halves_of(score_grad)
    grad_c = fine_dot(g_wide * carry, start) + low_dot(grads_high, b, TN) + low_dot(grads_low, b, TN)
    grad_b = fine_dot(scaled_wide * tail, end) + low_dot(grads_high, c, NN) + low_dot(grads_low, c, NN)

    @pl.when(pl.program_id(1) == 0)
    def _():
        grad_b_ref[0] = grad_b
        grad_c_ref[0] = grad_c

    @pl.when(pl.program_id(1) > 0)
    def _():
        grad_b_ref[0] = grad_b_ref[0] + grad_b
        grad_c_ref[0] = grad_c_ref[0] + grad_c

    weight, pre = weight_ref[...], pre_ref[0, 0]
    masks = same_segment(count, base_ref, starts_ref, weight.shape[0])
    total = conv_sum(ext, pre, halo_ref[0], weight, bias_ref[...], masks)
    sigma = sigmoid(total)
    grad_conv = (values * step + skip_ref[...] * g_wide) * (
        sigma * (1.0 + total * (1.0 - sigma))
    )
    moved[0:8, :] = jnp.zeros_like(moved[0:8, :])
    moved[8 + count :, :] = jnp.zeros_like(moved[8 + count :, :])
    sums = [jnp.sum(grad_conv * pre, axis=0, keepdims=True)]
    back = jnp.concatenate(
        [jnp.zeros((8, pre.shape[1]), jnp.float32), grad_conv * weight[0:1]], axis=0
    )
    for shift in range(1, weight.shape[0]):
        part = grad_conv * masks[shift - 1]
        sums.append(
            jnp.sum(part * ext[8 - shift : 8 - shift + count, :], axis=0, keepdims=True)
        )
        moved[8 : 8 + count, :] = part * weight[shift : shift + 1]
        back = back + moved[shift : shift + 8 + count, :]
    halo_out_ref[0] = back[:8]
    both_ref[0, 0] = back[8:].astype(jnp.bfloat16)
    edge_ref[0] = back[count:]
    sums.append(jnp.sum(grad_conv, axis=0, keepdims=True))
    sums.append(jnp.sum(g_wide * x_wide, axis=0, keepdims=True))
    sums.append(jnp.sum(start * end, axis=0, keepdims=True))
    sums.append(jnp.zeros((8 - len(sums), pre.shape[1]), jnp.float32))
    rows_ref[0] = jnp.concatenate(sums, axis=0)

    @pl.when(at_last)
    def _():
        for copy in sends():
            copy.wait()


def blocked(kernel, name, grid, ins, outs, scratch=(), micros=0, aliases=None, remote=None):
    moved = sum(item[0].size * item[0].dtype.itemsize for item in ins if item[1] != "any")
    moved += sum(
        math.prod(item[2]) * math.prod(grid) * jnp.dtype(item[1]).itemsize
        for item in outs
        if item[2] != "any"
    )

    def spec(item):
        if item[1] is None:
            return pl.BlockSpec(memory_space=pltpu.SMEM)
        if item[1] == "any":
            return pl.BlockSpec(memory_space=pl.ANY)
        return pl.BlockSpec(item[1], item[2])

    return pl.pallas_call(
        kernel,
        grid=grid,
        in_specs=[spec(item) for item in ins],
        out_specs=[spec(item[1:]) for item in outs],
        out_shape=[jax.ShapeDtypeStruct(item[0], item[1]) for item in outs],
        scratch_shapes=list(scratch),
        input_output_aliases=aliases or {},
        compiler_params=pltpu.CompilerParams(
            dimension_semantics=("arbitrary",) * len(grid),
            vmem_limit_bytes=VMEM_LIMIT,
            collective_id=remote,
            has_side_effects=remote is not None,
        ),
        cost_estimate=pl.CostEstimate(
            flops=micros * 1_000_000_000, bytes_accessed=moved, transcendentals=0
        ),
        name=name,
    )(*[item[0] for item in ins])


def body(
    tokens,
    norm_gain,
    in_weight,
    bc_weight,
    dt_weight,
    dt_bias,
    a_log,
    conv_weight,
    conv_bias,
    bc_conv_weight,
    bc_conv_bias,
    d_skip,
    gate_gain,
    out_weight,
    cotangent,
    seq_lengths,
):
    micro, length, width = tokens.shape
    heads = dt_bias.shape[0]
    inner = conv_bias.shape[0]
    head_dim = inner // heads
    state_size = bc_weight.shape[1] // 2
    taps = conv_weight.shape[0]
    total = micro * length
    head_count = lax.axis_size("head")
    full_inner = inner * head_count
    group = min(HEAD_GROUP, heads)
    groups = heads // group
    wide = group * head_dim
    base = lax.axis_index("seq").astype(jnp.int32) * length
    labels = segment_ids(seq_lengths, base - (taps - 1), length + taps - 1, micro)
    own_labels = labels[:, taps - 1 :]
    before_labels = labels[:, taps - 2]
    starts = jnp.cumsum(seq_lengths, axis=-1).astype(jnp.int32) - seq_lengths
    long_starts = jnp.full((micro - starts.shape[0], starts.shape[1]), FAR, jnp.int32)
    starts = jnp.concatenate([starts, long_starts.at[:, 0].set(0)], axis=0)
    base_item, starts_item = (base[None], None), (starts, None)

    flat = tokens.reshape(total, width).astype(jnp.float32)
    cot_flat = cotangent.reshape(total, width)
    _, norm_back = jax.vjp(rms_scale, flat, norm_gain)
    normed_low, gate_x, bc_pre, delta_pre = project(
        tokens.reshape(total, width), norm_gain, in_weight, bc_weight, dt_weight
    )
    gate_x = gate_x.reshape(2, micro, length, inner)
    bc_pre = bc_pre.reshape(micro, length, 2 * state_size)
    delta_pre = delta_pre.T
    left = shifted(
        jnp.concatenate(
            [gate_x[1, :, length - taps + 1 :], bc_pre[:, length - taps + 1 :]], axis=-1
        ),
        "seq",
        1,
    )
    left_x, left_bc = left[..., :inner], left[..., inner:]
    halo = jnp.pad(left_x, ((0, 0), (9 - taps, 0), (0, 0)))
    conv_many = jax.vmap(conv_silu, in_axes=(0, None, None, 0))
    bc_act, bc_conv_back = jax.vjp(
        lambda extended, weight, bias: conv_many(extended, weight, bias, labels),
        jnp.concatenate([left_bc, bc_pre], axis=1),
        bc_conv_weight,
        bc_conv_bias,
    )
    bc_low = bc_act.astype(jnp.bfloat16)
    b_low, c_low = bc_low[..., :state_size], bc_low[..., state_size:]
    (delta, decay), rate_back = jax.vjp(step_sizes, delta_pre, dt_bias, a_log)

    def by_micro(array):
        return array.reshape(heads, micro, length).transpose(1, 0, 2)

    def by_head(array):
        return array.transpose(1, 0, 2).reshape(heads, total)

    delta, decay = by_micro(delta), by_micro(decay)
    order = jnp.arange(length)
    running = jnp.einsum(
        "mhj,ji->mhi",
        decay,
        (order[:, None] <= order[None, :]).astype(jnp.float32),
        precision=HIGHEST,
    )
    device_log = running[:, :, -1]
    running_two = running * math.log2(math.e)
    live = (own_labels == before_labels[:, None]).astype(jnp.float32)
    last = (own_labels == own_labels[:, -1:]).astype(jnp.float32)
    carried = jnp.exp(running) * live[:, None]
    tail = jnp.exp(device_log[:, :, None] - running) * last[:, None]
    device_live = live[:, -1]
    gain_row, skip_row = gate_gain[None], jnp.repeat(d_skip, head_dim)[None]
    conv_row = conv_bias[None]

    grid = (micro, groups)
    token_block = (1, length, wide)
    in_token = lambda m, k: (m, 0, k)
    half_block = (1, 1, length, wide)
    in_gate, in_x = lambda m, k: (0, m, 0, k), lambda m, k: (1, m, 0, k)
    row_block, in_row = (1, group, length), lambda m, k: (m, k, 0)
    map_block, in_map = (1, length, state_size), lambda m, k: (m, 0, 0)
    state_block, in_state = (1, state_size, wide), in_token
    halo_block = (1, 8, wide)
    flat_block, in_flat = (1, wide), lambda m, k: (0, k)
    conv_item = (conv_weight, (taps, wide), in_flat)
    whole = (micro, length, inner)
    state_shape = (micro, state_size, inner)
    row_shape = (micro, heads, length)

    broad_group = min(BROAD_GROUP, heads)
    broad_groups, broad = heads // broad_group, broad_group * head_dim
    broad_token, broad_half = (1, length, broad), (1, 1, length, broad)
    broad_row, broad_state = (1, broad_group, length), (1, state_size, broad)
    exchange_log = jnp.where(device_live[:, None] > 0.0, device_log, DEAD)
    exchange_log = jnp.repeat(exchange_log, head_dim, axis=1)
    plans = scatter_plans(inner, axis_bits("seq"))
    parts = plans[-1]
    orders = tuple(order for order, _ in parts)
    tiled = (width >> axis_bits("seq")) % 128 == 0
    (incoming, x_low), (grad_gate_n, intra), arranged = exchange(
        (base[None], starts, gate_x, halo, conv_weight, conv_row, b_low, tail * delta),
        exchange_log,
        False,
        (cot_flat, normed_low) if tiled else (),
        orders if tiled else (),
        [
            (plain_steps, (), (cot_flat, out_weight), (total, inner)),
            (
                intra_steps,
                head_dim,
                (base[None], starts, b_low, c_low, running_two, delta, skip_row),
                whole,
            ),
        ],
        head_dim,
    )
    grad_gate_n = grad_gate_n.reshape(whole)
    if not tiled:
        arranged = arrange(cot_flat, orders) + arrange(normed_low, orders)
    cot_parts, normed_parts = arranged[: 2 * len(parts)], arranged[2 * len(parts) :]


    def first_stage(index):
        return lambda p, m, k: index(m + p * (micro - 1 - m), k + p * (broad_groups - 1 - k))

    def second_stage(index):
        return lambda p, m, k: index(m * p, k * p)

    def both_stages(index):
        return lambda p, m, k: index(m, k)

    head_bits = axis_bits("head")
    kept_shape = (micro * broad_groups, length, broad)
    sums_shape = (micro, length, 128)
    normed_gate, grad_gate_pre, grad_gate_x, grad_mixed, device_grad, gate_rows = blocked(
        functools.partial(gate_kernel, head_dim, float(full_inner), head_bits),
        "gate",
        (2, micro, broad_groups),
        [
            (intra, broad_token, first_stage(in_token)),
            (c_low, map_block, both_stages(in_map)),
            (carried, broad_row, both_stages(in_row)),
            (incoming, broad_state, first_stage(in_state)),
            (gate_x, broad_half, first_stage(in_gate)),
            (grad_gate_n, broad_token, first_stage(in_token)),
            (gain_row, (1, broad), both_stages(in_flat)),
        ],
        [
            (whole, jnp.bfloat16, broad_token, second_stage(in_token)),
            (whole, jnp.bfloat16, broad_token, second_stage(in_token)),
            ((2,) + whole, jnp.bfloat16, broad_half, second_stage(in_gate)),
            (whole, jnp.bfloat16, broad_token, second_stage(in_token)),
            (state_shape, jnp.float32, broad_state, second_stage(in_state)),
            ((micro, 8, inner), jnp.float32, (1, 8, broad), second_stage(in_token)),
        ],
        [
            pltpu.VMEM(kept_shape, jnp.float32),
            pltpu.VMEM(kept_shape, jnp.float32),
            pltpu.VMEM(kept_shape, jnp.float32),
            pltpu.VMEM((length, broad), jnp.bfloat16),
            pltpu.VMEM((length, broad), jnp.bfloat16),
            pltpu.VMEM((length, 128), jnp.float32),
            pltpu.VMEM((head_bits + 1,) + sums_shape, jnp.float32),
            pltpu.VMEM((head_bits,) + sums_shape, jnp.float32),
            pltpu.SemaphoreType.DMA((head_bits,)),
            pltpu.SemaphoreType.DMA((head_bits,)),
        ],
        30,
        None,
        4,
    )
    normed_gate = normed_gate.reshape(total, inner)
    grad_gate_pre = grad_gate_pre.reshape(total, inner)
    grad_gate_gain = jnp.sum(gate_rows, axis=(0, 1))

    half_shape = (width // 2, inner)
    paired = head_count == 2
    share = width // head_count
    outgoing, (out_sent, gate_sent), _ = exchange(
        device_grad,
        exchange_log,
        True,
        jobs=[
            (product_steps, plans[0], cot_parts[::2] + [normed_gate], half_shape),
            (product_steps, plans[1], normed_parts[::2] + [grad_gate_pre], half_shape),
        ],
    )
    (
        grad_gate_x,
        edge,
        halo_grad,
        conv_rows,
        direct,
        fading,
        grad_b,
        grad_c,
        *arrivals,
    ) = blocked(
        functools.partial(back_kernel, head_dim, plans),
        "back",
        grid,
        [
            base_item,
            starts_item,
            (x_low, token_block, in_token),
            (grad_mixed, token_block, in_token),
            (b_low, map_block, in_map),
            (c_low, map_block, in_map),
            (running_two, row_block, in_row),
            (delta, row_block, in_row),
            (carried, row_block, in_row),
            (tail, row_block, in_row),
            (incoming, state_block, in_state),
            (outgoing, state_block, in_state),
            (gate_x, half_block, in_x),
            (halo, halo_block, in_token),
            conv_item,
            (conv_row, flat_block, in_flat),
            (skip_row, flat_block, in_flat),
            (grad_gate_x, "any"),
            (out_sent, "any"),
            (gate_sent, "any"),
        ],
        [
            ((2,) + whole, jnp.bfloat16, half_block, in_x),
            ((micro, 8, inner), jnp.float32, halo_block, in_token),
            ((micro, 8, inner), jnp.float32, halo_block, in_token),
            ((micro, 8, inner), jnp.float32, halo_block, in_token),
            (row_shape, jnp.float32, row_block, in_row),
            (row_shape, jnp.float32, row_block, in_row),
            ((micro, length, state_size), jnp.float32, map_block, in_map),
            ((micro, length, state_size), jnp.float32, map_block, in_map),
        ]
        + [
            ((width // 2, sum(widths)), jnp.float32, "any")
            for plan in plans[:2]
            for _, widths in plan
        ],
        [
            pltpu.VMEM((length + 8, wide), jnp.float32),
            pltpu.VMEM((length + 16, wide), jnp.float32),
            pltpu.SemaphoreType.DMA((2 * len(parts),)),
            pltpu.SemaphoreType.DMA((2 * len(parts),)),
        ],
        80,
        {17: 0},
        3,
    )
    arrived = [arrivals[: len(parts)], arrivals[len(parts) :]]
    grad_bc = all_sum(jnp.concatenate([grad_b, grad_c], axis=-1), "head")
    pairs = conv_rows[:, taps + 2].reshape(micro, heads, head_dim)
    kept = jnp.sum(pairs, axis=-1) * jnp.exp(device_log) * device_live[:, None]
    grad_decay = by_head(fading + kept[:, :, None])
    grad_delta_pre, grad_dt_bias, grad_a_log = rate_back((by_head(direct), grad_decay))
    conv_rows = jnp.sum(conv_rows, axis=0)
    grad_conv_weight, grad_conv_bias = conv_rows[:taps], conv_rows[taps]
    grad_d_skip = jnp.sum(conv_rows[taps + 1].reshape(heads, head_dim), axis=-1)
    grad_bc_ext, grad_bc_conv_weight, grad_bc_conv_bias = bc_conv_back(grad_bc)
    right = shifted(
        jnp.concatenate([halo_grad[:, 9 - taps :], grad_bc_ext[:, : taps - 1]], axis=-1), "seq", -1
    )
    right_x, right_bc = right[..., :inner], right[..., inner:]
    grad_gate_x = lax.dynamic_update_slice(
        grad_gate_x,
        (edge[:, 9 - taps :] + right_x).astype(jnp.bfloat16)[None],
        (1, 0, length - taps + 1, 0),
    )
    grad_bc_pre = grad_bc_ext[:, taps - 1 :].at[:, length - taps + 1 :].add(right_bc)
    bc_flat = grad_bc_pre.reshape(total, 2 * state_size)
    grad_gate_x = grad_gate_x.reshape(2, total, inner)
    grad_steps = grad_delta_pre.T
    narrow_row = jnp.concatenate([bc_flat * (1.0 / head_count), grad_steps], axis=1)
    if paired:
        row_inputs = (
            in_weight,
            norm_gain[None],
            tokens.reshape(total, width),
            cot_flat,
            narrow_row,
            bc_weight,
            dt_weight,
            normed_gate,
            out_weight,
        )
        gain_grad = jnp.zeros_like(norm_gain)
    else:
        row_inputs = ()
        row_part = lax.dot_general(
            narrow_row,
            jnp.concatenate([bc_weight, dt_weight], axis=1),
            (NT, ((), ())),
            precision=HIGHEST,
            preferred_element_type=jnp.float32,
        ) + jnp.einsum(
            "ktc,dkc->td", grad_gate_x, in_weight, preferred_element_type=jnp.float32
        )
        grad_flat, gain_grad = norm_back(all_sum(row_part, "head"))
        grad_tokens = cot_flat.astype(jnp.float32) + grad_flat
        head_terms = lax.dot_general(
            normed_gate, out_weight, (NT, ((), ())), preferred_element_type=jnp.float32
        )
        summed = lax.psum_scatter(head_terms, "head", scatter_dimension=1, tiled=True)
        residual = lax.dynamic_slice_in_dim(flat, lax.axis_index("head") * share, share, 1)
        block_out = (residual + summed).astype(jnp.bfloat16)

    share_bc = 2 * state_size // head_count
    own_bc = lax.dynamic_slice_in_dim(bc_flat, lax.axis_index("head") * share_bc, share_bc, 1)
    across = share_bc + heads
    side = 0
    narrow_high, narrow_rest = halves_of(jnp.concatenate([own_bc, grad_steps], axis=1))
    both = jnp.concatenate([narrow_high, narrow_rest], axis=1)
    narrow = jnp.concatenate(
        [product(normed_parts[2 * side + 1], both), product(normed_parts[2 * side], both)], axis=0
    )
    narrow = narrow[:, :across] + narrow[:, across:]
    size = lax.axis_size("seq")
    row_count = width // size
    narrow = narrow.reshape(size, row_count, across)
    beside = 128 // heads
    narrow_bc = jnp.pad(narrow[:, :, :share_bc], ((0, 0), (0, 0), (0, -share_bc % 128)))
    narrow_steps = narrow[:, :, share_bc:].reshape(size, row_count // beside, 128)
    narrow_steps = jnp.pad(narrow_steps, ((0, 0), (0, 0), (0, narrow_bc.shape[2] - 128)))
    narrow = jnp.concatenate([narrow_bc, narrow_steps], axis=1)
    narrow_rows = narrow.shape[1]
    narrow = jnp.pad(narrow, ((0, 0), (0, -narrow_rows % 8), (0, 0)))
    narrow = narrow.reshape(-1, narrow.shape[2])

    small = [
        gain_grad,
        grad_bc_conv_weight,
        grad_bc_conv_bias,
        grad_dt_bias,
        grad_a_log,
        grad_d_skip,
        grad_conv_weight,
        grad_conv_bias,
        grad_gate_gain,
    ]
    row = jnp.concatenate([item.reshape(-1) for item in small])
    count = row.size
    row = jnp.pad(row, (0, -count % 1024)).reshape(-1, 128)

    (grad_out_weight, gate_block, x_block), gathered, row, *token_grads = finish(
        plans,
        [
            cot_parts[1::2] + [normed_gate] + arrived[0],
            normed_parts[1::2] + [grad_gate_pre] + arrived[1],
        ],
        normed_parts[::2],
        normed_parts[1::2],
        grad_gate_x,
        narrow,
        row,
        row_inputs,
    )
    if paired:
        grad_tokens, block_out = token_grads
    grad_tokens = grad_tokens.reshape(micro, length, width)
    block_out = block_out.reshape(micro, length, share)
    grad_in_weight = jnp.stack([gate_block, x_block], axis=1)
    grad_bc_weight = head_gather(gathered[:, :row_count, :share_bc].reshape(width, share_bc))
    grad_dt_weight = gathered[:, row_count:narrow_rows, :128].reshape(width, heads)
    row = row.reshape(-1)
    sizes, first = [], 0
    for item in small:
        sizes.append(row[first : first + item.size].reshape(item.shape))
        first += item.size
    (
        grad_norm_gain,
        grad_bc_conv_weight,
        grad_bc_conv_bias,
        grad_dt_bias,
        grad_a_log,
        grad_d_skip,
        grad_conv_weight,
        grad_conv_bias,
        grad_gate_gain,
    ) = sizes

    return (
        block_out,
        grad_tokens,
        grad_norm_gain,
        grad_in_weight,
        grad_bc_weight,
        grad_dt_weight,
        grad_dt_bias,
        grad_a_log,
        grad_d_skip,
        grad_conv_weight,
        grad_conv_bias,
        grad_bc_conv_weight,
        grad_bc_conv_bias,
        grad_gate_gain,
        grad_out_weight,
    )


def solution(mesh):
    return jax.shard_map(
        body,
        mesh=mesh,
        in_specs=(
            P(None, "seq", None),
            P(),
            P(None, None, "head"),
            P(),
            P(None, "head"),
            P("head"),
            P("head"),
            P(None, "head"),
            P("head"),
            P(),
            P(),
            P("head"),
            P("head"),
            P(None, "head"),
            P(None, "seq", None),
            P(),
        ),
        out_specs=(
            P(None, "seq", "head"),
            P(None, "seq", None),
            P(),
            P("seq", None, "head"),
            P(),
            P(None, "head"),
            P("head"),
            P("head"),
            P("head"),
            P(None, "head"),
            P("head"),
            P(),
            P(),
            P("head"),
            P("seq", "head"),
        ),
        check_vma=False,
    )
```

```python
import functools
import math

import jax
import jax.numpy as jnp
from jax import lax
from jax.experimental import pallas as pl
from jax.experimental.pallas import tpu as pltpu
from jax.sharding import PartitionSpec as P

EPSILON = 1e-05
HIGHEST = lax.Precision.HIGHEST


def shifted(shard, axis, by):
    length = lax.axis_size(axis)
    pairs = [(i, i + by) for i in range(length) if 0 <= i + by < length]
    return lax.ppermute(shard, axis, pairs)


def segment_ids(seq_lengths, first, count, micro):
    places = first + jnp.arange(count, dtype=jnp.int32)
    starts = jnp.cumsum(seq_lengths, axis=-1) - seq_lengths
    short_ids = (
        jnp.sum((starts[:, None, :] <= places[None, :, None]).astype(jnp.int32), axis=-1) - 1
    )
    long_ids = jnp.zeros((micro - seq_lengths.shape[0], count), jnp.int32)
    labels = jnp.concatenate([short_ids, long_ids], axis=0)
    return jnp.where(places[None, :] >= 0, labels, -1)


def rms_scale(values, gain):
    return values * lax.rsqrt(jnp.mean(values * values, axis=-1, keepdims=True) + EPSILON) * gain


def conv_silu(extended, weight, bias, labels):
    taps = weight.shape[0]
    count = extended.shape[0] - taps + 1
    own = labels[taps - 1 :]
    total = bias + weight[0] * extended[taps - 1 :]
    for shift in range(1, taps):
        first = taps - 1 - shift
        mask = (labels[first : first + count] == own).astype(extended.dtype)
        total = total + weight[shift] * extended[first : first + count] * mask[:, None]
    return jax.nn.silu(total)


def step_sizes(delta_pre, dt_bias, a_log):
    delta = jax.nn.softplus(delta_pre + dt_bias[:, None])
    return (delta, -jnp.exp(a_log)[:, None] * delta)


DEAD = -1e30
EXCHANGE_COST = 100_000_000_000
FINISH_LIMIT = 60 * 1024 * 1024
GROUP = 4


def exchange_kernel(length, reverse, orders, jobs, head_dim, log_ref, *refs):
    refs = list(refs)
    if head_dim:
        front_ins = [refs.pop(0) for _ in range(8)]
    else:
        part_ref = refs.pop(0)
    sources = [refs.pop(0) for _ in range(2 if orders else 0)]
    job_refs = [[refs.pop(0) for _ in range(job[2])] for job in jobs]
    out_ref = refs.pop(0)
    if head_dim:
        low_ref = refs.pop(0)
    steps = []
    for (make, plan, _), inputs in zip(jobs, job_refs):
        more = [low_ref] if make is intra_steps else []
        steps += make(inputs + more, refs.pop(0), plan)
    targets = [refs.pop(0) for _ in range(4 * len(orders))]
    (
        parts,
        logs,
        edge_in,
        edge_out,
        given,
        part_send,
        part_recv,
        log_send,
        log_recv,
        edge_send,
        edge_recv,
        given_send,
        given_recv,
        stage_sem,
        place_sem,
        staged,
        *front_keeps,
    ) = refs
    if head_dim:
        part_ref = front_keeps.pop(0)
    me = lax.axis_index("seq")
    bits = (length - 1).bit_length()
    placed = arrange_copies(bits, orders, me, staged, targets, place_sem)
    stages = [
        pltpu.make_async_copy(source, staged.at[k], stage_sem.at[k])
        for k, source in enumerate(sources)
    ]
    for copy in stages:
        copy.start()
    rank = lax.rem(me, GROUP)
    plane = me // GROUP
    first = me - rank
    mates = (
        rank + 1 - 2 * lax.rem(rank, 2),
        rank + 2 - 4 * (rank // 2),
        3 - rank,
    )
    micro = parts.shape[0]
    planes = length // GROUP
    begins, ends = plane == 0, plane == planes - 1
    if reverse:
        begins, ends = ends, begins
    onward = -GROUP if reverse else GROUP

    barrier = pltpu.get_barrier_semaphore()
    for mate in mates:
        pl.semaphore_signal(
            barrier, inc=1, device_id={"seq": first + mate}, device_id_type=pl.DeviceIdType.MESH
        )

    @pl.when(plane > 0)
    def _():
        pl.semaphore_signal(
            barrier, inc=1, device_id={"seq": me - GROUP}, device_id_type=pl.DeviceIdType.MESH
        )

    @pl.when(plane < planes - 1)
    def _():
        pl.semaphore_signal(
            barrier, inc=1, device_id={"seq": me + GROUP}, device_id_type=pl.DeviceIdType.MESH
        )

    above = jnp.where(plane < planes - 1, 1, 0)
    below = jnp.where(plane > 0, 1, 0)
    pl.semaphore_wait(barrier, 3 + above + below)

    def remote(src, dst, send, recv, target):
        return pltpu.make_async_remote_copy(
            src_ref=src,
            dst_ref=dst,
            send_sem=send,
            recv_sem=recv,
            device_id={"seq": target},
            device_id_type=pl.DeviceIdType.MESH,
        )

    def log_copy(slot):
        mate = mates[slot]
        return remote(
            log_ref.at[mate], logs.at[rank], log_send.at[slot], log_recv.at[slot], first + mate
        )

    quarter = edge_in.shape[2]

    def own_columns(place):
        return pl.ds(pl.multiple_of(place * quarter, quarter), quarter)

    def part_copy(m, slot):
        mate = mates[slot]
        return remote(
            part_ref.at[m, :, own_columns(mate)],
            parts.at[m, rank],
            part_send.at[m, slot],
            part_recv.at[m, slot],
            first + mate,
        )

    def edge_copy(m):
        return remote(edge_out.at[m], edge_in.at[m], edge_send.at[m], edge_recv.at[m], me + onward)

    def given_copy(m, slot):
        mate = mates[slot]
        return remote(
            given.at[m, mate],
            out_ref.at[m, :, own_columns(rank)],
            given_send.at[m, slot],
            given_recv.at[m, slot],
            first + mate,
        )

    for slot in range(3):
        log_copy(slot).start()
    def front_body(x, halo, weight, bias, b, tail, low):
        m = pl.program_id(0)
        front_kernel(
            head_dim,
            front_ins[0],
            front_ins[1],
            x,
            halo,
            weight,
            bias,
            b,
            tail,
            low,
            part_ref.at[pl.ds(m, 1)],
            *front_keeps,
        )
        for slot in range(3):
            part_copy(m, slot).start()

    if head_dim:
        x_ref, halo_ref, weight_ref, bias_ref, b_ref, tail_ref = front_ins[2:]
        by_micro = lambda shape: pl.BlockSpec((1,) + shape[1:], lambda m: (m, 0, 0))
        fixed = lambda shape: pl.BlockSpec(shape, lambda m: (0, 0))
        pltpu.emit_pipeline(
            front_body,
            grid=(micro,),
            in_specs=[
                pl.BlockSpec((1, 1) + x_ref.shape[2:], lambda m: (1, m, 0, 0)),
                by_micro(halo_ref.shape),
                fixed(weight_ref.shape),
                fixed(bias_ref.shape),
                by_micro(b_ref.shape),
                by_micro(tail_ref.shape),
            ],
            out_specs=[by_micro(low_ref.shape)],
        )(x_ref, halo_ref, weight_ref, bias_ref, b_ref, tail_ref, low_ref)
    else:
        for m in range(micro):
            for slot in range(3):
                part_copy(m, slot).start()
    logs[rank] = log_ref[rank]
    for m in range(micro):
        parts[m, rank] = part_ref[m, :, own_columns(rank)]

    @pl.when(begins)
    def _():
        edge_in[...] = jnp.zeros_like(edge_in)

    for copy in stages:
        copy.wait()
    for copy in placed:
        copy.start()
    for slot in range(3):
        log_copy(slot).wait()
    order = tuple(reversed(range(GROUP))) if reverse else tuple(range(GROUP))
    for m in range(micro):
        for step in steps[m * len(steps) // micro : (m + 1) * len(steps) // micro]:
            step()
        for slot in range(3):
            part_copy(m, slot).wait()
        factors = [jnp.exp(logs[t, m : m + 1, :]) for t in order]
        whole = jnp.exp(sum(logs[t, m : m + 1, :] for t in order))
        total = parts[m, order[0]]
        for t, factor in zip(order[1:], factors[1:]):
            total = total * factor + parts[m, t]

        @pl.when(jnp.logical_not(begins))
        def _():
            edge_copy(m).wait_recv()

        @pl.when(jnp.logical_not(ends))
        def _():
            edge_out[m] = total + whole * edge_in[m]
            edge_copy(m).start()

        running = edge_in[m]
        for place, (t, factor) in enumerate(zip(order, factors)):
            given[m, t] = running
            if place < GROUP - 1:
                running = running * factor + parts[m, t]
        for slot in range(3):
            given_copy(m, slot).start()
        out_ref[m, :, own_columns(rank)] = given[m, rank]
    for m in range(micro):
        for slot in range(3):
            given_copy(m, slot).wait()

        @pl.when(jnp.logical_not(ends))
        def _():
            edge_copy(m).wait_send()

    for copy in placed:
        copy.wait()


def exchange(parts, logs, reverse, sources=(), orders=(), jobs=(), head_dim=0):
    if head_dim:
        state_shape = (parts[6].shape[0], parts[6].shape[2], parts[2].shape[3])
        low_shape = parts[2].shape[1:]
    else:
        state_shape = parts.shape
    micro, rows, columns = state_shape
    quarter = columns // GROUP
    length = lax.axis_size("seq")
    spread = logs.reshape(micro, GROUP, quarter).transpose(1, 0, 2)
    shape = (micro, GROUP, rows, quarter)
    arranged = []
    for source in sources:
        half = jax.ShapeDtypeStruct((source.shape[0], source.shape[1] // 2), source.dtype)
        arranged += [half] * (2 * len(orders))
    vmem = pl.BlockSpec(memory_space=pltpu.VMEM)
    hbm = pl.BlockSpec(memory_space=pl.ANY)
    made = [jax.ShapeDtypeStruct(job[3], jnp.float32) for job in jobs]
    results = len(made)
    count = len(arranged)
    arranged = made + arranged
    job_inputs = [item for job in jobs for item in job[2]]
    plans = tuple((job[0], job[1], len(job[2])) for job in jobs)
    smem = pl.BlockSpec(memory_space=pltpu.SMEM)
    job_specs = [smem if item.dtype == jnp.int32 else hbm for item in job_inputs]
    out, *arranged = pl.pallas_call(
        functools.partial(exchange_kernel, length, reverse, orders, plans, head_dim),
        out_shape=[jax.ShapeDtypeStruct(state_shape, jnp.float32)]
        + ([jax.ShapeDtypeStruct(low_shape, jnp.bfloat16)] if head_dim else [])
        + arranged,
        in_specs=[vmem]
        + ([smem, smem] + [hbm] * 6 if head_dim else [vmem])
        + [hbm] * len(sources)
        + job_specs,
        out_specs=[vmem] + [hbm] * (len(arranged) + (1 if head_dim else 0)),
        scratch_shapes=[
            pltpu.VMEM(shape, jnp.float32),
            pltpu.VMEM((GROUP, micro, quarter), jnp.float32),
            pltpu.VMEM((micro, rows, quarter), jnp.float32),
            pltpu.VMEM((micro, rows, quarter), jnp.float32),
            pltpu.VMEM(shape, jnp.float32),
            pltpu.SemaphoreType.DMA((micro, 3)),
            pltpu.SemaphoreType.DMA((micro, 3)),
            pltpu.SemaphoreType.DMA((3,)),
            pltpu.SemaphoreType.DMA((3,)),
            pltpu.SemaphoreType.DMA((micro,)),
            pltpu.SemaphoreType.DMA((micro,)),
            pltpu.SemaphoreType.DMA((micro, 3)),
            pltpu.SemaphoreType.DMA((micro, 3)),
            pltpu.SemaphoreType.DMA((2,)),
            pltpu.SemaphoreType.DMA((max(count, 1) * max(length // 2, 1),)),
            pltpu.VMEM((2,) + sources[0].shape if sources else (2, 16, 128), jnp.bfloat16),
        ]
        + (
            [
                pltpu.VMEM(state_shape, jnp.float32),
                pltpu.VMEM((low_shape[1] + 8, columns), jnp.float32),
                pltpu.VMEM(low_shape[1:], jnp.bfloat16),
                pltpu.VMEM(low_shape[1:], jnp.bfloat16),
            ]
            if head_dim
            else []
        ),
        compiler_params=pltpu.CompilerParams(
            collective_id=1 if reverse else 0,
            has_side_effects=True,
            vmem_limit_bytes=FINISH_LIMIT,
        ),
        cost_estimate=pl.CostEstimate(
            flops=EXCHANGE_COST, bytes_accessed=0, transcendentals=0
        ),
        name="exchange_back" if reverse else "exchange",
    )(spread, *(parts if head_dim else (parts,)), *sources, *job_inputs)
    if head_dim:
        out = (out, arranged.pop(0))
    return out, arranged[:results], arranged[results:]


def xor_permute(value, axis, bit):
    size = lax.axis_size(axis)
    return lax.ppermute(value, axis, [(i, i ^ (1 << bit)) for i in range(size)])


def axis_bits(axis):
    return (lax.axis_size(axis) - 1).bit_length()


def own_bit(axis, bit):
    return lax.rem(lax.axis_index(axis) // (1 << bit), 2)


def all_sum(value, axis):
    for bit in range(axis_bits(axis)):
        value = value + xor_permute(value, axis, bit)
    return value


def scatter_plans(columns, bits):
    if bits < 3 or columns % 2048:
        return [[(tuple(range(bits)), (columns,))]] * 3
    rest = tuple(range(3, bits))
    unit = columns // 16
    orders = ((0, 1, 2), (1, 0, 2), (2, 0, 1), (2, 1, 0))
    shares = (
        ((3, 3), (2, 3), (3, 0), (0, 2)),
        ((3, 2), (3, 3), (3, 0), (0, 2)),
        ((4, 1), (2, 2), (3, 1), (2, 1)),
    )
    return [
        [
            (order + rest, tuple(unit * count for count in counts))
            for order, counts in zip(orders, share)
        ]
        for share in shares
    ]


def arranged_place(order, position, bits):
    return [(position >> (bits - 1 - t)) & 1 for t, _ in sorted(enumerate(order), key=lambda p: p[1])]


def arranged_block(order, position, bits, me):
    flips = arranged_place(order, position, bits)
    total = 0
    for bit, flip in enumerate(flips):
        mine = lax.rem(me // (1 << bit), 2)
        total = total + (1 << bit) * ((1 - mine) if flip else mine)
    return total


def arrange(left, orders):
    bits = axis_bits("seq")
    size = 1 << bits
    tokens, width = left.shape
    view = left.reshape(tokens, size, width // size)
    me = lax.axis_index("seq").astype(jnp.int32)
    results = []
    for order in orders:
        table = jnp.stack([arranged_block(order, j, bits, me) for j in range(size)])
        chosen = jnp.take(view, table, axis=1).reshape(tokens, width)
        results += [chosen[:, width // 2 :], chosen[:, : width // 2]]
    return results


def arrange_copies(bits, orders, me, staged, targets, sem):
    copies, number = [], 0
    half = 1 << (bits - 1)
    for source in range(len(targets) // (2 * len(orders)) if orders else 0):
        block = staged.shape[2] >> bits
        for order in orders:
            for begin in (half, 0):
                target = targets[number]
                for j in range(half):
                    place = arranged_block(order, begin + j, bits, me)
                    first = pl.multiple_of(place * block, block)
                    copies.append(
                        pltpu.make_async_copy(
                            staged.at[source, :, pl.ds(first, block)],
                            target.at[:, pl.ds(j * block, block)],
                            sem.at[number * half + j],
                        )
                    )
                number += 1
    return copies


def product(left, right):
    return lax.dot_general(left, right, (TN, ((), ())), preferred_element_type=jnp.float32)


def part_columns(parts):
    first, columns = 0, []
    for _, widths in parts:
        columns.append(pl.ds(first, sum(widths)))
        first += sum(widths)
    return columns


def product_steps(inputs, out_ref, parts):
    count = len(parts)
    lefts, right_ref, more = inputs[:count], inputs[count], inputs[count + 1 :]
    return [
        functools.partial(
            product_step, lefts[k], right_ref, more[k : k + 1], out_ref, columns.start, columns.size
        )
        for k, columns in enumerate(part_columns(parts))
    ]


def product_step(left_ref, right_ref, more, out_ref, first, width):
    tokens, rows = left_ref.shape
    tile = min(rows, 256)
    columns = pl.ds(first, width)

    def body(left, right, *rest):
        value = product(left[...], right[...])
        for item in rest[:-1]:
            value = value + item[...]
        rest[-1][...] = value

    tiled = pl.BlockSpec((tile, width), lambda i: (i, 0))
    pltpu.emit_pipeline(
        body,
        grid=(rows // tile,),
        in_specs=[
            pl.BlockSpec((tokens, tile), lambda i: (0, i)),
            pl.BlockSpec((tokens, width), lambda i: (0, 0)),
        ]
        + [tiled] * len(more),
        out_specs=[tiled],
    )(
        left_ref,
        right_ref.at[:, columns],
        *more,
        out_ref.at[:, columns],
    )


def plain_steps(inputs, out_ref, parts):
    left_ref, right_ref = inputs
    width = min(right_ref.shape[1], 512)
    return [
        functools.partial(plain_step, left_ref, right_ref, out_ref, first, width)
        for first in range(0, right_ref.shape[1], width)
    ]


def plain_step(left_ref, right_ref, out_ref, first, width):
    rows, depth = left_ref.shape
    tile = min(rows, 256)
    columns = pl.ds(first, width)

    def body(left, right, out):
        out[...] = low_dot(left[...], right[...], NN)

    pltpu.emit_pipeline(
        body,
        grid=(rows // tile,),
        in_specs=[
            pl.BlockSpec((tile, depth), lambda i: (i, 0)),
            pl.BlockSpec((depth, width), lambda i: (0, 0)),
        ],
        out_specs=[pl.BlockSpec((tile, width), lambda i: (i, 0))],
    )(left_ref, right_ref.at[:, columns], out_ref.at[:, columns])


def share_steps(inputs, out_refs, parts):
    left_ref, right_ref = inputs
    share = right_ref.shape[0] // 2
    mine = lax.axis_index("head") * share
    return [
        functools.partial(share_step, left_ref, right_ref, out_ref, first, share)
        for out_ref, first in zip(out_refs, (share - mine, mine))
    ]


def share_step(left_ref, right_ref, out_ref, first, share):
    rows, depth = left_ref.shape
    tile = min(rows, 256)
    width = min(share, 512)
    chosen = right_ref.at[pl.ds(pl.multiple_of(first, share), share)]

    def body(left, right, out):
        out[...] = low_dot(left[...], right[...], NT)

    pltpu.emit_pipeline(
        body,
        grid=(share // width, rows // tile),
        in_specs=[
            pl.BlockSpec((tile, depth), lambda j, i: (i, 0)),
            pl.BlockSpec((width, depth), lambda j, i: (j, 0)),
        ],
        out_specs=[pl.BlockSpec((tile, width), lambda j, i: (i, j))],
    )(left_ref, chosen, out_ref)


def row_step(grad_ref, weight_ref, narrow_ref, map_ref, step_ref, out_ref, first, rows):
    depth, halves, width = weight_ref.shape
    tile = min(depth, 256)

    def inner(held, sem):
        copy = pltpu.make_async_copy(grad_ref.at[:, pl.ds(first, rows)], held, sem)
        copy.start()
        copy.wait()

        def body(weight, narrow, map_weight, step_weight, out):
            turned_weight = jnp.swapaxes(weight[...], 0, 1)
            maps = map_weight.shape[1]
            high, rest = halves_of(narrow[...])
            total = low_dot(high[:, :maps], map_weight[...], NT) + low_dot(
                rest[:, :maps], map_weight[...], NT
            )
            total = total + low_dot(high[:, maps:], step_weight[...], NT)
            total = total + low_dot(rest[:, maps:], step_weight[...], NT)
            for half in range(halves):
                total = total + low_dot(held[half], turned_weight[half], NT)
            out[...] = total

        pltpu.emit_pipeline(
            body,
            grid=(depth // tile,),
            in_specs=[
                pl.BlockSpec((tile, halves, width), lambda j: (j, 0, 0)),
                pl.BlockSpec((rows, narrow_ref.shape[1]), lambda j: (0, 0)),
                pl.BlockSpec((tile, map_ref.shape[1]), lambda j: (j, 0)),
                pl.BlockSpec((tile, step_ref.shape[1]), lambda j: (j, 0)),
            ],
            out_specs=[pl.BlockSpec((rows, tile), lambda j: (0, j))],
        )(
            weight_ref,
            narrow_ref.at[pl.ds(first, rows)],
            map_ref,
            step_ref,
            out_ref.at[pl.ds(first, rows)],
        )

    pl.run_scoped(
        inner,
        pltpu.VMEM((halves, rows, width), jnp.bfloat16),
        pltpu.SemaphoreType.DMA,
    )


def token_step(
    gain_ref, gain_sum, tokens_ref, cot_ref, rows_refs, kept_ref, other_ref, grad_ref, block_ref
):
    count, width = tokens_ref.shape
    share = width // 2
    tile = min(count, 128)
    mine = lax.axis_index("head") == 0
    gain_sum[...] = jnp.zeros_like(gain_sum)

    def body(tokens, cot, own, other, kept, arrived, grad, block):
        values = tokens[...].astype(jnp.float32)
        pulls = own[...] + other[...]
        scale = lax.rsqrt(jnp.mean(values * values, axis=1, keepdims=True) + EPSILON)
        gained = pulls * gain_ref[...]
        cross = jnp.sum(gained * values, axis=1, keepdims=True)
        grad[...] = (
            cot[...].astype(jnp.float32)
            + gained * scale
            - values * (scale * scale * scale * cross * (1.0 / width))
        )
        parts = (pulls * values * scale).reshape(tile // 8, 8, width)
        gain_sum[...] = gain_sum[...] + jnp.sum(parts, axis=0)
        residual = jnp.where(mine, values[:, :share], values[:, share:])
        block[...] = (residual + kept[...] + arrived[...]).astype(jnp.bfloat16)

    full = pl.BlockSpec((tile, width), lambda i: (i, 0))
    half = pl.BlockSpec((tile, share), lambda i: (i, 0))
    pltpu.emit_pipeline(
        body,
        grid=(count // tile,),
        in_specs=[full] * 4 + [half] * 2,
        out_specs=[full, half],
    )(tokens_ref, cot_ref, *rows_refs, kept_ref, other_ref, grad_ref, block_ref)


def finish_kernel(plans, paired, bits, blocks, *refs):
    refs = list(refs)
    mats, parts = len(plans), plans[-1]
    take = lambda count: [refs.pop(0) for _ in range(count)]
    ins = [take(2 * len(parts) + 1) for _ in range(mats - 1)]
    last_sent, last_kept = take(len(parts)), take(len(parts))
    grad_ref, narrow_ref, vector_ref = take(3)
    if paired:
        weight_ref, gain_ref, tokens_ref, cot_ref = take(4)
        narrow_row_ref, map_ref, step_ref, gated_ref, out_weight_ref = take(5)
    outs = take(mats)
    gathered_ref, vector_out_ref = take(2)
    if paired:
        token_grad_ref, block_ref, row_ref, row_other_ref = take(4)
        share_sent_ref, share_kept_ref, share_other_ref = take(3)
    sent_ref, arrived_ref = take(2)
    made_refs = take(mats)
    me = lax.axis_index("seq")
    last_right = grad_ref.at[grad_ref.shape[0] - 1]
    columns_of = part_columns(parts)
    ins.append(last_kept + [last_right] + [arrived_ref.at[:, columns] for columns in columns_of])

    def partner(bit):
        return me + (1 << bit) * (1 - 2 * lax.rem(me // (1 << bit), 2))

    waves = []
    piece_count = len(parts[0][1])
    chain_count = 0
    for mat in range(mats):
        for piece in range(piece_count):
            wave, first = [], 0
            for order, widths in plans[mat]:
                if widths[piece]:
                    place = first + sum(widths[:piece])
                    keep = refs.pop(0)
                    recvs = take(bits - 1)
                    wave.append(
                        (chain_count, made_refs[mat], place, outs[mat], place, order[1:], keep, recvs)
                    )
                    chain_count += 1
                first += sum(widths)
            waves.append(wave)
    narrow_order = parts[0][0]
    narrow = (chain_count, narrow_ref, 0, None, 0, narrow_order, refs.pop(0), take(bits))
    vector_sums, vector_recvs, gain_sum, local_sem, send_sem, recv_sem = refs

    barrier = pltpu.get_barrier_semaphore()
    for bit in range(bits):
        pl.semaphore_signal(
            barrier,
            inc=1,
            device_id={"seq": partner(bit)},
            device_id_type=pl.DeviceIdType.MESH,
        )
    if paired:
        pl.semaphore_signal(
            barrier,
            inc=1,
            device_id={"head": 1 - lax.axis_index("head")},
            device_id_type=pl.DeviceIdType.MESH,
        )
    pl.semaphore_wait(barrier, bits + (1 if paired else 0))

    numbers = {}

    def remote_to(key, src, dst, target):
        number = numbers.setdefault(key, len(numbers))
        return pltpu.make_async_remote_copy(
            src_ref=src,
            dst_ref=dst,
            send_sem=send_sem.at[number],
            recv_sem=recv_sem.at[number],
            device_id=target,
            device_id_type=pl.DeviceIdType.MESH,
        )

    def remote(key, src, dst, bit):
        return remote_to(key, src, dst, {"seq": partner(bit)})

    def first_copy(k):
        region = (slice(None), columns_of[k])
        return remote(("first", k), sent_ref.at[region], arrived_ref.at[region], parts[k][0][0])

    def share_copy():
        return remote_to(
            "share", share_sent_ref, share_other_ref, {"head": 1 - lax.axis_index("head")}
        )

    def shares(part):
        share_steps(
            (gated_ref, out_weight_ref), (share_sent_ref, share_kept_ref), ()
        )[part]()
        if part == 0:
            share_copy().start()

    def row_copy():
        return remote_to("row", row_ref, row_other_ref, {"head": 1 - lax.axis_index("head")})

    def local_copy(chain):
        number, source, first, _, _, _, keep, _ = chain
        rows, columns = keep.shape
        return pltpu.make_async_copy(
            source.at[pl.ds(0, rows), pl.ds(first, columns)], keep, local_sem.at[number]
        )

    def chain_copy(chain, phase):
        number, source, first, _, _, order, keep, recvs = chain
        rows, columns = recvs[phase].shape
        if phase == 0:
            region = source.at[pl.ds(rows, rows), pl.ds(first, columns)]
        else:
            region = keep.at[pl.ds(rows, rows)]
        return remote((number, phase), region, recvs[phase], order[phase])

    made = set()

    def make(mat):
        if mat in made:
            return
        made.add(mat)
        if mat == mats - 1:
            for k in range(len(parts)):
                first_copy(k).wait_recv()
        for step in product_steps(ins[mat], made_refs[mat], plans[mat]):
            step()

    def begin(number):
        make(number // piece_count)
        for chain in waves[number]:
            chain_copy(chain, 0).start()
            local_copy(chain).start()

    def advance(chain, phase):
        if phase == 0:
            local_copy(chain).wait()
        chain_copy(chain, phase).wait_recv()
        number, _, _, out, place, order, keep, recvs = chain
        recv = recvs[phase]
        rows = recv.shape[0]
        slab = min(rows, 32)

        @pl.loop(0, rows // slab)
        def _(step):
            cut = pl.ds(pl.multiple_of(step * slab, slab), slab)
            keep[cut, :] = keep[cut, :] + recv[cut, :]

        if phase + 1 < len(order):
            chain_copy(chain, phase + 1).start()
        elif out is not None:
            out[:, place : place + keep.shape[1]] = keep[0:blocks, :]

    def vector_copy(phase):
        return remote(("vector", phase), vector_sums.at[phase], vector_recvs.at[phase], phase)

    def begin_vector():
        vector_sums[0] = vector_ref[...]
        if paired:
            total = jnp.sum(gain_sum[...], axis=0, keepdims=True)
            for place in range(total.shape[1] // 128):
                vector_sums[0, place : place + 1, :] = total[:, place * 128 : place * 128 + 128]
        vector_copy(0).start()

    def advance_vector(phase):
        vector_copy(phase).wait_recv()
        total = vector_sums[phase] + vector_recvs[phase]
        if phase + 1 < bits:
            vector_sums[phase + 1] = total
            vector_copy(phase + 1).start()
        else:
            vector_out_ref[...] = total

    gather_bits = tuple(reversed(range(bits)))

    def gather_copies(phase):
        free = gather_bits[:phase]
        fixed = sum(
            (1 << bit) * lax.rem(me // (1 << bit), 2) for bit in range(bits) if bit not in free
        )
        copies = []
        for number in range(1 << phase):
            block = fixed + sum(
                (1 << bit) * ((number >> place) & 1) for place, bit in enumerate(free)
            )
            region = gathered_ref.at[block]
            copies.append(remote(("gather", phase, number), region, region, gather_bits[phase]))
        return copies

    def narrow_halving(phase):
        advance(narrow, phase)
        if phase + 1 == bits:
            gathered_ref[me] = narrow[6][0 : gathered_ref.shape[1], :]
            for copy in gather_copies(0):
                copy.start()

    def narrow_gather(phase):
        for copy in gather_copies(phase):
            copy.wait_recv()
        if phase + 1 < bits:
            for copy in gather_copies(phase + 1):
                copy.start()

    def rows(part):
        count = row_ref.shape[0] // 2
        row_step(
            grad_ref,
            weight_ref,
            narrow_row_ref,
            map_ref,
            step_ref,
            row_ref,
            part * count,
            count,
        )
        if part == 1:
            row_copy().start()

    def token_rows():
        row_copy().wait()
        share_copy().wait()
        token_step(
            gain_ref,
            gain_sum,
            tokens_ref,
            cot_ref,
            (row_ref, row_other_ref),
            share_kept_ref,
            share_other_ref,
            token_grad_ref,
            block_ref,
        )

    narrow_steps = [functools.partial(narrow_halving, phase) for phase in range(bits)]
    narrow_steps += [functools.partial(narrow_gather, phase) for phase in range(bits)]
    fills = {}
    vector_tick = 0
    if paired:
        fills = {
            0: [functools.partial(rows, 0)],
            1: [functools.partial(rows, 1), functools.partial(shares, 0)],
            2: [functools.partial(shares, 1)],
            3: [token_rows],
        }
        vector_tick = 4

    chain_copy(narrow, 0).start()
    local_copy(narrow).start()
    sent_steps = product_steps(last_sent + [last_right], sent_ref, parts)
    for k, step in enumerate(sent_steps):
        step()
        first_copy(k).start()
    begun = min(2, len(waves))
    for number in range(begun):
        begin(number)
    if len(waves) > begun:
        make(begun // piece_count)
    ticks = max(len(waves) + bits - 2, 2 * bits, vector_tick + bits)
    for tick in range(ticks):
        if tick < len(narrow_steps):
            narrow_steps[tick]()
        for phase in range(bits - 1):
            number = tick - phase
            if 0 <= number < len(waves):
                for chain in waves[number]:
                    advance(chain, phase)
                if phase == 0 and number + 2 < len(waves):
                    begin(number + 2)
        if tick + 3 < len(waves):
            make((tick + 3) // piece_count)
        for step in fills.get(tick, ()):
            step()
        if tick == vector_tick:
            begin_vector()
        if 0 <= tick - vector_tick < bits:
            advance_vector(tick - vector_tick)
    for k in range(len(parts)):
        first_copy(k).wait_send()
    for wave in waves:
        for chain in wave:
            for phase in range(bits - 1):
                chain_copy(chain, phase).wait_send()
    for phase in range(bits):
        chain_copy(narrow, phase).wait_send()
        vector_copy(phase).wait_send()
        for copy in gather_copies(phase):
            copy.wait_send()


def finish(plans, mats, last_sent, last_kept, grad, narrow, vector, row_inputs):
    bits = axis_bits("seq")
    size = 1 << bits
    count, parts = len(plans), plans[-1]
    paired = bool(row_inputs)
    rows = last_kept[0].shape[1]
    blocks = rows // (size // 2)
    columns = sum(sum(widths) for _, widths in parts)
    scratch, copies, chains = [], 0, 0
    for plan in plans:
        for piece in range(len(parts[0][1])):
            for _, widths in plan:
                if widths[piece]:
                    scratch.append(pltpu.VMEM((rows // 2, widths[piece]), jnp.float32))
                    for phase in range(bits - 1):
                        scratch.append(
                            pltpu.VMEM(((rows // 2) >> phase, widths[piece]), jnp.float32)
                        )
                    copies += bits - 1
                    chains += 1
    narrow_rows = narrow.shape[0] // 2
    scratch.append(pltpu.VMEM((narrow_rows, narrow.shape[1]), jnp.float32))
    for phase in range(bits):
        scratch.append(pltpu.VMEM((narrow_rows >> phase, narrow.shape[1]), jnp.float32))
    copies += 2 * bits + size - 1 + len(parts) + 2
    scratch += [pltpu.VMEM((bits,) + vector.shape, jnp.float32)] * 2
    scratch += [
        pltpu.VMEM((8, row_inputs[1].shape[1] if paired else 128), jnp.float32),
        pltpu.SemaphoreType.DMA((chains + 1,)),
        pltpu.SemaphoreType.DMA((copies,)),
        pltpu.SemaphoreType.DMA((copies,)),
    ]
    vmem, hbm = pl.BlockSpec(memory_space=pltpu.VMEM), pl.BlockSpec(memory_space=pl.ANY)
    shapes = [jax.ShapeDtypeStruct((blocks, columns), jnp.float32) for _ in range(count)]
    shapes.append(
        jax.ShapeDtypeStruct((size, narrow.shape[0] // size, narrow.shape[1]), jnp.float32)
    )
    shapes.append(jax.ShapeDtypeStruct(vector.shape, jnp.float32))
    specs = [vmem] * len(shapes)
    if paired:
        tokens = row_inputs[2]
        token_shape = jax.ShapeDtypeStruct(tokens.shape, jnp.float32)
        block_shape = jax.ShapeDtypeStruct((tokens.shape[0], tokens.shape[1] // 2), jnp.bfloat16)
        share_shape = jax.ShapeDtypeStruct(block_shape.shape, jnp.float32)
        shapes += [token_shape, block_shape, token_shape, token_shape] + [share_shape] * 3
    half = jax.ShapeDtypeStruct((rows, columns), jnp.float32)
    shapes += [half] * (2 + count)
    specs += [hbm] * (len(shapes) - len(specs))
    flat = [item for mat in mats for item in mat] + last_sent + last_kept + [grad, narrow]
    row_specs = [hbm, vmem] + [hbm] * 7 if paired else []
    results = pl.pallas_call(
        functools.partial(finish_kernel, plans, paired, bits, blocks),
        out_shape=shapes,
        in_specs=[hbm] * len(flat) + [vmem] + row_specs,
        out_specs=specs,
        scratch_shapes=scratch,
        compiler_params=pltpu.CompilerParams(
            collective_id=2, has_side_effects=True, vmem_limit_bytes=FINISH_LIMIT
        ),
        name="finish",
    )(*flat, vector, *row_inputs)
    return (
        results[:count],
        results[count],
        results[count + 1],
        *(results[count + 2 : count + 4] if paired else ()),
    )


def head_gather(block):
    if lax.axis_size("head") != 2:
        return lax.all_gather(block, "head", axis=1, tiled=True)
    other = xor_permute(block, "head", 0)
    mine = lax.axis_index("head") == 0
    return jnp.concatenate(
        [jnp.where(mine, block, other), jnp.where(mine, other, block)], axis=1
    )


HEAD_GROUP = 8
BROAD_GROUP = 32
SLAB = 16
VMEM_LIMIT = 56 * 1024 * 1024
FAR = 1 << 30
NN = ((1,), (0,))
NT = ((1,), (1,))
TN = ((0,), (0,))


def low_dot(left, right, dims):
    return lax.dot_general(
        left.astype(jnp.bfloat16),
        right.astype(jnp.bfloat16),
        (dims, ((), ())),
        preferred_element_type=jnp.float32,
    )


def halves_of(value):
    high = value.astype(jnp.bfloat16)
    return high, (value - high.astype(jnp.float32)).astype(jnp.bfloat16)


def thirds_of(value):
    first = value.astype(jnp.bfloat16).astype(jnp.float32)
    second = (value - first).astype(jnp.bfloat16).astype(jnp.float32)
    return first, second, value - first - second


def spread_matrix(heads, head_dim):
    shape = (heads, heads * head_dim)
    rows = lax.broadcasted_iota(jnp.int32, shape, 0)
    columns = lax.broadcasted_iota(jnp.int32, shape, 1)
    return (columns // head_dim == rows).astype(jnp.float32)


def turned(rows, matrix):
    return low_dot(
        jnp.concatenate(thirds_of(rows), axis=0), jnp.concatenate([matrix] * 3, axis=0), TN
    )


def head_sums(spread, value):
    high, low = halves_of(value)
    return low_dot(spread, high, NT) + low_dot(spread, low, NT)


def map_dot(left, right):
    return low_dot(
        jnp.concatenate([left, left], axis=1), jnp.concatenate(halves_of(right), axis=0), NN
    )


def fine_dot(left, right):
    left_high, left_low = halves_of(left)
    right_high, right_low = halves_of(right)
    return (
        low_dot(left_high, right_high, NT)
        + low_dot(left_high, right_low, NT)
        + low_dot(left_low, right_high, NT)
    )


def sigmoid(value):
    return 0.5 + 0.5 * jnp.tanh(0.5 * value)


def segment_of(places, starts_ref, micro):
    label = jnp.zeros_like(places)
    for number in range(starts_ref.shape[1]):
        label = label + jnp.where(places >= starts_ref[micro, number], 1, 0)
    return label


def same_segment(count, base_ref, starts_ref, taps):
    micro = pl.program_id(0)
    places = base_ref[0] + lax.broadcasted_iota(jnp.int32, (count, 1), 0)
    own = segment_of(places, starts_ref, micro)
    return [
        jnp.where(segment_of(places - shift, starts_ref, micro) == own, 1.0, 0.0)
        for shift in range(1, taps)
    ]


def pair_labels(count, base_ref, starts_ref, micro):
    column = base_ref[0] + lax.broadcasted_iota(jnp.int32, (count, 1), 0)
    row = base_ref[0] + lax.broadcasted_iota(jnp.int32, (1, count), 1)
    return segment_of(column, starts_ref, micro) == segment_of(row, starts_ref, micro)


def conv_sum(ext, value, halo, weight, bias, masks):
    count = value.shape[0]
    ext[0:8, :] = halo
    ext[8 : 8 + count, :] = value
    total = bias + weight[0:1] * value
    for shift in range(1, weight.shape[0]):
        total = (
            total
            + weight[shift : shift + 1]
            * ext[8 - shift : 8 - shift + count, :]
            * masks[shift - 1]
        )
    return total


def project_kernel(
    tokens_ref, gain_ref, weight_ref, map_ref, step_ref, normed_ref, out_ref, map_out_ref, step_out_ref
):
    count = tokens_ref.shape[0]
    slab = min(count, 64)

    @pl.when(pl.program_id(0) == 0)
    def _():
        @pl.loop(0, count // slab)
        def _(step):
            cut = pl.ds(pl.multiple_of(step * slab, slab), slab)
            values = tokens_ref[cut, :].astype(jnp.float32)
            scale = lax.rsqrt(jnp.mean(values * values, axis=1, keepdims=True) + EPSILON)
            normed_ref[cut, :] = (values * scale * gain_ref[...]).astype(jnp.bfloat16)

        map_out_ref[...] = low_dot(normed_ref[...], map_ref[...], NN)
        step_out_ref[...] = low_dot(normed_ref[...], step_ref[...], NN)

    weight = jnp.swapaxes(weight_ref[...], 0, 1)
    for half in range(weight.shape[0]):
        out_ref[half] = low_dot(normed_ref[...], weight[half], NN)


def project(tokens, gain, weight, map_weight, step_weight):
    count, width = tokens.shape
    _, halves, columns = weight.shape
    tile = min(columns, 256)
    return pl.pallas_call(
        project_kernel,
        grid=(columns // tile,),
        in_specs=[
            pl.BlockSpec((count, width), lambda j: (0, 0)),
            pl.BlockSpec((1, width), lambda j: (0, 0)),
            pl.BlockSpec((width, halves, tile), lambda j: (0, 0, j)),
            pl.BlockSpec(map_weight.shape, lambda j: (0, 0)),
            pl.BlockSpec(step_weight.shape, lambda j: (0, 0)),
        ],
        out_specs=[
            pl.BlockSpec((count, width), lambda j: (0, 0)),
            pl.BlockSpec((halves, count, tile), lambda j: (0, 0, j)),
            pl.BlockSpec((count, map_weight.shape[1]), lambda j: (0, 0)),
            pl.BlockSpec((count, step_weight.shape[1]), lambda j: (0, 0)),
        ],
        out_shape=[
            jax.ShapeDtypeStruct((count, width), jnp.bfloat16),
            jax.ShapeDtypeStruct((halves, count, columns), jnp.float32),
            jax.ShapeDtypeStruct((count, map_weight.shape[1]), jnp.float32),
            jax.ShapeDtypeStruct((count, step_weight.shape[1]), jnp.float32),
        ],
        compiler_params=pltpu.CompilerParams(vmem_limit_bytes=VMEM_LIMIT),
        cost_estimate=pl.CostEstimate(
            flops=2 * count * width * columns * halves, bytes_accessed=0, transcendentals=0
        ),
        name="project",
    )(tokens, gain[None], weight, map_weight, step_weight)


def front_kernel(
    head_dim,
    base_ref,
    starts_ref,
    x_ref,
    halo_ref,
    weight_ref,
    bias_ref,
    b_ref,
    tail_ref,
    low_ref,
    state_ref,
    ext,
    high_keep,
    rest_keep,
):
    heads = tail_ref.shape[1]
    count = x_ref.shape[2]
    weight, bias = weight_ref[...], bias_ref[...]
    masks = same_segment(count, base_ref, starts_ref, weight.shape[0])
    scale = turned(tail_ref[0], spread_matrix(heads, head_dim))
    ext[0:8, :] = halo_ref[0]
    ext[8 : 8 + count, :] = x_ref[0, 0]
    for top in range(0, count, SLAB):
        cut = slice(top, top + SLAB)
        total = bias + weight[0:1] * ext[8 + top : 8 + top + SLAB, :]
        for shift in range(1, weight.shape[0]):
            first = 8 - shift + top
            total = (
                total
                + weight[shift : shift + 1] * ext[first : first + SLAB, :] * masks[shift - 1][cut]
            )
        act = (total * sigmoid(total)).astype(jnp.bfloat16)
        low_ref[0, cut, :] = act
        high, rest = halves_of(act.astype(jnp.float32) * scale[cut])
        high_keep[cut, :] = high
        rest_keep[cut, :] = rest
    state_ref[0] = low_dot(b_ref[0], high_keep[...], TN) + low_dot(b_ref[0], rest_keep[...], TN)


def intra_block(head_dim, valid, x, b, c, run_row, step_row, skip):
    heads, count = run_row.shape
    spread = spread_matrix(heads, head_dim)
    scores = jnp.where(valid, low_dot(c, b, NT), 0.0)
    wide = x.astype(jnp.float32)
    scaled = (wide * turned(step_row, spread)).astype(jnp.bfloat16)
    run = turned(run_row, spread_matrix(heads, 1))
    pair = 2 * head_dim
    middle = count // 2
    lane = lax.broadcasted_iota(jnp.int32, (count, pair), 1)
    results = []
    for first in range(0, heads, 2):
        block = scaled[:, first * head_dim : first * head_dim + pair]
        halves = []
        for head in (first, first + 1):
            strips = []
            for top, cut in ((0, middle), (middle, count)):
                gap = run[top:cut, head : head + 1] - run_row[head : head + 1, :cut]
                weights = jnp.exp2(jnp.minimum(gap, 0.0)) * scores[top:cut, :cut]
                strips.append(low_dot(weights, block[:cut], NN))
            halves.append(jnp.concatenate(strips, axis=0))
        results.append(jnp.where(lane < head_dim, halves[0], halves[1]))
    return jnp.concatenate(results, axis=1) + skip * wide


def intra_steps(inputs, out_ref, head_dim):
    return [
        functools.partial(intra_step, inputs, out_ref, head_dim, micro)
        for micro in range(out_ref.shape[0])
    ]


def intra_step(inputs, out_ref, head_dim, micro):
    base_ref, starts_ref, b_ref, c_ref, run_ref, step_ref, skip_ref, x_ref = inputs
    _, count, inner = x_ref.shape
    heads = run_ref.shape[1]
    group = min(HEAD_GROUP, heads)
    wide = group * head_dim

    def body(x, b, c, run, step, skip, out):
        rows = lax.broadcasted_iota(jnp.int32, (count, count), 0)
        columns = lax.broadcasted_iota(jnp.int32, (count, count), 1)
        valid = pair_labels(count, base_ref, starts_ref, micro) & (rows >= columns)
        out[...] = intra_block(
            head_dim, valid, x[...], b[...], c[...], run[...], step[...], skip[...]
        )

    token = pl.BlockSpec((count, wide), lambda k: (0, k))
    maps = pl.BlockSpec((count, b_ref.shape[2]), lambda k: (0, 0))
    row = pl.BlockSpec((group, count), lambda k: (k, 0))
    pltpu.emit_pipeline(
        body,
        grid=(inner // wide,),
        in_specs=[token, maps, maps, row, row, pl.BlockSpec((1, wide), lambda k: (0, k))],
        out_specs=[token],
    )(
        x_ref.at[micro],
        b_ref.at[micro],
        c_ref.at[micro],
        run_ref.at[micro],
        step_ref.at[micro],
        skip_ref,
        out_ref.at[micro],
    )


def gate_kernel(
    head_dim,
    full,
    bits,
    intra_ref,
    c_ref,
    carry_ref,
    begin_ref,
    gate_ref,
    cot_ref,
    gain_ref,
    norm_ref,
    grad_gate_ref,
    both_ref,
    grad_mixed_ref,
    start_ref,
    rows_ref,
    mixed_keep,
    gate_keep,
    cot_keep,
    high_keep,
    rest_keep,
    both_keep,
    sums,
    sums_in,
    send_sem,
    recv_sem,
):
    stage, micro, number = pl.program_id(0), pl.program_id(1), pl.program_id(2)
    groups = pl.num_programs(2)
    heads = carry_ref.shape[1]
    place = micro * groups + number
    carry = turned(carry_ref[0], spread_matrix(heads, head_dim))
    mine = lax.axis_index("head")

    def partner(bit):
        return {"head": mine + (1 << bit) * (1 - 2 * lax.rem(mine // (1 << bit), 2))}

    @pl.when((stage == 0) & (place == 0))
    def _():
        barrier = pltpu.get_barrier_semaphore()
        for bit in range(bits):
            pl.semaphore_signal(
                barrier, inc=1, device_id=partner(bit), device_id_type=pl.DeviceIdType.MESH
            )
        pl.semaphore_wait(barrier, bits)

    @pl.when(stage == 0)
    def _():
        inter = map_dot(c_ref[0], begin_ref[0])
        gain = gain_ref[...]
        for top in range(0, inter.shape[0], SLAB):
            cut = slice(top, top + SLAB)
            mixed = intra_ref[0, cut, :] + inter[cut] * carry[cut]
            gate, cot = gate_ref[0, 0, cut, :], cot_ref[0, cut, :]
            mixed_keep[place, cut, :] = mixed
            gate_keep[place, cut, :] = gate
            cot_keep[place, cut, :] = cot
            gated = mixed * (gate * sigmoid(gate))
            square = jnp.sum(gated * gated, axis=1, keepdims=True)
            cross = jnp.sum(cot * gain * gated, axis=1, keepdims=True)
            lane = lax.broadcasted_iota(jnp.int32, (SLAB, 128), 1)
            both_keep[cut, :] = jnp.where(lane == 0, square, jnp.where(lane == 1, cross, 0.0))

        @pl.when(number == 0)
        def _():
            sums[0, micro] = both_keep[...]

        @pl.when(number > 0)
        def _():
            sums[0, micro] = sums[0, micro] + both_keep[...]

    @pl.when((stage == 1) & (place == 0))
    def _():
        for bit in range(bits):
            copy = pltpu.make_async_remote_copy(
                src_ref=sums.at[bit],
                dst_ref=sums_in.at[bit],
                send_sem=send_sem.at[bit],
                recv_sem=recv_sem.at[bit],
                device_id=partner(bit),
                device_id_type=pl.DeviceIdType.MESH,
            )
            copy.start()
            copy.wait()
            sums[bit + 1] = sums[bit] + sums_in[bit]

    @pl.when(stage == 1)
    def _():
        gain = gain_ref[...]
        gains = jnp.zeros((8, gain.shape[1]), jnp.float32)
        for top in range(0, carry.shape[0], SLAB):
            cut = slice(top, top + SLAB)
            mixed, gate = mixed_keep[place, cut, :], gate_keep[place, cut, :]
            cot = cot_keep[place, cut, :]
            total = sums[bits, micro, cut, :]
            scale = lax.rsqrt(total[:, 0:1] / full + EPSILON)
            pull = scale * scale * scale * total[:, 1:2] / full
            sigma = sigmoid(gate)
            act = gate * sigma
            gated = mixed * act
            unit = gated * scale
            norm_ref[0, cut, :] = (unit * gain).astype(jnp.bfloat16)
            grad_gated = cot * gain * scale - gated * pull
            grad_gate = grad_gated * mixed * sigma * (1.0 + gate * (1.0 - sigma))
            grad_gate = grad_gate.astype(jnp.bfloat16)
            grad_gate_ref[0, cut, :] = grad_gate
            both_ref[0, 0, cut, :] = grad_gate
            grad_mixed = (grad_gated * act).astype(jnp.bfloat16)
            grad_mixed_ref[0, cut, :] = grad_mixed
            high, rest = halves_of(grad_mixed.astype(jnp.float32) * carry[cut])
            high_keep[cut, :] = high
            rest_keep[cut, :] = rest
            parts = (cot * unit).reshape(SLAB // 8, 8, cot.shape[1])
            gains = gains + jnp.sum(parts, axis=0)
        c = c_ref[0]
        start_ref[0] = low_dot(c, high_keep[...], TN) + low_dot(c, rest_keep[...], TN)
        rows_ref[0] = gains


def back_kernel(
    head_dim,
    plans,
    base_ref,
    starts_ref,
    x_ref,
    g_ref,
    b_ref,
    c_ref,
    run_ref,
    step_ref,
    carry_ref,
    tail_ref,
    start_ref,
    end_ref,
    pre_ref,
    halo_ref,
    weight_ref,
    bias_ref,
    skip_ref,
    both_in_ref,
    out_sent_ref,
    gate_sent_ref,
    both_ref,
    edge_ref,
    halo_out_ref,
    rows_ref,
    direct_ref,
    decay_ref,
    grad_b_ref,
    grad_c_ref,
    *refs,
):
    refs = list(refs)
    ext, moved, send_sem, recv_sem = refs[-4:]
    me = lax.axis_index("seq")

    def partner(bit):
        return me + (1 << bit) * (1 - 2 * lax.rem(me // (1 << bit), 2))

    def sends():
        copies = []
        for plan, source in zip(plans, (out_sent_ref, gate_sent_ref)):
            for (order, _), columns in zip(plan, part_columns(plan)):
                copies.append(
                    pltpu.make_async_remote_copy(
                        src_ref=source.at[:, columns],
                        dst_ref=refs[len(copies)],
                        send_sem=send_sem.at[len(copies)],
                        recv_sem=recv_sem.at[len(copies)],
                        device_id={"seq": partner(order[0])},
                        device_id_type=pl.DeviceIdType.MESH,
                    )
                )
        return copies

    at_first = (pl.program_id(0) == 0) & (pl.program_id(1) == 0)
    at_last = (pl.program_id(0) == pl.num_programs(0) - 1) & (
        pl.program_id(1) == pl.num_programs(1) - 1
    )
    used = sorted({order[0] for order, _ in plans[0]})

    @pl.when(at_first)
    def _():
        barrier = pltpu.get_barrier_semaphore()
        for bit in used:
            pl.semaphore_signal(
                barrier,
                inc=1,
                device_id={"seq": partner(bit)},
                device_id_type=pl.DeviceIdType.MESH,
            )
        pl.semaphore_wait(barrier, len(used))
        for copy in sends():
            copy.start()

    heads = step_ref.shape[1]
    count = x_ref.shape[1]
    spread = spread_matrix(heads, head_dim)
    x, g, b, c = x_ref[0], g_ref[0], b_ref[0], c_ref[0]
    x_wide, g_wide = x.astype(jnp.float32), g.astype(jnp.float32)
    rows = lax.broadcasted_iota(jnp.int32, (count, count), 0)
    columns = lax.broadcasted_iota(jnp.int32, (count, count), 1)
    valid = pair_labels(count, base_ref, starts_ref, pl.program_id(0)) & (
        columns >= rows
    )
    scores = jnp.where(valid, low_dot(b, c, NT), 0.0)
    upto = (rows >= columns).astype(jnp.bfloat16)
    before = (rows < columns).astype(jnp.float32)
    step = turned(step_ref[0], spread)
    carry = turned(carry_ref[0], spread)
    tail = turned(tail_ref[0], spread)
    scaled_wide = x_wide * step
    scaled, scaled_rest = halves_of(scaled_wide)
    start, end = start_ref[0], end_ref[0]
    run_row = run_ref[0]
    run = turned(run_row, spread_matrix(heads, 1))
    pair = 2 * head_dim
    lane = lax.broadcasted_iota(jnp.int32, (count, pair), 1)
    middle = count // 2
    score_grads = [
        jnp.zeros((middle, count), jnp.float32),
        jnp.zeros((count - middle, count - middle), jnp.float32),
    ]
    results, straddles = [], []
    for first in range(0, heads, 2):
        cut = slice(first * head_dim, first * head_dim + pair)
        g_block = g[:, cut]
        g_swap = jnp.concatenate([g_block[:, head_dim:], g_block[:, :head_dim]], axis=1)
        x_block, x_rest = scaled[:, cut], scaled_rest[:, cut]
        x_rest = jnp.concatenate([x_rest[:, head_dim:], x_rest[:, :head_dim]], axis=1)
        halves = []
        for head in (first, first + 1):
            own = (lane < head_dim) if head == first else (lane >= head_dim)
            x_own, g_own = jnp.where(own, x_block, x_rest), jnp.where(own, g_block, g_swap)
            strips, straddle = [], None
            for part, (top, cut) in enumerate(((0, middle), (middle, count))):
                gap = run_row[head : head + 1, top:] - run[top:cut, head : head + 1]
                fade = jnp.exp2(jnp.minimum(gap, 0.0))
                weights = fade * scores[top:cut, top:]
                strips.append(low_dot(weights, g_block[top:], NN))
                inner = low_dot(x_own[top:cut], g_own[top:], NT)
                score_grads[part] = score_grads[part] + fade * inner
                sums = low_dot(weights * inner, upto[top:, top:], NN)
                sums = jnp.sum(sums * before[top:cut, top:], axis=0, keepdims=True)
                if part == 0:
                    straddle = sums
                else:
                    straddle = jnp.concatenate(
                        [straddle[:, :middle], straddle[:, middle:] + sums], axis=1
                    )
            straddles.append(straddle)
            halves.append(jnp.concatenate(strips, axis=0))
        results.append(jnp.where(lane < head_dim, halves[0], halves[1]))
    score_grad = jnp.concatenate(
        [
            score_grads[0],
            jnp.concatenate([jnp.zeros((count - middle, middle), jnp.float32), score_grads[1]], axis=1),
        ],
        axis=0,
    )
    score_grad = jnp.where(valid, score_grad, 0.0)
    later = map_dot(b, end) * tail
    values = jnp.concatenate(results, axis=1) + later
    inter = map_dot(c, start) * carry
    direct_ref[0] = head_sums(spread, x_wide * values)
    given = head_sums(spread, scaled_wide * later)
    taken = head_sums(spread, g_wide * inter)
    flows = jnp.concatenate([given, taken], axis=0)
    flow_pieces = [item.astype(jnp.bfloat16) for item in thirds_of(flows)]
    after = (rows < columns).astype(jnp.bfloat16)
    flow_later = sum(low_dot(item, after, NN) for item in flow_pieces)
    flow_sooner = sum(low_dot(item, upto, NN) for item in flow_pieces)
    decay_ref[0] = (
        jnp.concatenate(straddles, axis=0) + flow_later[:heads] + flow_sooner[heads:]
    )
    grads_high, grads_low = halves_of(score_grad)
    grad_c = fine_dot(g_wide * carry, start) + low_dot(grads_high, b, TN) + low_dot(grads_low, b, TN)
    grad_b = fine_dot(scaled_wide * tail, end) + low_dot(grads_high, c, NN) + low_dot(grads_low, c, NN)

    @pl.when(pl.program_id(1) == 0)
    def _():
        grad_b_ref[0] = grad_b
        grad_c_ref[0] = grad_c

    @pl.when(pl.program_id(1) > 0)
    def _():
        grad_b_ref[0] = grad_b_ref[0] + grad_b
        grad_c_ref[0] = grad_c_ref[0] + grad_c

    weight, pre = weight_ref[...], pre_ref[0, 0]
    masks = same_segment(count, base_ref, starts_ref, weight.shape[0])
    total = conv_sum(ext, pre, halo_ref[0], weight, bias_ref[...], masks)
    sigma = sigmoid(total)
    grad_conv = (values * step + skip_ref[...] * g_wide) * (
        sigma * (1.0 + total * (1.0 - sigma))
    )
    moved[0:8, :] = jnp.zeros_like(moved[0:8, :])
    moved[8 + count :, :] = jnp.zeros_like(moved[8 + count :, :])
    sums = [jnp.sum(grad_conv * pre, axis=0, keepdims=True)]
    back = jnp.concatenate(
        [jnp.zeros((8, pre.shape[1]), jnp.float32), grad_conv * weight[0:1]], axis=0
    )
    for shift in range(1, weight.shape[0]):
        part = grad_conv * masks[shift - 1]
        sums.append(
            jnp.sum(part * ext[8 - shift : 8 - shift + count, :], axis=0, keepdims=True)
        )
        moved[8 : 8 + count, :] = part * weight[shift : shift + 1]
        back = back + moved[shift : shift + 8 + count, :]
    halo_out_ref[0] = back[:8]
    both_ref[0, 0] = back[8:].astype(jnp.bfloat16)
    edge_ref[0] = back[count:]
    sums.append(jnp.sum(grad_conv, axis=0, keepdims=True))
    sums.append(jnp.sum(g_wide * x_wide, axis=0, keepdims=True))
    sums.append(jnp.sum(start * end, axis=0, keepdims=True))
    sums.append(jnp.zeros((8 - len(sums), pre.shape[1]), jnp.float32))
    rows_ref[0] = jnp.concatenate(sums, axis=0)

    @pl.when(at_last)
    def _():
        for copy in sends():
            copy.wait()


def blocked(kernel, name, grid, ins, outs, scratch=(), micros=0, aliases=None, remote=None):
    moved = sum(item[0].size * item[0].dtype.itemsize for item in ins if item[1] != "any")
    moved += sum(
        math.prod(item[2]) * math.prod(grid) * jnp.dtype(item[1]).itemsize
        for item in outs
        if item[2] != "any"
    )

    def spec(item):
        if item[1] is None:
            return pl.BlockSpec(memory_space=pltpu.SMEM)
        if item[1] == "any":
            return pl.BlockSpec(memory_space=pl.ANY)
        return pl.BlockSpec(item[1], item[2])

    return pl.pallas_call(
        kernel,
        grid=grid,
        in_specs=[spec(item) for item in ins],
        out_specs=[spec(item[1:]) for item in outs],
        out_shape=[jax.ShapeDtypeStruct(item[0], item[1]) for item in outs],
        scratch_shapes=list(scratch),
        input_output_aliases=aliases or {},
        compiler_params=pltpu.CompilerParams(
            dimension_semantics=("arbitrary",) * len(grid),
            vmem_limit_bytes=VMEM_LIMIT,
            collective_id=remote,
            has_side_effects=remote is not None,
        ),
        cost_estimate=pl.CostEstimate(
            flops=micros * 1_000_000_000, bytes_accessed=moved, transcendentals=0
        ),
        name=name,
    )(*[item[0] for item in ins])


def body(
    tokens,
    norm_gain,
    in_weight,
    bc_weight,
    dt_weight,
    dt_bias,
    a_log,
    conv_weight,
    conv_bias,
    bc_conv_weight,
    bc_conv_bias,
    d_skip,
    gate_gain,
    out_weight,
    cotangent,
    seq_lengths,
):
    micro, length, width = tokens.shape
    heads = dt_bias.shape[0]
    inner = conv_bias.shape[0]
    head_dim = inner // heads
    state_size = bc_weight.shape[1] // 2
    taps = conv_weight.shape[0]
    total = micro * length
    head_count = lax.axis_size("head")
    full_inner = inner * head_count
    group = min(HEAD_GROUP, heads)
    groups = heads // group
    wide = group * head_dim
    base = lax.axis_index("seq").astype(jnp.int32) * length
    labels = segment_ids(seq_lengths, base - (taps - 1), length + taps - 1, micro)
    own_labels = labels[:, taps - 1 :]
    before_labels = labels[:, taps - 2]
    starts = jnp.cumsum(seq_lengths, axis=-1).astype(jnp.int32) - seq_lengths
    long_starts = jnp.full((micro - starts.shape[0], starts.shape[1]), FAR, jnp.int32)
    starts = jnp.concatenate([starts, long_starts.at[:, 0].set(0)], axis=0)
    base_item, starts_item = (base[None], None), (starts, None)

    flat = tokens.reshape(total, width).astype(jnp.float32)
    cot_flat = cotangent.reshape(total, width)
    _, norm_back = jax.vjp(rms_scale, flat, norm_gain)
    normed_low, gate_x, bc_pre, delta_pre = project(
        tokens.reshape(total, width), norm_gain, in_weight, bc_weight, dt_weight
    )
    gate_x = gate_x.reshape(2, micro, length, inner)
    bc_pre = bc_pre.reshape(micro, length, 2 * state_size)
    delta_pre = delta_pre.reshape(micro, length, heads).transpose(0, 2, 1)
    left = shifted(
        jnp.concatenate(
            [gate_x[1, :, length - taps + 1 :], bc_pre[:, length - taps + 1 :]], axis=-1
        ),
        "seq",
        1,
    )
    left_x, left_bc = left[..., :inner], left[..., inner:]
    halo = jnp.pad(left_x, ((0, 0), (9 - taps, 0), (0, 0)))
    conv_many = jax.vmap(conv_silu, in_axes=(0, None, None, 0))
    bc_act, bc_conv_back = jax.vjp(
        lambda extended, weight, bias: conv_many(extended, weight, bias, labels),
        jnp.concatenate([left_bc, bc_pre], axis=1),
        bc_conv_weight,
        bc_conv_bias,
    )
    bc_low = bc_act.astype(jnp.bfloat16)
    b_low, c_low = bc_low[..., :state_size], bc_low[..., state_size:]
    (delta, decay), rate_back = jax.vjp(step_sizes, delta_pre, dt_bias, a_log)

    order = jnp.arange(length)
    running = jnp.einsum(
        "mhj,ji->mhi",
        decay,
        (order[:, None] <= order[None, :]).astype(jnp.float32),
        precision=HIGHEST,
    )
    device_log = running[:, :, -1]
    running_two = running * math.log2(math.e)
    live = (own_labels == before_labels[:, None]).astype(jnp.float32)
    last = (own_labels == own_labels[:, -1:]).astype(jnp.float32)
    carried = jnp.exp(running) * live[:, None]
    tail = jnp.exp(device_log[:, :, None] - running) * last[:, None]
    device_live = live[:, -1]
    gain_row, skip_row = gate_gain[None], jnp.repeat(d_skip, head_dim)[None]
    conv_row = conv_bias[None]

    grid = (micro, groups)
    token_block = (1, length, wide)
    in_token = lambda m, k: (m, 0, k)
    half_block = (1, 1, length, wide)
    in_gate, in_x = lambda m, k: (0, m, 0, k), lambda m, k: (1, m, 0, k)
    row_block, in_row = (1, group, length), lambda m, k: (m, k, 0)
    map_block, in_map = (1, length, state_size), lambda m, k: (m, 0, 0)
    state_block, in_state = (1, state_size, wide), in_token
    halo_block = (1, 8, wide)
    flat_block, in_flat = (1, wide), lambda m, k: (0, k)
    conv_item = (conv_weight, (taps, wide), in_flat)
    whole = (micro, length, inner)
    state_shape = (micro, state_size, inner)
    row_shape = (micro, heads, length)

    broad_group = min(BROAD_GROUP, heads)
    broad_groups, broad = heads // broad_group, broad_group * head_dim
    broad_token, broad_half = (1, length, broad), (1, 1, length, broad)
    broad_row, broad_state = (1, broad_group, length), (1, state_size, broad)
    exchange_log = jnp.where(device_live[:, None] > 0.0, device_log, DEAD)
    exchange_log = jnp.repeat(exchange_log, head_dim, axis=1)
    plans = scatter_plans(inner, axis_bits("seq"))
    parts = plans[-1]
    orders = tuple(order for order, _ in parts)
    tiled = (width >> axis_bits("seq")) % 128 == 0
    (incoming, x_low), (grad_gate_n, intra), arranged = exchange(
        (base[None], starts, gate_x, halo, conv_weight, conv_row, b_low, tail * delta),
        exchange_log,
        False,
        (cot_flat, normed_low) if tiled else (),
        orders if tiled else (),
        [
            (plain_steps, (), (cot_flat, out_weight), (total, inner)),
            (
                intra_steps,
                head_dim,
                (base[None], starts, b_low, c_low, running_two, delta, skip_row),
                whole,
            ),
        ],
        head_dim,
    )
    grad_gate_n = grad_gate_n.reshape(whole)
    if not tiled:
        arranged = arrange(cot_flat, orders) + arrange(normed_low, orders)
    cot_parts, normed_parts = arranged[: 2 * len(parts)], arranged[2 * len(parts) :]


    def first_stage(index):
        return lambda p, m, k: index(m + p * (micro - 1 - m), k + p * (broad_groups - 1 - k))

    def second_stage(index):
        return lambda p, m, k: index(m * p, k * p)

    def both_stages(index):
        return lambda p, m, k: index(m, k)

    head_bits = axis_bits("head")
    kept_shape = (micro * broad_groups, length, broad)
    sums_shape = (micro, length, 128)
    normed_gate, grad_gate_pre, grad_gate_x, grad_mixed, device_grad, gate_rows = blocked(
        functools.partial(gate_kernel, head_dim, float(full_inner), head_bits),
        "gate",
        (2, micro, broad_groups),
        [
            (intra, broad_token, first_stage(in_token)),
            (c_low, map_block, both_stages(in_map)),
            (carried, broad_row, both_stages(in_row)),
            (incoming, broad_state, first_stage(in_state)),
            (gate_x, broad_half, first_stage(in_gate)),
            (grad_gate_n, broad_token, first_stage(in_token)),
            (gain_row, (1, broad), both_stages(in_flat)),
        ],
        [
            (whole, jnp.bfloat16, broad_token, second_stage(in_token)),
            (whole, jnp.bfloat16, broad_token, second_stage(in_token)),
            ((2,) + whole, jnp.bfloat16, broad_half, second_stage(in_gate)),
            (whole, jnp.bfloat16, broad_token, second_stage(in_token)),
            (state_shape, jnp.float32, broad_state, second_stage(in_state)),
            ((micro, 8, inner), jnp.float32, (1, 8, broad), second_stage(in_token)),
        ],
        [
            pltpu.VMEM(kept_shape, jnp.float32),
            pltpu.VMEM(kept_shape, jnp.float32),
            pltpu.VMEM(kept_shape, jnp.float32),
            pltpu.VMEM((length, broad), jnp.bfloat16),
            pltpu.VMEM((length, broad), jnp.bfloat16),
            pltpu.VMEM((length, 128), jnp.float32),
            pltpu.VMEM((head_bits + 1,) + sums_shape, jnp.float32),
            pltpu.VMEM((head_bits,) + sums_shape, jnp.float32),
            pltpu.SemaphoreType.DMA((head_bits,)),
            pltpu.SemaphoreType.DMA((head_bits,)),
        ],
        30,
        None,
        4,
    )
    normed_gate = normed_gate.reshape(total, inner)
    grad_gate_pre = grad_gate_pre.reshape(total, inner)
    grad_gate_gain = jnp.sum(gate_rows, axis=(0, 1))

    half_shape = (width // 2, inner)
    paired = head_count == 2
    share = width // head_count
    outgoing, (out_sent, gate_sent), _ = exchange(
        device_grad,
        exchange_log,
        True,
        jobs=[
            (product_steps, plans[0], cot_parts[::2] + [normed_gate], half_shape),
            (product_steps, plans[1], normed_parts[::2] + [grad_gate_pre], half_shape),
        ],
    )
    (
        grad_gate_x,
        edge,
        halo_grad,
        conv_rows,
        direct,
        fading,
        grad_b,
        grad_c,
        *arrivals,
    ) = blocked(
        functools.partial(back_kernel, head_dim, plans),
        "back",
        grid,
        [
            base_item,
            starts_item,
            (x_low, token_block, in_token),
            (grad_mixed, token_block, in_token),
            (b_low, map_block, in_map),
            (c_low, map_block, in_map),
            (running_two, row_block, in_row),
            (delta, row_block, in_row),
            (carried, row_block, in_row),
            (tail, row_block, in_row),
            (incoming, state_block, in_state),
            (outgoing, state_block, in_state),
            (gate_x, half_block, in_x),
            (halo, halo_block, in_token),
            conv_item,
            (conv_row, flat_block, in_flat),
            (skip_row, flat_block, in_flat),
            (grad_gate_x, "any"),
            (out_sent, "any"),
            (gate_sent, "any"),
        ],
        [
            ((2,) + whole, jnp.bfloat16, half_block, in_x),
            ((micro, 8, inner), jnp.float32, halo_block, in_token),
            ((micro, 8, inner), jnp.float32, halo_block, in_token),
            ((micro, 8, inner), jnp.float32, halo_block, in_token),
            (row_shape, jnp.float32, row_block, in_row),
            (row_shape, jnp.float32, row_block, in_row),
            ((micro, length, state_size), jnp.float32, map_block, in_map),
            ((micro, length, state_size), jnp.float32, map_block, in_map),
        ]
        + [
            ((width // 2, sum(widths)), jnp.float32, "any")
            for plan in plans[:2]
            for _, widths in plan
        ],
        [
            pltpu.VMEM((length + 8, wide), jnp.float32),
            pltpu.VMEM((length + 16, wide), jnp.float32),
            pltpu.SemaphoreType.DMA((2 * len(parts),)),
            pltpu.SemaphoreType.DMA((2 * len(parts),)),
        ],
        80,
        {17: 0},
        3,
    )
    arrived = [arrivals[: len(parts)], arrivals[len(parts) :]]
    grad_bc = all_sum(jnp.concatenate([grad_b, grad_c], axis=-1), "head")
    pairs = conv_rows[:, taps + 2].reshape(micro, heads, head_dim)
    kept = jnp.sum(pairs, axis=-1) * jnp.exp(device_log) * device_live[:, None]
    grad_delta_pre, grad_dt_bias, grad_a_log = rate_back((direct, fading + kept[:, :, None]))
    conv_rows = jnp.sum(conv_rows, axis=0)
    grad_conv_weight, grad_conv_bias = conv_rows[:taps], conv_rows[taps]
    grad_d_skip = jnp.sum(conv_rows[taps + 1].reshape(heads, head_dim), axis=-1)
    grad_bc_ext, grad_bc_conv_weight, grad_bc_conv_bias = bc_conv_back(grad_bc)
    right = shifted(
        jnp.concatenate([halo_grad[:, 9 - taps :], grad_bc_ext[:, : taps - 1]], axis=-1), "seq", -1
    )
    right_x, right_bc = right[..., :inner], right[..., inner:]
    grad_gate_x = lax.dynamic_update_slice(
        grad_gate_x,
        (edge[:, 9 - taps :] + right_x).astype(jnp.bfloat16)[None],
        (1, 0, length - taps + 1, 0),
    )
    grad_bc_pre = grad_bc_ext[:, taps - 1 :].at[:, length - taps + 1 :].add(right_bc)
    bc_flat = grad_bc_pre.reshape(total, 2 * state_size)
    grad_gate_x = grad_gate_x.reshape(2, total, inner)
    grad_steps = grad_delta_pre.transpose(0, 2, 1).reshape(total, heads)
    narrow_row = jnp.concatenate([bc_flat * (1.0 / head_count), grad_steps], axis=1)
    if paired:
        row_inputs = (
            in_weight,
            norm_gain[None],
            tokens.reshape(total, width),
            cot_flat,
            narrow_row,
            bc_weight,
            dt_weight,
            normed_gate,
            out_weight,
        )
        gain_grad = jnp.zeros_like(norm_gain)
    else:
        row_inputs = ()
        row_part = lax.dot_general(
            narrow_row,
            jnp.concatenate([bc_weight, dt_weight], axis=1),
            (NT, ((), ())),
            precision=HIGHEST,
            preferred_element_type=jnp.float32,
        ) + jnp.einsum(
            "ktc,dkc->td", grad_gate_x, in_weight, preferred_element_type=jnp.float32
        )
        grad_flat, gain_grad = norm_back(all_sum(row_part, "head"))
        grad_tokens = cot_flat.astype(jnp.float32) + grad_flat
        head_terms = lax.dot_general(
            normed_gate, out_weight, (NT, ((), ())), preferred_element_type=jnp.float32
        )
        summed = lax.psum_scatter(head_terms, "head", scatter_dimension=1, tiled=True)
        residual = lax.dynamic_slice_in_dim(flat, lax.axis_index("head") * share, share, 1)
        block_out = (residual + summed).astype(jnp.bfloat16)

    share_bc = 2 * state_size // head_count
    own_bc = lax.dynamic_slice_in_dim(bc_flat, lax.axis_index("head") * share_bc, share_bc, 1)
    across = share_bc + heads
    side = 0
    narrow_high, narrow_rest = halves_of(jnp.concatenate([own_bc, grad_steps], axis=1))
    both = jnp.concatenate([narrow_high, narrow_rest], axis=1)
    narrow = jnp.concatenate(
        [product(normed_parts[2 * side + 1], both), product(normed_parts[2 * side], both)], axis=0
    )
    narrow = narrow[:, :across] + narrow[:, across:]
    size = lax.axis_size("seq")
    row_count = width // size
    narrow = narrow.reshape(size, row_count, across)
    beside = 128 // heads
    narrow_bc = jnp.pad(narrow[:, :, :share_bc], ((0, 0), (0, 0), (0, -share_bc % 128)))
    narrow_steps = narrow[:, :, share_bc:].reshape(size, row_count // beside, 128)
    narrow_steps = jnp.pad(narrow_steps, ((0, 0), (0, 0), (0, narrow_bc.shape[2] - 128)))
    narrow = jnp.concatenate([narrow_bc, narrow_steps], axis=1)
    narrow_rows = narrow.shape[1]
    narrow = jnp.pad(narrow, ((0, 0), (0, -narrow_rows % 8), (0, 0)))
    narrow = narrow.reshape(-1, narrow.shape[2])

    small = [
        gain_grad,
        grad_bc_conv_weight,
        grad_bc_conv_bias,
        grad_dt_bias,
        grad_a_log,
        grad_d_skip,
        grad_conv_weight,
        grad_conv_bias,
        grad_gate_gain,
    ]
    row = jnp.concatenate([item.reshape(-1) for item in small])
    count = row.size
    row = jnp.pad(row, (0, -count % 1024)).reshape(-1, 128)

    (grad_out_weight, gate_block, x_block), gathered, row, *token_grads = finish(
        plans,
        [
            cot_parts[1::2] + [normed_gate] + arrived[0],
            normed_parts[1::2] + [grad_gate_pre] + arrived[1],
        ],
        normed_parts[::2],
        normed_parts[1::2],
        grad_gate_x,
        narrow,
        row,
        row_inputs,
    )
    if paired:
        grad_tokens, block_out = token_grads
    grad_tokens = grad_tokens.reshape(micro, length, width)
    block_out = block_out.reshape(micro, length, share)
    grad_in_weight = jnp.stack([gate_block, x_block], axis=1)
    grad_bc_weight = head_gather(gathered[:, :row_count, :share_bc].reshape(width, share_bc))
    grad_dt_weight = gathered[:, row_count:narrow_rows, :128].reshape(width, heads)
    row = row.reshape(-1)
    sizes, first = [], 0
    for item in small:
        sizes.append(row[first : first + item.size].reshape(item.shape))
        first += item.size
    (
        grad_norm_gain,
        grad_bc_conv_weight,
        grad_bc_conv_bias,
        grad_dt_bias,
        grad_a_log,
        grad_d_skip,
        grad_conv_weight,
        grad_conv_bias,
        grad_gate_gain,
    ) = sizes

    return (
        block_out,
        grad_tokens,
        grad_norm_gain,
        grad_in_weight,
        grad_bc_weight,
        grad_dt_weight,
        grad_dt_bias,
        grad_a_log,
        grad_d_skip,
        grad_conv_weight,
        grad_conv_bias,
        grad_bc_conv_weight,
        grad_bc_conv_bias,
        grad_gate_gain,
        grad_out_weight,
    )


def solution(mesh):
    return jax.shard_map(
        body,
        mesh=mesh,
        in_specs=(
            P(None, "seq", None),
            P(),
            P(None, None, "head"),
            P(),
            P(None, "head"),
            P("head"),
            P("head"),
            P(None, "head"),
            P("head"),
            P(),
            P(),
            P("head"),
            P("head"),
            P(None, "head"),
            P(None, "seq", None),
            P(),
        ),
        out_specs=(
            P(None, "seq", "head"),
            P(None, "seq", None),
            P(),
            P("seq", None, "head"),
            P(),
            P(None, "head"),
            P("head"),
            P("head"),
            P("head"),
            P(None, "head"),
            P("head"),
            P(),
            P(),
            P("head"),
            P("seq", "head"),
        ),
        check_vma=False,
    )
```
